32 devices in a mesh: lat: 8 (over z, y), lev: 4 (over x, core).
Axes of the slice: x: 2, y: 2, z: 4, core: 2. Of those that a mesh axis runs over, the one named last changes fastest.
Arguments:
- grid: bfloat16 [16, 160, 3200], P('lev', 'lat'), may hold values from -6 to 6
- dep_row: int32 [160, 3200], P('lat'), may hold values from 0 to 158, as said below
- dep_col: int32 [160, 3200], P('lat'), may hold values from 0 to 3199, as said below
- lat_frac: bfloat16 [160, 3200], P('lat'), may hold values from 0 to 1
- lon_frac: bfloat16 [160, 3200], P('lat'), may hold values from 0 to 1
- pair_ids: int32 [8], replicated, may hold values from 1 to 639, as said below
- analysis: bfloat16 [8, 160, 1280], P('lat', None, 'lev'), may hold values from -0.0078125 to 0.0078125
Outputs:
- spectral: float32 [8, 16, 2, 1280], P('lat', None, None, 'lev')
The draws below stay inside these ranges and needn't reach their ends.
Inputs may be any that keep to these rules, and one draw needn't show every extreme that they name: dep_row[j, i] lies from max(j - 2, 0) to min(j + 1, 158). dep_col[j, i] lies within 8 columns of i, modulo 3200. `pair_ids`: all distinct.
All inputs are finite; a program needn't handle non-finite values.
Results may differ from the reference program's by a relative error of at most 0.0046.
Values may be sent and summed in bfloat16 or wider, within the bound.
No kernel may reach another device: no remote copies, remote signals or barrier semaphores. Data moves between devices by JAX's collectives and lax.ppermute only.
A program may use at most 192 MiB of HBM per device.

```python
import math
import jax
import jax.numpy as jnp
from jax import lax

NMAX = 1279
NLON = 3200
REACH = 8
FIELDS = 4
LEVELS = 4
NLAT = 160
NCOL = 1280
PAIRS = 8


def draw_dep_row(key, part):
    key = jax.random.fold_in(key, 11)
    latitude = jnp.arange(NLAT, dtype=jnp.int32)[:, None]
    drift = jax.random.randint(key, (NLAT, NLON), -2, 2)
    return jnp.clip(latitude + drift, 0, NLAT - 2).astype(jnp.int32)


def draw_dep_col(key, part):
    key = jax.random.fold_in(key, 17)
    shift_key, east_key, gap_key = jax.random.split(key, 3)
    longitude = jnp.arange(NLON, dtype=jnp.int32)[None, :]
    shift = jax.random.randint(shift_key, (NLAT, NLON), -REACH, REACH + 1)
    east_most = jax.random.randint(east_key, (NLAT, 1), 0, NLON)
    west_most = (east_most + 1 + jax.random.randint(gap_key, (NLAT, 1), 0, NLON - 1)) % NLON
    shift = jnp.where(longitude == east_most, REACH, shift)
    shift = jnp.where(longitude == west_most, -REACH, shift)
    return ((longitude - shift) % NLON).astype(jnp.int32)


def draw_pair_ids(key, part):
    key = jax.random.fold_in(key, 23)
    first_key, second_key = jax.random.split(key)
    inner = jax.random.permutation(first_key, NMAX // 2 - 2)[:PAIRS - 2].astype(jnp.int32) + 2
    chosen = jnp.concatenate([jnp.array([1, NMAX // 2], dtype=jnp.int32), inner])
    return jax.random.permutation(second_key, chosen).astype(jnp.int32)


def steps_of(key, extent, pieces, smallest, high):
    loudness, own = 1.0, jax.random.fold_in(key, 6)
    for axis_at, parts in pieces:
        steps = jnp.exp(jax.random.uniform(jax.random.fold_in(own, axis_at), (parts,), jnp.float32, smallest / len(pieces), high / len(pieces)))
        loudness = loudness * jnp.repeat(steps, extent[axis_at] // parts).reshape([-1 if axis == axis_at else 1 for axis in range(len(extent))])
    return loudness


def centred(stream_key, extent, scale, bound, cuts=(), held_as=jnp.bfloat16):
    level = steps_of(stream_key, extent, cuts, -0.22, 0.18) if cuts else 1.0
    result = jax.random.normal(stream_key, extent, jnp.float32) * scale * level
    return jnp.minimum(jnp.maximum(result, -bound), bound).astype(held_as)


def setup_inputs(seed: int = 0) -> dict:
    key_list = jax.random.split(jax.random.key(seed), 8)
    grid = centred(key_list[0], (FIELDS * LEVELS, NLAT, NLON), 1.0, 6.0, ((0, 4), (1, 8)))
    dep_row = draw_dep_row(jax.random.fold_in(key_list[7], 71), 0)
    dep_col = draw_dep_col(jax.random.fold_in(key_list[7], 71), 0)
    lat_frac = jnp.clip(1.0 * jax.random.uniform(key_list[3], (NLAT, NLON), jnp.float32) ** steps_of(key_list[3], (NLAT, NLON), ((0, 8),), -0.2, 0.2), 0.0, 1.0).astype(jnp.bfloat16)
    lon_frac = jnp.clip(1.0 * jax.random.uniform(key_list[4], (NLAT, NLON), jnp.float32) ** steps_of(key_list[4], (NLAT, NLON), ((0, 8),), -0.2, 0.2), 0.0, 1.0).astype(jnp.bfloat16)
    pair_ids = draw_pair_ids(jax.random.fold_in(key_list[7], 71), 0)
    analysis = centred(key_list[6], (PAIRS, NLAT, NCOL), (NLAT * NLON) ** -0.5, 0.0078125, ((0, 8), (2, 4)))
    return {"grid": grid, "dep_row": dep_row, "dep_col": dep_col, "lat_frac": lat_frac, "lon_frac": lon_frac, "pair_ids": pair_ids, "analysis": analysis}


def fourier_basis(pair_ids, lon_count):
    longitude = jnp.arange(lon_count, dtype=jnp.int32)
    wavenumbers = jnp.stack([pair_ids, NMAX + 1 - pair_ids], axis=1).astype(jnp.int32)
    phase_turn = (longitude[:, None, None] * wavenumbers[None, :, :]) % lon_count
    angles = phase_turn.astype(jnp.float32) * (2.0 * math.pi / lon_count)
    basis_table = jnp.stack([jnp.cos(angles), -jnp.sin(angles)], axis=3)
    return basis_table.reshape(lon_count, -1).astype(jnp.bfloat16)


def reference(grid, dep_row, dep_col, lat_frac, lon_frac, pair_ids, analysis):
    slice_count = grid.shape[0]
    col_next = (dep_col + 1) % NLON
    row_next = dep_row + 1
    lat_weight = lat_frac.astype(jnp.float32)
    lon_weight = lon_frac.astype(jnp.float32)
    basis = fourier_basis(pair_ids, NLON).astype(jnp.float32)

    def per_slice(field_slab):
        west_low = field_slab[dep_row, dep_col].astype(jnp.float32)
        east_low = field_slab[dep_row, col_next].astype(jnp.float32)
        west_high = field_slab[row_next, dep_col].astype(jnp.float32)
        east_high = field_slab[row_next, col_next].astype(jnp.float32)
        departed = ((1.0 - lat_weight) * ((1.0 - lon_weight) * west_low + lon_weight * east_low)
                    + lat_weight * ((1.0 - lon_weight) * west_high + lon_weight * east_high)).astype(jnp.bfloat16)
        return jnp.dot(departed.astype(jnp.float32), basis, precision=lax.Precision.HIGHEST).astype(jnp.bfloat16)

    fourier = lax.map(per_slice, grid)
    stacked = fourier.reshape(slice_count, NLAT, PAIRS, 4).transpose(2, 0, 1, 3)
    columns = jnp.arange(NCOL, dtype=jnp.int32)

    def per_pair(pair_item):
        coeffs, values, pair_id = pair_item
        products = jnp.einsum("sjq,jc->sqc", coeffs.astype(jnp.float32), values.astype(jnp.float32),
                              precision=lax.Precision.HIGHEST)
        first_wave = (columns < NMAX + 1 - pair_id)[None, None, :]
        return jnp.where(first_wave, products[:, 0:2, :], products[:, 2:4, :])

    return lax.map(per_pair, (stacked, analysis, pair_ids))
```

```python
import functools
import math

import jax
import jax.numpy as jnp
import numpy as np
from jax import lax
from jax.experimental import pallas as pl
from jax.experimental.pallas import tpu as pltpu
from jax.sharding import PartitionSpec as P

NMAX = 1279
LANES = 128
RIM = 2
EDGE = 2 * RIM


def lane_gather(values, indices):
    numbers = lax.GatherDimensionNumbers(
        offset_dims=(),
        collapsed_slice_dims=(1,),
        start_index_map=(1,),
        operand_batching_dims=(0,),
        start_indices_batching_dims=(0,),
    )
    return lax.gather(
        values,
        indices[..., None],
        numbers,
        (1, 1),
        mode=lax.GatherScatterMode.PROMISE_IN_BOUNDS,
    )


def tile_at(t):
    return pl.ds(pl.multiple_of(t * LANES, LANES), LANES)


def neighbours(t, tiles):
    return jnp.where(t == 0, tiles - 1, t - 1), jnp.where(t == tiles - 1, 0, t + 1)


def lane_plan(dep_col, t, lon_count):
    lane = lax.broadcasted_iota(jnp.int32, dep_col.shape, 1)
    shift = dep_col - (lane + t * LANES)
    shift = jnp.where(shift > lon_count // 2, shift - lon_count, shift)
    shift = jnp.where(shift < -(lon_count // 2), shift + lon_count, shift)
    west = lane + shift
    east = west + 1
    west_lane = west & (LANES - 1)
    east_lane = east & (LANES - 1)
    return west_lane, west == west_lane, east_lane, east == east_lane


def row_weights(row_shift, lat_weight):
    low, high = 1.0 - lat_weight, lat_weight
    return [
        jnp.where(row_shift == step, low, 0.0) + jnp.where(row_shift == step - 1, high, 0.0)
        for step in range(-RIM, RIM + 1)
    ]


def interpolate(load, plan, weights, lon_weight):
    west_lane, west_own, east_lane, east_own = plan
    west_sum = east_sum = None
    for position, weight in enumerate(weights):
        own, beside = load(position)
        west = jnp.where(west_own, lane_gather(own, west_lane), lane_gather(beside, west_lane))
        east = jnp.where(east_own, lane_gather(own, east_lane), lane_gather(beside, east_lane))
        west_sum = weight * west if position == 0 else west_sum + weight * west
        east_sum = weight * east if position == 0 else east_sum + weight * east
    return (1.0 - lon_weight) * west_sum + lon_weight * east_sum


def beside_of(west_tile, east_tile):
    lane = lax.broadcasted_iota(jnp.int32, west_tile.shape, 1)
    return jnp.where(lane < LANES // 2, east_tile, west_tile)


def inner_kernel(
    place, pair_ids, grid, dep_row, dep_col, lat_frac, lon_frac,
    inner_out, basis_out, own_tiles, beside_tiles, departed, waves,
):
    slices, band_rows, lon_count = grid.shape
    tiles = lon_count // LANES
    inner = band_rows - 2 * RIM
    orders = basis_out.shape[0]
    first_row = place[0]

    def wave_rows(group, carry):
        row = lax.broadcasted_iota(jnp.int32, (16, LANES), 0)
        pair = pair_ids[4 * group + 3]
        for at in (2, 1, 0):
            pair = jnp.where(row < 4 * (at + 1), pair_ids[4 * group + at], pair)
        wave = jnp.where((row & 2) == 0, pair, NMAX + 1 - pair)
        waves[pl.ds(pl.multiple_of(group * 16, 16), 16), :] = wave.astype(jnp.float32)
        return carry

    lax.fori_loop(0, orders // 16, wave_rows, 0)

    def fill(t, carry):
        before, after = neighbours(t, tiles)
        for f in range(slices):
            own_tiles[t, f, 0:band_rows, :] = grid[f, :, tile_at(t)].astype(jnp.float32)
            beside_tiles[t, f, 0:band_rows, :] = beside_of(
                grid[f, :, tile_at(before)].astype(jnp.float32),
                grid[f, :, tile_at(after)].astype(jnp.float32),
            )
        return carry

    lax.fori_loop(0, tiles, fill, 0)

    def basis_tile(t, group):
        rows = pl.ds(pl.multiple_of(group * 16, 16), 16)
        lane = lax.broadcasted_iota(jnp.int32, (16, LANES), 1)
        row = lax.broadcasted_iota(jnp.int32, (16, LANES), 0)
        longitude = (lane + t * LANES).astype(jnp.float32)
        quarter = jnp.where((row & 1) == 0, 0.0, float(lon_count // 4))
        steps = longitude * waves[rows, :] + quarter
        turns = jnp.floor(steps * (1.0 / lon_count) + 0.5)
        angle = (lon_count // 4 - jnp.abs(steps - turns * lon_count)) * (2.0 * math.pi / lon_count)
        square = angle * angle
        series = jnp.float32(-1.0 / 39916800.0)
        for term in (1.0 / 362880.0, -1.0 / 5040.0, 1.0 / 120.0, -1.0 / 6.0, 1.0):
            series = series * square + term
        basis_out[rows, tile_at(t)] = (angle * series).astype(jnp.bfloat16)

    def tile(t, carry):
        cols = tile_at(t)
        groups = []
        for start in range(RIM, RIM + inner, 8):
            rows = slice(start, start + 8)
            latitude = first_row + start + lax.broadcasted_iota(jnp.int32, (8, LANES), 0)
            plan = lane_plan(dep_col[rows, cols], t, lon_count)
            weights = row_weights(
                dep_row[rows, cols] - latitude, lat_frac[:, cols].astype(jnp.float32)[rows]
            )
            lon_weight = lon_frac[:, cols].astype(jnp.float32)[rows]
            groups.append((start - RIM, plan, weights, lon_weight))
        for f in range(slices):
            parts = [
                interpolate(
                    lambda position, base=base: (
                        own_tiles[t, f, base + position : base + position + 8, :],
                        beside_tiles[t, f, base + position : base + position + 8, :],
                    ),
                    plan,
                    weights,
                    lon_weight,
                )
                for base, plan, weights, lon_weight in groups
            ]
            departed[f * inner : (f + 1) * inner, cols] = jnp.concatenate(parts, axis=0).astype(
                jnp.bfloat16
            )
        if orders <= 64:
            for group in range(orders // 16):
                basis_tile(t, group)
        else:
            lax.fori_loop(0, orders // 16, lambda g, c: (basis_tile(t, g), c)[1], 0)
        return carry

    lax.fori_loop(0, tiles, tile, 0)
    inner_out[...] = lax.dot_general(
        basis_out[...],
        departed[...],
        (((1,), (1,)), ((), ())),
        preferred_element_type=jnp.float32,
    )


def rim_kernel(
    place, low_halo, high_halo, rim_rows, dep_row, dep_col, lat_frac, lon_frac, basis, inner_fourier,
    fourier_out, own_tiles, beside_tiles, departed,
):
    _, slices, lon_count = rim_rows.shape
    band_rows = dep_row.shape[0]
    tiles = lon_count // LANES
    first_row = place[0]

    def source(position, cols):
        if position < RIM:
            low = low_halo[position, :, cols]
        else:
            low = rim_rows[position - RIM, :, cols]
        if position < EDGE:
            high = rim_rows[EDGE + position, :, cols]
        else:
            high = high_halo[position - EDGE, :, cols]
        return jnp.concatenate([low.astype(jnp.float32), high.astype(jnp.float32)], axis=0)

    def fill(t, carry):
        for position in range(RIM + EDGE):
            own_tiles[t, position] = source(position, tile_at(t))
        return carry

    lax.fori_loop(0, tiles, fill, 0)

    def fill_beside(t, carry):
        before, after = neighbours(t, tiles)
        for position in range(RIM + EDGE):
            beside_tiles[t, position] = beside_of(
                own_tiles[before, position], own_tiles[after, position]
            )
        return carry

    lax.fori_loop(0, tiles, fill_beside, 0)

    def spread(values, out_row):
        high_row = band_rows - RIM + out_row
        return jnp.concatenate(
            [
                jnp.broadcast_to(values[row : row + 1], (slices, LANES))
                for row in (out_row, high_row)
            ],
            axis=0,
        )

    def tile(t, carry):
        cols = tile_at(t)
        side = jnp.where(
            lax.broadcasted_iota(jnp.int32, (2 * slices, LANES), 0) < slices, 0, band_rows - RIM
        )
        row_tile, col_tile = dep_row[:, cols], dep_col[:, cols]
        lat_tile = lat_frac[:, cols].astype(jnp.float32)
        lon_tile = lon_frac[:, cols].astype(jnp.float32)
        parts = []
        for out_row in range(RIM):
            plan = lane_plan(spread(col_tile, out_row), t, lon_count)
            weights = row_weights(
                spread(row_tile, out_row) - (first_row + out_row + side),
                spread(lat_tile, out_row),
            )
            parts.append(
                interpolate(
                    lambda position, out_row=out_row: (
                        own_tiles[t, out_row + position],
                        beside_tiles[t, out_row + position],
                    ),
                    plan,
                    weights,
                    spread(lon_tile, out_row),
                )
            )
        departed[:, cols] = jnp.concatenate(parts, axis=0).astype(jnp.bfloat16)
        return carry

    lax.fori_loop(0, tiles, tile, 0)
    rim_fourier = lax.dot_general(
        basis[...],
        departed[...],
        (((1,), (1,)), ((), ())),
        preferred_element_type=jnp.float32,
    )
    for pair in range(fourier_out.shape[0]):
        fourier_out[pair] = jnp.concatenate(
            [inner_fourier[4 * pair : 4 * pair + 4, :], rim_fourier[4 * pair : 4 * pair + 4, :]],
            axis=1,
        ).astype(jnp.bfloat16)


def legendre_kernel(place, pair_ids, coeffs, spread_analysis, out, *, bands, levs, slices):
    rows = spread_analysis.shape[1]
    col_count = spread_analysis.shape[2]
    inner = rows // slices - EDGE
    column = lax.broadcasted_iota(jnp.int32, (1, rows), 1)
    edge_slice = column - inner * slices
    slice_of = jnp.where(edge_slice < 0, column // inner, edge_slice % slices)

    def add(band, total):
        block = jnp.concatenate(
            [coeffs[band * levs + lev, 0].astype(jnp.float32) for lev in range(levs)], axis=0
        )
        masked = jnp.concatenate(
            [jnp.where(slice_of == f, block, 0.0) for f in range(slices)], axis=0
        ).astype(jnp.bfloat16)
        return total + jnp.dot(masked, spread_analysis[band], preferred_element_type=jnp.float32)

    total = jnp.zeros((slices * levs * 4, col_count), jnp.float32)
    if bands <= 16:
        for band in range(bands):
            total = add(band, total)
    else:
        total = lax.fori_loop(0, bands, add, total)
    pair_id = pair_ids[place[0]]
    columns = place[1] + lax.broadcasted_iota(jnp.int32, (2, col_count), 1)
    first_wave = columns < NMAX + 1 - pair_id
    for f in range(slices):
        for lev in range(levs):
            at = (f * levs + lev) * 4
            out[lev * slices + f] = jnp.where(first_wave, total[at : at + 2], total[at + 2 : at + 4])


def shards(grid, dep_row, dep_col, lat_frac, lon_frac, pair_ids, analysis):
    slices, band_rows, lon_count = grid.shape
    pairs = pair_ids.shape[0]
    col_count = analysis.shape[2]
    bands, levs = lax.axis_size("lat"), lax.axis_size("lev")
    inner = band_rows - 2 * RIM
    tiles = lon_count // LANES
    lat_at, lev_at = lax.axis_index("lat"), lax.axis_index("lev")
    band_start = jnp.reshape(lat_at * band_rows, (1,)).astype(jnp.int32)
    vmem = pl.BlockSpec(memory_space=pltpu.VMEM)
    smem = pl.BlockSpec(memory_space=pltpu.SMEM)
    params = pltpu.CompilerParams(vmem_limit_bytes=48 * 2**20)

    rim_rows = jnp.concatenate([grid[:, :EDGE], grid[:, band_rows - EDGE :]], axis=1)
    rim_rows = rim_rows.transpose(1, 0, 2)
    low_halo = lax.ppermute(rim_rows[2 * EDGE - RIM :], "lat", [(i, i + 1) for i in range(bands - 1)])
    high_halo = lax.ppermute(rim_rows[:RIM], "lat", [(i + 1, i) for i in range(bands - 1)])

    tile_shape = (tiles, slices, -(-band_rows // 8) * 8, LANES)
    inner_fourier, basis = pl.pallas_call(
        inner_kernel,
        out_shape=(
            jax.ShapeDtypeStruct((4 * pairs, slices * inner), jnp.float32),
            jax.ShapeDtypeStruct((4 * pairs, lon_count), jnp.bfloat16),
        ),
        in_specs=[smem, smem] + [vmem] * 5,
        out_specs=(vmem, vmem),
        scratch_shapes=[
            pltpu.VMEM(tile_shape, jnp.float32),
            pltpu.VMEM(tile_shape, jnp.float32),
            pltpu.VMEM((slices * inner, lon_count), jnp.bfloat16),
            pltpu.VMEM((4 * pairs, LANES), jnp.float32),
        ],
        compiler_params=params,
        cost_estimate=pl.CostEstimate(flops=100_000_000, bytes_accessed=2_000_000, transcendentals=0),
    )(band_start, pair_ids, grid, dep_row, dep_col, lat_frac, lon_frac)

    fourier = pl.pallas_call(
        rim_kernel,
        out_shape=jax.ShapeDtypeStruct((pairs, 4, slices * band_rows), jnp.bfloat16),
        in_specs=[smem] + [vmem] * 9,
        out_specs=vmem,
        scratch_shapes=[
            pltpu.VMEM((tiles, RIM + EDGE, 2 * slices, LANES), jnp.float32),
            pltpu.VMEM((tiles, RIM + EDGE, 2 * slices, LANES), jnp.float32),
            pltpu.VMEM((2 * RIM * slices, lon_count), jnp.bfloat16),
        ],
        compiler_params=params,
    )(band_start, low_halo, high_halo, rim_rows, dep_row, dep_col, lat_frac, lon_frac, basis, inner_fourier)

    values = analysis[0].reshape(bands, band_rows, col_count)
    spread_rows = [values[:, RIM : RIM + inner]] * slices
    for row in range(RIM):
        spread_rows += [values[:, row : row + 1]] * slices
        spread_rows += [values[:, band_rows - RIM + row : band_rows - RIM + row + 1]] * slices
    spread_analysis = jnp.concatenate(spread_rows, axis=1)

    if bands <= 16:
        coeffs = lax.all_gather(fourier, ("lat", "lev"), axis=0, tiled=False)
        own_block = pl.BlockSpec(
            (bands * levs, 1, 4, slices * band_rows), lambda place: (0, place[0], 0, 0)
        )
        picked = None
    else:
        arrived = lax.all_to_all(fourier, "lat", split_axis=0, concat_axis=0, tiled=True)
        coeffs = lax.all_gather(arrived, "lev", axis=1, tiled=False)
        coeffs = coeffs.reshape(bands * levs, 1, 4, slices * band_rows)
        own_block = pl.BlockSpec((bands * levs, 1, 4, slices * band_rows), lambda *_: (0, 0, 0, 0))
    place = jnp.stack([lat_at, lev_at * col_count]).astype(jnp.int32)
    if bands <= 16:
        coeffs = lax.dynamic_slice_in_dim(coeffs, lat_at, 1, axis=1)
    out = pl.pallas_call(
        functools.partial(legendre_kernel, bands=bands, levs=levs, slices=slices),
        out_shape=jax.ShapeDtypeStruct((levs * slices, 2, col_count), jnp.float32),
        in_specs=[smem, smem, vmem, vmem],
        out_specs=vmem,
        compiler_params=params,
    )(place, pair_ids, coeffs, spread_analysis)
    return out[None]


def solution(mesh):
    return jax.shard_map(
        shards,
        mesh=mesh,
        in_specs=(
            P("lev", "lat", None),
            P("lat", None),
            P("lat", None),
            P("lat", None),
            P("lat", None),
            P(),
            P("lat", None, "lev"),
        ),
        out_specs=P("lat", None, None, "lev"),
        check_vma=False,
    )
```

```python
import functools
import math

import jax
import jax.numpy as jnp
from jax import lax
from jax.experimental import pallas as pl
from jax.experimental.pallas import tpu as pltpu
from jax.sharding import PartitionSpec as P

NMAX = 1279
LANES = 128
RIM = 2
EDGE = 2 * RIM
REACH = 8
SPAN = LANES - 2 * REACH - 1
CODE = 4096


def lane_gather(values, indices):
    numbers = lax.GatherDimensionNumbers(
        offset_dims=(),
        collapsed_slice_dims=(1,),
        start_index_map=(1,),
        operand_batching_dims=(0,),
        start_indices_batching_dims=(0,),
    )
    return lax.gather(
        values,
        indices[..., None],
        numbers,
        (1, 1),
        mode=lax.GatherScatterMode.PROMISE_IN_BOUNDS,
    )


def tile_at(t):
    return pl.ds(pl.multiple_of(t * LANES, LANES), LANES)


def cut_of(start, lon_count):
    tiles = lon_count // LANES
    start = start + lon_count
    first = start // LANES
    first = jnp.where(first >= tiles, first - tiles, first)
    second = jnp.where(first == tiles - 1, 0, first + 1)
    return tile_at(first), tile_at(second), start % LANES


def join(first, second, lane_at):
    lane = lax.broadcasted_iota(jnp.int32, first.shape, 1)
    return jnp.where(lane >= lane_at, first, second)


def turn(joined, lane_at):
    return pltpu.roll(joined, (LANES - lane_at) % LANES, 1)


def lane_plan(code, start, latitude, lon_count):
    west = (code & (CODE - 1)) - (start - REACH)
    west = jnp.where(west > lon_count // 2, west - lon_count, west)
    west = jnp.where(west < -(lon_count // 2), west + lon_count, west)
    west_lane = (west & (LANES - 1)).astype(jnp.int16)
    east_lane = ((west + 1) & (LANES - 1)).astype(jnp.int16)
    row_shift = (code // CODE - latitude).astype(jnp.float32).astype(jnp.bfloat16)
    return west_lane, east_lane, row_shift


def corner_weights(lat_weight, lon_weight):
    south, north = 1.0 - lat_weight, lat_weight
    west, east = 1.0 - lon_weight, lon_weight
    return south * west, south * east, north * west, north * east


def interpolate(sources, plan, weights):
    west_lane, east_lane, row_shift = plan
    masks = [row_shift == float(step) for step in range(-RIM, RIM - 1)]

    def pick(gathered):
        low, high = gathered[2 * RIM - 1], gathered[2 * RIM]
        for position in range(2 * RIM - 2, -1, -1):
            low = jnp.where(masks[position], gathered[position], low)
            high = jnp.where(masks[position], gathered[position + 1], high)
        return low.astype(jnp.float32), high.astype(jnp.float32)

    west_low, west_high = pick([lane_gather(source, west_lane) for source in sources])
    east_low, east_high = pick([lane_gather(source, east_lane) for source in sources])
    departed = (
        weights[0] * west_low
        + weights[1] * east_low
        + weights[2] * west_high
        + weights[3] * east_high
    )
    return departed.astype(jnp.bfloat16)


def inner_kernel(
    place, pair_ids, grid, dep_row, dep_col, lat_frac, lon_frac,
    inner_out, basis_out, windows, plans, departed, waves,
):
    slices, band_rows, lon_count = grid.shape
    inner = band_rows - 2 * RIM
    orders = basis_out.shape[0]
    first_row = place[0]

    def wave_rows(group, carry):
        row = lax.broadcasted_iota(jnp.int32, (16, LANES), 0)
        pair = jnp.full((16, LANES), pair_ids[4 * group + 3], jnp.int32)
        for at in (2, 1, 0):
            pair = jnp.where(row < 4 * (at + 1), pair_ids[4 * group + at], pair)
        wave = jnp.where((row & 2) == 0, pair, NMAX + 1 - pair)
        waves[pl.ds(pl.multiple_of(group * 16, 16), 16), :] = wave.astype(jnp.float32)
        return carry

    lax.fori_loop(0, orders // 16, wave_rows, 0)

    def basis_tile(t, group):
        rows = pl.ds(pl.multiple_of(group * 16, 16), 16)
        lane = lax.broadcasted_iota(jnp.int32, (16, LANES), 1)
        row = lax.broadcasted_iota(jnp.int32, (16, LANES), 0)
        longitude = lane + t * SPAN
        quarter = jnp.where((row & 1) == 0, 0.0, float(lon_count // 4))
        steps = longitude.astype(jnp.float32) * waves[rows, :] + quarter
        turns = jnp.floor(steps * (1.0 / lon_count) + 0.5)
        angle = (lon_count // 4 - jnp.abs(steps - turns * lon_count)) * (2.0 * math.pi / lon_count)
        square = angle * angle
        series = jnp.float32(-1.0 / 39916800.0)
        for term in (1.0 / 362880.0, -1.0 / 5040.0, 1.0 / 120.0, -1.0 / 6.0, 1.0):
            series = series * square + term
        held = (lane < SPAN) & (longitude < lon_count)
        basis_out[rows, tile_at(t)] = jnp.where(held, angle * series, 0.0).astype(jnp.bfloat16)

    def window(t, slot):
        start = t * SPAN
        first, second, lane_at = cut_of(start - REACH, lon_count)
        for f in range(slices):
            joined = join(
                grid[f, :, first].astype(jnp.float32),
                grid[f, :, second].astype(jnp.float32),
                lane_at,
            )
            windows[slot, f, 0:band_rows, :] = turn(joined, lane_at)
        first, second, lane_at = cut_of(start, lon_count)
        plans[slot, 0, 0:band_rows, :] = join(
            (dep_row[:, first] * CODE + dep_col[:, first]).astype(jnp.float32),
            (dep_row[:, second] * CODE + dep_col[:, second]).astype(jnp.float32),
            lane_at,
        )
        for at, frac in ((1, lat_frac), (2, lon_frac)):
            plans[slot, at, 0:band_rows, :] = join(
                frac[:, first].astype(jnp.float32), frac[:, second].astype(jnp.float32), lane_at
            )
        code, lat_weight, lon_weight = [
            turn(plans[slot, at, RIM : RIM + inner, :], lane_at) for at in range(3)
        ]
        latitude = first_row + RIM + lax.broadcasted_iota(jnp.int32, (inner, LANES), 0)
        plan = lane_plan(code.astype(jnp.int32), start, latitude, lon_count)
        weights = corner_weights(lat_weight, lon_weight)
        for f in range(slices):
            sources = [
                windows[slot, f, position : position + inner, :].astype(jnp.bfloat16)
                for position in range(2 * RIM + 1)
            ]
            departed[f * inner : (f + 1) * inner, tile_at(t)] = interpolate(sources, plan, weights)
        if orders <= 64:
            for group in range(orders // 16):
                basis_tile(t, group)
        else:
            lax.fori_loop(0, orders // 16, lambda g, c: (basis_tile(t, g), c)[1], 0)

    count = basis_out.shape[1] // LANES

    def pair_of_windows(step, carry):
        window(2 * step, 0)
        window(2 * step + 1, 1)
        return carry

    lax.fori_loop(0, count // 2, pair_of_windows, 0)
    if count % 2:
        window(count - 1, 0)
    inner_out[...] = lax.dot_general(
        basis_out[...],
        departed[...],
        (((1,), (1,)), ((), ())),
        preferred_element_type=jnp.float32,
    )


def rim_kernel(
    place, low_halo, high_halo, rim_rows, dep_row, dep_col, lat_frac, lon_frac, basis, inner_fourier,
    fourier_out, plans, departed,
):
    _, slices, lon_count = rim_rows.shape
    band_rows = dep_row.shape[0]
    first_row = place[0]
    last = band_rows // 8 * 8

    def source(position, cols):
        if position < RIM:
            low = low_halo[position, :, cols]
        else:
            low = rim_rows[position - RIM, :, cols]
        if position < EDGE:
            high = rim_rows[EDGE + position, :, cols]
        else:
            high = high_halo[position - EDGE, :, cols]
        return jnp.concatenate([low.astype(jnp.float32), high.astype(jnp.float32)], axis=0)

    def spread(slot, at):
        pieces = []
        for out_row in range(RIM):
            for row in (out_row, 8 + band_rows - RIM + out_row - last):
                pieces.append(
                    jnp.broadcast_to(plans[slot, at, row : row + 1, :], (slices, LANES))
                )
        return jnp.concatenate(pieces, axis=0)

    def window(t, slot):
        start = t * SPAN
        first, second, lane_at = cut_of(start - REACH, lon_count)
        tiles = [
            turn(join(source(position, first), source(position, second), lane_at), lane_at)
            for position in range(RIM + EDGE)
        ]
        first, second, lane_at = cut_of(start, lon_count)
        codes = [
            (dep_row[:, cols] * CODE + dep_col[:, cols]).astype(jnp.float32)
            for cols in (first, second)
        ]
        arrays = [codes] + [
            [frac[:, cols].astype(jnp.float32) for cols in (first, second)]
            for frac in (lat_frac, lon_frac)
        ]
        for at, (west_part, east_part) in enumerate(arrays):
            plans[slot, at, 0:8, :] = turn(join(west_part[:8], east_part[:8], lane_at), lane_at)
            plans[slot, at, 8 : 8 + band_rows - last, :] = turn(
                join(west_part[last:], east_part[last:], lane_at), lane_at
            )
        place_of = lax.broadcasted_iota(jnp.int32, (2 * RIM * slices, LANES), 0)
        latitude = (
            first_row
            + place_of // (2 * slices)
            + jnp.where(place_of % (2 * slices) < slices, 0, band_rows - RIM)
        )
        plan = lane_plan(spread(slot, 0).astype(jnp.int32), start, latitude, lon_count)
        weights = corner_weights(spread(slot, 1), spread(slot, 2))
        sources = [
            jnp.concatenate(tiles[position : position + RIM], axis=0).astype(jnp.bfloat16)
            for position in range(2 * RIM + 1)
        ]
        departed[:, tile_at(t)] = interpolate(sources, plan, weights)

    count = basis.shape[1] // LANES

    def pair_of_windows(step, carry):
        window(2 * step, 0)
        window(2 * step + 1, 1)
        return carry

    lax.fori_loop(0, count // 2, pair_of_windows, 0)
    if count % 2:
        window(count - 1, 0)
    rim_fourier = lax.dot_general(
        basis[...],
        departed[...],
        (((1,), (1,)), ((), ())),
        preferred_element_type=jnp.float32,
    )
    levs = fourier_out.shape[1]
    for pair in range(fourier_out.shape[0]):
        block = jnp.concatenate(
            [inner_fourier[4 * pair : 4 * pair + 4, :], rim_fourier[4 * pair : 4 * pair + 4, :]],
            axis=1,
        ).astype(jnp.bfloat16)
        for lev in range(levs):
            fourier_out[pair, lev] = block


def legendre_kernel(place, pair_ids, coeffs, spread_analysis, out, *, bands, levs, slices):
    rows = spread_analysis.shape[1]
    col_count = spread_analysis.shape[2]
    inner = rows // slices - EDGE
    column = lax.broadcasted_iota(jnp.int32, (1, rows), 1)
    edge_slice = column - inner * slices
    slice_of = jnp.where(edge_slice < 0, column // inner, edge_slice % slices)

    def add(band, total):
        block = jnp.concatenate(
            [coeffs[band * levs + lev].astype(jnp.float32) for lev in range(levs)], axis=0
        )
        masked = jnp.concatenate(
            [jnp.where(slice_of == f, block, 0.0) for f in range(slices)], axis=0
        ).astype(jnp.bfloat16)
        return total + jnp.dot(masked, spread_analysis[band], preferred_element_type=jnp.float32)

    total = jnp.zeros((slices * levs * 4, col_count), jnp.float32)
    if bands <= 16:
        for band in range(bands):
            total = add(band, total)
    else:
        total = lax.fori_loop(0, bands, add, total)
    pair_id = pair_ids[place[0]]
    columns = place[1] + lax.broadcasted_iota(jnp.int32, (2, col_count), 1)
    first_wave = columns < NMAX + 1 - pair_id
    for f in range(slices):
        for lev in range(levs):
            at = (f * levs + lev) * 4
            out[lev * slices + f] = jnp.where(first_wave, total[at : at + 2], total[at + 2 : at + 4])


def shards(grid, dep_row, dep_col, lat_frac, lon_frac, pair_ids, analysis):
    slices, band_rows, lon_count = grid.shape
    pairs = pair_ids.shape[0]
    col_count = analysis.shape[2]
    bands, levs = lax.axis_size("lat"), lax.axis_size("lev")
    inner = band_rows - 2 * RIM
    lat_at, lev_at = lax.axis_index("lat"), lax.axis_index("lev")
    band_start = jnp.reshape(lat_at * band_rows, (1,)).astype(jnp.int32)
    vmem = pl.BlockSpec(memory_space=pltpu.VMEM)
    smem = pl.BlockSpec(memory_space=pltpu.SMEM)
    params = pltpu.CompilerParams(vmem_limit_bytes=48 * 2**20)

    rim_rows = jnp.concatenate([grid[:, :EDGE], grid[:, band_rows - EDGE :]], axis=1)
    rim_rows = rim_rows.transpose(1, 0, 2)
    low_halo = lax.ppermute(rim_rows[2 * EDGE - RIM :], "lat", [(i, i + 1) for i in range(bands - 1)])
    high_halo = lax.ppermute(rim_rows[:RIM], "lat", [(i + 1, i) for i in range(bands - 1)])

    windows = -(-lon_count // SPAN)
    held_rows = -(-band_rows // 8) * 8
    inner_fourier, basis = pl.pallas_call(
        inner_kernel,
        out_shape=(
            jax.ShapeDtypeStruct((4 * pairs, slices * inner), jnp.float32),
            jax.ShapeDtypeStruct((4 * pairs, windows * LANES), jnp.bfloat16),
        ),
        in_specs=[smem, smem] + [vmem] * 5,
        out_specs=(vmem, vmem),
        scratch_shapes=[
            pltpu.VMEM((2, slices, held_rows, LANES), jnp.float32),
            pltpu.VMEM((2, 3, held_rows, LANES), jnp.float32),
            pltpu.VMEM((slices * inner, windows * LANES), jnp.bfloat16),
            pltpu.VMEM((4 * pairs, LANES), jnp.float32),
        ],
        compiler_params=params,
        cost_estimate=pl.CostEstimate(flops=100_000_000, bytes_accessed=2_000_000, transcendentals=0),
    )(band_start, pair_ids, grid, dep_row, dep_col, lat_frac, lon_frac)

    fourier = pl.pallas_call(
        rim_kernel,
        out_shape=jax.ShapeDtypeStruct((pairs, levs, 4, slices * band_rows), jnp.bfloat16),
        in_specs=[smem] + [vmem] * 9,
        out_specs=vmem,
        scratch_shapes=[
            pltpu.VMEM((2, 3, 16, LANES), jnp.float32),
            pltpu.VMEM((2 * RIM * slices, windows * LANES), jnp.bfloat16),
        ],
        compiler_params=params,
    )(band_start, low_halo, high_halo, rim_rows, dep_row, dep_col, lat_frac, lon_frac, basis, inner_fourier)

    values = analysis[0].reshape(bands, band_rows, col_count)
    spread_rows = [values[:, RIM : RIM + inner]] * slices
    for row in range(RIM):
        spread_rows += [values[:, row : row + 1]] * slices
        spread_rows += [values[:, band_rows - RIM + row : band_rows - RIM + row + 1]] * slices
    spread_analysis = jnp.concatenate(spread_rows, axis=1)

    coeffs = lax.all_to_all(
        fourier.reshape(pairs * levs, 4, slices * band_rows),
        ("lat", "lev"),
        split_axis=0,
        concat_axis=0,
        tiled=True,
    )
    place = jnp.stack([lat_at, lev_at * col_count]).astype(jnp.int32)
    out = pl.pallas_call(
        functools.partial(legendre_kernel, bands=bands, levs=levs, slices=slices),
        out_shape=jax.ShapeDtypeStruct((levs * slices, 2, col_count), jnp.float32),
        in_specs=[smem, smem, vmem, vmem],
        out_specs=vmem,
        compiler_params=params,
    )(place, pair_ids, coeffs, spread_analysis)
    return out[None]


def solution(mesh):
    return jax.shard_map(
        shards,
        mesh=mesh,
        in_specs=(
            P("lev", "lat", None),
            P("lat", None),
            P("lat", None),
            P("lat", None),
            P("lat", None),
            P(),
            P("lat", None, "lev"),
        ),
        out_specs=P("lat", None, None, "lev"),
        check_vma=False,
    )
```

```python
import functools
import math

import jax
import jax.numpy as jnp
from jax import lax
from jax.experimental import pallas as pl
from jax.experimental.pallas import tpu as pltpu
from jax.sharding import PartitionSpec as P

NMAX = 1279
LANES = 128
RIM = 2
EDGE = 2 * RIM
REACH = 8
SPAN = LANES - 2 * REACH - 1
ROW_CODE = 32
AT_ONCE = 4


def lane_gather(values, indices):
    numbers = lax.GatherDimensionNumbers(
        offset_dims=(),
        collapsed_slice_dims=(1,),
        start_index_map=(1,),
        operand_batching_dims=(0,),
        start_indices_batching_dims=(0,),
    )
    return lax.gather(
        values,
        indices[..., None],
        numbers,
        (1, 1),
        mode=lax.GatherScatterMode.PROMISE_IN_BOUNDS,
    )


def tile_at(t):
    return pl.ds(pl.multiple_of(t * LANES, LANES), LANES)


def cut_of(start, lon_count):
    tiles = lon_count // LANES
    start = start + lon_count
    first = start // LANES
    first = jnp.where(first >= tiles, first - tiles, first)
    second = jnp.where(first == tiles - 1, 0, first + 1)
    return tile_at(first), tile_at(second), start % LANES


def cut(first, second, lane_at):
    lane = lax.broadcasted_iota(jnp.int32, first.shape, 1).astype(jnp.int16)
    joined = jnp.where(lane >= jnp.asarray(lane_at, jnp.int16), first, second)
    return pltpu.roll(joined, (LANES - lane_at) % LANES, 1)


def lane_plan(code):
    code = code.astype(jnp.int32)
    west = lax.broadcasted_iota(jnp.int32, code.shape, 1) + code % ROW_CODE
    west_lane = (west & (LANES - 1)).astype(jnp.int16)
    east_lane = ((west + 1) & (LANES - 1)).astype(jnp.int16)
    row_step = (code // ROW_CODE).astype(jnp.float32).astype(jnp.bfloat16)
    return west_lane, east_lane, row_step


def corner_weights(lat_weight, lon_weight):
    south, north = 1.0 - lat_weight, lat_weight
    west, east = 1.0 - lon_weight, lon_weight
    return south * west, south * east, north * west, north * east


def interpolate(sources, plan, weights):
    west_lane, east_lane, row_step = plan
    masks = [row_step == float(step) for step in range(2 * RIM - 1)]

    def pick(gathered):
        low, high = gathered[2 * RIM - 1], gathered[2 * RIM]
        for position in range(2 * RIM - 2, -1, -1):
            low = jnp.where(masks[position], gathered[position], low)
            high = jnp.where(masks[position], gathered[position + 1], high)
        return low.astype(jnp.float32), high.astype(jnp.float32)

    west_low, west_high = pick([lane_gather(source, west_lane) for source in sources])
    east_low, east_high = pick([lane_gather(source, east_lane) for source in sources])
    departed = (
        weights[0] * west_low
        + weights[1] * east_low
        + weights[2] * west_high
        + weights[3] * east_high
    )
    return departed.astype(jnp.bfloat16)


def in_steps(count, at_once, window):
    def several(step, carry):
        for slot in range(at_once):
            window(step * at_once + slot, slot)
        return carry

    lax.fori_loop(0, count // at_once, several, 0)
    for slot in range(count % at_once):
        window(count - count % at_once + slot, slot)


def pack_kernel(
    place, grid, dep_row, dep_col, lat_frac, lon_frac, own_out, sent_out, plan_out, held
):
    slices, band_rows, lon_count = grid.shape
    inner = band_rows - 2 * RIM
    first_row = place[0]
    fields = slices * EDGE

    def tile(t, slot):
        cols = tile_at(t)
        row = lax.broadcasted_iota(jnp.int32, (band_rows, LANES), 0)
        lane = lax.broadcasted_iota(jnp.int32, (band_rows, LANES), 1)
        shift = dep_col[:, cols] - (lane + t * LANES)
        shift = jnp.where(shift > lon_count // 2, shift - lon_count, shift)
        shift = jnp.where(shift < -(lon_count // 2), shift + lon_count, shift)
        row_step = dep_row[:, cols] - (first_row + row) + RIM
        held[slot, 0, 0:band_rows, :] = (row_step * ROW_CODE + shift + REACH).astype(jnp.float32)
        held[slot, 1, 0:band_rows, :] = lat_frac[:, cols].astype(jnp.float32)
        held[slot, 2, 0:band_rows, :] = lon_frac[:, cols].astype(jnp.float32)
        values = [grid[f, :, cols].astype(jnp.float32) for f in range(slices)]
        for out, start, plan_start in (
            (own_out, 0, 0),
            (sent_out, band_rows - EDGE, band_rows - RIM),
        ):
            block = [value[start : start + EDGE] for value in values]
            block += [held[slot, at, plan_start : plan_start + RIM, :] for at in range(3)]
            block.append(jnp.zeros((RIM, LANES), jnp.float32))
            out[:, cols] = jnp.concatenate(block, axis=0).astype(jnp.bfloat16)
        for at in range(3):
            plan_out[at * inner : (at + 1) * inner, cols] = held[
                slot, at, RIM : RIM + inner, :
            ].astype(jnp.bfloat16)

    in_steps(lon_count // LANES, 5, tile)


def inner_kernel(
    pair_ids, grid, plans, inner_out, basis_out, windows, departed, waves
):
    slices, band_rows, lon_count = grid.shape
    inner = band_rows - 2 * RIM
    orders = basis_out.shape[0]

    def wave_rows(group, carry):
        row = lax.broadcasted_iota(jnp.int32, (16, LANES), 0)
        pair = jnp.full((16, LANES), pair_ids[4 * group + 3], jnp.int32)
        for at in (2, 1, 0):
            pair = jnp.where(row < 4 * (at + 1), pair_ids[4 * group + at], pair)
        wave = jnp.where((row & 2) == 0, pair, NMAX + 1 - pair)
        waves[pl.ds(pl.multiple_of(group * 16, 16), 16), :] = wave.astype(jnp.float32)
        return carry

    lax.fori_loop(0, orders // 16, wave_rows, 0)

    def basis_tile(t, group):
        rows = pl.ds(pl.multiple_of(group * 16, 16), 16)
        lane = lax.broadcasted_iota(jnp.int32, (16, LANES), 1)
        row = lax.broadcasted_iota(jnp.int32, (16, LANES), 0)
        longitude = lane + t * SPAN
        quarter = jnp.where((row & 1) == 0, 0.0, float(lon_count // 4))
        steps = longitude.astype(jnp.float32) * waves[rows, :] + quarter
        turns = jnp.floor(steps * (1.0 / lon_count) + 0.5)
        angle = (lon_count // 4 - jnp.abs(steps - turns * lon_count)) * (2.0 * math.pi / lon_count)
        square = angle * angle
        series = jnp.float32(-1.0 / 39916800.0)
        for term in (1.0 / 362880.0, -1.0 / 5040.0, 1.0 / 120.0, -1.0 / 6.0, 1.0):
            series = series * square + term
        taken = (lane < SPAN) & (longitude < lon_count)
        basis_out[rows, tile_at(t)] = jnp.where(taken, angle * series, 0.0).astype(jnp.bfloat16)

    def window(t, slot):
        first, second, lane_at = cut_of(t * SPAN - REACH, lon_count)
        for f in range(slices):
            windows[slot, f, 0:band_rows, :] = cut(
                grid[f, :, first], grid[f, :, second], lane_at
            ).astype(jnp.float32)
        first, second, lane_at = cut_of(t * SPAN, lon_count)
        code, lat_weight, lon_weight = [
            cut(
                plans[at * inner : (at + 1) * inner, first],
                plans[at * inner : (at + 1) * inner, second],
                lane_at,
            ).astype(jnp.float32)
            for at in range(3)
        ]
        plan = lane_plan(code)
        weights = corner_weights(lat_weight, lon_weight)
        for f in range(slices):
            sources = [
                windows[slot, f, position : position + inner, :].astype(jnp.bfloat16)
                for position in range(2 * RIM + 1)
            ]
            departed[f * inner : (f + 1) * inner, tile_at(t)] = interpolate(sources, plan, weights)
        if orders <= 64:
            for group in range(orders // 16):
                basis_tile(t, group)
        else:
            lax.fori_loop(0, orders // 16, lambda g, c: (basis_tile(t, g), c)[1], 0)

    in_steps(basis_out.shape[1] // LANES, 2, window)
    inner_out[...] = lax.dot_general(
        basis_out[...],
        departed[...],
        (((1,), (1,)), ((), ())),
        preferred_element_type=jnp.float32,
    )


def rim_kernel(arrived, own, basis, inner_fourier, fourier_out, windows, plans, departed, *, slices):
    lon_count = arrived.shape[1]
    fields = slices * EDGE
    sublane = lax.broadcasted_iota(jnp.int32, (2 * EDGE, LANES), 0)

    def window(t, slot):
        first, second, lane_at = cut_of(t * SPAN - REACH, lon_count)
        for side, ref in enumerate((arrived, own)):
            block = cut(ref[0:fields, first], ref[0:fields, second], lane_at).astype(jnp.float32)
            for f in range(slices):
                at = 2 * EDGE * (f + 1) + EDGE * side
                windows[slot, at : at + EDGE, :] = block[f * EDGE : (f + 1) * EDGE]
        first, second, lane_at = cut_of(t * SPAN, lon_count)
        for side, ref in enumerate((arrived, own)):
            block = cut(ref[fields:, first], ref[fields:, second], lane_at).astype(jnp.float32)
            for at in range(3):
                for copy in range(2):
                    row = EDGE * copy + RIM * side
                    plans[slot, at, row : row + RIM, :] = block[RIM * at : RIM * (at + 1)]
        code, lat_weight, lon_weight = [
            jnp.concatenate([plans[slot, at]] * (slices // 2), axis=0) for at in range(3)
        ]
        plan = lane_plan(code)
        weights = corner_weights(lat_weight, lon_weight)

        def source(position):
            pieces = []
            for f in range(0, slices, 2):
                low = 2 * EDGE * (f + 1) + position
                high = 2 * EDGE * (f + 2) + position - EDGE
                pieces.append(
                    jnp.where(
                        sublane < EDGE,
                        windows[slot, low : low + 2 * EDGE, :],
                        windows[slot, high : high + 2 * EDGE, :],
                    )
                )
            return jnp.concatenate(pieces, axis=0).astype(jnp.bfloat16)

        sources = [source(position) for position in range(2 * RIM + 1)]
        departed[:, tile_at(t)] = interpolate(sources, plan, weights)

    in_steps(basis.shape[1] // LANES, AT_ONCE, window)
    rim_fourier = lax.dot_general(
        basis[...],
        departed[...],
        (((1,), (1,)), ((), ())),
        preferred_element_type=jnp.float32,
    )
    levs = fourier_out.shape[1]
    for pair in range(fourier_out.shape[0]):
        block = jnp.concatenate(
            [inner_fourier[4 * pair : 4 * pair + 4, :], rim_fourier[4 * pair : 4 * pair + 4, :]],
            axis=1,
        ).astype(jnp.bfloat16)
        for lev in range(levs):
            fourier_out[pair, lev] = block


def legendre_kernel(place, pair_ids, coeffs, spread_analysis, out, *, bands, levs, slices):
    rows = spread_analysis.shape[1]
    col_count = spread_analysis.shape[2]
    inner = rows // slices - EDGE
    column = lax.broadcasted_iota(jnp.int32, (1, rows), 1)
    rim_at = column - inner * slices
    slice_of = jnp.where(rim_at < 0, column // inner, rim_at // EDGE)

    def add(band, total):
        block = jnp.concatenate(
            [coeffs[band * levs + lev].astype(jnp.float32) for lev in range(levs)], axis=0
        )
        masked = jnp.concatenate(
            [jnp.where(slice_of == f, block, 0.0) for f in range(slices)], axis=0
        ).astype(jnp.bfloat16)
        return total + jnp.dot(masked, spread_analysis[band], preferred_element_type=jnp.float32)

    total = jnp.zeros((slices * levs * 4, col_count), jnp.float32)
    if bands <= 16:
        for band in range(bands):
            total = add(band, total)
    else:
        total = lax.fori_loop(0, bands, add, total)
    pair_id = pair_ids[place[0]]
    columns = place[1] + lax.broadcasted_iota(jnp.int32, (2, col_count), 1)
    first_wave = columns < NMAX + 1 - pair_id
    for f in range(slices):
        for lev in range(levs):
            at = (f * levs + lev) * 4
            out[lev * slices + f] = jnp.where(first_wave, total[at : at + 2], total[at + 2 : at + 4])


def shards(grid, dep_row, dep_col, lat_frac, lon_frac, pair_ids, analysis):
    slices, band_rows, lon_count = grid.shape
    pairs = pair_ids.shape[0]
    col_count = analysis.shape[2]
    bands, levs = lax.axis_size("lat"), lax.axis_size("lev")
    inner = band_rows - 2 * RIM
    windows = -(-lon_count // SPAN)
    held_rows = -(-band_rows // 8) * 8
    lat_at, lev_at = lax.axis_index("lat"), lax.axis_index("lev")
    band_start = jnp.reshape(lat_at * band_rows, (1,)).astype(jnp.int32)
    vmem = pl.BlockSpec(memory_space=pltpu.VMEM)
    smem = pl.BlockSpec(memory_space=pltpu.SMEM)
    params = pltpu.CompilerParams(vmem_limit_bytes=48 * 2**20)

    rim_shape = jax.ShapeDtypeStruct((slices * EDGE + 4 * RIM, lon_count), jnp.bfloat16)
    own_rim, sent_rim, plans = pl.pallas_call(
        pack_kernel,
        out_shape=(
            rim_shape,
            rim_shape,
            jax.ShapeDtypeStruct((3 * inner, lon_count), jnp.bfloat16),
        ),
        in_specs=[smem] + [vmem] * 5,
        out_specs=(vmem,) * 3,
        scratch_shapes=[pltpu.VMEM((5, 3, held_rows, LANES), jnp.float32)],
        compiler_params=params,
    )(band_start, grid, dep_row, dep_col, lat_frac, lon_frac)
    arrived_rim = lax.ppermute(sent_rim, "lat", [(i, (i + 1) % bands) for i in range(bands)])

    inner_fourier, basis = pl.pallas_call(
        inner_kernel,
        out_shape=(
            jax.ShapeDtypeStruct((4 * pairs, slices * inner), jnp.float32),
            jax.ShapeDtypeStruct((4 * pairs, windows * LANES), jnp.bfloat16),
        ),
        in_specs=[smem] + [vmem] * 2,
        out_specs=(vmem, vmem),
        scratch_shapes=[
            pltpu.VMEM((2, slices, held_rows, LANES), jnp.float32),
            pltpu.VMEM((slices * inner, windows * LANES), jnp.bfloat16),
            pltpu.VMEM((4 * pairs, LANES), jnp.float32),
        ],
        compiler_params=params,
        cost_estimate=pl.CostEstimate(flops=100_000_000, bytes_accessed=2_000_000, transcendentals=0),
    )(pair_ids, grid, plans)

    fourier = pl.pallas_call(
        functools.partial(rim_kernel, slices=slices),
        out_shape=jax.ShapeDtypeStruct((pairs, levs, 4, slices * band_rows), jnp.bfloat16),
        in_specs=[vmem] * 4,
        out_specs=vmem,
        scratch_shapes=[
            pltpu.VMEM((AT_ONCE, 2 * EDGE * (slices + 2), LANES), jnp.float32),
            pltpu.VMEM((AT_ONCE, 3, 2 * EDGE, LANES), jnp.float32),
            pltpu.VMEM((2 * RIM * slices, windows * LANES), jnp.bfloat16),
        ],
        compiler_params=params,
    )(arrived_rim, own_rim, basis, inner_fourier)

    values = analysis[0].reshape(bands, band_rows, col_count)
    before = jnp.roll(values[:, band_rows - RIM :], 1, axis=0)
    spread_analysis = jnp.concatenate(
        [values[:, RIM : RIM + inner]] * slices + [before, values[:, :RIM]] * slices, axis=1
    )
    coeffs = lax.all_to_all(
        fourier.reshape(pairs * levs, 4, slices * band_rows),
        ("lat", "lev"),
        split_axis=0,
        concat_axis=0,
        tiled=True,
    )
    place = jnp.stack([lat_at, lev_at * col_count]).astype(jnp.int32)
    out = pl.pallas_call(
        functools.partial(legendre_kernel, bands=bands, levs=levs, slices=slices),
        out_shape=jax.ShapeDtypeStruct((levs * slices, 2, col_count), jnp.float32),
        in_specs=[smem, smem, vmem, vmem],
        out_specs=vmem,
        compiler_params=params,
    )(place, pair_ids, coeffs, spread_analysis)
    return out[None]


def solution(mesh):
    return jax.shard_map(
        shards,
        mesh=mesh,
        in_specs=(
            P("lev", "lat", None),
            P("lat", None),
            P("lat", None),
            P("lat", None),
            P("lat", None),
            P(),
            P("lat", None, "lev"),
        ),
        out_specs=P("lat", None, None, "lev"),
        check_vma=False,
    )
```

```python
import functools
import math

import jax
import jax.numpy as jnp
from jax import lax
from jax.experimental import pallas as pl
from jax.experimental.pallas import tpu as pltpu
from jax.sharding import PartitionSpec as P

NMAX = 1279
LANES = 128
RIM = 2
EDGE = 2 * RIM
REACH = 8
SPAN = LANES - 2 * REACH - 1
ROW_BITS = 5
AT_ONCE = 4


def lane_gather(values, indices):
    numbers = lax.GatherDimensionNumbers(
        offset_dims=(),
        collapsed_slice_dims=(1,),
        start_index_map=(1,),
        operand_batching_dims=(0,),
        start_indices_batching_dims=(0,),
    )
    return lax.gather(
        values,
        indices[..., None],
        numbers,
        (1, 1),
        mode=lax.GatherScatterMode.PROMISE_IN_BOUNDS,
    )


def tile_at(t):
    return pl.ds(pl.multiple_of(t * LANES, LANES), LANES)


def cut_of(start, lon_count):
    tiles = lon_count // LANES
    start = jnp.asarray(start, jnp.int32) + lon_count
    first = start >> LANES.bit_length() - 1
    first = jnp.where(first >= tiles, first - tiles, first)
    second = jnp.where(first == tiles - 1, 0, first + 1)
    return tile_at(first), tile_at(second), start & LANES - 1


def cut(first, second, lane_at):
    lane = lax.broadcasted_iota(jnp.int32, first.shape, 1).astype(jnp.int16)
    joined = jnp.where(lane >= lane_at.astype(jnp.int16), first, second)
    return pltpu.roll(joined, (LANES - lane_at) & LANES - 1, 1)


def lane_plan(code):
    code = code.astype(jnp.int32)
    west = lax.broadcasted_iota(jnp.int32, code.shape, 1) + (code & (1 << ROW_BITS) - 1)
    west_lane = (west & (LANES - 1)).astype(jnp.int16)
    east_lane = ((west + 1) & (LANES - 1)).astype(jnp.int16)
    row_step = (code >> ROW_BITS).astype(jnp.float32).astype(jnp.bfloat16)
    return west_lane, east_lane, row_step


def corner_weights(lat_weight, lon_weight):
    south, north = 1.0 - lat_weight, lat_weight
    west, east = 1.0 - lon_weight, lon_weight
    return south * west, south * east, north * west, north * east


def interpolate(sources, plan, weights):
    west_lane, east_lane, row_step = plan
    masks = [row_step == float(step) for step in range(2 * RIM - 1)]

    def pick(gathered):
        low, high = gathered[2 * RIM - 1], gathered[2 * RIM]
        for position in range(2 * RIM - 2, -1, -1):
            low = jnp.where(masks[position], gathered[position], low)
            high = jnp.where(masks[position], gathered[position + 1], high)
        return low.astype(jnp.float32), high.astype(jnp.float32)

    west_low, west_high = pick([lane_gather(source, west_lane) for source in sources])
    east_low, east_high = pick([lane_gather(source, east_lane) for source in sources])
    departed = (
        weights[0] * west_low
        + weights[1] * east_low
        + weights[2] * west_high
        + weights[3] * east_high
    )
    return departed.astype(jnp.bfloat16)


def in_steps(count, at_once, window):
    def several(step, carry):
        for slot in range(at_once):
            window(step * at_once + slot, slot)
        return carry

    lax.fori_loop(0, count // at_once, several, 0)
    for slot in range(count % at_once):
        window(count - count % at_once + slot, slot)


def pack_kernel(
    band_start, col_start, pair_ids, grid, dep_row, dep_col, lat_frac, lon_frac,
    own_out, sent_out, grid_out, plan_out, waves_out, limit_out, held, rows,
):
    band_rows, slices, lon_count = grid.shape
    inner = band_rows - 2 * RIM
    fields = slices * EDGE
    first_row = band_start[0]

    def tile(t, slot):
        cols = tile_at(t)
        for row in range(band_rows):
            rows[slot, row * slices : (row + 1) * slices, :] = grid[row, :, cols].astype(
                jnp.float32
            )
        row = lax.broadcasted_iota(jnp.int32, (band_rows, LANES), 0)
        lane = lax.broadcasted_iota(jnp.int32, (band_rows, LANES), 1)
        shift = dep_col[:, cols] - (lane + t * LANES)
        shift = jnp.where(shift > lon_count // 2, shift - lon_count, shift)
        shift = jnp.where(shift < -(lon_count // 2), shift + lon_count, shift)
        row_step = dep_row[:, cols] - (first_row + row) + RIM
        held[slot, 0, 0:band_rows, :] = ((row_step << ROW_BITS) + shift + REACH).astype(
            jnp.float32
        )
        held[slot, 1, 0:band_rows, :] = lat_frac[:, cols].astype(jnp.float32)
        held[slot, 2, 0:band_rows, :] = lon_frac[:, cols].astype(jnp.float32)
        grid_out[:, cols] = rows[slot].astype(jnp.bfloat16)
        for out, start, plan_start in (
            (own_out, 0, 0),
            (sent_out, slices * band_rows - fields, band_rows - RIM),
        ):
            block = [rows[slot, start : start + fields, :]]
            block += [held[slot, at, plan_start : plan_start + RIM, :] for at in range(3)]
            block.append(jnp.zeros((RIM, LANES), jnp.float32))
            out[:, cols] = jnp.concatenate(block, axis=0).astype(jnp.bfloat16)
        for at in range(3):
            plan_out[at * inner : (at + 1) * inner, cols] = held[
                slot, at, RIM : RIM + inner, :
            ].astype(jnp.bfloat16)

    in_steps(lon_count // LANES, 5, tile)

    def wave_rows(group, carry):
        row = lax.broadcasted_iota(jnp.int32, (16, LANES), 0)
        pair = jnp.full((16, LANES), pair_ids[4 * group + 3], jnp.int32)
        for at in (2, 1, 0):
            pair = jnp.where(row < 4 * (at + 1), pair_ids[4 * group + at], pair)
        wave = jnp.where((row & 2) == 0, pair, NMAX + 1 - pair)
        waves_out[pl.ds(pl.multiple_of(group * 16, 16), 16), :] = wave.astype(jnp.float32)
        return carry

    lax.fori_loop(0, waves_out.shape[0] // 16, wave_rows, 0)
    limit = NMAX + 1 - pair_ids[first_row // band_rows] - col_start[0]
    limit_out[...] = jnp.full(limit_out.shape, limit, jnp.int32)


def inner_kernel(grid, plans, waves, inner_out, basis_out, windows, departed, *, slices):
    lon_count = grid.shape[1]
    inner = plans.shape[0] // 3
    orders = basis_out.shape[0]

    def basis_tile(t, group):
        rows = pl.ds(pl.multiple_of(group * 16, 16), 16)
        lane = lax.broadcasted_iota(jnp.int32, (16, LANES), 1)
        row = lax.broadcasted_iota(jnp.int32, (16, LANES), 0)
        longitude = lane + t * SPAN
        quarter = jnp.where((row & 1) == 0, 0.0, float(lon_count // 4))
        steps = longitude.astype(jnp.float32) * waves[rows, :] + quarter
        turns = jnp.floor(steps * (1.0 / lon_count) + 0.5)
        angle = (lon_count // 4 - jnp.abs(steps - turns * lon_count)) * (2.0 * math.pi / lon_count)
        square = angle * angle
        series = jnp.float32(-1.0 / 39916800.0)
        for term in (1.0 / 362880.0, -1.0 / 5040.0, 1.0 / 120.0, -1.0 / 6.0, 1.0):
            series = series * square + term
        taken = (lane < SPAN) & (longitude < lon_count)
        basis_out[rows, tile_at(t)] = jnp.where(taken, angle * series, 0.0).astype(jnp.bfloat16)

    def window(t, slot):
        first, second, lane_at = cut_of(t * SPAN - REACH, lon_count)
        windows[slot] = cut(grid[:, first], grid[:, second], lane_at).astype(jnp.float32)
        first, second, lane_at = cut_of(t * SPAN, lon_count)
        code, lat_weight, lon_weight = [
            cut(
                plans[at * inner : (at + 1) * inner, first],
                plans[at * inner : (at + 1) * inner, second],
                lane_at,
            ).astype(jnp.float32)
            for at in range(3)
        ]
        plan = lane_plan(code)
        weights = corner_weights(lat_weight, lon_weight)
        for f in range(slices):
            sources = [
                windows[slot, pl.ds(slices * position + f, inner, stride=slices), :].astype(
                    jnp.bfloat16
                )
                for position in range(2 * RIM + 1)
            ]
            departed[f * inner : (f + 1) * inner, tile_at(t)] = interpolate(sources, plan, weights)
        if orders <= 64:
            for group in range(orders // 16):
                basis_tile(t, group)
        else:
            lax.fori_loop(0, orders // 16, lambda g, c: (basis_tile(t, g), c)[1], 0)

    in_steps(basis_out.shape[1] // LANES, 2, window)
    inner_out[...] = lax.dot_general(
        basis_out[...],
        departed[...],
        (((1,), (1,)), ((), ())),
        preferred_element_type=jnp.float32,
    )


def rim_kernel(arrived, own, basis, inner_fourier, fourier_out, windows, plans, departed, *, slices):
    lon_count = arrived.shape[1]
    fields = slices * EDGE
    sublane = lax.broadcasted_iota(jnp.int32, (2 * slices, LANES), 0)

    def window(t, slot):
        first, second, lane_at = cut_of(t * SPAN - REACH, lon_count)
        for side, ref in enumerate((arrived, own)):
            windows[slot, fields * side : fields * (side + 1), :] = cut(
                ref[0:fields, first], ref[0:fields, second], lane_at
            ).astype(jnp.float32)
        first, second, lane_at = cut_of(t * SPAN, lon_count)
        for side, ref in enumerate((arrived, own)):
            plans[slot, 8 * side : 8 * (side + 1), :] = cut(
                ref[fields:, first], ref[fields:, second], lane_at
            ).astype(jnp.float32)

        def spread(at):
            pieces = []
            for side in range(2):
                two = [
                    jnp.broadcast_to(plans[slot, row : row + 1, :], (2 * slices, LANES))
                    for row in range(8 * side + RIM * at, 8 * side + RIM * (at + 1))
                ]
                pieces.append(jnp.where(sublane < slices, two[0], two[1]))
            return jnp.concatenate(pieces, axis=0)

        plan = lane_plan(spread(0))
        weights = corner_weights(spread(1), spread(2))
        sources = [
            windows[slot, slices * position : slices * position + fields, :].astype(jnp.bfloat16)
            for position in range(2 * RIM + 1)
        ]
        departed[:, tile_at(t)] = interpolate(sources, plan, weights)

    in_steps(basis.shape[1] // LANES, AT_ONCE, window)
    rim_fourier = lax.dot_general(
        basis[...],
        departed[...],
        (((1,), (1,)), ((), ())),
        preferred_element_type=jnp.float32,
    )
    levs = fourier_out.shape[1]
    for pair in range(fourier_out.shape[0]):
        block = jnp.concatenate(
            [inner_fourier[4 * pair : 4 * pair + 4, :], rim_fourier[4 * pair : 4 * pair + 4, :]],
            axis=1,
        ).astype(jnp.bfloat16)
        for lev in range(levs):
            fourier_out[pair, lev] = block


def legendre_kernel(limit, coeffs, spread_analysis, out, spread_coeffs, *, levs, slices):
    members, _, rows = coeffs.shape
    bands = members // levs
    col_count = spread_analysis.shape[1]
    inner = rows // slices - EDGE
    column = lax.broadcasted_iota(jnp.int32, (1, LANES), 1)
    rim_at = column - inner * slices
    slice_of = jnp.where(rim_at < 0, column // inner, rim_at % slices)
    slice_of = jnp.where(column < rows, slice_of, -1)

    def spread(band):
        block = jnp.concatenate(
            [coeffs[band * levs + lev].astype(jnp.float32) for lev in range(levs)], axis=0
        )
        block = jnp.concatenate(
            [block, jnp.zeros((block.shape[0], LANES - rows), jnp.float32)], axis=1
        )
        spread_coeffs[:, tile_at(band)] = jnp.concatenate(
            [jnp.where(slice_of == f, block, 0.0) for f in range(slices)], axis=0
        ).astype(jnp.bfloat16)

    if bands <= 16:
        for band in range(bands):
            spread(band)
    else:
        lax.fori_loop(0, bands, lambda band, carry: (spread(band), carry)[1], 0)
    total = jnp.dot(
        spread_coeffs[...], spread_analysis[...], preferred_element_type=jnp.float32
    )
    first_wave = lax.broadcasted_iota(jnp.int32, (2, col_count), 1) < limit[0:1, 0:1]
    for f in range(slices):
        for lev in range(levs):
            at = (f * levs + lev) * 4
            out[lev * slices + f] = jnp.where(first_wave, total[at : at + 2], total[at + 2 : at + 4])


def shards(grid, dep_row, dep_col, lat_frac, lon_frac, pair_ids, analysis):
    slices, band_rows, lon_count = grid.shape
    pairs = pair_ids.shape[0]
    col_count = analysis.shape[2]
    bands, levs = lax.axis_size("lat"), lax.axis_size("lev")
    inner = band_rows - 2 * RIM
    windows = -(-lon_count // SPAN)
    held_rows = -(-band_rows // 8) * 8
    fields = slices * EDGE
    band_start = jnp.reshape(lax.axis_index("lat") * band_rows, (1,)).astype(jnp.int32)
    col_start = jnp.reshape(lax.axis_index("lev") * col_count, (1,)).astype(jnp.int32)
    vmem = pl.BlockSpec(memory_space=pltpu.VMEM)
    smem = pl.BlockSpec(memory_space=pltpu.SMEM)
    params = pltpu.CompilerParams(vmem_limit_bytes=48 * 2**20)

    rim_shape = jax.ShapeDtypeStruct((fields + 4 * RIM, lon_count), jnp.bfloat16)
    own_rim, sent_rim, rows, plans, waves, limit = pl.pallas_call(
        pack_kernel,
        out_shape=(
            rim_shape,
            rim_shape,
            jax.ShapeDtypeStruct((band_rows * slices, lon_count), jnp.bfloat16),
            jax.ShapeDtypeStruct((3 * inner, lon_count), jnp.bfloat16),
            jax.ShapeDtypeStruct((4 * pairs, LANES), jnp.float32),
            jax.ShapeDtypeStruct((8, LANES), jnp.int32),
        ),
        in_specs=[smem] * 3 + [vmem] * 5,
        out_specs=(vmem,) * 6,
        scratch_shapes=[
            pltpu.VMEM((5, 3, held_rows, LANES), jnp.float32),
            pltpu.VMEM((5, band_rows * slices, LANES), jnp.float32),
        ],
        compiler_params=params,
    )(
        band_start, col_start, pair_ids, grid.transpose(1, 0, 2), dep_row, dep_col, lat_frac, lon_frac
    )
    arrived_rim = lax.ppermute(sent_rim, "lat", [(i, (i + 1) % bands) for i in range(bands)])

    inner_fourier, basis = pl.pallas_call(
        functools.partial(inner_kernel, slices=slices),
        out_shape=(
            jax.ShapeDtypeStruct((4 * pairs, slices * inner), jnp.float32),
            jax.ShapeDtypeStruct((4 * pairs, windows * LANES), jnp.bfloat16),
        ),
        in_specs=[vmem] * 3,
        out_specs=(vmem, vmem),
        scratch_shapes=[
            pltpu.VMEM((2, band_rows * slices, LANES), jnp.float32),
            pltpu.VMEM((slices * inner, windows * LANES), jnp.bfloat16),
        ],
        compiler_params=params,
        cost_estimate=pl.CostEstimate(flops=100_000_000, bytes_accessed=2_000_000, transcendentals=0),
    )(rows, plans, waves)

    fourier = pl.pallas_call(
        functools.partial(rim_kernel, slices=slices),
        out_shape=jax.ShapeDtypeStruct((pairs, levs, 4, slices * band_rows), jnp.bfloat16),
        in_specs=[vmem] * 4,
        out_specs=vmem,
        scratch_shapes=[
            pltpu.VMEM((AT_ONCE, 2 * fields, LANES), jnp.float32),
            pltpu.VMEM((AT_ONCE, 16, LANES), jnp.float32),
            pltpu.VMEM((fields, windows * LANES), jnp.bfloat16),
        ],
        compiler_params=params,
    )(arrived_rim, own_rim, basis, inner_fourier)

    values = analysis[0].reshape(bands, band_rows, col_count)
    before = jnp.roll(values[:, band_rows - RIM :], 1, axis=0)
    spread_rows = [values[:, RIM : RIM + inner]] * slices
    for rim in (before, values[:, :RIM]):
        for row in range(RIM):
            spread_rows += [rim[:, row : row + 1]] * slices
    spread_rows.append(jnp.zeros((bands, LANES - slices * band_rows, col_count), jnp.bfloat16))
    spread_analysis = jnp.concatenate(spread_rows, axis=1).reshape(bands * LANES, col_count)

    coeffs = lax.all_to_all(
        fourier.reshape(pairs * levs, 4, slices * band_rows),
        ("lat", "lev"),
        split_axis=0,
        concat_axis=0,
        tiled=True,
    )
    out = pl.pallas_call(
        functools.partial(legendre_kernel, levs=levs, slices=slices),
        out_shape=jax.ShapeDtypeStruct((levs * slices, 2, col_count), jnp.float32),
        in_specs=[vmem] * 3,
        out_specs=vmem,
        scratch_shapes=[pltpu.VMEM((4 * levs * slices, bands * LANES), jnp.bfloat16)],
        compiler_params=params,
    )(limit, coeffs, spread_analysis)
    return out[None]


def solution(mesh):
    return jax.shard_map(
        shards,
        mesh=mesh,
        in_specs=(
            P("lev", "lat", None),
            P("lat", None),
            P("lat", None),
            P("lat", None),
            P("lat", None),
            P(),
            P("lat", None, "lev"),
        ),
        out_specs=P("lat", None, None, "lev"),
        check_vma=False,
    )
```

```python
import functools
import math

import jax
import jax.numpy as jnp
from jax import lax
from jax.experimental import pallas as pl
from jax.experimental.pallas import tpu as pltpu
from jax.sharding import PartitionSpec as P

NMAX = 1279
LANES = 128
RIM = 2
EDGE = 2 * RIM
REACH = 8
SPAN = LANES - 2 * REACH - 1
ROW_BITS = 5
INNER_AT_ONCE = 2
RIM_AT_ONCE = 4


def lane_gather(values, indices):
    numbers = lax.GatherDimensionNumbers(
        offset_dims=(),
        collapsed_slice_dims=(1,),
        start_index_map=(1,),
        operand_batching_dims=(0,),
        start_indices_batching_dims=(0,),
    )
    return lax.gather(
        values,
        indices[..., None],
        numbers,
        (1, 1),
        mode=lax.GatherScatterMode.PROMISE_IN_BOUNDS,
    )


def tile_at(t):
    return pl.ds(pl.multiple_of(t * LANES, LANES), LANES)


def cut_of(start, lon_count):
    tiles = lon_count // LANES
    start = jnp.asarray(start, jnp.int32) + lon_count
    first = start >> LANES.bit_length() - 1
    first = jnp.where(first >= tiles, first - tiles, first)
    second = jnp.where(first == tiles - 1, 0, first + 1)
    return tile_at(first), tile_at(second), start & LANES - 1


def cut(first, second, lane_at):
    lane = lax.broadcasted_iota(jnp.int32, first.shape, 1).astype(jnp.int16)
    joined = jnp.where(lane >= lane_at.astype(jnp.int16), first, second)
    return pltpu.roll(joined, (LANES - lane_at) & LANES - 1, 1)


def lane_plan(code):
    code = code.astype(jnp.int32)
    west = lax.broadcasted_iota(jnp.int32, code.shape, 1) + (code & (1 << ROW_BITS) - 1)
    west_lane = (west & (LANES - 1)).astype(jnp.int16)
    east_lane = ((west + 1) & (LANES - 1)).astype(jnp.int16)
    row_step = (code >> ROW_BITS).astype(jnp.float32).astype(jnp.bfloat16)
    return west_lane, east_lane, row_step


def corner_weights(lat_weight, lon_weight):
    south, north = 1.0 - lat_weight, lat_weight
    west, east = 1.0 - lon_weight, lon_weight
    return south * west, south * east, north * west, north * east


def interpolate(sources, plan, weights):
    west_lane, east_lane, row_step = plan
    masks = [row_step == float(step) for step in range(2 * RIM - 1)]

    def pick(gathered):
        low, high = gathered[2 * RIM - 1], gathered[2 * RIM]
        for position in range(2 * RIM - 2, -1, -1):
            low = jnp.where(masks[position], gathered[position], low)
            high = jnp.where(masks[position], gathered[position + 1], high)
        return low.astype(jnp.float32), high.astype(jnp.float32)

    west_low, west_high = pick([lane_gather(source, west_lane) for source in sources])
    east_low, east_high = pick([lane_gather(source, east_lane) for source in sources])
    departed = (
        weights[0] * west_low
        + weights[1] * east_low
        + weights[2] * west_high
        + weights[3] * east_high
    )
    return departed.astype(jnp.bfloat16)


def in_groups(count, at_once, group):
    def step(at, carry):
        group([at * at_once + slot for slot in range(at_once)])
        return carry

    lax.fori_loop(0, count // at_once, step, 0)
    if count % at_once:
        group(list(range(count - count % at_once, count)))


def pack_kernel(
    band_start, col_start, pair_ids_at, grid_at, dep_row_at, dep_col_at, lat_frac_at, lon_frac_at,
    own_out, sent_out, grid_out, plan_out, waves_out, limit_out,
    pair_ids, grid, dep_row, dep_col, lat_frac, lon_frac, held, rows, arrivals,
):
    copies = [
        pltpu.make_async_copy(source, target, arrivals.at[at])
        for at, (source, target) in enumerate(
            (
                (grid_at, grid),
                (dep_row_at, dep_row),
                (dep_col_at, dep_col),
                (lat_frac_at, lat_frac),
                (lon_frac_at, lon_frac),
                (pair_ids_at, pair_ids),
            )
        )
    ]
    for copy in copies:
        copy.start()
    for copy in copies:
        copy.wait()
    band_rows, slices, lon_count = grid.shape
    inner = band_rows - 2 * RIM
    fields = slices * EDGE
    first_row = band_start[0]

    def tile(t, slot):
        cols = tile_at(t)
        for row in range(band_rows):
            rows[slot, row * slices : (row + 1) * slices, :] = grid[row, :, cols].astype(
                jnp.float32
            )
        row = lax.broadcasted_iota(jnp.int32, (band_rows, LANES), 0)
        lane = lax.broadcasted_iota(jnp.int32, (band_rows, LANES), 1)
        shift = dep_col[:, cols] - (lane + t * LANES)
        shift = jnp.where(shift > lon_count // 2, shift - lon_count, shift)
        shift = jnp.where(shift < -(lon_count // 2), shift + lon_count, shift)
        row_step = dep_row[:, cols] - (first_row + row) + RIM
        held[slot, 0, 0:band_rows, :] = ((row_step << ROW_BITS) + shift + REACH).astype(
            jnp.float32
        )
        held[slot, 1, 0:band_rows, :] = lat_frac[:, cols].astype(jnp.float32)
        held[slot, 2, 0:band_rows, :] = lon_frac[:, cols].astype(jnp.float32)
        grid_out[:, cols] = rows[slot].astype(jnp.bfloat16)
        for out, start, plan_start in (
            (own_out, slices * band_rows - fields, band_rows - RIM),
            (sent_out, 0, 0),
        ):
            block = [rows[slot, start : start + fields, :]]
            block += [held[slot, at, plan_start : plan_start + RIM, :] for at in range(3)]
            block.append(jnp.zeros((RIM, LANES), jnp.float32))
            out[:, cols] = jnp.concatenate(block, axis=0).astype(jnp.bfloat16)
        for at in range(3):
            plan_out[at * inner : (at + 1) * inner, cols] = held[
                slot, at, RIM : RIM + inner, :
            ].astype(jnp.bfloat16)

    for t in range(lon_count // LANES):
        tile(t, t % 5)

    def wave_rows(group, carry):
        row = lax.broadcasted_iota(jnp.int32, (16, LANES), 0)
        pair = jnp.full((16, LANES), pair_ids[4 * group + 3], jnp.int32)
        for at in (2, 1, 0):
            pair = jnp.where(row < 4 * (at + 1), pair_ids[4 * group + at], pair)
        wave = jnp.where((row & 2) == 0, pair, NMAX + 1 - pair)
        waves_out[pl.ds(pl.multiple_of(group * 16, 16), 16), :] = wave.astype(jnp.float32)
        return carry

    lax.fori_loop(0, waves_out.shape[0] // 16, wave_rows, 0)
    limit = NMAX + 1 - pair_ids[first_row // band_rows] - col_start[0]
    limit_out[...] = jnp.full(limit_out.shape, limit, jnp.int32)


def inner_kernel(grid, plans, waves, inner_out, basis_out, windows, departed, *, slices):
    lon_count = grid.shape[1]
    inner = plans.shape[0] // 3
    orders = basis_out.shape[0]

    def basis_tile(t, group):
        lane = lax.broadcasted_iota(jnp.int32, (16, LANES), 1)
        row = lax.broadcasted_iota(jnp.int32, (16, LANES), 0)
        longitude = lane + t * SPAN
        quarter = jnp.where((row & 1) == 0, 0.0, float(lon_count // 4))
        wave = waves[pl.ds(pl.multiple_of(group * 16, 16), 16), :]
        steps = longitude.astype(jnp.float32) * wave + quarter
        turns = jnp.floor(steps * (1.0 / lon_count) + 0.5)
        angle = (lon_count // 4 - jnp.abs(steps - turns * lon_count)) * (2.0 * math.pi / lon_count)
        square = angle * angle
        series = jnp.float32(-1.0 / 39916800.0)
        for term in (1.0 / 362880.0, -1.0 / 5040.0, 1.0 / 120.0, -1.0 / 6.0, 1.0):
            series = series * square + term
        taken = (lane < SPAN) & (longitude < lon_count)
        return jnp.where(taken, angle * series, 0.0).astype(jnp.bfloat16)

    inline = orders <= 64

    def group_of(ts):
        blocks, plan_blocks = [], []
        for t in ts:
            first, second, lane_at = cut_of(t * SPAN - REACH, lon_count)
            blocks.append(cut(grid[:, first], grid[:, second], lane_at).astype(jnp.float32))
            first, second, lane_at = cut_of(t * SPAN, lon_count)
            plan_blocks.append(
                [
                    cut(
                        plans[at * inner : (at + 1) * inner, first],
                        plans[at * inner : (at + 1) * inner, second],
                        lane_at,
                    ).astype(jnp.float32)
                    for at in range(3)
                ]
            )
        for slot, block in enumerate(blocks):
            windows[slot] = block
        results = []
        for slot, (code, lat_weight, lon_weight) in enumerate(plan_blocks):
            plan = lane_plan(code)
            weights = corner_weights(lat_weight, lon_weight)
            for f in range(slices):
                sources = [
                    windows[slot, pl.ds(slices * position + f, inner, stride=slices), :].astype(
                        jnp.bfloat16
                    )
                    for position in range(2 * RIM + 1)
                ]
                results.append((ts[slot], f, interpolate(sources, plan, weights)))
        waves_here = [
            (t, group, basis_tile(t, group))
            for t in ts
            for group in range(orders // 16 if inline else 0)
        ]
        for t, f, result in results:
            departed[f * inner : (f + 1) * inner, tile_at(t)] = result
        for t, group, result in waves_here:
            basis_out[group * 16 : (group + 1) * 16, tile_at(t)] = result

    count = basis_out.shape[1] // LANES
    in_groups(count, INNER_AT_ONCE, group_of)
    if not inline:

        def basis_rows(group, carry):
            rows = pl.ds(pl.multiple_of(group * 16, 16), 16)

            def one(t, inner_carry):
                basis_out[rows, tile_at(t)] = basis_tile(t, group)
                return inner_carry

            return lax.fori_loop(0, count, one, carry)

        lax.fori_loop(0, orders // 16, basis_rows, 0)
    inner_out[...] = lax.dot_general(
        basis_out[...],
        departed[...],
        (((1,), (1,)), ((), ())),
        preferred_element_type=jnp.float32,
    )


def rim_kernel(
    band_start, own, arrived, sent, basis, inner_fourier, fourier_out, windows, plans, departed, top,
    *, slices,
):
    lon_count = arrived.shape[1]
    fields = slices * EDGE
    sublane = lax.broadcasted_iota(jnp.int32, (2 * slices, LANES), 0)

    def spread(slot, at):
        pieces = []
        for side in range(2):
            two = [
                jnp.broadcast_to(plans[slot, row : row + 1, :], (2 * slices, LANES))
                for row in range(8 * side + RIM * at, 8 * side + RIM * (at + 1))
            ]
            pieces.append(jnp.where(sublane < slices, two[0], two[1]))
        return jnp.concatenate(pieces, axis=0)

    def rim_sums(sides):
        def group_of(ts):
            blocks, plan_blocks = [], []
            for t in ts:
                first, second, lane_at = cut_of(t * SPAN - REACH, lon_count)
                blocks.append(
                    [
                        cut(ref[0:fields, first], ref[0:fields, second], lane_at)
                        for ref in sides
                    ]
                )
                first, second, lane_at = cut_of(t * SPAN, lon_count)
                plan_blocks.append(
                    [cut(ref[fields:, first], ref[fields:, second], lane_at) for ref in sides]
                )
            for slot in range(len(ts)):
                for side in range(2):
                    windows[slot, fields * side : fields * (side + 1), :] = blocks[slot][
                        side
                    ].astype(jnp.float32)
                    plans[slot, 8 * side : 8 * (side + 1), :] = plan_blocks[slot][side].astype(
                        jnp.float32
                    )
            results = []
            for slot in range(len(ts)):
                plan = lane_plan(spread(slot, 0))
                weights = corner_weights(spread(slot, 1), spread(slot, 2))
                sources = [
                    windows[slot, slices * position : slices * position + fields, :].astype(
                        jnp.bfloat16
                    )
                    for position in range(2 * RIM + 1)
                ]
                results.append(interpolate(sources, plan, weights))
            for t, result in zip(ts, results):
                departed[:, tile_at(t)] = result

        in_groups(basis.shape[1] // LANES, RIM_AT_ONCE, group_of)
        return lax.dot_general(
            basis[...],
            departed[...],
            (((1,), (1,)), ((), ())),
            preferred_element_type=jnp.float32,
        )

    top[...] = jnp.zeros(top.shape, jnp.float32)

    @pl.when(band_start[0] == 0)
    def _():
        top[...] = rim_sums((sent, sent))

    rim_fourier = rim_sums((own, arrived))
    top_fourier = top[:, RIM * slices :]
    levs = fourier_out.shape[1]
    for pair in range(fourier_out.shape[0]):
        rows = slice(4 * pair, 4 * pair + 4)
        block = jnp.concatenate(
            [inner_fourier[rows, :], rim_fourier[rows, :], top_fourier[rows, :]], axis=1
        ).astype(jnp.bfloat16)
        for lev in range(levs):
            fourier_out[pair, lev] = block


def legendre_kernel(limit, coeffs, spread_analysis, out, spread_coeffs, *, levs, slices):
    members, _, rows = coeffs.shape
    bands = members // levs
    col_count = spread_analysis.shape[1]
    inner = rows // slices - EDGE - RIM
    column = lax.broadcasted_iota(jnp.int32, (1, LANES), 1)
    rim_at = column - inner * slices
    slice_of = jnp.where(rim_at < 0, column // inner, rim_at % slices)
    slice_of = jnp.where(column < rows, slice_of, -1)

    def spread(band):
        block = jnp.concatenate(
            [coeffs[band * levs + lev].astype(jnp.float32) for lev in range(levs)], axis=0
        )
        block = jnp.concatenate(
            [block, jnp.zeros((block.shape[0], LANES - rows), jnp.float32)], axis=1
        )
        spread_coeffs[:, tile_at(band)] = jnp.concatenate(
            [jnp.where(slice_of == f, block, 0.0) for f in range(slices)], axis=0
        ).astype(jnp.bfloat16)

    if bands <= 16:
        for band in range(bands):
            spread(band)
    else:
        lax.fori_loop(0, bands, lambda band, carry: (spread(band), carry)[1], 0)
    total = jnp.dot(
        spread_coeffs[...], spread_analysis[...], preferred_element_type=jnp.float32
    )
    first_wave = lax.broadcasted_iota(jnp.int32, (2, col_count), 1) < limit[0:1, 0:1]
    for f in range(slices):
        for lev in range(levs):
            at = (f * levs + lev) * 4
            out[lev * slices + f] = jnp.where(first_wave, total[at : at + 2], total[at + 2 : at + 4])


def shards(grid, dep_row, dep_col, lat_frac, lon_frac, pair_ids, analysis):
    slices, band_rows, lon_count = grid.shape
    pairs = pair_ids.shape[0]
    col_count = analysis.shape[2]
    bands, levs = lax.axis_size("lat"), lax.axis_size("lev")
    inner = band_rows - 2 * RIM
    windows = -(-lon_count // SPAN)
    held_rows = -(-band_rows // 8) * 8
    fields = slices * EDGE
    band_start = jnp.reshape(lax.axis_index("lat") * band_rows, (1,)).astype(jnp.int32)
    col_start = jnp.reshape(lax.axis_index("lev") * col_count, (1,)).astype(jnp.int32)
    vmem = pl.BlockSpec(memory_space=pltpu.VMEM)
    smem = pl.BlockSpec(memory_space=pltpu.SMEM)
    params = pltpu.CompilerParams(vmem_limit_bytes=48 * 2**20)

    rim_shape = jax.ShapeDtypeStruct((fields + 4 * RIM, lon_count), jnp.bfloat16)
    own_rim, sent_rim, rows, plans, waves, limit = pl.pallas_call(
        pack_kernel,
        out_shape=(
            rim_shape,
            rim_shape,
            jax.ShapeDtypeStruct((band_rows * slices, lon_count), jnp.bfloat16),
            jax.ShapeDtypeStruct((3 * inner, lon_count), jnp.bfloat16),
            jax.ShapeDtypeStruct((4 * pairs, LANES), jnp.float32),
            jax.ShapeDtypeStruct((8, LANES), jnp.int32),
        ),
        in_specs=[smem] * 2 + [pl.BlockSpec(memory_space=pltpu.HBM)] * 6,
        out_specs=(vmem,) * 6,
        scratch_shapes=[
            pltpu.SMEM(pair_ids.shape, jnp.int32),
            pltpu.VMEM((band_rows, slices, lon_count), jnp.bfloat16),
            pltpu.VMEM((band_rows, lon_count), jnp.int32),
            pltpu.VMEM((band_rows, lon_count), jnp.int32),
            pltpu.VMEM((band_rows, lon_count), jnp.bfloat16),
            pltpu.VMEM((band_rows, lon_count), jnp.bfloat16),
            pltpu.VMEM((5, 3, held_rows, LANES), jnp.float32),
            pltpu.VMEM((5, band_rows * slices, LANES), jnp.float32),
            pltpu.SemaphoreType.DMA((6,)),
        ],
        compiler_params=params,
    )(
        band_start, col_start, pair_ids, grid.transpose(1, 0, 2), dep_row, dep_col, lat_frac, lon_frac
    )
    arrived_rim = lax.ppermute(sent_rim, "lat", [(i + 1, i) for i in range(bands - 1)])

    inner_fourier, basis = pl.pallas_call(
        functools.partial(inner_kernel, slices=slices),
        out_shape=(
            jax.ShapeDtypeStruct((4 * pairs, slices * inner), jnp.float32),
            jax.ShapeDtypeStruct((4 * pairs, windows * LANES), jnp.bfloat16),
        ),
        in_specs=[vmem] * 3,
        out_specs=(vmem, vmem),
        scratch_shapes=[
            pltpu.VMEM((INNER_AT_ONCE, band_rows * slices, LANES), jnp.float32),
            pltpu.VMEM((slices * inner, windows * LANES), jnp.bfloat16),
        ],
        compiler_params=params,
        cost_estimate=pl.CostEstimate(flops=100_000_000, bytes_accessed=2_000_000, transcendentals=0),
    )(rows, plans, waves)

    held_coeffs = slices * (band_rows + RIM)
    fourier = pl.pallas_call(
        functools.partial(rim_kernel, slices=slices),
        out_shape=jax.ShapeDtypeStruct((pairs, levs, 4, held_coeffs), jnp.bfloat16),
        in_specs=[smem] + [vmem] * 5,
        out_specs=vmem,
        scratch_shapes=[
            pltpu.VMEM((RIM_AT_ONCE, 2 * fields, LANES), jnp.float32),
            pltpu.VMEM((RIM_AT_ONCE, 16, LANES), jnp.float32),
            pltpu.VMEM((fields, windows * LANES), jnp.bfloat16),
            pltpu.VMEM((4 * pairs, fields), jnp.float32),
        ],
        compiler_params=params,
    )(band_start, own_rim, arrived_rim, sent_rim, basis, inner_fourier)

    values = analysis[0].reshape(bands, band_rows, col_count)
    after = jnp.concatenate([values[1:, :RIM], jnp.zeros_like(values[:1, :RIM])], axis=0)
    spread_rows = [values[:, RIM : RIM + inner]] * slices
    for rim in (values[:, band_rows - RIM :], after, values[:, :RIM]):
        for row in range(RIM):
            spread_rows += [rim[:, row : row + 1]] * slices
    spread_rows.append(jnp.zeros((bands, LANES - held_coeffs, col_count), jnp.bfloat16))
    spread_analysis = jnp.concatenate(spread_rows, axis=1).reshape(bands * LANES, col_count)

    coeffs = lax.all_to_all(
        fourier.reshape(pairs * levs, 4, held_coeffs),
        ("lat", "lev"),
        split_axis=0,
        concat_axis=0,
        tiled=True,
    )
    out = pl.pallas_call(
        functools.partial(legendre_kernel, levs=levs, slices=slices),
        out_shape=jax.ShapeDtypeStruct((levs * slices, 2, col_count), jnp.float32),
        in_specs=[vmem] * 3,
        out_specs=vmem,
        scratch_shapes=[pltpu.VMEM((4 * levs * slices, bands * LANES), jnp.bfloat16)],
        compiler_params=params,
    )(limit, coeffs, spread_analysis)
    return out[None]


def solution(mesh):
    return jax.shard_map(
        shards,
        mesh=mesh,
        in_specs=(
            P("lev", "lat", None),
            P("lat", None),
            P("lat", None),
            P("lat", None),
            P("lat", None),
            P(),
            P("lat", None, "lev"),
        ),
        out_specs=P("lat", None, None, "lev"),
        check_vma=False,
    )
```

```python
import functools
import math

import jax
import jax.numpy as jnp
from jax import lax
from jax.experimental import pallas as pl
from jax.experimental.pallas import tpu as pltpu
from jax.sharding import PartitionSpec as P

NMAX = 1279
LANES = 128
RIM = 2
EDGE = 2 * RIM
REACH = 8
SPAN = LANES - 2 * REACH - 1
ROW_BITS = 5
INNER_AT_ONCE = 2
RIM_AT_ONCE = 4


def lane_gather(values, indices):
    numbers = lax.GatherDimensionNumbers(
        offset_dims=(),
        collapsed_slice_dims=(1,),
        start_index_map=(1,),
        operand_batching_dims=(0,),
        start_indices_batching_dims=(0,),
    )
    return lax.gather(
        values,
        indices[..., None],
        numbers,
        (1, 1),
        mode=lax.GatherScatterMode.PROMISE_IN_BOUNDS,
    )


def tile_at(t):
    return pl.ds(pl.multiple_of(t * LANES, LANES), LANES)


def cut_of(start, lon_count):
    tiles = lon_count // LANES
    start = jnp.asarray(start, jnp.int32) + lon_count
    first = start >> LANES.bit_length() - 1
    first = jnp.where(first >= tiles, first - tiles, first)
    second = jnp.where(first == tiles - 1, 0, first + 1)
    return tile_at(first), tile_at(second), start & LANES - 1


def cut(first, second, lane_at):
    lane = lax.broadcasted_iota(jnp.int32, first.shape, 1).astype(jnp.int16)
    joined = jnp.where(lane >= lane_at.astype(jnp.int16), first, second)
    return pltpu.roll(joined, (LANES - lane_at) & LANES - 1, 1)


def lane_plan(code):
    code = code.astype(jnp.int32)
    west = lax.broadcasted_iota(jnp.int32, code.shape, 1) + (code & (1 << ROW_BITS) - 1)
    west_lane = (west & (LANES - 1)).astype(jnp.int16)
    east_lane = ((west + 1) & (LANES - 1)).astype(jnp.int16)
    row_step = (code >> ROW_BITS).astype(jnp.float32).astype(jnp.bfloat16)
    return west_lane, east_lane, row_step


def corner_weights(lat_weight, lon_weight):
    south, north = 1.0 - lat_weight, lat_weight
    west, east = 1.0 - lon_weight, lon_weight
    return south * west, south * east, north * west, north * east


def interpolate(sources, plan, weights):
    west_lane, east_lane, row_step = plan
    masks = [row_step == float(step) for step in range(2 * RIM - 1)]

    def pick(gathered):
        low, high = gathered[2 * RIM - 1], gathered[2 * RIM]
        for position in range(2 * RIM - 2, -1, -1):
            low = jnp.where(masks[position], gathered[position], low)
            high = jnp.where(masks[position], gathered[position + 1], high)
        return low.astype(jnp.float32), high.astype(jnp.float32)

    west_low, west_high = pick([lane_gather(source, west_lane) for source in sources])
    east_low, east_high = pick([lane_gather(source, east_lane) for source in sources])
    departed = (
        weights[0] * west_low
        + weights[1] * east_low
        + weights[2] * west_high
        + weights[3] * east_high
    )
    return departed.astype(jnp.bfloat16)


def in_groups(count, at_once, group):
    def step(at, carry):
        group([at * at_once + slot for slot in range(at_once)])
        return carry

    lax.fori_loop(0, count // at_once, step, 0)
    if count % at_once:
        group(list(range(count - count % at_once, count)))


def pack_kernel(
    band_start, rows, dep_row, dep_col, lat_frac, lon_frac, own_out, sent_out, plan_out, held
):
    band_rows, lon_count = dep_row.shape
    inner = band_rows - 2 * RIM
    fields = rows.shape[0] // band_rows * EDGE
    first_row = band_start[0]

    for t in range(lon_count // LANES):
        cols, slot = tile_at(t), t % 5
        row = lax.broadcasted_iota(jnp.int32, (band_rows, LANES), 0)
        lane = lax.broadcasted_iota(jnp.int32, (band_rows, LANES), 1)
        shift = dep_col[:, cols] - (lane + t * LANES)
        shift = jnp.where(shift > lon_count // 2, shift - lon_count, shift)
        shift = jnp.where(shift < -(lon_count // 2), shift + lon_count, shift)
        row_step = dep_row[:, cols] - (first_row + row) + RIM
        held[slot, 0, 0:band_rows, :] = row_step.astype(jnp.float32)
        held[slot, 1, 0:band_rows, :] = (shift + REACH).astype(jnp.float32)
        held[slot, 2, 0:band_rows, :] = lat_frac[:, cols].astype(jnp.float32)
        held[slot, 3, 0:band_rows, :] = lon_frac[:, cols].astype(jnp.float32)
        for out, start, plan_start in (
            (own_out, 0, 0),
            (sent_out, rows.shape[0] - fields, band_rows - RIM),
        ):
            out[0:fields, cols] = rows[start : start + fields, cols]
            out[fields:, cols] = jnp.concatenate(
                [held[slot, at, plan_start : plan_start + RIM, :] for at in range(4)], axis=0
            ).astype(jnp.bfloat16)
        middle = [held[slot, at, RIM : RIM + inner, :] for at in range(4)]
        middle = [middle[0] * (1 << ROW_BITS) + middle[1], middle[2], middle[3]]
        for at in range(3):
            plan_out[at * inner : (at + 1) * inner, cols] = middle[at].astype(jnp.bfloat16)


def basis_kernel(place, pair_ids, basis_out, limit_out, waves, *, lon_count):
    orders = basis_out.shape[0]

    def wave_rows(group, carry):
        row = lax.broadcasted_iota(jnp.int32, (16, LANES), 0)
        pair = jnp.full((16, LANES), pair_ids[4 * group + 3], jnp.int32)
        for at in (2, 1, 0):
            pair = jnp.where(row < 4 * (at + 1), pair_ids[4 * group + at], pair)
        wave = jnp.where((row & 2) == 0, pair, NMAX + 1 - pair)
        waves[pl.ds(pl.multiple_of(group * 16, 16), 16), :] = wave.astype(jnp.float32)
        return carry

    lax.fori_loop(0, orders // 16, wave_rows, 0)

    def tile(t):
        def rows_of(group, carry):
            rows = pl.ds(pl.multiple_of(group * 16, 16), 16)
            lane = lax.broadcasted_iota(jnp.int32, (16, LANES), 1)
            row = lax.broadcasted_iota(jnp.int32, (16, LANES), 0)
            longitude = lane + t * SPAN
            quarter = jnp.where((row & 1) == 0, 0.0, float(lon_count // 4))
            steps = longitude.astype(jnp.float32) * waves[rows, :] + quarter
            turns = jnp.floor(steps * (1.0 / lon_count) + 0.5)
            angle = lon_count // 4 - jnp.abs(steps - turns * lon_count)
            angle = angle * (2.0 * math.pi / lon_count)
            square = angle * angle
            series = jnp.float32(-1.0 / 39916800.0)
            for term in (1.0 / 362880.0, -1.0 / 5040.0, 1.0 / 120.0, -1.0 / 6.0, 1.0):
                series = series * square + term
            taken = (lane < SPAN) & (longitude < lon_count)
            basis_out[rows, tile_at(t)] = jnp.where(taken, angle * series, 0.0).astype(
                jnp.bfloat16
            )
            return carry

        lax.fori_loop(0, orders // 16, rows_of, 0, unroll=orders <= 64)

    for t in range(basis_out.shape[1] // LANES):
        tile(t)
    limit = NMAX + 1 - pair_ids[place[0]] - place[1]
    limit_out[...] = jnp.full(limit_out.shape, limit, jnp.int32)


def inner_kernel(grid, plans, departed, windows, *, slices):
    lon_count = grid.shape[1]
    inner = plans.shape[0] // 3

    def group_of(ts):
        blocks, plan_blocks = [], []
        for t in ts:
            first, second, lane_at = cut_of(t * SPAN - REACH, lon_count)
            blocks.append(cut(grid[:, first], grid[:, second], lane_at).astype(jnp.float32))
            first, second, lane_at = cut_of(t * SPAN, lon_count)
            plan_blocks.append(
                [
                    cut(
                        plans[at * inner : (at + 1) * inner, first],
                        plans[at * inner : (at + 1) * inner, second],
                        lane_at,
                    ).astype(jnp.float32)
                    for at in range(3)
                ]
            )
        for slot, block in enumerate(blocks):
            windows[slot] = block
        results = []
        for slot, (code, lat_weight, lon_weight) in enumerate(plan_blocks):
            plan = lane_plan(code)
            weights = corner_weights(lat_weight, lon_weight)
            for f in range(slices):
                sources = [
                    windows[slot, pl.ds(slices * position + f, inner, stride=slices), :].astype(
                        jnp.bfloat16
                    )
                    for position in range(2 * RIM + 1)
                ]
                results.append((ts[slot], f, interpolate(sources, plan, weights)))
        for t, f, result in results:
            departed[f * inner : (f + 1) * inner, tile_at(t)] = result

    in_groups(departed.shape[1] // LANES, INNER_AT_ONCE, group_of)


def rim_kernel(
    arrived, own, basis, inner_departed, fourier_out, windows, departed, *, slices
):
    lon_count = arrived.shape[1]
    fields = slices * EDGE
    sides = (arrived, own)
    wanted = lax.broadcasted_iota(jnp.int32, (3 * fields, 16), 0)
    held = lax.broadcasted_iota(jnp.int32, (3 * fields, 16), 1)
    kind, rim_row = wanted // fields, wanted % fields // slices
    base = rim_row // RIM * 8 + rim_row % RIM
    spread = jnp.where((kind == 0) & (held == base), float(1 << ROW_BITS), 0.0)
    spread += jnp.where(held == base + RIM * (kind + 1), 1.0, 0.0)
    spread = spread.astype(jnp.bfloat16)

    def group_of(ts):
        blocks, plan_blocks = [], []
        for t in ts:
            first, second, lane_at = cut_of(t * SPAN - REACH, lon_count)
            blocks.append(
                [cut(ref[0:fields, first], ref[0:fields, second], lane_at) for ref in sides]
            )
            first, second, lane_at = cut_of(t * SPAN, lon_count)
            plan_block = jnp.concatenate(
                [cut(ref[fields:, first], ref[fields:, second], lane_at) for ref in sides], axis=0
            )
            plan_blocks.append(jnp.dot(spread, plan_block, preferred_element_type=jnp.float32))
        for slot in range(len(ts)):
            for side in range(2):
                windows[slot, fields * side : fields * (side + 1), :] = blocks[slot][side].astype(
                    jnp.float32
                )
        results = []
        for slot in range(len(ts)):
            code, lat_weight, lon_weight = [
                plan_blocks[slot][fields * at : fields * (at + 1)] for at in range(3)
            ]
            sources = [
                windows[slot, slices * position : slices * position + fields, :].astype(
                    jnp.bfloat16
                )
                for position in range(2 * RIM + 1)
            ]
            results.append(
                interpolate(sources, lane_plan(code), corner_weights(lat_weight, lon_weight))
            )
        for t, result in zip(ts, results):
            departed[:, tile_at(t)] = result

    in_groups(basis.shape[1] // LANES, RIM_AT_ONCE, group_of)
    fourier = jnp.concatenate(
        [
            lax.dot_general(
                basis[...],
                values[...],
                (((1,), (1,)), ((), ())),
                preferred_element_type=jnp.float32,
            )
            for values in (inner_departed, departed)
        ],
        axis=1,
    )
    levs = fourier_out.shape[1]
    for pair in range(fourier_out.shape[0]):
        block = fourier[4 * pair : 4 * pair + 4].astype(jnp.bfloat16)
        for lev in range(levs):
            fourier_out[pair, lev] = block


def legendre_kernel(limit, coeffs, spread_analysis, out, spread_coeffs, *, levs, slices):
    members, _, rows = coeffs.shape
    bands = members // levs
    col_count = spread_analysis.shape[1]
    inner = rows // slices - EDGE
    column = lax.broadcasted_iota(jnp.int32, (1, LANES), 1)
    rim_at = column - inner * slices
    slice_of = jnp.where(rim_at < 0, column // inner, rim_at % slices)
    slice_of = jnp.where(column < rows, slice_of, -1)

    def spread(band):
        block = jnp.concatenate(
            [coeffs[band * levs + lev].astype(jnp.float32) for lev in range(levs)], axis=0
        )
        block = jnp.concatenate(
            [block, jnp.zeros((block.shape[0], LANES - rows), jnp.float32)], axis=1
        )
        spread_coeffs[:, tile_at(band)] = jnp.concatenate(
            [jnp.where(slice_of == f, block, 0.0) for f in range(slices)], axis=0
        ).astype(jnp.bfloat16)

    if bands <= 16:
        for band in range(bands):
            spread(band)
    else:
        lax.fori_loop(0, bands, lambda band, carry: (spread(band), carry)[1], 0)
    total = jnp.dot(
        spread_coeffs[...], spread_analysis[...], preferred_element_type=jnp.float32
    )
    first_wave = lax.broadcasted_iota(jnp.int32, (2, col_count), 1) < limit[0:1, 0:1]
    for f in range(slices):
        for lev in range(levs):
            at = (f * levs + lev) * 4
            out[lev * slices + f] = jnp.where(first_wave, total[at : at + 2], total[at + 2 : at + 4])


def shards(grid, dep_row, dep_col, lat_frac, lon_frac, pair_ids, analysis):
    slices, band_rows, lon_count = grid.shape
    pairs = pair_ids.shape[0]
    col_count = analysis.shape[2]
    bands, levs = lax.axis_size("lat"), lax.axis_size("lev")
    inner = band_rows - 2 * RIM
    windows = -(-lon_count // SPAN)
    held_rows = -(-band_rows // 8) * 8
    fields = slices * EDGE
    band_start = jnp.reshape(lax.axis_index("lat") * band_rows, (1,)).astype(jnp.int32)
    place = jnp.stack([lax.axis_index("lat"), lax.axis_index("lev") * col_count])
    vmem = pl.BlockSpec(memory_space=pltpu.VMEM)
    smem = pl.BlockSpec(memory_space=pltpu.SMEM)
    params = pltpu.CompilerParams(vmem_limit_bytes=48 * 2**20)

    rows = grid.transpose(1, 0, 2).reshape(band_rows * slices, lon_count)
    rim_shape = jax.ShapeDtypeStruct((fields + 4 * RIM, lon_count), jnp.bfloat16)
    own_rim, sent_rim, plans = pl.pallas_call(
        pack_kernel,
        out_shape=(
            rim_shape,
            rim_shape,
            jax.ShapeDtypeStruct((3 * inner, lon_count), jnp.bfloat16),
        ),
        in_specs=[smem] + [vmem] * 5,
        out_specs=(vmem,) * 3,
        scratch_shapes=[pltpu.VMEM((5, 4, held_rows, LANES), jnp.float32)],
        compiler_params=params,
    )(band_start, rows, dep_row, dep_col, lat_frac, lon_frac)
    arrived_rim = lax.ppermute(sent_rim, "lat", [(i, (i + 1) % bands) for i in range(bands)])

    inner_departed = pl.pallas_call(
        functools.partial(inner_kernel, slices=slices),
        out_shape=jax.ShapeDtypeStruct((slices * inner, windows * LANES), jnp.bfloat16),
        in_specs=[vmem] * 2,
        out_specs=vmem,
        scratch_shapes=[pltpu.VMEM((INNER_AT_ONCE, band_rows * slices, LANES), jnp.float32)],
        compiler_params=params,
        cost_estimate=pl.CostEstimate(flops=100_000_000, bytes_accessed=2_000_000, transcendentals=0),
    )(rows, plans)

    basis, limit = pl.pallas_call(
        functools.partial(basis_kernel, lon_count=lon_count),
        out_shape=(
            jax.ShapeDtypeStruct((4 * pairs, windows * LANES), jnp.bfloat16),
            jax.ShapeDtypeStruct((8, LANES), jnp.int32),
        ),
        in_specs=[smem] * 2,
        out_specs=(vmem,) * 2,
        scratch_shapes=[pltpu.VMEM((4 * pairs, LANES), jnp.float32)],
        compiler_params=params,
    )(place, pair_ids)

    held_coeffs = slices * band_rows
    fourier = pl.pallas_call(
        functools.partial(rim_kernel, slices=slices),
        out_shape=jax.ShapeDtypeStruct((pairs, levs, 4, held_coeffs), jnp.bfloat16),
        in_specs=[vmem] * 4,
        out_specs=vmem,
        scratch_shapes=[
            pltpu.VMEM((RIM_AT_ONCE, 2 * fields, LANES), jnp.float32),
            pltpu.VMEM((fields, windows * LANES), jnp.bfloat16),
        ],
        compiler_params=params,
    )(arrived_rim, own_rim, basis, inner_departed)

    values = analysis[0].reshape(bands, band_rows, col_count)
    before = jnp.roll(values[:, band_rows - RIM :], 1, axis=0)
    spread_rows = [values[:, RIM : RIM + inner]] * slices
    for rim in (before, values[:, :RIM]):
        for row in range(RIM):
            spread_rows += [rim[:, row : row + 1]] * slices
    spread_rows.append(jnp.zeros((bands, LANES - held_coeffs, col_count), jnp.bfloat16))
    spread_analysis = jnp.concatenate(spread_rows, axis=1).reshape(bands * LANES, col_count)

    coeffs = lax.all_to_all(
        fourier.reshape(pairs * levs, 4, held_coeffs),
        ("lat", "lev"),
        split_axis=0,
        concat_axis=0,
        tiled=True,
    )
    out = pl.pallas_call(
        functools.partial(legendre_kernel, levs=levs, slices=slices),
        out_shape=jax.ShapeDtypeStruct((levs * slices, 2, col_count), jnp.float32),
        in_specs=[vmem] * 3,
        out_specs=vmem,
        scratch_shapes=[pltpu.VMEM((4 * levs * slices, bands * LANES), jnp.bfloat16)],
        compiler_params=params,
    )(limit, coeffs, spread_analysis)
    return out[None]


def solution(mesh):
    return jax.shard_map(
        shards,
        mesh=mesh,
        in_specs=(
            P("lev", "lat", None),
            P("lat", None),
            P("lat", None),
            P("lat", None),
            P("lat", None),
            P(),
            P("lat", None, "lev"),
        ),
        out_specs=P("lat", None, None, "lev"),
        check_vma=False,
    )
```

```python
import functools
import math

import jax
import jax.numpy as jnp
from jax import lax
from jax.experimental import pallas as pl
from jax.experimental.pallas import tpu as pltpu
from jax.sharding import PartitionSpec as P

NMAX = 1279
LANES = 128
RIM = 2
EDGE = 2 * RIM
REACH = 8
SPAN = LANES - 2 * REACH - 1
ROW_BITS = 5
INNER_AT_ONCE = 2
RIM_AT_ONCE = 4


def lane_gather(values, indices):
    numbers = lax.GatherDimensionNumbers(
        offset_dims=(),
        collapsed_slice_dims=(1,),
        start_index_map=(1,),
        operand_batching_dims=(0,),
        start_indices_batching_dims=(0,),
    )
    return lax.gather(
        values,
        indices[..., None],
        numbers,
        (1, 1),
        mode=lax.GatherScatterMode.PROMISE_IN_BOUNDS,
    )


def tile_at(t):
    return slice(t * LANES, (t + 1) * LANES)


def cut_of(start, lon_count):
    tiles = lon_count // LANES
    first, lane_at = divmod(start % lon_count, LANES)
    return tile_at(first), tile_at((first + 1) % tiles), lane_at


def cut(first, second, lane_at):
    if lane_at == 0:
        return first
    lane = lax.broadcasted_iota(jnp.int32, first.shape, 1).astype(jnp.int16)
    joined = jnp.where(lane >= jnp.int16(lane_at), first, second)
    return pltpu.roll(joined, LANES - lane_at, 1)


def lane_plan(code):
    code = code.astype(jnp.int32)
    west = lax.broadcasted_iota(jnp.int32, code.shape, 1) + (code & (1 << ROW_BITS) - 1)
    west_lane = (west & (LANES - 1)).astype(jnp.int16)
    east_lane = ((west + 1) & (LANES - 1)).astype(jnp.int16)
    row_step = (code >> ROW_BITS).astype(jnp.float32).astype(jnp.bfloat16)
    return west_lane, east_lane, row_step


def corner_weights(lat_weight, lon_weight):
    south, north = 1.0 - lat_weight, lat_weight
    west, east = 1.0 - lon_weight, lon_weight
    return south * west, south * east, north * west, north * east


def interpolate(sources, plan, weights):
    west_lane, east_lane, row_step = plan
    masks = [row_step == float(step) for step in range(2 * RIM - 1)]

    def pick(gathered):
        low, high = gathered[2 * RIM - 1], gathered[2 * RIM]
        for position in range(2 * RIM - 2, -1, -1):
            low = jnp.where(masks[position], gathered[position], low)
            high = jnp.where(masks[position], gathered[position + 1], high)
        return low.astype(jnp.float32), high.astype(jnp.float32)

    west_low, west_high = pick([lane_gather(source, west_lane) for source in sources])
    east_low, east_high = pick([lane_gather(source, east_lane) for source in sources])
    departed = (
        weights[0] * west_low
        + weights[1] * east_low
        + weights[2] * west_high
        + weights[3] * east_high
    )
    return departed.astype(jnp.bfloat16)


def in_groups(count, at_once, group):
    for at in range(0, count, at_once):
        group(list(range(at, min(at + at_once, count))))


def pack_kernel(
    band_start, rows, dep_row, dep_col, lat_frac, lon_frac, own_out, sent_out, plan_out, held
):
    band_rows, lon_count = dep_row.shape
    inner = band_rows - 2 * RIM
    fields = rows.shape[0] // band_rows * EDGE
    first_row = band_start[0]

    for t in range(lon_count // LANES):
        cols, slot = tile_at(t), t % 5
        row = lax.broadcasted_iota(jnp.int32, (band_rows, LANES), 0)
        lane = lax.broadcasted_iota(jnp.int32, (band_rows, LANES), 1)
        shift = dep_col[:, cols] - (lane + t * LANES)
        shift = jnp.where(shift > lon_count // 2, shift - lon_count, shift)
        shift = jnp.where(shift < -(lon_count // 2), shift + lon_count, shift)
        row_step = dep_row[:, cols] - (first_row + row) + RIM
        held[slot, 0, 0:band_rows, :] = row_step.astype(jnp.float32)
        held[slot, 1, 0:band_rows, :] = (shift + REACH).astype(jnp.float32)
        held[slot, 2, 0:band_rows, :] = lat_frac[:, cols].astype(jnp.float32)
        held[slot, 3, 0:band_rows, :] = lon_frac[:, cols].astype(jnp.float32)
        for out, start, plan_start in (
            (own_out, 0, 0),
            (sent_out, rows.shape[0] - fields, band_rows - RIM),
        ):
            out[0:fields, cols] = rows[start : start + fields, cols]
            out[fields:, cols] = jnp.concatenate(
                [held[slot, at, plan_start : plan_start + RIM, :] for at in range(4)], axis=0
            ).astype(jnp.bfloat16)
        middle = [held[slot, at, RIM : RIM + inner, :] for at in range(4)]
        middle = [middle[0] * (1 << ROW_BITS) + middle[1], middle[2], middle[3]]
        for at in range(3):
            plan_out[at * inner : (at + 1) * inner, cols] = middle[at].astype(jnp.bfloat16)


def fill_waves(pair_ids, waves):
    def rows_of(group, carry):
        row = lax.broadcasted_iota(jnp.int32, (16, LANES), 0)
        pair = jnp.full((16, LANES), pair_ids[4 * group + 3], jnp.int32)
        for at in (2, 1, 0):
            pair = jnp.where(row < 4 * (at + 1), pair_ids[4 * group + at], pair)
        wave = jnp.where((row & 2) == 0, pair, NMAX + 1 - pair)
        waves[pl.ds(pl.multiple_of(group * 16, 16), 16), :] = wave.astype(jnp.float32)
        return carry

    lax.fori_loop(0, waves.shape[0] // 16, rows_of, 0)


def basis_tile(t, wave, lon_count):
    lane = lax.broadcasted_iota(jnp.int32, (16, LANES), 1)
    row = lax.broadcasted_iota(jnp.int32, (16, LANES), 0)
    longitude = lane + t * SPAN
    quarter = jnp.where((row & 1) == 0, 0.0, float(lon_count // 4))
    steps = longitude.astype(jnp.float32) * wave + quarter
    turns = jnp.floor(steps * (1.0 / lon_count) + 0.5)
    angle = lon_count // 4 - jnp.abs(steps - turns * lon_count)
    angle = angle * (2.0 * math.pi / lon_count)
    square = angle * angle
    series = jnp.float32(-1.0 / 39916800.0)
    for term in (1.0 / 362880.0, -1.0 / 5040.0, 1.0 / 120.0, -1.0 / 6.0, 1.0):
        series = series * square + term
    taken = (lane < SPAN) & (longitude < lon_count)
    return jnp.where(taken, angle * series, 0.0).astype(jnp.bfloat16)


def inner_kernel(grid, plans, departed, windows, *, slices):
    lon_count = grid.shape[1]
    inner = plans.shape[0] // 3

    def group_of(ts):
        blocks, plan_blocks = [], []
        for t in ts:
            first, second, lane_at = cut_of(t * SPAN - REACH, lon_count)
            blocks.append(cut(grid[:, first], grid[:, second], lane_at).astype(jnp.float32))
            first, second, lane_at = cut_of(t * SPAN, lon_count)
            plan_blocks.append(
                [
                    cut(
                        plans[at * inner : (at + 1) * inner, first],
                        plans[at * inner : (at + 1) * inner, second],
                        lane_at,
                    ).astype(jnp.float32)
                    for at in range(3)
                ]
            )
        for slot, block in enumerate(blocks):
            windows[slot] = block
        results = []
        for slot, (code, lat_weight, lon_weight) in enumerate(plan_blocks):
            plan = lane_plan(code)
            weights = corner_weights(lat_weight, lon_weight)
            for f in range(slices):
                sources = [
                    windows[slot, pl.ds(slices * position + f, inner, stride=slices), :].astype(
                        jnp.bfloat16
                    )
                    for position in range(2 * RIM + 1)
                ]
                results.append((ts[slot], f, interpolate(sources, plan, weights)))
        for t, f, result in results:
            departed[f * inner : (f + 1) * inner, tile_at(t)] = result

    in_groups(departed.shape[1] // LANES, INNER_AT_ONCE, group_of)


def rim_kernel(
    pair_ids, arrived, own, inner_departed, fourier_out, windows, departed, basis, waves, *, slices
):
    lon_count = arrived.shape[1]
    fields = slices * EDGE
    sides = (arrived, own)
    wanted = lax.broadcasted_iota(jnp.int32, (3 * fields, 16), 0)
    held = lax.broadcasted_iota(jnp.int32, (3 * fields, 16), 1)
    kind, rim_row = wanted // fields, wanted % fields // slices
    base = rim_row // RIM * 8 + rim_row % RIM
    spread = jnp.where((kind == 0) & (held == base), float(1 << ROW_BITS), 0.0)
    spread += jnp.where(held == base + RIM * (kind + 1), 1.0, 0.0)
    spread = spread.astype(jnp.bfloat16)

    def group_of(ts):
        blocks, plan_blocks = [], []
        for t in ts:
            first, second, lane_at = cut_of(t * SPAN - REACH, lon_count)
            blocks.append(
                [cut(ref[0:fields, first], ref[0:fields, second], lane_at) for ref in sides]
            )
            first, second, lane_at = cut_of(t * SPAN, lon_count)
            plan_block = jnp.concatenate(
                [cut(ref[fields:, first], ref[fields:, second], lane_at) for ref in sides], axis=0
            )
            plan_blocks.append(jnp.dot(spread, plan_block, preferred_element_type=jnp.float32))
        for slot in range(len(ts)):
            for side in range(2):
                windows[slot, fields * side : fields * (side + 1), :] = blocks[slot][side].astype(
                    jnp.float32
                )
        results = []
        for slot in range(len(ts)):
            code, lat_weight, lon_weight = [
                plan_blocks[slot][fields * at : fields * (at + 1)] for at in range(3)
            ]
            sources = [
                windows[slot, slices * position : slices * position + fields, :].astype(
                    jnp.bfloat16
                )
                for position in range(2 * RIM + 1)
            ]
            results.append(
                interpolate(sources, lane_plan(code), corner_weights(lat_weight, lon_weight))
            )
        for t, result in zip(ts, results):
            departed[:, tile_at(t)] = result
            for at in range(0, waves.shape[0] if few else 0, 16):
                basis[at : at + 16, tile_at(t)] = basis_tile(t, waves[at : at + 16, :], lon_count)

    fill_waves(pair_ids, waves)
    few = waves.shape[0] <= 64
    if not few:

        def rows_of(group, carry):
            rows = pl.ds(pl.multiple_of(group * 16, 16), 16)
            for t in range(basis.shape[1] // LANES):
                basis[rows, tile_at(t)] = basis_tile(t, waves[rows, :], lon_count)
            return carry

        lax.fori_loop(0, waves.shape[0] // 16, rows_of, 0)
    in_groups(basis.shape[1] // LANES, RIM_AT_ONCE, group_of)
    fourier = jnp.concatenate(
        [
            lax.dot_general(
                basis[...],
                values[...],
                (((1,), (1,)), ((), ())),
                preferred_element_type=jnp.float32,
            )
            for values in (inner_departed, departed)
        ],
        axis=1,
    )
    levs = fourier_out.shape[1]
    for pair in range(fourier_out.shape[0]):
        block = fourier[4 * pair : 4 * pair + 4].astype(jnp.bfloat16)
        for lev in range(levs):
            fourier_out[pair, lev] = block


def legendre_kernel(place, pair_ids, coeffs, spread_analysis, out, spread_coeffs, *, levs, slices):
    members, _, rows = coeffs.shape
    bands = members // levs
    col_count = spread_analysis.shape[1]
    inner = rows // slices - EDGE
    column = lax.broadcasted_iota(jnp.int32, (1, LANES), 1)
    rim_at = column - inner * slices
    slice_of = jnp.where(rim_at < 0, column // inner, rim_at % slices)
    slice_of = jnp.where(column < rows, slice_of, -1)

    def spread(band):
        block = jnp.concatenate(
            [coeffs[band * levs + lev].astype(jnp.float32) for lev in range(levs)], axis=0
        )
        block = jnp.concatenate(
            [block, jnp.zeros((block.shape[0], LANES - rows), jnp.float32)], axis=1
        )
        spread_coeffs[:, tile_at(band)] = jnp.concatenate(
            [jnp.where(slice_of == f, block, 0.0) for f in range(slices)], axis=0
        ).astype(jnp.bfloat16)

    for band in range(bands):
        spread(band)
    total = jnp.dot(
        spread_coeffs[...], spread_analysis[...], preferred_element_type=jnp.float32
    )
    columns = place[1] + lax.broadcasted_iota(jnp.int32, (2, col_count), 1)
    first_wave = columns < NMAX + 1 - pair_ids[place[0]]
    for f in range(slices):
        for lev in range(levs):
            at = (f * levs + lev) * 4
            out[lev * slices + f] = jnp.where(first_wave, total[at : at + 2], total[at + 2 : at + 4])


def shards(grid, dep_row, dep_col, lat_frac, lon_frac, pair_ids, analysis):
    slices, band_rows, lon_count = grid.shape
    pairs = pair_ids.shape[0]
    col_count = analysis.shape[2]
    bands, levs = lax.axis_size("lat"), lax.axis_size("lev")
    inner = band_rows - 2 * RIM
    windows = -(-lon_count // SPAN)
    held_rows = -(-band_rows // 8) * 8
    fields = slices * EDGE
    band_start = jnp.reshape(lax.axis_index("lat") * band_rows, (1,)).astype(jnp.int32)
    place = jnp.stack([lax.axis_index("lat"), lax.axis_index("lev") * col_count])
    vmem = pl.BlockSpec(memory_space=pltpu.VMEM)
    smem = pl.BlockSpec(memory_space=pltpu.SMEM)
    params = pltpu.CompilerParams(vmem_limit_bytes=48 * 2**20)

    rows = grid.transpose(1, 0, 2).reshape(band_rows * slices, lon_count)
    rim_shape = jax.ShapeDtypeStruct((fields + 4 * RIM, lon_count), jnp.bfloat16)
    own_rim, sent_rim, plans = pl.pallas_call(
        pack_kernel,
        out_shape=(
            rim_shape,
            rim_shape,
            jax.ShapeDtypeStruct((3 * inner, lon_count), jnp.bfloat16),
        ),
        in_specs=[smem] + [vmem] * 5,
        out_specs=(vmem,) * 3,
        scratch_shapes=[pltpu.VMEM((5, 4, held_rows, LANES), jnp.float32)],
        compiler_params=params,
    )(band_start, rows, dep_row, dep_col, lat_frac, lon_frac)
    arrived_rim = lax.ppermute(sent_rim, "lat", [(i, (i + 1) % bands) for i in range(bands)])

    inner_departed = pl.pallas_call(
        functools.partial(inner_kernel, slices=slices),
        out_shape=jax.ShapeDtypeStruct((slices * inner, windows * LANES), jnp.bfloat16),
        in_specs=[vmem] * 2,
        out_specs=vmem,
        scratch_shapes=[pltpu.VMEM((INNER_AT_ONCE, band_rows * slices, LANES), jnp.float32)],
        compiler_params=params,
        cost_estimate=pl.CostEstimate(flops=100_000_000, bytes_accessed=2_000_000, transcendentals=0),
    )(rows, plans)

    held_coeffs = slices * band_rows
    fourier = pl.pallas_call(
        functools.partial(rim_kernel, slices=slices),
        out_shape=jax.ShapeDtypeStruct((pairs, levs, 4, held_coeffs), jnp.bfloat16),
        in_specs=[smem] + [vmem] * 3,
        out_specs=vmem,
        scratch_shapes=[
            pltpu.VMEM((RIM_AT_ONCE, 2 * fields, LANES), jnp.float32),
            pltpu.VMEM((fields, windows * LANES), jnp.bfloat16),
            pltpu.VMEM((4 * pairs, windows * LANES), jnp.bfloat16),
            pltpu.VMEM((4 * pairs, LANES), jnp.float32),
        ],
        compiler_params=params,
    )(pair_ids, arrived_rim, own_rim, inner_departed)
    fourier, analysis = lax.optimization_barrier((fourier, analysis))

    values = analysis[0].reshape(bands, band_rows, col_count)
    before = jnp.roll(values[:, band_rows - RIM :], 1, axis=0)
    spread_rows = [values[:, RIM : RIM + inner]] * slices
    for rim in (before, values[:, :RIM]):
        for row in range(RIM):
            spread_rows += [rim[:, row : row + 1]] * slices
    spread_rows.append(jnp.zeros((bands, LANES - held_coeffs, col_count), jnp.bfloat16))
    spread_analysis = jnp.concatenate(spread_rows, axis=1).reshape(bands * LANES, col_count)

    coeffs = lax.all_to_all(
        fourier.reshape(pairs * levs, 4, held_coeffs),
        ("lat", "lev"),
        split_axis=0,
        concat_axis=0,
        tiled=True,
    )
    out = pl.pallas_call(
        functools.partial(legendre_kernel, levs=levs, slices=slices),
        out_shape=jax.ShapeDtypeStruct((levs * slices, 2, col_count), jnp.float32),
        in_specs=[smem] * 2 + [vmem] * 2,
        out_specs=vmem,
        scratch_shapes=[pltpu.VMEM((4 * levs * slices, bands * LANES), jnp.bfloat16)],
        compiler_params=params,
    )(place, pair_ids, coeffs, spread_analysis)
    return out[None]


def solution(mesh):
    return jax.shard_map(
        shards,
        mesh=mesh,
        in_specs=(
            P("lev", "lat", None),
            P("lat", None),
            P("lat", None),
            P("lat", None),
            P("lat", None),
            P(),
            P("lat", None, "lev"),
        ),
        out_specs=P("lat", None, None, "lev"),
        check_vma=False,
    )
```

```python
import functools
import math

import jax
import jax.numpy as jnp
from jax import lax
from jax.experimental import pallas as pl
from jax.experimental.pallas import tpu as pltpu
from jax.sharding import PartitionSpec as P

NMAX = 1279
LANES = 128
RIM = 2
EDGE = 2 * RIM
REACH = 8
SPAN = LANES - 2 * REACH - 1
ROW_BITS = 5
INNER_AT_ONCE = 2
RIM_AT_ONCE = 4


def lane_gather(values, indices):
    numbers = lax.GatherDimensionNumbers(
        offset_dims=(),
        collapsed_slice_dims=(1,),
        start_index_map=(1,),
        operand_batching_dims=(0,),
        start_indices_batching_dims=(0,),
    )
    return lax.gather(
        values,
        indices[..., None],
        numbers,
        (1, 1),
        mode=lax.GatherScatterMode.PROMISE_IN_BOUNDS,
    )


def tile_at(t):
    return slice(t * LANES, (t + 1) * LANES)


def cut_of(start, lon_count):
    tiles = lon_count // LANES
    first, lane_at = divmod(start % lon_count, LANES)
    return tile_at(first), tile_at((first + 1) % tiles), lane_at


def cut(first, second, lane_at):
    if lane_at == 0:
        return first
    lane = lax.broadcasted_iota(jnp.int32, first.shape, 1).astype(jnp.int16)
    joined = jnp.where(lane >= jnp.int16(lane_at), first, second)
    return pltpu.roll(joined, LANES - lane_at, 1)


def lane_plan(code):
    code = code.astype(jnp.int32)
    west = lax.broadcasted_iota(jnp.int32, code.shape, 1) + (code & (1 << ROW_BITS) - 1)
    west_lane = (west & (LANES - 1)).astype(jnp.int16)
    east_lane = ((west + 1) & (LANES - 1)).astype(jnp.int16)
    row_step = (code >> ROW_BITS).astype(jnp.float32).astype(jnp.bfloat16)
    return west_lane, east_lane, row_step


def corner_weights(lat_weight, lon_weight):
    south, north = 1.0 - lat_weight, lat_weight
    west, east = 1.0 - lon_weight, lon_weight
    return south * west, south * east, north * west, north * east


def interpolate(sources, plan, weights):
    west_lane, east_lane, row_step = plan
    masks = [row_step == float(step) for step in range(2 * RIM - 1)]

    def pick(gathered):
        low, high = gathered[2 * RIM - 1], gathered[2 * RIM]
        for position in range(2 * RIM - 2, -1, -1):
            low = jnp.where(masks[position], gathered[position], low)
            high = jnp.where(masks[position], gathered[position + 1], high)
        return low.astype(jnp.float32), high.astype(jnp.float32)

    west_low, west_high = pick([lane_gather(source, west_lane) for source in sources])
    east_low, east_high = pick([lane_gather(source, east_lane) for source in sources])
    departed = (
        weights[0] * west_low
        + weights[1] * east_low
        + weights[2] * west_high
        + weights[3] * east_high
    )
    return departed.astype(jnp.bfloat16)


def in_groups(count, at_once, group):
    for at in range(0, count, at_once):
        group(list(range(at, min(at + at_once, count))))


def pack_kernel(
    band_start, rows, dep_row, dep_col, lat_frac, lon_frac, own_out, sent_out, plan_out, held
):
    band_rows, lon_count = dep_row.shape
    inner = band_rows - 2 * RIM
    fields = rows.shape[0] // band_rows * EDGE
    first_row = band_start[0]

    for t in range(lon_count // LANES):
        cols, slot = tile_at(t), t % 5
        row = lax.broadcasted_iota(jnp.int32, (band_rows, LANES), 0)
        lane = lax.broadcasted_iota(jnp.int32, (band_rows, LANES), 1)
        shift = dep_col[:, cols] - (lane + t * LANES)
        shift = jnp.where(shift > lon_count // 2, shift - lon_count, shift)
        shift = jnp.where(shift < -(lon_count // 2), shift + lon_count, shift)
        row_step = dep_row[:, cols] - (first_row + row) + RIM
        held[slot, 0, 0:band_rows, :] = row_step.astype(jnp.float32)
        held[slot, 1, 0:band_rows, :] = (shift + REACH).astype(jnp.float32)
        held[slot, 2, 0:band_rows, :] = lat_frac[:, cols].astype(jnp.float32)
        held[slot, 3, 0:band_rows, :] = lon_frac[:, cols].astype(jnp.float32)
        for out, start, plan_start in (
            (own_out, 0, 0),
            (sent_out, rows.shape[0] - fields, band_rows - RIM),
        ):
            out[0:fields, cols] = rows[start : start + fields, cols]
            out[fields:, cols] = jnp.concatenate(
                [held[slot, at, plan_start : plan_start + RIM, :] for at in range(4)], axis=0
            ).astype(jnp.bfloat16)
        middle = [held[slot, at, RIM : RIM + inner, :] for at in range(4)]
        middle = [middle[0] * (1 << ROW_BITS) + middle[1], middle[2], middle[3]]
        for at in range(3):
            plan_out[at * inner : (at + 1) * inner, cols] = middle[at].astype(jnp.bfloat16)


def waves_of(ids, group):
    pair = jnp.concatenate(
        [jnp.broadcast_to(ids[pl.ds(4 * group + at, 1), :], (4, LANES)) for at in range(4)], axis=0
    )
    row = lax.broadcasted_iota(jnp.int32, (16, LANES), 0)
    return jnp.where((row & 2) == 0, pair, NMAX + 1 - pair)


def basis_tile(t, wave, lon_count):
    lane = lax.broadcasted_iota(jnp.int32, (16, LANES), 1)
    row = lax.broadcasted_iota(jnp.int32, (16, LANES), 0)
    longitude = lane + t * SPAN
    quarter = jnp.where((row & 1) == 0, 0.0, float(lon_count // 4))
    steps = longitude.astype(jnp.float32) * wave + quarter
    turns = jnp.floor(steps * (1.0 / lon_count) + 0.5)
    angle = lon_count // 4 - jnp.abs(steps - turns * lon_count)
    angle = angle * (2.0 * math.pi / lon_count)
    square = angle * angle
    series = jnp.float32(-1.0 / 39916800.0)
    for term in (1.0 / 362880.0, -1.0 / 5040.0, 1.0 / 120.0, -1.0 / 6.0, 1.0):
        series = series * square + term
    taken = (lane < SPAN) & (longitude < lon_count)
    return jnp.where(taken, angle * series, 0.0).astype(jnp.bfloat16)


def add_up(basis, values):
    return lax.dot_general(
        basis, values, (((1,), (1,)), ((), ())), preferred_element_type=jnp.float32
    )


def inner_kernel(grid, plans, ids, fourier_out, basis, windows, departed, *, slices):
    lon_count = grid.shape[1]
    inner = plans.shape[0] // 3
    groups = ids.shape[0] // 4
    few = groups <= 4
    waves = [waves_of(ids, at) for at in range(groups if few else 0)]

    def group_of(ts):
        blocks, plan_blocks = [], []
        for t in ts:
            first, second, lane_at = cut_of(t * SPAN - REACH, lon_count)
            blocks.append(cut(grid[:, first], grid[:, second], lane_at).astype(jnp.float32))
            first, second, lane_at = cut_of(t * SPAN, lon_count)
            plan_blocks.append(
                [
                    cut(
                        plans[at * inner : (at + 1) * inner, first],
                        plans[at * inner : (at + 1) * inner, second],
                        lane_at,
                    ).astype(jnp.float32)
                    for at in range(3)
                ]
            )
        for slot, block in enumerate(blocks):
            windows[slot] = block
        results = []
        for slot, (code, lat_weight, lon_weight) in enumerate(plan_blocks):
            plan = lane_plan(code)
            weights = corner_weights(lat_weight, lon_weight)
            for f in range(slices):
                sources = [
                    windows[slot, pl.ds(slices * position + f, inner, stride=slices), :].astype(
                        jnp.bfloat16
                    )
                    for position in range(2 * RIM + 1)
                ]
                results.append((ts[slot], f, interpolate(sources, plan, weights)))
        for t, f, result in results:
            departed[f * inner : (f + 1) * inner, tile_at(t)] = result
        for t in ts if few else ():
            for at, wave in enumerate(waves):
                basis[16 * at : 16 * at + 16, tile_at(t)] = basis_tile(t, wave, lon_count)

    if not few:

        def rows_of(group, carry):
            rows = pl.ds(pl.multiple_of(group * 16, 16), 16)
            for t in range(basis.shape[1] // LANES):
                basis[rows, tile_at(t)] = basis_tile(t, waves_of(ids, group), lon_count)
            return carry

        lax.fori_loop(0, groups, rows_of, 0)
    in_groups(departed.shape[1] // LANES, INNER_AT_ONCE, group_of)
    fourier_out[...] = add_up(basis[...], departed[...])


def rim_kernel(
    arrived, own, basis, inner_fourier, fourier_out, windows, departed, *, slices, owners
):
    lon_count = arrived.shape[1]
    fields = slices * EDGE
    sides = (arrived, own)
    wanted = lax.broadcasted_iota(jnp.int32, (3 * fields, 16), 0)
    held = lax.broadcasted_iota(jnp.int32, (3 * fields, 16), 1)
    kind, rim_row = wanted // fields, wanted % fields // slices
    base = rim_row // RIM * 8 + rim_row % RIM
    spread = jnp.where((kind == 0) & (held == base), float(1 << ROW_BITS), 0.0)
    spread += jnp.where(held == base + RIM * (kind + 1), 1.0, 0.0)
    spread = spread.astype(jnp.bfloat16)

    def group_of(ts):
        blocks, plan_blocks = [], []
        for t in ts:
            first, second, lane_at = cut_of(t * SPAN - REACH, lon_count)
            blocks.append(
                [cut(ref[0:fields, first], ref[0:fields, second], lane_at) for ref in sides]
            )
            first, second, lane_at = cut_of(t * SPAN, lon_count)
            plan_block = jnp.concatenate(
                [cut(ref[fields:, first], ref[fields:, second], lane_at) for ref in sides], axis=0
            )
            plan_blocks.append(jnp.dot(spread, plan_block, preferred_element_type=jnp.float32))
        for slot in range(len(ts)):
            for side in range(2):
                windows[slot, fields * side : fields * (side + 1), :] = blocks[slot][side].astype(
                    jnp.float32
                )
        results = []
        for slot in range(len(ts)):
            code, lat_weight, lon_weight = [
                plan_blocks[slot][fields * at : fields * (at + 1)] for at in range(3)
            ]
            sources = [
                windows[slot, slices * position : slices * position + fields, :].astype(
                    jnp.bfloat16
                )
                for position in range(2 * RIM + 1)
            ]
            results.append(
                interpolate(sources, lane_plan(code), corner_weights(lat_weight, lon_weight))
            )
        for t, result in zip(ts, results):
            departed[:, tile_at(t)] = result

    in_groups(basis.shape[1] // LANES, RIM_AT_ONCE, group_of)
    fourier = jnp.concatenate([inner_fourier[...], add_up(basis[...], departed[...])], axis=1)
    for at, pair in enumerate(owners):
        fourier_out[at] = fourier[4 * pair : 4 * pair + 4].astype(jnp.bfloat16)


def legendre_kernel(first_wave, coeffs, spread_analysis, out, spread_coeffs, *, levs, slices, order):
    members, _, rows = coeffs.shape
    bands = members // levs
    col_count = spread_analysis.shape[1]
    inner = rows // slices - EDGE
    column = lax.broadcasted_iota(jnp.int32, (1, LANES), 1)
    rim_at = column - inner * slices
    slice_of = jnp.where(rim_at < 0, column // inner, rim_at % slices)
    slice_of = jnp.where(column < rows, slice_of, -1)

    def spread(band):
        block = jnp.concatenate(
            [coeffs[order.index(band * levs + lev)].astype(jnp.float32) for lev in range(levs)],
            axis=0,
        )
        block = jnp.concatenate(
            [block, jnp.zeros((block.shape[0], LANES - rows), jnp.float32)], axis=1
        )
        spread_coeffs[:, tile_at(band)] = jnp.concatenate(
            [jnp.where(slice_of == f, block, 0.0) for f in range(slices)], axis=0
        ).astype(jnp.bfloat16)

    for band in range(bands):
        spread(band)
    total = jnp.dot(
        spread_coeffs[...], spread_analysis[...], preferred_element_type=jnp.float32
    )
    first = first_wave[0:2, :] > 0.0
    for f in range(slices):
        for lev in range(levs):
            at = (f * levs + lev) * 4
            out[lev * slices + f] = jnp.where(first, total[at : at + 2], total[at + 2 : at + 4])


def shards(grid, dep_row, dep_col, lat_frac, lon_frac, pair_ids, analysis):
    slices, band_rows, lon_count = grid.shape
    pairs = pair_ids.shape[0]
    col_count = analysis.shape[2]
    bands, levs = lax.axis_size("lat"), lax.axis_size("lev")
    inner = band_rows - 2 * RIM
    windows = -(-lon_count // SPAN)
    held_rows = -(-band_rows // 8) * 8
    fields = slices * EDGE
    band_start = jnp.reshape(lax.axis_index("lat") * band_rows, (1,)).astype(jnp.int32)
    vmem = pl.BlockSpec(memory_space=pltpu.VMEM)
    smem = pl.BlockSpec(memory_space=pltpu.SMEM)
    params = pltpu.CompilerParams(vmem_limit_bytes=48 * 2**20)

    rows = grid.transpose(1, 0, 2).reshape(band_rows * slices, lon_count)
    rim_shape = jax.ShapeDtypeStruct((fields + 4 * RIM, lon_count), jnp.bfloat16)
    own_rim, sent_rim, plans = pl.pallas_call(
        pack_kernel,
        out_shape=(
            rim_shape,
            rim_shape,
            jax.ShapeDtypeStruct((3 * inner, lon_count), jnp.bfloat16),
        ),
        in_specs=[smem] + [vmem] * 5,
        out_specs=(vmem,) * 3,
        scratch_shapes=[pltpu.VMEM((5, 4, held_rows, LANES), jnp.float32)],
        compiler_params=params,
    )(band_start, rows, dep_row, dep_col, lat_frac, lon_frac)
    arrived_rim = lax.ppermute(sent_rim, "lat", [(i, (i + 1) % bands) for i in range(bands)])

    plans, ids = lax.optimization_barrier((plans, pair_ids))
    ids = jnp.broadcast_to(ids.astype(jnp.float32)[:, None], (pairs, LANES))
    inner_fourier, basis = pl.pallas_call(
        functools.partial(inner_kernel, slices=slices),
        out_shape=(
            jax.ShapeDtypeStruct((4 * pairs, slices * inner), jnp.float32),
            jax.ShapeDtypeStruct((4 * pairs, windows * LANES), jnp.bfloat16),
        ),
        in_specs=[vmem] * 3,
        out_specs=(vmem,) * 2,
        scratch_shapes=[
            pltpu.VMEM((INNER_AT_ONCE, band_rows * slices, LANES), jnp.float32),
            pltpu.VMEM((slices * inner, windows * LANES), jnp.bfloat16),
        ],
        compiler_params=params,
        cost_estimate=pl.CostEstimate(flops=100_000_000, bytes_accessed=2_000_000, transcendentals=0),
    )(rows, plans, ids)

    held_coeffs = slices * band_rows
    members = bands * levs
    order = [(at + members // 2) % members for at in range(members)]
    fourier = pl.pallas_call(
        functools.partial(
            rim_kernel, slices=slices, owners=[member // levs for member in order]
        ),
        out_shape=jax.ShapeDtypeStruct((members, 4, held_coeffs), jnp.bfloat16),
        in_specs=[vmem] * 4,
        out_specs=vmem,
        scratch_shapes=[
            pltpu.VMEM((RIM_AT_ONCE, 2 * fields, LANES), jnp.float32),
            pltpu.VMEM((fields, windows * LANES), jnp.bfloat16),
        ],
        compiler_params=params,
    )(arrived_rim, own_rim, basis, inner_fourier)
    fourier, analysis, late_ids = lax.optimization_barrier((fourier, analysis, pair_ids))

    values = analysis[0].reshape(bands, band_rows, col_count)
    before = jnp.roll(values[:, band_rows - RIM :], 1, axis=0)
    spread_rows = [values[:, RIM : RIM + inner]] * slices
    for rim in (before, values[:, :RIM]):
        for row in range(RIM):
            spread_rows += [rim[:, row : row + 1]] * slices
    spread_rows.append(jnp.zeros((bands, LANES - held_coeffs, col_count), jnp.bfloat16))
    spread_analysis = jnp.concatenate(spread_rows, axis=1).reshape(bands * LANES, col_count)

    own_id = lax.dynamic_slice_in_dim(late_ids, lax.axis_index("lat"), 1)
    columns = lax.axis_index("lev") * col_count + jnp.arange(col_count, dtype=jnp.int32)
    first_wave = jnp.where(columns < NMAX + 1 - own_id, 1.0, 0.0)
    first_wave = jnp.broadcast_to(first_wave[None, :], (8, col_count))

    coeffs = lax.all_to_all(
        fourier, ("lat", "lev"), split_axis=0, concat_axis=0, axis_index_groups=[order], tiled=True
    )
    out = pl.pallas_call(
        functools.partial(legendre_kernel, levs=levs, slices=slices, order=order),
        out_shape=jax.ShapeDtypeStruct((levs * slices, 2, col_count), jnp.float32),
        in_specs=[vmem] * 3,
        out_specs=vmem,
        scratch_shapes=[pltpu.VMEM((4 * levs * slices, bands * LANES), jnp.bfloat16)],
        compiler_params=params,
    )(first_wave, coeffs, spread_analysis)
    return out[None]


def solution(mesh):
    return jax.shard_map(
        shards,
        mesh=mesh,
        in_specs=(
            P("lev", "lat", None),
            P("lat", None),
            P("lat", None),
            P("lat", None),
            P("lat", None),
            P(),
            P("lat", None, "lev"),
        ),
        out_specs=P("lat", None, None, "lev"),
        check_vma=False,
    )
```

```python
import functools
import math

import jax
import jax.numpy as jnp
from jax import lax
from jax.experimental import pallas as pl
from jax.experimental.pallas import tpu as pltpu
from jax.sharding import PartitionSpec as P

NMAX = 1279
LANES = 128
RIM = 2
EDGE = 2 * RIM
REACH = 8
SPAN = LANES - 2 * REACH - 1
ROW_BITS = 5
INNER_AT_ONCE = 2
RIM_AT_ONCE = 4
SUM_AT_ONCE = 8


def lane_gather(values, indices):
    numbers = lax.GatherDimensionNumbers(
        offset_dims=(),
        collapsed_slice_dims=(1,),
        start_index_map=(1,),
        operand_batching_dims=(0,),
        start_indices_batching_dims=(0,),
    )
    return lax.gather(
        values,
        indices[..., None],
        numbers,
        (1, 1),
        mode=lax.GatherScatterMode.PROMISE_IN_BOUNDS,
    )


def tile_at(t):
    return slice(t * LANES, (t + 1) * LANES)


def cut_of(start, lon_count):
    tiles = lon_count // LANES
    first, lane_at = divmod(start % lon_count, LANES)
    return tile_at(first), tile_at((first + 1) % tiles), lane_at


def cut(first, second, lane_at):
    if lane_at == 0:
        return first
    lane = lax.broadcasted_iota(jnp.int32, first.shape, 1).astype(jnp.int16)
    joined = jnp.where(lane >= jnp.int16(lane_at), first, second)
    return pltpu.roll(joined, LANES - lane_at, 1)


def lane_plan(code):
    code = code.astype(jnp.int32)
    west = lax.broadcasted_iota(jnp.int32, code.shape, 1) + (code & (1 << ROW_BITS) - 1)
    west_lane = (west & (LANES - 1)).astype(jnp.int16)
    east_lane = ((west + 1) & (LANES - 1)).astype(jnp.int16)
    row_step = (code >> ROW_BITS).astype(jnp.float32).astype(jnp.bfloat16)
    return west_lane, east_lane, row_step


def corner_weights(lat_weight, lon_weight):
    south, north = 1.0 - lat_weight, lat_weight
    west, east = 1.0 - lon_weight, lon_weight
    return south * west, south * east, north * west, north * east


def interpolate(sources, plan, weights):
    west_lane, east_lane, row_step = plan
    masks = [row_step == float(step) for step in range(2 * RIM - 1)]

    def pick(gathered):
        low, high = gathered[2 * RIM - 1], gathered[2 * RIM]
        for position in range(2 * RIM - 2, -1, -1):
            low = jnp.where(masks[position], gathered[position], low)
            high = jnp.where(masks[position], gathered[position + 1], high)
        return low.astype(jnp.float32), high.astype(jnp.float32)

    west_low, west_high = pick([lane_gather(source, west_lane) for source in sources])
    east_low, east_high = pick([lane_gather(source, east_lane) for source in sources])
    departed = (
        weights[0] * west_low
        + weights[1] * east_low
        + weights[2] * west_high
        + weights[3] * east_high
    )
    return departed.astype(jnp.bfloat16)


def in_groups(count, at_once, group):
    for at in range(0, count, at_once):
        group(list(range(at, min(at + at_once, count))))


def pack_kernel(
    band_start, grid_at, dep_row_at, dep_col_at, lat_frac_at, lon_frac_at,
    own_out, sent_out, plan_out,
    last_rows, dep_row, dep_col, lat_frac, lon_frac, held, joined, arrivals,
):
    band_rows, lon_count = dep_row.shape
    copies = [
        pltpu.make_async_copy(source, target, arrivals.at[at])
        for at, (source, target) in enumerate(
            (
                (dep_row_at, dep_row),
                (dep_col_at, dep_col),
                (lat_frac_at, lat_frac),
                (lon_frac_at, lon_frac),
                (grid_at.at[band_rows - EDGE : band_rows], last_rows),
            )
        )
    ]
    for copy in copies:
        copy.start()
    for copy in copies:
        copy.wait()
    inner = band_rows - 2 * RIM
    slices = last_rows.shape[1]
    fields = slices * EDGE
    first_row = band_start[0]

    for t in range(lon_count // LANES):
        cols, slot = tile_at(t), t % 5
        row = lax.broadcasted_iota(jnp.int32, (band_rows, LANES), 0)
        lane = lax.broadcasted_iota(jnp.int32, (band_rows, LANES), 1)
        shift = dep_col[:, cols] - (lane + t * LANES)
        shift = jnp.where(shift > lon_count // 2, shift - lon_count, shift)
        shift = jnp.where(shift < -(lon_count // 2), shift + lon_count, shift)
        row_step = dep_row[:, cols] - (first_row + row) + RIM
        held[slot, 0, 0:band_rows, :] = row_step.astype(jnp.float32)
        held[slot, 1, 0:band_rows, :] = (shift + REACH).astype(jnp.float32)
        held[slot, 2, 0:band_rows, :] = lat_frac[:, cols].astype(jnp.float32)
        held[slot, 3, 0:band_rows, :] = lon_frac[:, cols].astype(jnp.float32)
        for at in range(EDGE):
            joined[slot, at * slices : (at + 1) * slices, :] = last_rows[at, :, cols].astype(
                jnp.float32
            )
        sent_out[0:fields, cols] = joined[slot].astype(jnp.bfloat16)
        for out, to, start in ((own_out, 0, 0), (sent_out, fields, band_rows - RIM)):
            out[to : to + 4 * RIM, cols] = jnp.concatenate(
                [held[slot, at, start : start + RIM, :] for at in range(4)], axis=0
            ).astype(jnp.bfloat16)
        middle = [held[slot, at, RIM : RIM + inner, :] for at in range(4)]
        middle = [middle[0] * (1 << ROW_BITS) + middle[1], middle[2], middle[3]]
        for at in range(3):
            plan_out[at * inner : (at + 1) * inner, cols] = middle[at].astype(jnp.bfloat16)


def waves_of(ids, group):
    pair = jnp.concatenate(
        [jnp.broadcast_to(ids[pl.ds(4 * group + at, 1), :], (4, LANES)) for at in range(4)], axis=0
    )
    row = lax.broadcasted_iota(jnp.int32, (16, LANES), 0)
    return jnp.where((row & 2) == 0, pair, NMAX + 1 - pair)


def basis_tile(t, wave, lon_count):
    lane = lax.broadcasted_iota(jnp.int32, (16, LANES), 1)
    row = lax.broadcasted_iota(jnp.int32, (16, LANES), 0)
    longitude = lane + t * SPAN
    quarter = jnp.where((row & 1) == 0, 0.0, float(lon_count // 4))
    steps = longitude.astype(jnp.float32) * wave + quarter
    turns = jnp.floor(steps * (1.0 / lon_count) + 0.5)
    angle = lon_count // 4 - jnp.abs(steps - turns * lon_count)
    angle = angle * (2.0 * math.pi / lon_count)
    square = angle * angle
    series = jnp.float32(-1.0 / 39916800.0)
    for term in (1.0 / 362880.0, -1.0 / 5040.0, 1.0 / 120.0, -1.0 / 6.0, 1.0):
        series = series * square + term
    taken = (lane < SPAN) & (longitude < lon_count)
    return jnp.where(taken, angle * series, 0.0).astype(jnp.bfloat16)


def add_up(basis, values):
    total = None
    for at in range(0, basis.shape[1], SUM_AT_ONCE * LANES):
        cols = slice(at, min(at + SUM_AT_ONCE * LANES, basis.shape[1]))
        part = lax.dot_general(
            basis[:, cols],
            values[:, cols],
            (((1,), (1,)), ((), ())),
            preferred_element_type=jnp.float32,
        )
        total = part if total is None else total + part
    return total


def inner_kernel(grid, plans, ids, fourier_out, basis, windows, departed, *, slices):
    lon_count = grid.shape[1]
    inner = plans.shape[0] // 3
    groups = ids.shape[0] // 4
    few = groups <= 4
    waves = [waves_of(ids, at) for at in range(groups if few else 0)]

    def group_of(ts):
        blocks, plan_blocks = [], []
        for t in ts:
            first, second, lane_at = cut_of(t * SPAN - REACH, lon_count)
            blocks.append(cut(grid[:, first], grid[:, second], lane_at).astype(jnp.float32))
            first, second, lane_at = cut_of(t * SPAN, lon_count)
            plan_blocks.append(
                [
                    cut(
                        plans[at * inner : (at + 1) * inner, first],
                        plans[at * inner : (at + 1) * inner, second],
                        lane_at,
                    ).astype(jnp.float32)
                    for at in range(3)
                ]
            )
        for slot, block in enumerate(blocks):
            windows[slot] = block
        results = []
        for slot, (code, lat_weight, lon_weight) in enumerate(plan_blocks):
            plan = lane_plan(code)
            weights = corner_weights(lat_weight, lon_weight)
            for f in range(slices):
                sources = [
                    windows[slot, pl.ds(slices * position + f, inner, stride=slices), :].astype(
                        jnp.bfloat16
                    )
                    for position in range(2 * RIM + 1)
                ]
                results.append((ts[slot], f, interpolate(sources, plan, weights)))
        for t, f, result in results:
            departed[f * inner : (f + 1) * inner, tile_at(t)] = result
        for t in ts if few else ():
            for at, wave in enumerate(waves):
                basis[16 * at : 16 * at + 16, tile_at(t)] = basis_tile(t, wave, lon_count)

    if not few:

        def rows_of(group, carry):
            rows = pl.ds(pl.multiple_of(group * 16, 16), 16)
            for t in range(basis.shape[1] // LANES):
                basis[rows, tile_at(t)] = basis_tile(t, waves_of(ids, group), lon_count)
            return carry

        lax.fori_loop(0, groups, rows_of, 0)
    in_groups(departed.shape[1] // LANES, INNER_AT_ONCE, group_of)
    fourier_out[...] = add_up(basis, departed)


def rim_kernel(
    arrived, rows, own, basis, inner_fourier, fourier_out, windows, departed, *, slices, owners
):
    lon_count = arrived.shape[1]
    fields = slices * EDGE
    wanted = lax.broadcasted_iota(jnp.int32, (3 * fields, 16), 0)
    held = lax.broadcasted_iota(jnp.int32, (3 * fields, 16), 1)
    kind, rim_row = wanted // fields, wanted % fields // slices
    base = rim_row // RIM * 8 + rim_row % RIM
    spread = jnp.where((kind == 0) & (held == base), float(1 << ROW_BITS), 0.0)
    spread += jnp.where(held == base + RIM * (kind + 1), 1.0, 0.0)
    spread = spread.astype(jnp.bfloat16)

    def group_of(ts):
        blocks, plan_blocks = [], []
        for t in ts:
            first, second, lane_at = cut_of(t * SPAN - REACH, lon_count)
            blocks.append(
                [
                    cut(ref[0:fields, first], ref[0:fields, second], lane_at)
                    for ref in (arrived, rows)
                ]
            )
            first, second, lane_at = cut_of(t * SPAN, lon_count)
            plan_block = jnp.concatenate(
                [
                    cut(arrived[fields:, first], arrived[fields:, second], lane_at),
                    cut(own[:, first], own[:, second], lane_at),
                ],
                axis=0,
            )
            plan_blocks.append(jnp.dot(spread, plan_block, preferred_element_type=jnp.float32))
        for slot in range(len(ts)):
            for side in range(2):
                windows[slot, fields * side : fields * (side + 1), :] = blocks[slot][side].astype(
                    jnp.float32
                )
        results = []
        for slot in range(len(ts)):
            code, lat_weight, lon_weight = [
                plan_blocks[slot][fields * at : fields * (at + 1)] for at in range(3)
            ]
            sources = [
                windows[slot, slices * position : slices * position + fields, :].astype(
                    jnp.bfloat16
                )
                for position in range(2 * RIM + 1)
            ]
            results.append(
                interpolate(sources, lane_plan(code), corner_weights(lat_weight, lon_weight))
            )
        for t, result in zip(ts, results):
            departed[:, tile_at(t)] = result

    in_groups(basis.shape[1] // LANES, RIM_AT_ONCE, group_of)
    fourier = jnp.concatenate([inner_fourier[...], add_up(basis, departed)], axis=1)
    for at, pair in enumerate(owners):
        fourier_out[at] = fourier[4 * pair : 4 * pair + 4].astype(jnp.bfloat16)


def legendre_kernel(first_wave, coeffs, spread_analysis, out, spread_coeffs, *, levs, slices):
    members, _, rows = coeffs.shape
    bands = members // levs
    col_count = spread_analysis.shape[1]
    inner = rows // slices - EDGE
    column = lax.broadcasted_iota(jnp.int32, (1, LANES), 1)
    rim_at = column - inner * slices
    slice_of = jnp.where(rim_at < 0, column // inner, rim_at % slices)
    slice_of = jnp.where(column < rows, slice_of, -1)

    def spread(band):
        block = jnp.concatenate(
            [coeffs[band * levs + lev].astype(jnp.float32) for lev in range(levs)],
            axis=0,
        )
        block = jnp.concatenate(
            [block, jnp.zeros((block.shape[0], LANES - rows), jnp.float32)], axis=1
        )
        spread_coeffs[:, tile_at(band)] = jnp.concatenate(
            [jnp.where(slice_of == f, block, 0.0) for f in range(slices)], axis=0
        ).astype(jnp.bfloat16)

    for band in range(bands):
        spread(band)
    total = jnp.dot(
        spread_coeffs[...], spread_analysis[...], preferred_element_type=jnp.float32
    )
    first = first_wave[0:2, :] > 0.0
    for f in range(slices):
        for lev in range(levs):
            at = (f * levs + lev) * 4
            out[lev * slices + f] = jnp.where(first, total[at : at + 2], total[at + 2 : at + 4])


def shards(grid, dep_row, dep_col, lat_frac, lon_frac, pair_ids, analysis):
    slices, band_rows, lon_count = grid.shape
    pairs = pair_ids.shape[0]
    col_count = analysis.shape[2]
    bands, levs = lax.axis_size("lat"), lax.axis_size("lev")
    inner = band_rows - 2 * RIM
    windows = -(-lon_count // SPAN)
    held_rows = -(-band_rows // 8) * 8
    fields = slices * EDGE
    band_start = jnp.reshape(lax.axis_index("lat") * band_rows, (1,)).astype(jnp.int32)
    vmem = pl.BlockSpec(memory_space=pltpu.VMEM)
    smem = pl.BlockSpec(memory_space=pltpu.SMEM)
    params = pltpu.CompilerParams(vmem_limit_bytes=48 * 2**20)

    by_row = grid.transpose(1, 0, 2)
    own_rim, sent_rim, plans = pl.pallas_call(
        pack_kernel,
        out_shape=(
            jax.ShapeDtypeStruct((4 * RIM, lon_count), jnp.bfloat16),
            jax.ShapeDtypeStruct((fields + 4 * RIM, lon_count), jnp.bfloat16),
            jax.ShapeDtypeStruct((3 * inner, lon_count), jnp.bfloat16),
        ),
        in_specs=[smem] + [pl.BlockSpec(memory_space=pl.ANY)] * 5,
        out_specs=(vmem,) * 3,
        scratch_shapes=[
            pltpu.VMEM((EDGE, slices, lon_count), jnp.bfloat16),
            pltpu.VMEM((band_rows, lon_count), jnp.int32),
            pltpu.VMEM((band_rows, lon_count), jnp.int32),
            pltpu.VMEM((band_rows, lon_count), jnp.bfloat16),
            pltpu.VMEM((band_rows, lon_count), jnp.bfloat16),
            pltpu.VMEM((5, 4, held_rows, LANES), jnp.float32),
            pltpu.VMEM((5, fields, LANES), jnp.float32),
            pltpu.SemaphoreType.DMA((5,)),
        ],
        compiler_params=pltpu.CompilerParams(vmem_limit_bytes=127 * 2**19),
    )(band_start, by_row, dep_row, dep_col, lat_frac, lon_frac)
    arrived_rim = lax.ppermute(sent_rim, "lat", [(i, (i + 1) % bands) for i in range(bands)])

    plans, ids, by_row = lax.optimization_barrier((plans, pair_ids, by_row))
    rows = by_row.reshape(band_rows * slices, lon_count)
    ids = jnp.broadcast_to(ids.astype(jnp.float32)[:, None], (pairs, LANES))
    inner_fourier, basis = pl.pallas_call(
        functools.partial(inner_kernel, slices=slices),
        out_shape=(
            jax.ShapeDtypeStruct((4 * pairs, slices * inner), jnp.float32),
            jax.ShapeDtypeStruct((4 * pairs, windows * LANES), jnp.bfloat16),
        ),
        in_specs=[vmem] * 3,
        out_specs=(vmem,) * 2,
        scratch_shapes=[
            pltpu.VMEM((INNER_AT_ONCE, band_rows * slices, LANES), jnp.float32),
            pltpu.VMEM((slices * inner, windows * LANES), jnp.bfloat16),
        ],
        compiler_params=params,
        cost_estimate=pl.CostEstimate(flops=100_000_000, bytes_accessed=2_000_000, transcendentals=0),
    )(rows, plans, ids)

    held_coeffs = slices * band_rows
    members = bands * levs
    fourier = pl.pallas_call(
        functools.partial(
            rim_kernel, slices=slices, owners=[member // levs for member in range(members)]
        ),
        out_shape=jax.ShapeDtypeStruct((members, 4, held_coeffs), jnp.bfloat16),
        in_specs=[vmem] * 5,
        out_specs=vmem,
        scratch_shapes=[
            pltpu.VMEM((RIM_AT_ONCE, 2 * fields, LANES), jnp.float32),
            pltpu.VMEM((fields, windows * LANES), jnp.bfloat16),
        ],
        compiler_params=params,
    )(arrived_rim, rows, own_rim, basis, inner_fourier)
    fourier, analysis, late_ids = lax.optimization_barrier((fourier, analysis, pair_ids))

    values = analysis[0].reshape(bands, band_rows, col_count)
    before = jnp.roll(values[:, band_rows - RIM :], 1, axis=0)
    spread_rows = [values[:, RIM : RIM + inner]] * slices
    for rim in (before, values[:, :RIM]):
        for row in range(RIM):
            spread_rows += [rim[:, row : row + 1]] * slices
    spread_rows.append(jnp.zeros((bands, LANES - held_coeffs, col_count), jnp.bfloat16))
    spread_analysis = jnp.concatenate(spread_rows, axis=1).reshape(bands * LANES, col_count)

    own_id = lax.dynamic_slice_in_dim(late_ids, lax.axis_index("lat"), 1)
    columns = lax.axis_index("lev") * col_count + jnp.arange(col_count, dtype=jnp.int32)
    first_wave = jnp.where(columns < NMAX + 1 - own_id, 1.0, 0.0)
    first_wave = jnp.broadcast_to(first_wave[None, :], (8, col_count))

    coeffs = lax.all_to_all(
        fourier, ("lat", "lev"), split_axis=0, concat_axis=0, tiled=True
    )
    out = pl.pallas_call(
        functools.partial(legendre_kernel, levs=levs, slices=slices),
        out_shape=jax.ShapeDtypeStruct((levs * slices, 2, col_count), jnp.float32),
        in_specs=[vmem] * 3,
        out_specs=vmem,
        scratch_shapes=[pltpu.VMEM((4 * levs * slices, bands * LANES), jnp.bfloat16)],
        compiler_params=params,
    )(first_wave, coeffs, spread_analysis)
    return out[None]


def solution(mesh):
    return jax.shard_map(
        shards,
        mesh=mesh,
        in_specs=(
            P("lev", "lat", None),
            P("lat", None),
            P("lat", None),
            P("lat", None),
            P("lat", None),
            P(),
            P("lat", None, "lev"),
        ),
        out_specs=P("lat", None, None, "lev"),
        check_vma=False,
    )
```

```python
import functools
import math

import jax
import jax.numpy as jnp
from jax import lax
from jax.experimental import pallas as pl
from jax.experimental.pallas import tpu as pltpu
from jax.sharding import PartitionSpec as P

NMAX = 1279
LANES = 128
RIM = 2
EDGE = 2 * RIM
REACH = 8
SPAN = LANES - 2 * REACH - 1
ROW_BITS = 5
INNER_AT_ONCE = 2
RIM_AT_ONCE = 4


def lane_gather(values, indices):
    numbers = lax.GatherDimensionNumbers(
        offset_dims=(),
        collapsed_slice_dims=(1,),
        start_index_map=(1,),
        operand_batching_dims=(0,),
        start_indices_batching_dims=(0,),
    )
    return lax.gather(
        values,
        indices[..., None],
        numbers,
        (1, 1),
        mode=lax.GatherScatterMode.PROMISE_IN_BOUNDS,
    )


def tile_at(t):
    return slice(t * LANES, (t + 1) * LANES)


def cut_of(start, lon_count):
    tiles = lon_count // LANES
    first, lane_at = divmod(start % lon_count, LANES)
    return tile_at(first), tile_at((first + 1) % tiles), lane_at


def cut(first, second, lane_at):
    if lane_at == 0:
        return first
    lane = lax.broadcasted_iota(jnp.int32, first.shape, 1).astype(jnp.int16)
    joined = jnp.where(lane >= jnp.int16(lane_at), first, second)
    return pltpu.roll(joined, LANES - lane_at, 1)


def lane_plan(code):
    code = code.astype(jnp.int32)
    west = lax.broadcasted_iota(jnp.int32, code.shape, 1) + (code & (1 << ROW_BITS) - 1)
    west_lane = (west & (LANES - 1)).astype(jnp.int16)
    east_lane = ((west + 1) & (LANES - 1)).astype(jnp.int16)
    row_step = (code >> ROW_BITS).astype(jnp.float32).astype(jnp.bfloat16)
    return west_lane, east_lane, row_step


def corner_weights(lat_weight, lon_weight):
    south, north = 1.0 - lat_weight, lat_weight
    west, east = 1.0 - lon_weight, lon_weight
    return south * west, south * east, north * west, north * east


def interpolate(sources, plan, weights):
    west_lane, east_lane, row_step = plan
    masks = [row_step == float(step) for step in range(2 * RIM - 1)]

    def pick(gathered):
        low, high = gathered[2 * RIM - 1], gathered[2 * RIM]
        for position in range(2 * RIM - 2, -1, -1):
            low = jnp.where(masks[position], gathered[position], low)
            high = jnp.where(masks[position], gathered[position + 1], high)
        return low.astype(jnp.float32), high.astype(jnp.float32)

    west_low, west_high = pick([lane_gather(source, west_lane) for source in sources])
    east_low, east_high = pick([lane_gather(source, east_lane) for source in sources])
    departed = (
        weights[0] * west_low
        + weights[1] * east_low
        + weights[2] * west_high
        + weights[3] * east_high
    )
    return departed


def in_groups(count, at_once, group):
    for at in range(0, count, at_once):
        group(list(range(at, min(at + at_once, count))))


def pack_kernel(
    band_start, rows, dep_row, dep_col, lat_frac, lon_frac, own_out, sent_out, plan_out, held
):
    band_rows, lon_count = dep_row.shape
    inner = band_rows - 2 * RIM
    slices = rows.shape[0] // band_rows
    rim = RIM * slices
    first_row = band_start[0]

    for t in range(lon_count // LANES):
        cols, slot = tile_at(t), t % 5
        row = lax.broadcasted_iota(jnp.int32, (band_rows, LANES), 0)
        lane = lax.broadcasted_iota(jnp.int32, (band_rows, LANES), 1)
        shift = dep_col[:, cols] - (lane + t * LANES)
        shift = jnp.where(shift > lon_count // 2, shift - lon_count, shift)
        shift = jnp.where(shift < -(lon_count // 2), shift + lon_count, shift)
        row_step = dep_row[:, cols] - (first_row + row) + RIM
        held[slot, 0, 0:band_rows, :] = row_step.astype(jnp.float32)
        held[slot, 1, 0:band_rows, :] = (shift + REACH).astype(jnp.float32)
        held[slot, 2, 0:band_rows, :] = lat_frac[:, cols].astype(jnp.float32)
        held[slot, 3, 0:band_rows, :] = lon_frac[:, cols].astype(jnp.float32)
        for out, first_of, start in (
            (own_out, jnp.zeros((rim, LANES), jnp.float32), 0),
            (sent_out, rows[rows.shape[0] - 2 * rim :, cols].astype(jnp.float32)[rim:], band_rows - RIM),
        ):
            out[:, cols] = jnp.concatenate(
                [first_of] + [held[slot, at, start : start + RIM, :] for at in range(4)], axis=0
            ).astype(jnp.bfloat16)
        middle = [held[slot, at, RIM : RIM + inner, :] for at in range(4)]
        middle = [middle[0] * (1 << ROW_BITS) + middle[1], middle[2], middle[3]]
        for at in range(3):
            plan_out[at * inner : (at + 1) * inner, cols] = middle[at].astype(jnp.bfloat16)


def waves_of(ids, group):
    pair = jnp.concatenate(
        [jnp.broadcast_to(ids[pl.ds(4 * group + at, 1), :], (4, LANES)) for at in range(4)], axis=0
    )
    row = lax.broadcasted_iota(jnp.int32, (16, LANES), 0)
    return jnp.where((row & 2) == 0, pair, NMAX + 1 - pair)


def basis_tile(t, wave, lon_count):
    lane = lax.broadcasted_iota(jnp.int32, (16, LANES), 1)
    row = lax.broadcasted_iota(jnp.int32, (16, LANES), 0)
    longitude = lane + t * SPAN
    quarter = jnp.where((row & 1) == 0, 0.0, float(lon_count // 4))
    steps = longitude.astype(jnp.float32) * wave + quarter
    turns = jnp.floor(steps * (1.0 / lon_count) + 0.5)
    angle = lon_count // 4 - jnp.abs(steps - turns * lon_count)
    angle = angle * (2.0 * math.pi / lon_count)
    square = angle * angle
    series = jnp.float32(-1.0 / 39916800.0)
    for term in (1.0 / 362880.0, -1.0 / 5040.0, 1.0 / 120.0, -1.0 / 6.0, 1.0):
        series = series * square + term
    taken = (lane < SPAN) & (longitude < lon_count)
    return jnp.where(taken, angle * series, 0.0).astype(jnp.bfloat16)


def rim_spread(slices):
    fields = EDGE * slices
    shape = (3 * fields, 2 * RIM * (slices + 4))
    wanted = lax.broadcasted_iota(jnp.int32, shape, 0)
    held = lax.broadcasted_iota(jnp.int32, shape, 1)
    kind, rim_row = wanted // fields, wanted % fields // slices
    base = rim_row // RIM * RIM * (slices + 4) + RIM * slices + rim_row % RIM
    spread = jnp.where((kind == 0) & (held == base), float(1 << ROW_BITS), 0.0)
    spread += jnp.where(held == base + RIM * (kind + 1), 1.0, 0.0)
    return spread.astype(jnp.bfloat16)


def rim_plan(spread, packed):
    plan = jnp.dot(spread, jnp.concatenate(packed, axis=0), preferred_element_type=jnp.float32)
    fields = spread.shape[0] // 3
    code, lat_weight, lon_weight = [plan[fields * at : fields * (at + 1)] for at in range(3)]
    return lane_plan(code), corner_weights(lat_weight, lon_weight)


def add_up(basis, values):
    return lax.dot_general(
        basis, values, (((1,), (1,)), ((), ())), preferred_element_type=jnp.float32
    )


def inner_kernel(
    grid, plans, sent, ids, fourier_out, basis, windows, departed, last_departed, *, slices
):
    lon_count = grid.shape[1]
    inner = plans.shape[0] // 3
    rim = RIM * slices
    spread = rim_spread(slices)
    for slot in range(INNER_AT_ONCE):
        windows[slot, grid.shape[0] :, :] = jnp.zeros((rim, LANES), jnp.float32)
    groups = ids.shape[0] // 4
    few = groups <= 4
    waves = [waves_of(ids, at) for at in range(groups if few else 0)]

    def group_of(ts):
        blocks, plan_blocks, last_plans = [], [], []
        for t in ts:
            first, second, lane_at = cut_of(t * SPAN - REACH, lon_count)
            blocks.append(cut(grid[:, first], grid[:, second], lane_at).astype(jnp.float32))
            first, second, lane_at = cut_of(t * SPAN, lon_count)
            last_plans.append(cut(sent[:, first], sent[:, second], lane_at))
            plan_blocks.append(
                [
                    cut(
                        plans[at * inner : (at + 1) * inner, first],
                        plans[at * inner : (at + 1) * inner, second],
                        lane_at,
                    ).astype(jnp.float32)
                    for at in range(3)
                ]
            )
        for slot, block in enumerate(blocks):
            windows[slot, 0 : grid.shape[0], :] = block
        results = []
        for slot, (code, lat_weight, lon_weight) in enumerate(plan_blocks):
            plan = lane_plan(code)
            weights = corner_weights(lat_weight, lon_weight)
            for f in range(slices):
                sources = [
                    windows[slot, pl.ds(slices * position + f, inner, stride=slices), :].astype(
                        jnp.bfloat16
                    )
                    for position in range(2 * RIM + 1)
                ]
                results.append((ts[slot], f, interpolate(sources, plan, weights)))
        two = [0, len(ts) - 1]
        last_rows = grid.shape[0] - slices * EDGE
        sources = [
            jnp.concatenate(
                [
                    windows[slot, last_rows + slices * position : last_rows + slices * position + rim]
                    for slot in two
                ],
                axis=0,
            ).astype(jnp.bfloat16)
            for position in range(2 * RIM + 1)
        ]
        last = interpolate(sources, *rim_plan(spread, [last_plans[slot] for slot in two]))
        for t, f, result in results:
            departed[f * inner : (f + 1) * inner, tile_at(t)] = result.astype(jnp.bfloat16)
        for slot, t in enumerate(ts):
            last_departed[:, tile_at(t)] = jnp.concatenate(
                [last[rim * slot : rim * (slot + 1)], jnp.zeros((rim, LANES), jnp.float32)], axis=0
            ).astype(jnp.bfloat16)
        for t in ts if few else ():
            for at, wave in enumerate(waves):
                basis[16 * at : 16 * at + 16, tile_at(t)] = basis_tile(t, wave, lon_count)

    if not few:

        def rows_of(group, carry):
            rows = pl.ds(pl.multiple_of(group * 16, 16), 16)
            for t in range(basis.shape[1] // LANES):
                basis[rows, tile_at(t)] = basis_tile(t, waves_of(ids, group), lon_count)
            return carry

        lax.fori_loop(0, groups, rows_of, 0)
    in_groups(departed.shape[1] // LANES, INNER_AT_ONCE, group_of)
    fourier_out[...] = jnp.concatenate(
        [add_up(basis[...], departed[...]), add_up(basis[...], last_departed[...])[:, :rim]], axis=1
    )


def rim_kernel(
    arrived, rows, own, basis, inner_fourier, fourier_out, windows, departed, *, slices, levs
):
    lon_count = arrived.shape[1]
    rim, fields = RIM * slices, EDGE * slices
    spread = rim_spread(slices)
    sublane = lax.broadcasted_iota(jnp.int32, (rim, LANES), 0)

    def source(slot, position):
        start = slices * position
        before = jnp.zeros((rim, LANES), jnp.float32)
        if position == 2 * RIM - 1:
            before = jnp.where(sublane < slices, before, windows[slot, slices : slices + rim, :])
        elif position == 2 * RIM:
            before = windows[slot, rim : 2 * rim, :]
        return jnp.concatenate([before, windows[slot, start : start + rim, :]], axis=0).astype(
            jnp.bfloat16
        )

    def group_of(ts):
        blocks, plan_blocks = [], []
        for t in ts:
            first, second, lane_at = cut_of(t * SPAN - REACH, lon_count)
            blocks.append(
                [
                    cut(arrived[:, first], arrived[:, second], lane_at).astype(jnp.float32)[:rim],
                    cut(rows[0:fields, first], rows[0:fields, second], lane_at).astype(jnp.float32),
                ]
            )
            first, second, lane_at = cut_of(t * SPAN, lon_count)
            plan_blocks.append(
                [cut(ref[:, first], ref[:, second], lane_at) for ref in (arrived, own)]
            )
        for slot, (before, first_rows) in enumerate(blocks):
            windows[slot, 0:rim, :] = before
            windows[slot, rim : rim + fields, :] = first_rows
        results = [
            interpolate(
                [source(slot, position) for position in range(2 * RIM + 1)],
                *rim_plan(spread, plan_blocks[slot]),
            )
            for slot in range(len(ts))
        ]
        for t, result in zip(ts, results):
            departed[:, tile_at(t)] = result.astype(jnp.bfloat16)

    in_groups(basis.shape[1] // LANES, RIM_AT_ONCE, group_of)
    fourier = jnp.concatenate([inner_fourier[...], add_up(basis[...], departed[...])], axis=1)
    for at in range(fourier_out.shape[0]):
        pair = at // levs
        fourier_out[at] = fourier[4 * pair : 4 * pair + 4].astype(jnp.bfloat16)


def legendre_kernel(first_wave, coeffs, spread_analysis, out, spread_coeffs, *, levs, slices):
    members, _, rows = coeffs.shape
    bands = members // levs
    col_count = spread_analysis.shape[1]
    inner = rows // slices - EDGE - RIM
    column = lax.broadcasted_iota(jnp.int32, (1, LANES), 1)
    rim_at = column - inner * slices
    slice_of = jnp.where(rim_at < 0, column // inner, rim_at % slices)
    slice_of = jnp.where(column < rows, slice_of, -1)

    def spread(band):
        block = jnp.concatenate(
            [coeffs[band * levs + lev].astype(jnp.float32) for lev in range(levs)],
            axis=0,
        )
        block = jnp.concatenate(
            [block, jnp.zeros((block.shape[0], LANES - rows), jnp.float32)], axis=1
        )
        spread_coeffs[:, tile_at(band)] = jnp.concatenate(
            [jnp.where(slice_of == f, block, 0.0) for f in range(slices)], axis=0
        ).astype(jnp.bfloat16)

    for band in range(bands):
        spread(band)
    total = jnp.dot(
        spread_coeffs[...], spread_analysis[...], preferred_element_type=jnp.float32
    )
    first = first_wave[0:2, :] > 0.0
    for f in range(slices):
        for lev in range(levs):
            at = (f * levs + lev) * 4
            out[lev * slices + f] = jnp.where(first, total[at : at + 2], total[at + 2 : at + 4])


def shards(grid, dep_row, dep_col, lat_frac, lon_frac, pair_ids, analysis):
    slices, band_rows, lon_count = grid.shape
    pairs = pair_ids.shape[0]
    col_count = analysis.shape[2]
    bands, levs = lax.axis_size("lat"), lax.axis_size("lev")
    inner = band_rows - 2 * RIM
    windows = -(-lon_count // SPAN)
    held_rows = -(-band_rows // 8) * 8
    fields = slices * EDGE
    band_start = jnp.reshape(lax.axis_index("lat") * band_rows, (1,)).astype(jnp.int32)
    vmem = pl.BlockSpec(memory_space=pltpu.VMEM)
    smem = pl.BlockSpec(memory_space=pltpu.SMEM)
    params = pltpu.CompilerParams(vmem_limit_bytes=48 * 2**20)

    rows = grid.transpose(1, 0, 2).reshape(band_rows * slices, lon_count)
    rim_shape = jax.ShapeDtypeStruct((RIM * (slices + 4), lon_count), jnp.bfloat16)
    own_rim, sent_rim, plans = pl.pallas_call(
        pack_kernel,
        out_shape=(
            rim_shape,
            rim_shape,
            jax.ShapeDtypeStruct((3 * inner, lon_count), jnp.bfloat16),
        ),
        in_specs=[smem] + [vmem] * 5,
        out_specs=(vmem,) * 3,
        scratch_shapes=[pltpu.VMEM((5, 4, held_rows, LANES), jnp.float32)],
        compiler_params=params,
    )(band_start, rows, dep_row, dep_col, lat_frac, lon_frac)
    arrived_rim = lax.ppermute(sent_rim, "lat", [(i, (i + 1) % bands) for i in range(bands)])

    plans, ids = lax.optimization_barrier((plans, pair_ids))
    ids = jnp.broadcast_to(ids.astype(jnp.float32)[:, None], (pairs, LANES))
    inner_fourier, basis = pl.pallas_call(
        functools.partial(inner_kernel, slices=slices),
        out_shape=(
            jax.ShapeDtypeStruct((4 * pairs, slices * (inner + RIM)), jnp.float32),
            jax.ShapeDtypeStruct((4 * pairs, windows * LANES), jnp.bfloat16),
        ),
        in_specs=[vmem] * 4,
        out_specs=(vmem,) * 2,
        scratch_shapes=[
            pltpu.VMEM((INNER_AT_ONCE, (band_rows + RIM) * slices, LANES), jnp.float32),
            pltpu.VMEM((slices * inner, windows * LANES), jnp.bfloat16),
            pltpu.VMEM((2 * RIM * slices, windows * LANES), jnp.bfloat16),
        ],
        compiler_params=params,
        cost_estimate=pl.CostEstimate(flops=100_000_000, bytes_accessed=2_000_000, transcendentals=0),
    )(rows, plans, sent_rim, ids)

    held_coeffs = slices * (band_rows + RIM)
    fourier = pl.pallas_call(
        functools.partial(rim_kernel, slices=slices, levs=levs),
        out_shape=jax.ShapeDtypeStruct((bands * levs, 4, held_coeffs), jnp.bfloat16),
        in_specs=[vmem] * 5,
        out_specs=vmem,
        scratch_shapes=[
            pltpu.VMEM((RIM_AT_ONCE, (RIM + EDGE) * slices, LANES), jnp.float32),
            pltpu.VMEM((fields, windows * LANES), jnp.bfloat16),
        ],
        compiler_params=params,
    )(arrived_rim, rows, own_rim, basis, inner_fourier)
    fourier, analysis, late_ids = lax.optimization_barrier((fourier, analysis, pair_ids))

    values = analysis[0].reshape(bands, band_rows, col_count)
    before = jnp.roll(values[:, band_rows - RIM :], 1, axis=0)
    spread_rows = [values[:, RIM : RIM + inner]] * slices
    for rim in (values[:, band_rows - RIM :], before, values[:, :RIM]):
        for row in range(RIM):
            spread_rows += [rim[:, row : row + 1]] * slices
    spread_rows.append(jnp.zeros((bands, LANES - held_coeffs, col_count), jnp.bfloat16))
    spread_analysis = jnp.concatenate(spread_rows, axis=1).reshape(bands * LANES, col_count)

    own_id = lax.dynamic_slice_in_dim(late_ids, lax.axis_index("lat"), 1)
    columns = lax.axis_index("lev") * col_count + jnp.arange(col_count, dtype=jnp.int32)
    first_wave = jnp.where(columns < NMAX + 1 - own_id, 1.0, 0.0)
    first_wave = jnp.broadcast_to(first_wave[None, :], (8, col_count))

    coeffs = lax.all_to_all(
        fourier, ("lat", "lev"), split_axis=0, concat_axis=0, tiled=True
    )
    out = pl.pallas_call(
        functools.partial(legendre_kernel, levs=levs, slices=slices),
        out_shape=jax.ShapeDtypeStruct((levs * slices, 2, col_count), jnp.float32),
        in_specs=[vmem] * 3,
        out_specs=vmem,
        scratch_shapes=[pltpu.VMEM((4 * levs * slices, bands * LANES), jnp.bfloat16)],
        compiler_params=params,
    )(first_wave, coeffs, spread_analysis)
    return out[None]


def solution(mesh):
    return jax.shard_map(
        shards,
        mesh=mesh,
        in_specs=(
            P("lev", "lat", None),
            P("lat", None),
            P("lat", None),
            P("lat", None),
            P("lat", None),
            P(),
            P("lat", None, "lev"),
        ),
        out_specs=P("lat", None, None, "lev"),
        check_vma=False,
    )
```

```python
import functools
import math

import jax
import jax.numpy as jnp
from jax import lax
from jax.experimental import pallas as pl
from jax.experimental.pallas import tpu as pltpu
from jax.sharding import PartitionSpec as P

NMAX = 1279
LANES = 128
RIM = 2
EDGE = 2 * RIM
REACH = 8
SPAN = LANES - 2 * REACH - 1
ROW_BITS = 5
INNER_AT_ONCE = 2
RIM_AT_ONCE = 4


def lane_gather(values, indices):
    numbers = lax.GatherDimensionNumbers(
        offset_dims=(),
        collapsed_slice_dims=(1,),
        start_index_map=(1,),
        operand_batching_dims=(0,),
        start_indices_batching_dims=(0,),
    )
    return lax.gather(
        values,
        indices[..., None],
        numbers,
        (1, 1),
        mode=lax.GatherScatterMode.PROMISE_IN_BOUNDS,
    )


def tile_at(t):
    return slice(t * LANES, (t + 1) * LANES)


def cut(arrays, t, lon_count, steps):
    tiles = lon_count // LANES
    first, lane_at = divmod((t * SPAN - REACH) % lon_count, LANES)
    second = (first + 1) % tiles
    chosen = jnp.where(steps[...] == jnp.int16(lane_at), jnp.bfloat16(1), jnp.bfloat16(0))
    columns = jnp.concatenate(
        [
            jnp.concatenate([array[:, tile_at(tile)] for array in arrays], axis=0)
            for tile in (first, second)
        ],
        axis=1,
    )
    return jnp.dot(columns, chosen, preferred_element_type=jnp.float32)


def fill_steps(steps):
    shape = steps.shape
    step = lax.broadcasted_iota(jnp.int32, shape, 0) - lax.broadcasted_iota(jnp.int32, shape, 1)
    steps[...] = step.astype(jnp.int16)


def lane_plan(code):
    code = code.astype(jnp.int32)
    lane = lax.broadcasted_iota(jnp.int32, code.shape, 1)
    west = lane - REACH + (code & (1 << ROW_BITS) - 1)
    west_lane = (west & (LANES - 1)).astype(jnp.int16)
    east_lane = ((west + 1) & (LANES - 1)).astype(jnp.int16)
    row_step = (code >> ROW_BITS).astype(jnp.float32).astype(jnp.bfloat16)
    return west_lane, east_lane, row_step


def corner_weights(lat_weight, lon_weight):
    south, north = 1.0 - lat_weight, lat_weight
    west, east = 1.0 - lon_weight, lon_weight
    return south * west, south * east, north * west, north * east


def interpolate(sources, plan, weights):
    west_lane, east_lane, row_step = plan
    masks = [row_step == float(step) for step in range(2 * RIM - 1)]

    def pick(gathered):
        low, high = gathered[2 * RIM - 1], gathered[2 * RIM]
        for position in range(2 * RIM - 2, -1, -1):
            low = jnp.where(masks[position], gathered[position], low)
            high = jnp.where(masks[position], gathered[position + 1], high)
        return low.astype(jnp.float32), high.astype(jnp.float32)

    west_low, west_high = pick([lane_gather(source, west_lane) for source in sources])
    east_low, east_high = pick([lane_gather(source, east_lane) for source in sources])
    departed = (
        weights[0] * west_low
        + weights[1] * east_low
        + weights[2] * west_high
        + weights[3] * east_high
    )
    return departed


def in_groups(count, at_once, group):
    for at in range(0, count, at_once):
        group(list(range(at, min(at + at_once, count))))


def pack_kernel(
    band_start, rows, dep_row, dep_col, lat_frac, lon_frac, own_out, sent_out, plan_out, held
):
    band_rows, lon_count = dep_row.shape
    inner = band_rows - 2 * RIM
    slices = rows.shape[0] // band_rows
    rim = RIM * slices
    first_row = band_start[0]

    for t in range(lon_count // LANES):
        cols, slot = tile_at(t), t % 5
        row = lax.broadcasted_iota(jnp.int32, (band_rows, LANES), 0)
        lane = lax.broadcasted_iota(jnp.int32, (band_rows, LANES), 1)
        shift = dep_col[:, cols] - (lane + t * LANES)
        shift = jnp.where(shift > lon_count // 2, shift - lon_count, shift)
        shift = jnp.where(shift < -(lon_count // 2), shift + lon_count, shift)
        row_step = dep_row[:, cols] - (first_row + row) + RIM
        held[slot, 0, 0:band_rows, :] = row_step.astype(jnp.float32)
        held[slot, 1, 0:band_rows, :] = (shift + REACH).astype(jnp.float32)
        held[slot, 2, 0:band_rows, :] = lat_frac[:, cols].astype(jnp.float32)
        held[slot, 3, 0:band_rows, :] = lon_frac[:, cols].astype(jnp.float32)
        edges = rows[0 : 2 * rim, cols], rows[rows.shape[0] - 2 * rim :, cols]
        first_rows, last_rows = [edge.astype(jnp.float32) for edge in edges]
        for out, grid_rows, start in (
            (own_out, first_rows[:rim], 0),
            (sent_out, last_rows[rim:], band_rows - RIM),
        ):
            out[:, cols] = jnp.concatenate(
                [grid_rows] + [held[slot, at, start : start + RIM, :] for at in range(4)], axis=0
            ).astype(jnp.bfloat16)
        middle = [held[slot, at, RIM : RIM + inner, :] for at in range(4)]
        middle = [middle[0] * (1 << ROW_BITS) + middle[1], middle[2], middle[3]]
        for at in range(3):
            plan_out[at * inner : (at + 1) * inner, cols] = middle[at].astype(jnp.bfloat16)


def waves_of(ids, group):
    pair = jnp.concatenate(
        [jnp.broadcast_to(ids[pl.ds(4 * group + at, 1), :], (4, LANES)) for at in range(4)], axis=0
    )
    row = lax.broadcasted_iota(jnp.int32, (16, LANES), 0)
    return jnp.where((row & 2) == 0, pair, NMAX + 1 - pair)


def basis_tile(t, wave, lon_count):
    lane = lax.broadcasted_iota(jnp.int32, (16, LANES), 1)
    row = lax.broadcasted_iota(jnp.int32, (16, LANES), 0)
    longitude = lane + (t * SPAN - REACH)
    quarter = jnp.where((row & 1) == 0, 0.0, float(lon_count // 4))
    steps = longitude.astype(jnp.float32) * wave + quarter
    turns = jnp.floor(steps * (1.0 / lon_count) + 0.5)
    angle = lon_count // 4 - jnp.abs(steps - turns * lon_count)
    angle = angle * (2.0 * math.pi / lon_count)
    square = angle * angle
    series = jnp.float32(-1.0 / 39916800.0)
    for term in (1.0 / 362880.0, -1.0 / 5040.0, 1.0 / 120.0, -1.0 / 6.0, 1.0):
        series = series * square + term
    taken = (lane >= REACH) & (lane < REACH + SPAN) & (longitude < lon_count)
    return jnp.where(taken, angle * series, 0.0).astype(jnp.bfloat16)


def rim_spread(slices):
    fields = EDGE * slices
    shape = (3 * fields, 2 * RIM * (slices + 4))
    wanted = lax.broadcasted_iota(jnp.int32, shape, 0)
    held = lax.broadcasted_iota(jnp.int32, shape, 1)
    kind, rim_row = wanted // fields, wanted % fields // slices
    base = rim_row // RIM * RIM * (slices + 4) + RIM * slices + rim_row % RIM
    spread = jnp.where((kind == 0) & (held == base), float(1 << ROW_BITS), 0.0)
    spread += jnp.where(held == base + RIM * (kind + 1), 1.0, 0.0)
    return spread.astype(jnp.bfloat16)


def rim_plan(spread, packed):
    plan = jnp.dot(spread, packed.astype(jnp.bfloat16), preferred_element_type=jnp.float32)
    fields = spread.shape[0] // 3
    code, lat_weight, lon_weight = [plan[fields * at : fields * (at + 1)] for at in range(3)]
    return lane_plan(code), corner_weights(lat_weight, lon_weight)


def add_up(basis, values):
    return lax.dot_general(
        basis, values, (((1,), (1,)), ((), ())), preferred_element_type=jnp.float32
    )


def inner_kernel(
    grid, plans, own, sent, ids,
    fourier_out, basis, windows, departed, rim_departed, steps, *, slices,
):
    lon_count = grid.shape[1]
    inner = plans.shape[0] // 3
    rim, fields, held = RIM * slices, EDGE * slices, grid.shape[0]
    plan_end = held + 3 * inner
    spread = rim_spread(slices)
    fill_steps(steps)
    for slot in range(INNER_AT_ONCE):
        windows[slot, 0:rim, :] = jnp.zeros((rim, LANES), jnp.float32)
        windows[slot, rim + held :, :] = jnp.zeros((rim, LANES), jnp.float32)
    groups = ids.shape[0] // 4
    few = groups <= 4
    waves = [waves_of(ids, at) for at in range(groups if few else 0)]

    def group_of(ts):
        blocks = [cut((grid, plans, own, sent), t, lon_count, steps) for t in ts]
        for slot, block in enumerate(blocks):
            windows[slot, rim : rim + held, :] = block[:held]
        results, rim_results = [], []
        for slot, t in enumerate(ts):
            code, lat_weight, lon_weight = [
                blocks[slot][held + at * inner : held + (at + 1) * inner] for at in range(3)
            ]
            plan = lane_plan(code)
            weights = corner_weights(lat_weight, lon_weight)
            for f in range(slices):
                sources = [
                    windows[
                        slot, pl.ds(rim + slices * position + f, inner, stride=slices), :
                    ].astype(jnp.bfloat16)
                    for position in range(2 * RIM + 1)
                ]
                results.append((t, f, interpolate(sources, plan, weights)))
            sources = [
                jnp.concatenate(
                    [
                        windows[slot, start + slices * position : start + slices * position + rim, :]
                        for start in (0, held - rim)
                    ],
                    axis=0,
                ).astype(jnp.bfloat16)
                for position in range(2 * RIM + 1)
            ]
            rim_results.append(interpolate(sources, *rim_plan(spread, blocks[slot][plan_end:])))
        for t, f, result in results:
            departed[f * inner : (f + 1) * inner, tile_at(t)] = result.astype(jnp.bfloat16)
        for t, result in zip(ts, rim_results):
            rim_departed[:, tile_at(t)] = result.astype(jnp.bfloat16)
        for t in ts if few else ():
            for at, wave in enumerate(waves):
                basis[16 * at : 16 * at + 16, tile_at(t)] = basis_tile(t, wave, lon_count)

    if not few:

        def rows_of(group, carry):
            rows = pl.ds(pl.multiple_of(group * 16, 16), 16)
            for t in range(basis.shape[1] // LANES):
                basis[rows, tile_at(t)] = basis_tile(t, waves_of(ids, group), lon_count)
            return carry

        lax.fori_loop(0, groups, rows_of, 0)
    in_groups(departed.shape[1] // LANES, INNER_AT_ONCE, group_of)
    fourier_out[...] = jnp.concatenate(
        [add_up(basis[...], departed[...]), add_up(basis[...], rim_departed[...])], axis=1
    )


def rim_kernel(
    arrived, own, basis, inner_fourier, fourier_out, windows, departed, steps, *, slices, levs
):
    lon_count = arrived.shape[1]
    rim, fields = RIM * slices, EDGE * slices
    spread = rim_spread(slices)
    fill_steps(steps)
    out_row = lax.broadcasted_iota(jnp.int32, (fields, LANES), 0) // slices
    far_step = jnp.where(out_row < RIM, 2 * RIM, 0)
    near_step = jnp.where(out_row == RIM - 1, 2 * RIM - 1, jnp.where(out_row == RIM, 1, -2))

    def part(source, plan, weights, step):
        west_lane, east_lane, row_step = plan
        source = source.astype(jnp.bfloat16)
        low, high = row_step == step, row_step == step - 1
        west = jnp.where(low, weights[0], jnp.where(high, weights[2], 0.0))
        east = jnp.where(low, weights[1], jnp.where(high, weights[3], 0.0))
        return west * lane_gather(source, west_lane).astype(
            jnp.float32
        ) + east * lane_gather(source, east_lane).astype(jnp.float32)

    def group_of(ts):
        blocks = [cut((arrived, own), t, lon_count, steps) for t in ts]
        for slot, block in enumerate(blocks):
            windows[slot, 0:rim, :] = block[:rim]
            windows[slot, rim:, :] = block[fields : fields + rim]
        for slot, t in enumerate(ts):
            block = blocks[slot]
            (west_lane, east_lane, row_step), weights = rim_plan(spread, block)
            plan = west_lane, east_lane, row_step.astype(jnp.float32).astype(jnp.int32)
            far = jnp.concatenate([block[fields : fields + rim], block[:rim]], axis=0)
            near = jnp.concatenate([windows[slot, slices : slices + rim, :]] * 2, axis=0)
            result = part(far, plan, weights, far_step) + part(near, plan, weights, near_step)
            departed[:, tile_at(t)] = result.astype(jnp.bfloat16)

    in_groups(basis.shape[1] // LANES, RIM_AT_ONCE, group_of)
    fourier = jnp.concatenate([inner_fourier[...], add_up(basis[...], departed[...])], axis=1)
    for at in range(fourier_out.shape[0]):
        pair = at // levs
        fourier_out[at] = fourier[4 * pair : 4 * pair + 4].astype(jnp.bfloat16)


def legendre_kernel(first_wave, coeffs, spread_analysis, out, spread_coeffs, *, levs, slices):
    members, _, rows = coeffs.shape
    bands = members // levs
    col_count = spread_analysis.shape[1]
    inner = rows // slices - 2 * EDGE
    column = lax.broadcasted_iota(jnp.int32, (1, LANES), 1)
    rim_at = column - inner * slices
    slice_of = jnp.where(rim_at < 0, column // inner, rim_at % slices)
    slice_of = jnp.where(column < rows, slice_of, -1)

    def spread(band):
        block = jnp.concatenate(
            [coeffs[band * levs + lev].astype(jnp.float32) for lev in range(levs)],
            axis=0,
        )
        block = jnp.concatenate(
            [block, jnp.zeros((block.shape[0], LANES - rows), jnp.float32)], axis=1
        )
        spread_coeffs[:, tile_at(band)] = jnp.concatenate(
            [jnp.where(slice_of == f, block, 0.0) for f in range(slices)], axis=0
        ).astype(jnp.bfloat16)

    for band in range(bands):
        spread(band)
    total = None
    for at in range(0, bands * LANES, 2 * LANES):
        part = slice(at, min(at + 2 * LANES, bands * LANES))
        product = jnp.dot(
            spread_coeffs[:, part], spread_analysis[part, :], preferred_element_type=jnp.float32
        )
        total = product if total is None else total + product
    first = first_wave[0:2, :] > 0.0
    for f in range(slices):
        for lev in range(levs):
            at = (f * levs + lev) * 4
            out[lev * slices + f] = jnp.where(first, total[at : at + 2], total[at + 2 : at + 4])


def shards(grid, dep_row, dep_col, lat_frac, lon_frac, pair_ids, analysis):
    slices, band_rows, lon_count = grid.shape
    pairs = pair_ids.shape[0]
    col_count = analysis.shape[2]
    bands, levs = lax.axis_size("lat"), lax.axis_size("lev")
    inner = band_rows - 2 * RIM
    windows = -(-lon_count // SPAN)
    held_rows = -(-band_rows // 8) * 8
    fields = slices * EDGE
    band_start = jnp.reshape(lax.axis_index("lat") * band_rows, (1,)).astype(jnp.int32)
    vmem = pl.BlockSpec(memory_space=pltpu.VMEM)
    smem = pl.BlockSpec(memory_space=pltpu.SMEM)
    params = pltpu.CompilerParams(vmem_limit_bytes=48 * 2**20)

    rows = grid.transpose(1, 0, 2).reshape(band_rows * slices, lon_count)
    rim_shape = jax.ShapeDtypeStruct((RIM * (slices + 4), lon_count), jnp.bfloat16)
    own_rim, sent_rim, plans = pl.pallas_call(
        pack_kernel,
        out_shape=(
            rim_shape,
            rim_shape,
            jax.ShapeDtypeStruct((3 * inner, lon_count), jnp.bfloat16),
        ),
        in_specs=[smem] + [vmem] * 5,
        out_specs=(vmem,) * 3,
        scratch_shapes=[pltpu.VMEM((5, 4, held_rows, LANES), jnp.float32)],
        compiler_params=params,
    )(band_start, rows, dep_row, dep_col, lat_frac, lon_frac)
    arrived_rim = lax.ppermute(sent_rim, "lat", [(i, (i + 1) % bands) for i in range(bands)])

    plans, ids = lax.optimization_barrier((plans, pair_ids))
    ids = jnp.broadcast_to(ids.astype(jnp.float32)[:, None], (pairs, LANES))
    inner_fourier, basis = pl.pallas_call(
        functools.partial(inner_kernel, slices=slices),
        out_shape=(
            jax.ShapeDtypeStruct((4 * pairs, slices * band_rows), jnp.float32),
            jax.ShapeDtypeStruct((4 * pairs, windows * LANES), jnp.bfloat16),
        ),
        in_specs=[vmem] * 5,
        out_specs=(vmem,) * 2,
        scratch_shapes=[
            pltpu.VMEM((INNER_AT_ONCE, (band_rows + 2 * RIM) * slices, LANES), jnp.float32),
            pltpu.VMEM((slices * inner, windows * LANES), jnp.bfloat16),
            pltpu.VMEM((fields, windows * LANES), jnp.bfloat16),
            pltpu.VMEM((2 * LANES, LANES), jnp.int16),
        ],
        compiler_params=params,
        cost_estimate=pl.CostEstimate(flops=100_000_000, bytes_accessed=2_000_000, transcendentals=0),
    )(rows, plans, own_rim, sent_rim, ids)

    held_coeffs = slices * (band_rows + EDGE)
    fourier = pl.pallas_call(
        functools.partial(rim_kernel, slices=slices, levs=levs),
        out_shape=jax.ShapeDtypeStruct((bands * levs, 4, held_coeffs), jnp.bfloat16),
        in_specs=[vmem] * 4,
        out_specs=vmem,
        scratch_shapes=[
            pltpu.VMEM((RIM_AT_ONCE, fields, LANES), jnp.float32),
            pltpu.VMEM((fields, windows * LANES), jnp.bfloat16),
            pltpu.VMEM((2 * LANES, LANES), jnp.int16),
        ],
        compiler_params=params,
    )(arrived_rim, own_rim, basis, inner_fourier)
    fourier, late_ids = lax.optimization_barrier((fourier, pair_ids))
    own_id = lax.dynamic_slice_in_dim(late_ids, lax.axis_index("lat"), 1)
    own_id, analysis = lax.optimization_barrier((own_id, analysis))

    values = analysis[0].reshape(bands, band_rows, col_count)
    before = jnp.roll(values[:, band_rows - RIM :], 1, axis=0)
    spread_rows = [values[:, RIM : RIM + inner]] * slices
    for rim in (values[:, :RIM], values[:, band_rows - RIM :], before, values[:, :RIM]):
        for row in range(RIM):
            spread_rows += [rim[:, row : row + 1]] * slices
    spread_rows.append(jnp.zeros((bands, LANES - held_coeffs, col_count), jnp.bfloat16))
    spread_analysis = jnp.concatenate(spread_rows, axis=1).reshape(bands * LANES, col_count)

    columns = lax.axis_index("lev") * col_count + jnp.arange(col_count, dtype=jnp.int32)
    first_wave = jnp.where(columns < NMAX + 1 - own_id, 1.0, 0.0)
    first_wave = jnp.broadcast_to(first_wave[None, :], (8, col_count))

    coeffs = lax.all_to_all(
        fourier, ("lat", "lev"), split_axis=0, concat_axis=0, tiled=True
    )
    out = pl.pallas_call(
        functools.partial(legendre_kernel, levs=levs, slices=slices),
        out_shape=jax.ShapeDtypeStruct((levs * slices, 2, col_count), jnp.float32),
        in_specs=[vmem] * 3,
        out_specs=vmem,
        scratch_shapes=[pltpu.VMEM((4 * levs * slices, bands * LANES), jnp.bfloat16)],
        compiler_params=params,
    )(first_wave, coeffs, spread_analysis)
    return out[None]


def solution(mesh):
    return jax.shard_map(
        shards,
        mesh=mesh,
        in_specs=(
            P("lev", "lat", None),
            P("lat", None),
            P("lat", None),
            P("lat", None),
            P("lat", None),
            P(),
            P("lat", None, "lev"),
        ),
        out_specs=P("lat", None, None, "lev"),
        check_vma=False,
    )
```

```python
import functools
import math

import jax
import jax.numpy as jnp
from jax import lax
from jax.experimental import pallas as pl
from jax.experimental.pallas import tpu as pltpu
from jax.sharding import PartitionSpec as P

NMAX = 1279
LANES = 128
RIM = 2
EDGE = 2 * RIM
REACH = 8
SPAN = LANES - 2 * REACH - 1
ROW_BITS = 5
INNER_AT_ONCE = 2
RIM_AT_ONCE = 4


def lane_gather(values, indices):
    numbers = lax.GatherDimensionNumbers(
        offset_dims=(),
        collapsed_slice_dims=(1,),
        start_index_map=(1,),
        operand_batching_dims=(0,),
        start_indices_batching_dims=(0,),
    )
    return lax.gather(
        values,
        indices[..., None],
        numbers,
        (1, 1),
        mode=lax.GatherScatterMode.PROMISE_IN_BOUNDS,
    )


def tile_at(t):
    return slice(t * LANES, (t + 1) * LANES)


def cut(arrays, t, lon_count, steps):
    tiles = lon_count // LANES
    first, lane_at = divmod((t * SPAN - REACH) % lon_count, LANES)
    second = (first + 1) % tiles
    chosen = jnp.where(steps[...] == jnp.int16(lane_at), jnp.bfloat16(1), jnp.bfloat16(0))
    columns = jnp.concatenate(
        [
            jnp.concatenate([array[:, tile_at(tile)] for array in arrays], axis=0)
            for tile in (first, second)
        ],
        axis=1,
    )
    return jnp.dot(columns, chosen, preferred_element_type=jnp.float32)


def fill_steps(steps):
    shape = steps.shape
    step = lax.broadcasted_iota(jnp.int32, shape, 0) - lax.broadcasted_iota(jnp.int32, shape, 1)
    steps[...] = step.astype(jnp.int16)


def lane_plan(code):
    code = code.astype(jnp.int32)
    lane = lax.broadcasted_iota(jnp.int32, code.shape, 1)
    west = lane - REACH + (code & (1 << ROW_BITS) - 1)
    west_lane = (west & (LANES - 1)).astype(jnp.int16)
    east_lane = ((west + 1) & (LANES - 1)).astype(jnp.int16)
    row_step = (code >> ROW_BITS).astype(jnp.float32).astype(jnp.bfloat16)
    return west_lane, east_lane, row_step


def corner_weights(lat_weight, lon_weight):
    south, north = 1.0 - lat_weight, lat_weight
    west, east = 1.0 - lon_weight, lon_weight
    return south * west, south * east, north * west, north * east


def interpolate(sources, plan, weights):
    west_lane, east_lane, row_step = plan
    masks = [row_step == float(step) for step in range(2 * RIM - 1)]

    def pick(gathered):
        low, high = gathered[2 * RIM - 1], gathered[2 * RIM]
        for position in range(2 * RIM - 2, -1, -1):
            low = jnp.where(masks[position], gathered[position], low)
            high = jnp.where(masks[position], gathered[position + 1], high)
        return low.astype(jnp.float32), high.astype(jnp.float32)

    west_low, west_high = pick([lane_gather(source, west_lane) for source in sources])
    east_low, east_high = pick([lane_gather(source, east_lane) for source in sources])
    departed = (
        weights[0] * west_low
        + weights[1] * east_low
        + weights[2] * west_high
        + weights[3] * east_high
    )
    return departed


def in_groups(count, at_once, group):
    for at in range(0, count, at_once):
        group(list(range(at, min(at + at_once, count))))


def pack_kernel(
    band_start, rows, dep_row, dep_col, lat_frac, lon_frac, own_out, sent_out, plan_out, held
):
    band_rows, lon_count = dep_row.shape
    inner = band_rows - 2 * RIM
    slices = rows.shape[0] // band_rows
    rim = RIM * slices
    first_row = band_start[0]

    for t in range(lon_count // LANES):
        cols, slot = tile_at(t), t % 5
        row = lax.broadcasted_iota(jnp.int32, (band_rows, LANES), 0)
        lane = lax.broadcasted_iota(jnp.int32, (band_rows, LANES), 1)
        shift = dep_col[:, cols] - (lane + t * LANES)
        shift = jnp.where(shift > lon_count // 2, shift - lon_count, shift)
        shift = jnp.where(shift < -(lon_count // 2), shift + lon_count, shift)
        row_step = dep_row[:, cols] - (first_row + row) + RIM
        held[slot, 0, 0:band_rows, :] = row_step.astype(jnp.float32)
        held[slot, 1, 0:band_rows, :] = (shift + REACH).astype(jnp.float32)
        held[slot, 2, 0:band_rows, :] = lat_frac[:, cols].astype(jnp.float32)
        held[slot, 3, 0:band_rows, :] = lon_frac[:, cols].astype(jnp.float32)
        edges = rows[0 : 2 * rim, cols], rows[rows.shape[0] - 2 * rim :, cols]
        first_rows, last_rows = [edge.astype(jnp.float32) for edge in edges]
        for out, grid_rows, start in (
            (own_out, first_rows[:rim], 0),
            (sent_out, last_rows[rim:], band_rows - RIM),
        ):
            out[:, cols] = jnp.concatenate(
                [grid_rows] + [held[slot, at, start : start + RIM, :] for at in range(4)], axis=0
            ).astype(jnp.bfloat16)
        middle = [held[slot, at, RIM : RIM + inner, :] for at in range(4)]
        middle = [middle[0] * (1 << ROW_BITS) + middle[1], middle[2], middle[3]]
        for at in range(3):
            plan_out[at * inner : (at + 1) * inner, cols] = middle[at].astype(jnp.bfloat16)


def waves_of(ids, group):
    pair = jnp.concatenate(
        [jnp.broadcast_to(ids[pl.ds(4 * group + at, 1), :], (4, LANES)) for at in range(4)], axis=0
    )
    row = lax.broadcasted_iota(jnp.int32, (16, LANES), 0)
    return jnp.where((row & 2) == 0, pair, NMAX + 1 - pair)


def basis_tile(t, wave, lon_count):
    lane = lax.broadcasted_iota(jnp.int32, (16, LANES), 1)
    row = lax.broadcasted_iota(jnp.int32, (16, LANES), 0)
    longitude = lane + (t * SPAN - REACH)
    quarter = jnp.where((row & 1) == 0, 0.0, float(lon_count // 4))
    steps = longitude.astype(jnp.float32) * wave + quarter
    turns = jnp.floor(steps * (1.0 / lon_count) + 0.5)
    angle = lon_count // 4 - jnp.abs(steps - turns * lon_count)
    angle = angle * (2.0 * math.pi / lon_count)
    square = angle * angle
    series = jnp.float32(-1.0 / 39916800.0)
    for term in (1.0 / 362880.0, -1.0 / 5040.0, 1.0 / 120.0, -1.0 / 6.0, 1.0):
        series = series * square + term
    taken = (lane >= REACH) & (lane < REACH + SPAN) & (longitude < lon_count)
    return jnp.where(taken, angle * series, 0.0).astype(jnp.bfloat16)


def rim_spread(slices):
    fields = EDGE * slices
    shape = (3 * fields, 2 * RIM * (slices + 4))
    wanted = lax.broadcasted_iota(jnp.int32, shape, 0)
    held = lax.broadcasted_iota(jnp.int32, shape, 1)
    kind, rim_row = wanted // fields, wanted % fields // slices
    base = rim_row // RIM * RIM * (slices + 4) + RIM * slices + rim_row % RIM
    spread = jnp.where((kind == 0) & (held == base), float(1 << ROW_BITS), 0.0)
    spread += jnp.where(held == base + RIM * (kind + 1), 1.0, 0.0)
    return spread.astype(jnp.bfloat16)


def rim_plan(spread, packed):
    plan = jnp.dot(spread, packed.astype(jnp.bfloat16), preferred_element_type=jnp.float32)
    fields = spread.shape[0] // 3
    code, lat_weight, lon_weight = [plan[fields * at : fields * (at + 1)] for at in range(3)]
    return lane_plan(code), corner_weights(lat_weight, lon_weight)


def spread_rows(analysis, out, band_rows, slices):
    inner = band_rows - EDGE
    rim = RIM * slices
    place = lax.broadcasted_iota(jnp.int32, (LANES, 1), 0)
    edge = place - slices * inner
    edge_row = edge // slices
    row = jnp.where(edge < 0, RIM + place % inner, edge_row)
    row = jnp.where(edge >= rim, band_rows - EDGE + edge_row, row)
    row = jnp.where(edge >= 2 * rim, edge_row - 3 * RIM, row)
    row = jnp.where(edge >= 4 * rim, -band_rows, row)
    for band in range(out.shape[0] // LANES):
        start = max(0, band * band_rows - RIM) // 16 * 16
        end = min(analysis.shape[0], -(-(band + 1) * band_rows // 16) * 16)
        column = lax.broadcasted_iota(jnp.int32, (LANES, end - start), 1) + start
        chosen = jnp.where((column - band * band_rows == row) & (row >= -RIM), 1.0, 0.0)
        out[band * LANES : (band + 1) * LANES, :] = jnp.dot(
            chosen.astype(jnp.bfloat16),
            analysis[start:end, :],
            preferred_element_type=jnp.float32,
        ).astype(jnp.bfloat16)


def add_up(basis, values):
    return lax.dot_general(
        basis, values, (((1,), (1,)), ((), ())), preferred_element_type=jnp.float32
    )


def inner_kernel(
    grid, plans, own, sent, ids, analysis,
    fourier_out, basis, spread_analysis, windows, departed, rim_departed, steps, *, slices,
):
    lon_count = grid.shape[1]
    inner = plans.shape[0] // 3
    rim, fields, held = RIM * slices, EDGE * slices, grid.shape[0]
    plan_end = held + 3 * inner
    spread = rim_spread(slices)
    fill_steps(steps)
    for slot in range(windows.shape[0]):
        windows[slot, 0:rim, :] = jnp.zeros((rim, LANES), jnp.float32)
        windows[slot, rim + held :, :] = jnp.zeros((rim, LANES), jnp.float32)
    groups = ids.shape[0] // 4
    few = groups <= 4
    waves = [waves_of(ids, at) for at in range(groups if few else 0)]

    def group_of(ts):
        blocks = [cut((grid, plans, own, sent), t, lon_count, steps) for t in ts]
        for t, block in zip(ts, blocks):
            windows[t, rim : rim + held, :] = block[:held]
        results, rim_results = [], []
        for slot, t in enumerate(ts):
            code, lat_weight, lon_weight = [
                blocks[slot][held + at * inner : held + (at + 1) * inner] for at in range(3)
            ]
            plan = lane_plan(code)
            weights = corner_weights(lat_weight, lon_weight)
            for f in range(slices):
                sources = [
                    windows[
                        t, pl.ds(rim + slices * position + f, inner, stride=slices), :
                    ].astype(jnp.bfloat16)
                    for position in range(2 * RIM + 1)
                ]
                results.append((t, f, interpolate(sources, plan, weights)))
            sources = [
                jnp.concatenate(
                    [
                        windows[t, start : start + rim, :]
                        for start in (slices * position, held - rim + slices * position)
                    ],
                    axis=0,
                ).astype(jnp.bfloat16)
                for position in range(2 * RIM + 1)
            ]
            rim_results.append(interpolate(sources, *rim_plan(spread, blocks[slot][plan_end:])))
        for t, f, result in results:
            departed[f * inner : (f + 1) * inner, tile_at(t)] = result.astype(jnp.bfloat16)
        for t, result in zip(ts, rim_results):
            rim_departed[:, tile_at(t)] = result.astype(jnp.bfloat16)
        for t in ts if few else ():
            for at, wave in enumerate(waves):
                basis[16 * at : 16 * at + 16, tile_at(t)] = basis_tile(t, wave, lon_count)

    if not few:

        def rows_of(group, carry):
            rows = pl.ds(pl.multiple_of(group * 16, 16), 16)
            for t in range(basis.shape[1] // LANES):
                basis[rows, tile_at(t)] = basis_tile(t, waves_of(ids, group), lon_count)
            return carry

        lax.fori_loop(0, groups, rows_of, 0)
    in_groups(departed.shape[1] // LANES, INNER_AT_ONCE, group_of)
    spread_rows(analysis, spread_analysis, inner + EDGE, slices)
    fourier_out[...] = jnp.concatenate(
        [add_up(basis[...], departed[...]), add_up(basis[...], rim_departed[...])], axis=1
    )


def rim_kernel(
    arrived, own, basis, inner_fourier, fourier_out, windows, departed, steps, *, slices, levs
):
    lon_count = arrived.shape[1]
    rim, fields = RIM * slices, EDGE * slices
    spread = rim_spread(slices)
    fill_steps(steps)
    out_row = lax.broadcasted_iota(jnp.int32, (fields, LANES), 0) // slices
    far_step = jnp.where(out_row < RIM, 2 * RIM, 0)
    near_step = jnp.where(out_row == RIM - 1, 2 * RIM - 1, jnp.where(out_row == RIM, 1, -2))

    def part(source, plan, weights, step):
        west_lane, east_lane, row_step = plan
        source = source.astype(jnp.bfloat16)
        low, high = row_step == step, row_step == step - 1
        west = jnp.where(low, weights[0], jnp.where(high, weights[2], 0.0))
        east = jnp.where(low, weights[1], jnp.where(high, weights[3], 0.0))
        return west * lane_gather(source, west_lane).astype(
            jnp.float32
        ) + east * lane_gather(source, east_lane).astype(jnp.float32)

    def group_of(ts):
        blocks = [cut((arrived, own), t, lon_count, steps) for t in ts]
        for t, block in zip(ts, blocks):
            windows[t, 0:rim, :] = block[:rim]
            windows[t, rim:, :] = block[fields : fields + rim]
        for slot, t in enumerate(ts):
            block = blocks[slot]
            (west_lane, east_lane, row_step), weights = rim_plan(spread, block)
            plan = west_lane, east_lane, row_step.astype(jnp.float32).astype(jnp.int32)
            far = jnp.concatenate([block[fields : fields + rim], block[:rim]], axis=0)
            near = jnp.concatenate([windows[t, slices : slices + rim, :]] * 2, axis=0)
            result = part(far, plan, weights, far_step) + part(near, plan, weights, near_step)
            departed[:, tile_at(t)] = result.astype(jnp.bfloat16)

    in_groups(basis.shape[1] // LANES, RIM_AT_ONCE, group_of)
    fourier = jnp.concatenate([inner_fourier[...], add_up(basis[...], departed[...])], axis=1)
    for at in range(fourier_out.shape[0]):
        pair = at // levs
        fourier_out[at] = fourier[4 * pair : 4 * pair + 4].astype(jnp.bfloat16)


def legendre_kernel(first_wave, coeffs, spread_analysis, out, spread_coeffs, *, levs, slices):
    members, _, rows = coeffs.shape
    bands = members // levs
    col_count = spread_analysis.shape[1]
    inner = rows // slices - 2 * EDGE
    column = lax.broadcasted_iota(jnp.int32, (1, LANES), 1)
    rim_at = column - inner * slices
    slice_of = jnp.where(rim_at < 0, column // inner, rim_at % slices)
    slice_of = jnp.where(column < rows, slice_of, -1)

    def spread(band):
        block = jnp.concatenate(
            [coeffs[band * levs + lev].astype(jnp.float32) for lev in range(levs)],
            axis=0,
        )
        block = jnp.concatenate(
            [block, jnp.zeros((block.shape[0], LANES - rows), jnp.float32)], axis=1
        )
        spread_coeffs[:, tile_at(band)] = jnp.concatenate(
            [jnp.where(slice_of == f, block, 0.0) for f in range(slices)], axis=0
        ).astype(jnp.bfloat16)

    for band in range(bands):
        spread(band)
    total = None
    for at in range(0, bands * LANES, 2 * LANES):
        part = slice(at, min(at + 2 * LANES, bands * LANES))
        product = jnp.dot(
            spread_coeffs[:, part], spread_analysis[part, :], preferred_element_type=jnp.float32
        )
        total = product if total is None else total + product
    first = first_wave[0:2, :] > 0.0
    for f in range(slices):
        for lev in range(levs):
            at = (f * levs + lev) * 4
            out[lev * slices + f] = jnp.where(first, total[at : at + 2], total[at + 2 : at + 4])


def shards(grid, dep_row, dep_col, lat_frac, lon_frac, pair_ids, analysis):
    slices, band_rows, lon_count = grid.shape
    pairs = pair_ids.shape[0]
    col_count = analysis.shape[2]
    bands, levs = lax.axis_size("lat"), lax.axis_size("lev")
    inner = band_rows - 2 * RIM
    windows = -(-lon_count // SPAN)
    held_rows = -(-band_rows // 8) * 8
    fields = slices * EDGE
    band_start = jnp.reshape(lax.axis_index("lat") * band_rows, (1,)).astype(jnp.int32)
    vmem = pl.BlockSpec(memory_space=pltpu.VMEM)
    smem = pl.BlockSpec(memory_space=pltpu.SMEM)
    params = pltpu.CompilerParams(vmem_limit_bytes=48 * 2**20)

    rows = grid.transpose(1, 0, 2).reshape(band_rows * slices, lon_count)
    rim_shape = jax.ShapeDtypeStruct((RIM * (slices + 4), lon_count), jnp.bfloat16)
    own_rim, sent_rim, plans = pl.pallas_call(
        pack_kernel,
        out_shape=(
            rim_shape,
            rim_shape,
            jax.ShapeDtypeStruct((3 * inner, lon_count), jnp.bfloat16),
        ),
        in_specs=[smem] + [vmem] * 5,
        out_specs=(vmem,) * 3,
        scratch_shapes=[pltpu.VMEM((5, 4, held_rows, LANES), jnp.float32)],
        compiler_params=params,
    )(band_start, rows, dep_row, dep_col, lat_frac, lon_frac)
    arrived_rim = lax.ppermute(sent_rim, "lat", [(i, (i + 1) % bands) for i in range(bands)])

    plans, ids = lax.optimization_barrier((plans, pair_ids))
    ids = jnp.broadcast_to(ids.astype(jnp.float32)[:, None], (pairs, LANES))
    inner_fourier, basis, spread_analysis = pl.pallas_call(
        functools.partial(inner_kernel, slices=slices),
        out_shape=(
            jax.ShapeDtypeStruct((4 * pairs, slices * band_rows), jnp.float32),
            jax.ShapeDtypeStruct((4 * pairs, windows * LANES), jnp.bfloat16),
            jax.ShapeDtypeStruct((bands * LANES, col_count), jnp.bfloat16),
        ),
        in_specs=[vmem] * 6,
        out_specs=(vmem,) * 3,
        scratch_shapes=[
            pltpu.VMEM((windows, (band_rows + 2 * RIM) * slices, LANES), jnp.float32),
            pltpu.VMEM((slices * inner, windows * LANES), jnp.bfloat16),
            pltpu.VMEM((fields, windows * LANES), jnp.bfloat16),
            pltpu.VMEM((2 * LANES, LANES), jnp.int16),
        ],
        compiler_params=params,
        cost_estimate=pl.CostEstimate(flops=100_000_000, bytes_accessed=2_000_000, transcendentals=0),
    )(rows, plans, own_rim, sent_rim, ids, analysis[0])

    held_coeffs = slices * (band_rows + EDGE)
    fourier = pl.pallas_call(
        functools.partial(rim_kernel, slices=slices, levs=levs),
        out_shape=jax.ShapeDtypeStruct((bands * levs, 4, held_coeffs), jnp.bfloat16),
        in_specs=[vmem] * 4,
        out_specs=vmem,
        scratch_shapes=[
            pltpu.VMEM((windows, fields, LANES), jnp.float32),
            pltpu.VMEM((fields, windows * LANES), jnp.bfloat16),
            pltpu.VMEM((2 * LANES, LANES), jnp.int16),
        ],
        compiler_params=params,
    )(arrived_rim, own_rim, basis, inner_fourier)
    fourier, late_ids = lax.optimization_barrier((fourier, pair_ids))
    own_id = lax.dynamic_slice_in_dim(late_ids, lax.axis_index("lat"), 1)

    columns = lax.axis_index("lev") * col_count + jnp.arange(col_count, dtype=jnp.int32)
    first_wave = jnp.where(columns < NMAX + 1 - own_id, 1.0, 0.0)
    first_wave = jnp.broadcast_to(first_wave[None, :], (8, col_count))

    coeffs = lax.all_to_all(
        fourier, ("lat", "lev"), split_axis=0, concat_axis=0, tiled=True
    )
    out = pl.pallas_call(
        functools.partial(legendre_kernel, levs=levs, slices=slices),
        out_shape=jax.ShapeDtypeStruct((levs * slices, 2, col_count), jnp.float32),
        in_specs=[vmem] * 3,
        out_specs=vmem,
        scratch_shapes=[pltpu.VMEM((4 * levs * slices, bands * LANES), jnp.bfloat16)],
        compiler_params=params,
    )(first_wave, coeffs, spread_analysis)
    return out[None]


def solution(mesh):
    return jax.shard_map(
        shards,
        mesh=mesh,
        in_specs=(
            P("lev", "lat", None),
            P("lat", None),
            P("lat", None),
            P("lat", None),
            P("lat", None),
            P(),
            P("lat", None, "lev"),
        ),
        out_specs=P("lat", None, None, "lev"),
        check_vma=False,
    )
```

```python
import functools
import math

import jax
import jax.numpy as jnp
from jax import lax
from jax.experimental import pallas as pl
from jax.experimental.pallas import tpu as pltpu
from jax.sharding import PartitionSpec as P

NMAX = 1279
LANES = 128
RIM = 2
EDGE = 2 * RIM
REACH = 8
SPAN = LANES - 2 * REACH - 1
ROW_BITS = 5
INNER_AT_ONCE = 2
RIM_AT_ONCE = 4


def lane_gather(values, indices):
    numbers = lax.GatherDimensionNumbers(
        offset_dims=(),
        collapsed_slice_dims=(1,),
        start_index_map=(1,),
        operand_batching_dims=(0,),
        start_indices_batching_dims=(0,),
    )
    return lax.gather(
        values,
        indices[..., None],
        numbers,
        (1, 1),
        mode=lax.GatherScatterMode.PROMISE_IN_BOUNDS,
    )


def tile_at(t):
    return slice(t * LANES, (t + 1) * LANES)


def cut(arrays, t, lon_count, steps):
    tiles = lon_count // LANES
    first, lane_at = divmod((t * SPAN - REACH) % lon_count, LANES)
    second = (first + 1) % tiles
    chosen = jnp.where(steps[...] == jnp.int16(lane_at), jnp.bfloat16(1), jnp.bfloat16(0))
    columns = jnp.concatenate(
        [
            jnp.concatenate([array[:, tile_at(tile)] for array in arrays], axis=0)
            for tile in (first, second)
        ],
        axis=1,
    )
    return jnp.dot(columns, chosen, preferred_element_type=jnp.float32)


def turned(array, t, lon_count):
    tiles = lon_count // LANES
    first, lane_at = divmod((t * SPAN - REACH) % lon_count, LANES)
    if lane_at == 0:
        return array[:, tile_at(first)]
    joined = array[:, tile_at(first)], array[:, tile_at((first + 1) % tiles)]
    lane = lax.broadcasted_iota(jnp.int32, joined[0].shape, 1).astype(jnp.int16)
    return pltpu.roll(jnp.where(lane >= jnp.int16(lane_at), *joined), LANES - lane_at, 1)


def fill_steps(steps):
    shape = steps.shape
    step = lax.broadcasted_iota(jnp.int32, shape, 0) - lax.broadcasted_iota(jnp.int32, shape, 1)
    steps[...] = step.astype(jnp.int16)


def lane_plan(code):
    code = code.astype(jnp.int32)
    lane = lax.broadcasted_iota(jnp.int32, code.shape, 1)
    west = lane - REACH + (code & (1 << ROW_BITS) - 1)
    west_lane = (west & (LANES - 1)).astype(jnp.int16)
    east_lane = ((west + 1) & (LANES - 1)).astype(jnp.int16)
    return west_lane, east_lane, code >> ROW_BITS


def corner_weights(lat_weight, lon_weight):
    south, north = 1.0 - lat_weight, lat_weight
    west, east = 1.0 - lon_weight, lon_weight
    return south * west, south * east, north * west, north * east


def interpolate(sources, plan, weights):
    west_lane, east_lane, row_step = plan
    row_step = row_step.astype(jnp.float32).astype(jnp.bfloat16)
    masks = [row_step == float(step) for step in range(2 * RIM - 1)]

    def pick(gathered):
        low, high = gathered[2 * RIM - 1], gathered[2 * RIM]
        for position in range(2 * RIM - 2, -1, -1):
            low = jnp.where(masks[position], gathered[position], low)
            high = jnp.where(masks[position], gathered[position + 1], high)
        return low.astype(jnp.float32), high.astype(jnp.float32)

    west_low, west_high = pick([lane_gather(source, west_lane) for source in sources])
    east_low, east_high = pick([lane_gather(source, east_lane) for source in sources])
    departed = (
        weights[0] * west_low
        + weights[1] * east_low
        + weights[2] * west_high
        + weights[3] * east_high
    )
    return departed


def in_groups(count, at_once, group):
    for at in range(0, count, at_once):
        group(list(range(at, min(at + at_once, count))))


def pack_kernel(
    band_start, rows, dep_row, dep_col, lat_frac, lon_frac, own_out, sent_out, plan_out, held
):
    band_rows, lon_count = dep_row.shape
    inner = band_rows - 2 * RIM
    slices = rows.shape[0] // band_rows
    rim = RIM * slices
    first_row = band_start[0]

    for t in range(lon_count // LANES):
        cols, slot = tile_at(t), t % 5
        row = lax.broadcasted_iota(jnp.int32, (band_rows, LANES), 0)
        lane = lax.broadcasted_iota(jnp.int32, (band_rows, LANES), 1)
        shift = dep_col[:, cols] - (lane + t * LANES)
        shift = jnp.where(shift > lon_count // 2, shift - lon_count, shift)
        shift = jnp.where(shift < -(lon_count // 2), shift + lon_count, shift)
        row_step = dep_row[:, cols] - (first_row + row) + RIM
        held[slot, 0, 0:band_rows, :] = row_step.astype(jnp.float32)
        held[slot, 1, 0:band_rows, :] = (shift + REACH).astype(jnp.float32)
        held[slot, 2, 0:band_rows, :] = lat_frac[:, cols].astype(jnp.float32)
        held[slot, 3, 0:band_rows, :] = lon_frac[:, cols].astype(jnp.float32)
        edges = rows[0 : 2 * rim, cols], rows[rows.shape[0] - 2 * rim :, cols]
        first_rows, last_rows = [edge.astype(jnp.float32) for edge in edges]
        for out, grid_rows, start in (
            (own_out, first_rows[:rim], 0),
            (sent_out, last_rows[rim:], band_rows - RIM),
        ):
            out[:, cols] = jnp.concatenate(
                [grid_rows] + [held[slot, at, start : start + RIM, :] for at in range(4)], axis=0
            ).astype(jnp.bfloat16)
        middle = [held[slot, at, RIM : RIM + inner, :] for at in range(4)]
        middle = [middle[0] * (1 << ROW_BITS) + middle[1], middle[2], middle[3]]
        for at in range(3):
            plan_out[at * inner : (at + 1) * inner, cols] = middle[at].astype(jnp.bfloat16)


def waves_of(ids, group):
    pair = jnp.concatenate(
        [jnp.broadcast_to(ids[pl.ds(4 * group + at, 1), :], (4, LANES)) for at in range(4)], axis=0
    )
    row = lax.broadcasted_iota(jnp.int32, (16, LANES), 0)
    return jnp.where((row & 2) == 0, pair, NMAX + 1 - pair)


def basis_tile(t, wave, lon_count):
    lane = lax.broadcasted_iota(jnp.int32, (16, LANES), 1)
    row = lax.broadcasted_iota(jnp.int32, (16, LANES), 0)
    longitude = lane + (t * SPAN - REACH)
    quarter = jnp.where((row & 1) == 0, 0.0, float(lon_count // 4))
    steps = longitude.astype(jnp.float32) * wave + quarter
    turns = jnp.floor(steps * (1.0 / lon_count) + 0.5)
    angle = lon_count // 4 - jnp.abs(steps - turns * lon_count)
    angle = angle * (2.0 * math.pi / lon_count)
    square = angle * angle
    series = jnp.float32(-1.0 / 39916800.0)
    for term in (1.0 / 362880.0, -1.0 / 5040.0, 1.0 / 120.0, -1.0 / 6.0, 1.0):
        series = series * square + term
    taken = (lane >= REACH) & (lane < REACH + SPAN) & (longitude < lon_count)
    return jnp.where(taken, angle * series, 0.0).astype(jnp.bfloat16)


def rim_spread(slices):
    fields = EDGE * slices
    shape = (3 * fields, 2 * RIM * (slices + 4))
    wanted = lax.broadcasted_iota(jnp.int32, shape, 0)
    held = lax.broadcasted_iota(jnp.int32, shape, 1)
    kind, rim_row = wanted // fields, wanted % fields // slices
    base = rim_row // RIM * RIM * (slices + 4) + RIM * slices + rim_row % RIM
    spread = jnp.where((kind == 0) & (held == base), float(1 << ROW_BITS), 0.0)
    spread += jnp.where(held == base + RIM * (kind + 1), 1.0, 0.0)
    return spread.astype(jnp.bfloat16)


def rim_plan(spread, packed):
    plan = jnp.dot(spread, packed.astype(jnp.bfloat16), preferred_element_type=jnp.float32)
    fields = spread.shape[0] // 3
    return [plan[fields * at : fields * (at + 1)] for at in range(3)]


def spread_rows(analysis, out, band_rows, slices):
    inner = band_rows - EDGE
    rim = RIM * slices
    place = lax.broadcasted_iota(jnp.int32, (LANES, 1), 0)
    edge = place - slices * inner
    edge_row = edge // slices
    row = jnp.where(edge < 0, RIM + place % inner, edge_row)
    row = jnp.where(edge >= rim, band_rows - EDGE + edge_row, row)
    row = jnp.where(edge >= 2 * rim, edge_row - 3 * RIM, row)
    row = jnp.where(edge >= 4 * rim, -band_rows, row)
    for band in range(out.shape[0] // LANES):
        start = max(0, band * band_rows - RIM) // 16 * 16
        end = min(analysis.shape[0], -(-(band + 1) * band_rows // 16) * 16)
        column = lax.broadcasted_iota(jnp.int32, (LANES, end - start), 1) + start
        chosen = jnp.where((column - band * band_rows == row) & (row >= -RIM), 1.0, 0.0)
        out[band * LANES : (band + 1) * LANES, :] = jnp.dot(
            chosen.astype(jnp.bfloat16),
            analysis[start:end, :],
            preferred_element_type=jnp.float32,
        ).astype(jnp.bfloat16)


def add_up(basis, values):
    return lax.dot_general(
        basis, values, (((1,), (1,)), ((), ())), preferred_element_type=jnp.float32
    )


def inner_kernel(
    grid, plans, own, sent, ids, analysis,
    fourier_out, basis, spread_analysis, windows, departed, rim_departed, steps, *, slices,
):
    lon_count = grid.shape[1]
    inner = plans.shape[0] // 3
    rim, fields, held = RIM * slices, EDGE * slices, grid.shape[0]
    plan_end = held + 3 * inner
    spread = rim_spread(slices)
    fill_steps(steps)
    for slot in range(windows.shape[0]):
        windows[slot, 0:rim, :] = jnp.zeros((rim, LANES), jnp.float32)
        windows[slot, rim + held :, :] = jnp.zeros((rim, LANES), jnp.float32)
    groups = ids.shape[0] // 4
    few = groups <= 4
    waves = [waves_of(ids, at) for at in range(groups if few else 0)]

    def group_of(ts):
        blocks = [cut((grid, plans, own, sent), t, lon_count, steps) for t in ts]
        for t, block in zip(ts, blocks):
            windows[t, rim : rim + held, :] = block[:held]
        results, rim_results = [], []
        for slot, t in enumerate(ts):
            code, lat_weight, lon_weight = [
                blocks[slot][held + at * inner : held + (at + 1) * inner] for at in range(3)
            ]
            plan = lane_plan(code)
            weights = corner_weights(lat_weight, lon_weight)
            for f in range(slices):
                sources = [
                    windows[
                        t, pl.ds(rim + slices * position + f, inner, stride=slices), :
                    ].astype(jnp.bfloat16)
                    for position in range(2 * RIM + 1)
                ]
                results.append((t, f, interpolate(sources, plan, weights)))
            sources = [
                jnp.concatenate(
                    [
                        windows[t, start : start + rim, :]
                        for start in (slices * position, held - rim + slices * position)
                    ],
                    axis=0,
                ).astype(jnp.bfloat16)
                for position in range(2 * RIM + 1)
            ]
            code, lat_weight, lon_weight = rim_plan(spread, blocks[slot][plan_end:])
            weights = corner_weights(lat_weight, lon_weight)
            rim_results.append(interpolate(sources, lane_plan(code), weights))
        for t, f, result in results:
            departed[f * inner : (f + 1) * inner, tile_at(t)] = result.astype(jnp.bfloat16)
        for t, result in zip(ts, rim_results):
            rim_departed[:, tile_at(t)] = result.astype(jnp.bfloat16)
        for t in ts if few else ():
            for at, wave in enumerate(waves):
                basis[16 * at : 16 * at + 16, tile_at(t)] = basis_tile(t, wave, lon_count)

    if not few:

        def rows_of(group, carry):
            rows = pl.ds(pl.multiple_of(group * 16, 16), 16)
            for t in range(basis.shape[1] // LANES):
                basis[rows, tile_at(t)] = basis_tile(t, waves_of(ids, group), lon_count)
            return carry

        lax.fori_loop(0, groups, rows_of, 0)
    in_groups(departed.shape[1] // LANES, INNER_AT_ONCE, group_of)
    spread_rows(analysis, spread_analysis, inner + EDGE, slices)
    fourier_out[...] = jnp.concatenate(
        [add_up(basis[...], departed[...]), add_up(basis[...], rim_departed[...])], axis=1
    )


def rim_kernel(
    arrived, own, basis, inner_fourier, fourier_out, windows, plans, departed, *, slices, levs
):
    lon_count = arrived.shape[1]
    rim, fields = RIM * slices, EDGE * slices
    spread = rim_spread(slices)
    out_row = lax.broadcasted_iota(jnp.int32, (fields, LANES), 0) // slices
    far_step = jnp.where(out_row < RIM, 2 * RIM, 0)
    near_step = jnp.where(out_row == RIM - 1, 2 * RIM - 1, jnp.where(out_row == RIM, 1, -2))

    def part(source, lanes, row_step, lat_weight, lon_weight, step):
        west, east = [lane_gather(source, lane).astype(jnp.float32) for lane in lanes]
        row_weight = jnp.where(
            row_step == step,
            1.0 - lat_weight,
            jnp.where(row_step == step - 1, lat_weight, 0.0),
        )
        return row_weight * (west + lon_weight * (east - west))

    def prepare(ts):
        packed = [[turned(side, t, lon_count) for side in (arrived, own)] for t in ts]
        for t, sides in zip(ts, packed):
            for at, plan in enumerate(rim_plan(spread, jnp.concatenate(sides, axis=0))):
                plans[t, at] = plan
            for at, side in enumerate(sides):
                windows[t, rim * at : rim * (at + 1), :] = side.astype(jnp.float32)[:rim]

    def finish(ts):
        for t in ts:
            west_lane, east_lane, row_step = lane_plan(plans[t, 0])
            plan = (west_lane, east_lane), row_step, plans[t, 1], plans[t, 2]
            far = jnp.concatenate([windows[t, rim:, :], windows[t, 0:rim, :]], axis=0)
            near = jnp.concatenate([windows[t, slices : slices + rim, :]] * 2, axis=0)
            result = part(far.astype(jnp.bfloat16), *plan, far_step)
            result += part(near.astype(jnp.bfloat16), *plan, near_step)
            departed[:, tile_at(t)] = result.astype(jnp.bfloat16)

    count = basis.shape[1] // LANES
    in_groups(count, RIM_AT_ONCE, prepare)
    in_groups(count, RIM_AT_ONCE, finish)
    fourier = jnp.concatenate([inner_fourier[...], add_up(basis[...], departed[...])], axis=1)
    for at in range(fourier_out.shape[0]):
        pair = at // levs
        fourier_out[at] = fourier[4 * pair : 4 * pair + 4].astype(jnp.bfloat16)


def legendre_kernel(first_wave, coeffs, spread_analysis, out, spread_coeffs, *, levs, slices):
    members, _, rows = coeffs.shape
    bands = members // levs
    col_count = spread_analysis.shape[1]
    inner = rows // slices - 2 * EDGE
    column = lax.broadcasted_iota(jnp.int32, (1, LANES), 1)
    rim_at = column - inner * slices
    slice_of = jnp.where(rim_at < 0, column // inner, rim_at % slices)
    slice_of = jnp.where(column < rows, slice_of, -1)

    def spread(band):
        block = jnp.concatenate(
            [coeffs[band * levs + lev].astype(jnp.float32) for lev in range(levs)],
            axis=0,
        )
        block = jnp.concatenate(
            [block, jnp.zeros((block.shape[0], LANES - rows), jnp.float32)], axis=1
        )
        spread_coeffs[:, tile_at(band)] = jnp.concatenate(
            [jnp.where(slice_of == f, block, 0.0) for f in range(slices)], axis=0
        ).astype(jnp.bfloat16)

    for band in range(bands):
        spread(band)
    total = None
    for at in range(0, bands * LANES, 2 * LANES):
        part = slice(at, min(at + 2 * LANES, bands * LANES))
        product = jnp.dot(
            spread_coeffs[:, part], spread_analysis[part, :], preferred_element_type=jnp.float32
        )
        total = product if total is None else total + product
    first = first_wave[0:2, :] > 0.0
    for f in range(slices):
        for lev in range(levs):
            at = (f * levs + lev) * 4
            out[lev * slices + f] = jnp.where(first, total[at : at + 2], total[at + 2 : at + 4])


def shards(grid, dep_row, dep_col, lat_frac, lon_frac, pair_ids, analysis):
    slices, band_rows, lon_count = grid.shape
    pairs = pair_ids.shape[0]
    col_count = analysis.shape[2]
    bands, levs = lax.axis_size("lat"), lax.axis_size("lev")
    inner = band_rows - 2 * RIM
    windows = -(-lon_count // SPAN)
    held_rows = -(-band_rows // 8) * 8
    fields = slices * EDGE
    band_start = jnp.reshape(lax.axis_index("lat") * band_rows, (1,)).astype(jnp.int32)
    vmem = pl.BlockSpec(memory_space=pltpu.VMEM)
    smem = pl.BlockSpec(memory_space=pltpu.SMEM)
    params = pltpu.CompilerParams(vmem_limit_bytes=48 * 2**20)

    rows = grid.transpose(1, 0, 2).reshape(band_rows * slices, lon_count)
    rim_shape = jax.ShapeDtypeStruct((RIM * (slices + 4), lon_count), jnp.bfloat16)
    own_rim, sent_rim, plans = pl.pallas_call(
        pack_kernel,
        out_shape=(
            rim_shape,
            rim_shape,
            jax.ShapeDtypeStruct((3 * inner, lon_count), jnp.bfloat16),
        ),
        in_specs=[smem] + [vmem] * 5,
        out_specs=(vmem,) * 3,
        scratch_shapes=[pltpu.VMEM((5, 4, held_rows, LANES), jnp.float32)],
        compiler_params=params,
    )(band_start, rows, dep_row, dep_col, lat_frac, lon_frac)
    arrived_rim = lax.ppermute(sent_rim, "lat", [(i, (i + 1) % bands) for i in range(bands)])

    plans, ids = lax.optimization_barrier((plans, pair_ids))
    ids = jnp.broadcast_to(ids.astype(jnp.float32)[:, None], (pairs, LANES))
    inner_fourier, basis, spread_analysis = pl.pallas_call(
        functools.partial(inner_kernel, slices=slices),
        out_shape=(
            jax.ShapeDtypeStruct((4 * pairs, slices * band_rows), jnp.float32),
            jax.ShapeDtypeStruct((4 * pairs, windows * LANES), jnp.bfloat16),
            jax.ShapeDtypeStruct((bands * LANES, col_count), jnp.bfloat16),
        ),
        in_specs=[vmem] * 6,
        out_specs=(vmem,) * 3,
        scratch_shapes=[
            pltpu.VMEM((windows, (band_rows + 2 * RIM) * slices, LANES), jnp.float32),
            pltpu.VMEM((slices * inner, windows * LANES), jnp.bfloat16),
            pltpu.VMEM((fields, windows * LANES), jnp.bfloat16),
            pltpu.VMEM((2 * LANES, LANES), jnp.int16),
        ],
        compiler_params=params,
        cost_estimate=pl.CostEstimate(flops=100_000_000, bytes_accessed=2_000_000, transcendentals=0),
    )(rows, plans, own_rim, sent_rim, ids, analysis[0])

    held_coeffs = slices * (band_rows + EDGE)
    fourier = pl.pallas_call(
        functools.partial(rim_kernel, slices=slices, levs=levs),
        out_shape=jax.ShapeDtypeStruct((bands * levs, 4, held_coeffs), jnp.bfloat16),
        in_specs=[vmem] * 4,
        out_specs=vmem,
        scratch_shapes=[
            pltpu.VMEM((windows, fields, LANES), jnp.float32),
            pltpu.VMEM((windows, 3, fields, LANES), jnp.float32),
            pltpu.VMEM((fields, windows * LANES), jnp.bfloat16),
        ],
        compiler_params=params,
    )(arrived_rim, own_rim, basis, inner_fourier)
    fourier, late_ids = lax.optimization_barrier((fourier, pair_ids))
    own_id = lax.dynamic_slice_in_dim(late_ids, lax.axis_index("lat"), 1)

    columns = lax.axis_index("lev") * col_count + jnp.arange(col_count, dtype=jnp.int32)
    first_wave = jnp.where(columns < NMAX + 1 - own_id, 1.0, 0.0)
    first_wave = jnp.broadcast_to(first_wave[None, :], (8, col_count))

    coeffs = lax.all_to_all(
        fourier, ("lat", "lev"), split_axis=0, concat_axis=0, tiled=True
    )
    out = pl.pallas_call(
        functools.partial(legendre_kernel, levs=levs, slices=slices),
        out_shape=jax.ShapeDtypeStruct((levs * slices, 2, col_count), jnp.float32),
        in_specs=[vmem] * 3,
        out_specs=vmem,
        scratch_shapes=[pltpu.VMEM((4 * levs * slices, bands * LANES), jnp.bfloat16)],
        compiler_params=params,
    )(first_wave, coeffs, spread_analysis)
    return out[None]


def solution(mesh):
    return jax.shard_map(
        shards,
        mesh=mesh,
        in_specs=(
            P("lev", "lat", None),
            P("lat", None),
            P("lat", None),
            P("lat", None),
            P("lat", None),
            P(),
            P("lat", None, "lev"),
        ),
        out_specs=P("lat", None, None, "lev"),
        check_vma=False,
    )
```

```python
import functools
import math

import jax
import jax.numpy as jnp
from jax import lax
from jax.experimental import pallas as pl
from jax.experimental.pallas import tpu as pltpu
from jax.sharding import PartitionSpec as P

NMAX = 1279
LANES = 128
RIM = 2
EDGE = 2 * RIM
REACH = 8
SPAN = LANES - 2 * REACH - 1
ROW_BITS = 5
INNER_AT_ONCE = 2
RIM_AT_ONCE = 8
SUM_AT_ONCE = 4


def lane_gather(values, indices):
    numbers = lax.GatherDimensionNumbers(
        offset_dims=(),
        collapsed_slice_dims=(1,),
        start_index_map=(1,),
        operand_batching_dims=(0,),
        start_indices_batching_dims=(0,),
    )
    return lax.gather(
        values,
        indices[..., None],
        numbers,
        (1, 1),
        mode=lax.GatherScatterMode.PROMISE_IN_BOUNDS,
    )


def tile_at(t):
    return slice(t * LANES, (t + 1) * LANES)


def cut(arrays, t, lon_count, steps):
    tiles = lon_count // LANES
    first, lane_at = divmod((t * SPAN - REACH) % lon_count, LANES)
    second = (first + 1) % tiles
    chosen = jnp.where(steps[...] == jnp.int16(lane_at), jnp.bfloat16(1), jnp.bfloat16(0))
    columns = jnp.concatenate(
        [
            jnp.concatenate([array[:, tile_at(tile)] for array in arrays], axis=0)
            for tile in (first, second)
        ],
        axis=1,
    )
    return jnp.dot(columns, chosen, preferred_element_type=jnp.float32)


def turned(array, t, lon_count):
    tiles = lon_count // LANES
    first, lane_at = divmod((t * SPAN - REACH) % lon_count, LANES)
    if lane_at == 0:
        return array[:, tile_at(first)]
    joined = array[:, tile_at(first)], array[:, tile_at((first + 1) % tiles)]
    lane = lax.broadcasted_iota(jnp.int32, joined[0].shape, 1).astype(jnp.int16)
    return pltpu.roll(jnp.where(lane >= jnp.int16(lane_at), *joined), LANES - lane_at, 1)


def fill_steps(steps):
    shape = steps.shape
    step = lax.broadcasted_iota(jnp.int32, shape, 0) - lax.broadcasted_iota(jnp.int32, shape, 1)
    steps[...] = step.astype(jnp.int16)


def lane_plan(code):
    code = code.astype(jnp.int32)
    lane = lax.broadcasted_iota(jnp.int32, code.shape, 1)
    west = lane - REACH + (code & (1 << ROW_BITS) - 1)
    west_lane = (west & (LANES - 1)).astype(jnp.int16)
    east_lane = ((west + 1) & (LANES - 1)).astype(jnp.int16)
    return west_lane, east_lane, code >> ROW_BITS


def corner_weights(lat_weight, lon_weight):
    south, north = 1.0 - lat_weight, lat_weight
    west, east = 1.0 - lon_weight, lon_weight
    return south * west, south * east, north * west, north * east


def interpolate(sources, plan, weights):
    west_lane, east_lane, row_step = plan
    row_step = row_step.astype(jnp.float32).astype(jnp.bfloat16)
    masks = [row_step == float(step) for step in range(2 * RIM - 1)]
    last = 2 * RIM - 1

    def pick(gathered):
        if len(gathered) > 2 * RIM:
            low, high = gathered[last], gathered[last + 1]
        else:
            zero = jnp.zeros_like(gathered[0])
            low = jnp.where(row_step == float(last), gathered[last], zero)
            high = jnp.where(row_step == -1.0, gathered[0], zero)
        for position in range(last - 1, -1, -1):
            low = jnp.where(masks[position], gathered[position], low)
            high = jnp.where(masks[position], gathered[position + 1], high)
        return low.astype(jnp.float32), high.astype(jnp.float32)

    west_low, west_high = pick([lane_gather(source, west_lane) for source in sources])
    east_low, east_high = pick([lane_gather(source, east_lane) for source in sources])
    departed = (
        weights[0] * west_low
        + weights[1] * east_low
        + weights[2] * west_high
        + weights[3] * east_high
    )
    return departed


def groups_of(count, at_once):
    return [range(at, min(at + at_once, count)) for at in range(0, count, at_once)]


def pack_kernel(
    band_start, rows, dep_row, dep_col, lat_frac, lon_frac, own_out, sent_out, plan_out, held
):
    band_rows, lon_count = dep_row.shape
    inner = band_rows - 2 * RIM
    slices = rows.shape[0] // band_rows
    rim = RIM * slices
    first_row = band_start[0]

    for t in range(lon_count // LANES):
        cols, slot = tile_at(t), t % 5
        row = lax.broadcasted_iota(jnp.int32, (band_rows, LANES), 0)
        lane = lax.broadcasted_iota(jnp.int32, (band_rows, LANES), 1)
        shift = dep_col[:, cols] - (lane + t * LANES)
        shift = jnp.where(shift > lon_count // 2, shift - lon_count, shift)
        shift = jnp.where(shift < -(lon_count // 2), shift + lon_count, shift)
        row_step = dep_row[:, cols] - (first_row + row) + RIM
        held[slot, 0, 0:band_rows, :] = row_step.astype(jnp.float32)
        held[slot, 1, 0:band_rows, :] = (shift + REACH).astype(jnp.float32)
        held[slot, 2, 0:band_rows, :] = lat_frac[:, cols].astype(jnp.float32)
        held[slot, 3, 0:band_rows, :] = lon_frac[:, cols].astype(jnp.float32)
        edges = rows[0 : 2 * rim, cols], rows[rows.shape[0] - 2 * rim :, cols]
        first_rows, last_rows = [edge.astype(jnp.float32) for edge in edges]
        for out, grid_rows, start in (
            (own_out, first_rows[:rim], 0),
            (sent_out, last_rows[rim:], band_rows - RIM),
        ):
            out[:, cols] = jnp.concatenate(
                [grid_rows] + [held[slot, at, start : start + RIM, :] for at in range(4)], axis=0
            ).astype(jnp.bfloat16)
        middle = [held[slot, at, RIM : RIM + inner, :] for at in range(4)]
        middle = [middle[0] * (1 << ROW_BITS) + middle[1], middle[2], middle[3]]
        for at in range(3):
            plan_out[at * inner : (at + 1) * inner, cols] = middle[at].astype(jnp.bfloat16)


def waves_of(ids, group):
    pair = jnp.concatenate(
        [jnp.broadcast_to(ids[pl.ds(4 * group + at, 1), :], (4, LANES)) for at in range(4)], axis=0
    )
    row = lax.broadcasted_iota(jnp.int32, (16, LANES), 0)
    return jnp.where((row & 2) == 0, pair, NMAX + 1 - pair)


def basis_tile(t, wave, lon_count):
    lane = lax.broadcasted_iota(jnp.int32, (16, LANES), 1)
    row = lax.broadcasted_iota(jnp.int32, (16, LANES), 0)
    longitude = lane + (t * SPAN - REACH)
    quarter = jnp.where((row & 1) == 0, 0.0, float(lon_count // 4))
    steps = longitude.astype(jnp.float32) * wave + quarter
    turns = jnp.floor(steps * (1.0 / lon_count) + 0.5)
    angle = lon_count // 4 - jnp.abs(steps - turns * lon_count)
    angle = angle * (2.0 * math.pi / lon_count)
    square = angle * angle
    series = jnp.float32(-1.0 / 39916800.0)
    for term in (1.0 / 362880.0, -1.0 / 5040.0, 1.0 / 120.0, -1.0 / 6.0, 1.0):
        series = series * square + term
    taken = (lane >= REACH) & (lane < REACH + SPAN) & (longitude < lon_count)
    return jnp.where(taken, angle * series, 0.0).astype(jnp.bfloat16)


def rim_spread(slices):
    fields = EDGE * slices
    shape = (3 * fields, 2 * RIM * (slices + 4))
    wanted = lax.broadcasted_iota(jnp.int32, shape, 0)
    held = lax.broadcasted_iota(jnp.int32, shape, 1)
    kind, rim_row = wanted // fields, wanted % fields // slices
    base = rim_row // RIM * RIM * (slices + 4) + RIM * slices + rim_row % RIM
    spread = jnp.where((kind == 0) & (held == base), float(1 << ROW_BITS), 0.0)
    spread += jnp.where(held == base + RIM * (kind + 1), 1.0, 0.0)
    return spread.astype(jnp.bfloat16)


def rim_plan(spread, packed):
    plan = jnp.dot(spread, packed.astype(jnp.bfloat16), preferred_element_type=jnp.float32)
    fields = spread.shape[0] // 3
    return [plan[fields * at : fields * (at + 1)] for at in range(3)]


def spread_rows(analysis, out, band_rows, slices):
    inner = band_rows - EDGE
    rim = RIM * slices
    place = lax.broadcasted_iota(jnp.int32, (LANES, 1), 0)
    edge = place - slices * inner
    edge_row = edge // slices
    row = jnp.where(edge < 0, RIM + place % inner, edge_row)
    row = jnp.where(edge >= rim, band_rows - EDGE + edge_row, row)
    row = jnp.where(edge >= 2 * rim, edge_row - 3 * RIM, row)
    row = jnp.where(edge >= 4 * rim, -band_rows, row)
    for band in range(out.shape[0] // LANES):
        start = max(0, band * band_rows - RIM) // 16 * 16
        end = min(analysis.shape[0], -(-(band + 1) * band_rows // 16) * 16)
        column = lax.broadcasted_iota(jnp.int32, (LANES, end - start), 1) + start
        chosen = jnp.where((column - band * band_rows == row) & (row >= -RIM), 1.0, 0.0)
        out[band * LANES : (band + 1) * LANES, :] = jnp.dot(
            chosen.astype(jnp.bfloat16),
            analysis[start:end, :],
            preferred_element_type=jnp.float32,
        ).astype(jnp.bfloat16)


def add_up(total, basis, values, windows):
    cols = slice(windows[0] * LANES, (windows[-1] + 1) * LANES)
    part = lax.dot_general(
        basis[:, cols], values[:, cols], (((1,), (1,)), ((), ())), preferred_element_type=jnp.float32
    )
    return part if total is None else total + part


def inner_kernel(
    grid, plans, own, sent, ids, analysis,
    fourier_out, basis, spread_analysis, windows, held_plans, departed, rim_departed, steps, *, slices,
):
    lon_count = grid.shape[1]
    inner = plans.shape[0] // 3
    rim, fields, held = RIM * slices, EDGE * slices, grid.shape[0]
    spread = rim_spread(slices)
    fill_steps(steps)
    rim_base = jnp.where(lax.broadcasted_iota(jnp.int32, (fields, LANES), 0) < rim, 1, 0)
    quads = ids.shape[0] // 4
    few = quads <= 4
    waves = [waves_of(ids, at) for at in range(quads if few else 0)]

    def prepare(ts):
        for t in ts:
            block = cut((grid, plans, own, sent), t, lon_count, steps)
            windows[t, rim : rim + held, :] = block[:held]
            windows[t, 0:rim, :] = jnp.zeros((rim, LANES), jnp.float32)
            windows[t, rim + held :, :] = jnp.zeros((rim, LANES), jnp.float32)
            held_plans[t, 0 : 3 * inner, :] = block[held : held + 3 * inner]
            for at, plan in enumerate(rim_plan(spread, block[held + 3 * inner :])):
                start = 3 * inner + at * fields
                held_plans[t, start : start + fields, :] = plan

    def finish(ts):
        results, rim_results = [], []
        for t in ts:
            code, lat_weight, lon_weight = [
                held_plans[t, at * inner : (at + 1) * inner, :] for at in range(3)
            ]
            plan = lane_plan(code)
            weights = corner_weights(lat_weight, lon_weight)
            for f in range(slices):
                sources = [
                    windows[
                        t, pl.ds(rim + slices * position + f, inner, stride=slices), :
                    ].astype(jnp.bfloat16)
                    for position in range(2 * RIM + 1)
                ]
                results.append((t, f, interpolate(sources, plan, weights)))
            sources = [
                jnp.concatenate(
                    [
                        windows[t, start : start + rim, :]
                        for start in (slices * (position + 1), held - rim + slices * position)
                    ],
                    axis=0,
                ).astype(jnp.bfloat16)
                for position in range(2 * RIM)
            ]
            code, lat_weight, lon_weight = [
                held_plans[t, 3 * inner + at * fields : 3 * inner + (at + 1) * fields, :]
                for at in range(3)
            ]
            west_lane, east_lane, row_step = lane_plan(code)
            weights = corner_weights(lat_weight, lon_weight)
            plan = west_lane, east_lane, row_step - rim_base
            rim_results.append((t, interpolate(sources, plan, weights)))
        for t, f, result in results:
            departed[f * inner : (f + 1) * inner, tile_at(t)] = result.astype(jnp.bfloat16)
        for t, result in rim_results:
            rim_departed[:, tile_at(t)] = result.astype(jnp.bfloat16)
        for t in ts if few else ():
            for at, wave in enumerate(waves):
                basis[16 * at : 16 * at + 16, tile_at(t)] = basis_tile(t, wave, lon_count)

    if not few:

        def rows_of(group, carry):
            rows = pl.ds(pl.multiple_of(group * 16, 16), 16)
            for t in range(basis.shape[1] // LANES):
                basis[rows, tile_at(t)] = basis_tile(t, waves_of(ids, group), lon_count)
            return carry

        lax.fori_loop(0, quads, rows_of, 0)
    count = departed.shape[1] // LANES
    groups = groups_of(count, INNER_AT_ONCE)
    totals = [None, None]
    prepare(groups[0])
    for at, ts in enumerate(groups):
        if at + 1 < len(groups):
            prepare(groups[at + 1])
        finish(ts)
        first = max(0, at // SUM_AT_ONCE * SUM_AT_ONCE)
        if at % SUM_AT_ONCE == SUM_AT_ONCE - 1 or at + 1 == len(groups):
            done = range(groups[first][0], ts[-1] + 1)
            totals = [
                add_up(total, basis, values, done)
                for total, values in zip(totals, (departed, rim_departed))
            ]
    spread_rows(analysis, spread_analysis, inner + EDGE, slices)
    fourier_out[...] = jnp.concatenate(totals, axis=1)


def rim_kernel(
    arrived, own, basis, inner_fourier, fourier_out, windows, plans, departed, *, slices, levs
):
    lon_count = arrived.shape[1]
    rim, fields = RIM * slices, EDGE * slices
    spread = rim_spread(slices)
    out_row = lax.broadcasted_iota(jnp.int32, (fields, LANES), 0) // slices
    far_step = jnp.where(out_row < RIM, 2 * RIM, 0)
    near_step = jnp.where(out_row == RIM - 1, 2 * RIM - 1, jnp.where(out_row == RIM, 1, -2))

    def part(source, lanes, row_step, lat_weight, lon_weight, step):
        west, east = [lane_gather(source, lane).astype(jnp.float32) for lane in lanes]
        row_weight = jnp.where(
            row_step == step,
            1.0 - lat_weight,
            jnp.where(row_step == step - 1, lat_weight, 0.0),
        )
        return row_weight * (west + lon_weight * (east - west))

    def prepare(ts):
        for t in ts:
            sides = [turned(side, t, lon_count) for side in (arrived, own)]
            for at, plan in enumerate(rim_plan(spread, jnp.concatenate(sides, axis=0))):
                plans[t, at] = plan
            for at, side in enumerate(sides):
                windows[t, rim * at : rim * (at + 1), :] = side.astype(jnp.float32)[:rim]

    def finish(ts):
        for t in ts:
            west_lane, east_lane, row_step = lane_plan(plans[t, 0])
            plan = (west_lane, east_lane), row_step, plans[t, 1], plans[t, 2]
            far = jnp.concatenate([windows[t, rim:, :], windows[t, 0:rim, :]], axis=0)
            near = jnp.concatenate([windows[t, slices : slices + rim, :]] * 2, axis=0)
            result = part(far.astype(jnp.bfloat16), *plan, far_step)
            result += part(near.astype(jnp.bfloat16), *plan, near_step)
            departed[:, tile_at(t)] = result.astype(jnp.bfloat16)

    count = basis.shape[1] // LANES
    prepare(range(count))
    total = None
    for ts in groups_of(count, RIM_AT_ONCE):
        finish(ts)
        total = add_up(total, basis, departed, ts)
    fourier = jnp.concatenate([inner_fourier[...], total], axis=1)
    for at in range(fourier_out.shape[0]):
        pair = at // levs
        fourier_out[at] = fourier[4 * pair : 4 * pair + 4].astype(jnp.bfloat16)


def legendre_kernel(first_wave, coeffs, spread_analysis, out, spread_coeffs, *, levs, slices):
    members, _, rows = coeffs.shape
    bands = members // levs
    col_count = spread_analysis.shape[1]
    inner = rows // slices - 2 * EDGE
    column = lax.broadcasted_iota(jnp.int32, (1, LANES), 1)
    rim_at = column - inner * slices
    slice_of = jnp.where(rim_at < 0, column // inner, rim_at % slices)
    slice_of = jnp.where(column < rows, slice_of, -1)

    def spread(band):
        block = jnp.concatenate(
            [coeffs[band * levs + lev].astype(jnp.float32) for lev in range(levs)],
            axis=0,
        )
        block = jnp.concatenate(
            [block, jnp.zeros((block.shape[0], LANES - rows), jnp.float32)], axis=1
        )
        spread_coeffs[:, tile_at(band)] = jnp.concatenate(
            [jnp.where(slice_of == f, block, 0.0) for f in range(slices)], axis=0
        ).astype(jnp.bfloat16)

    for band in range(bands):
        spread(band)
    total = None
    for at in range(0, bands * LANES, 2 * LANES):
        part = slice(at, min(at + 2 * LANES, bands * LANES))
        product = jnp.dot(
            spread_coeffs[:, part], spread_analysis[part, :], preferred_element_type=jnp.float32
        )
        total = product if total is None else total + product
    first = first_wave[0:2, :] > 0.0
    for f in range(slices):
        for lev in range(levs):
            at = (f * levs + lev) * 4
            out[lev * slices + f] = jnp.where(first, total[at : at + 2], total[at + 2 : at + 4])


def shards(grid, dep_row, dep_col, lat_frac, lon_frac, pair_ids, analysis):
    slices, band_rows, lon_count = grid.shape
    pairs = pair_ids.shape[0]
    col_count = analysis.shape[2]
    bands, levs = lax.axis_size("lat"), lax.axis_size("lev")
    inner = band_rows - 2 * RIM
    windows = -(-lon_count // SPAN)
    held_rows = -(-band_rows // 8) * 8
    fields = slices * EDGE
    band_start = jnp.reshape(lax.axis_index("lat") * band_rows, (1,)).astype(jnp.int32)
    vmem = pl.BlockSpec(memory_space=pltpu.VMEM)
    smem = pl.BlockSpec(memory_space=pltpu.SMEM)
    params = pltpu.CompilerParams(vmem_limit_bytes=48 * 2**20)

    rows = grid.transpose(1, 0, 2).reshape(band_rows * slices, lon_count)
    rim_shape = jax.ShapeDtypeStruct((RIM * (slices + 4), lon_count), jnp.bfloat16)
    own_rim, sent_rim, plans = pl.pallas_call(
        pack_kernel,
        out_shape=(
            rim_shape,
            rim_shape,
            jax.ShapeDtypeStruct((3 * inner, lon_count), jnp.bfloat16),
        ),
        in_specs=[smem] + [vmem] * 5,
        out_specs=(vmem,) * 3,
        scratch_shapes=[pltpu.VMEM((5, 4, held_rows, LANES), jnp.float32)],
        compiler_params=params,
    )(band_start, rows, dep_row, dep_col, lat_frac, lon_frac)
    arrived_rim = lax.ppermute(sent_rim, "lat", [(i, (i + 1) % bands) for i in range(bands)])

    plans, ids = lax.optimization_barrier((plans, pair_ids))
    ids = jnp.broadcast_to(ids.astype(jnp.float32)[:, None], (pairs, LANES))
    inner_fourier, basis, spread_analysis = pl.pallas_call(
        functools.partial(inner_kernel, slices=slices),
        out_shape=(
            jax.ShapeDtypeStruct((4 * pairs, slices * band_rows), jnp.float32),
            jax.ShapeDtypeStruct((4 * pairs, windows * LANES), jnp.bfloat16),
            jax.ShapeDtypeStruct((bands * LANES, col_count), jnp.bfloat16),
        ),
        in_specs=[vmem] * 6,
        out_specs=(vmem,) * 3,
        scratch_shapes=[
            pltpu.VMEM((windows, (band_rows + 2 * RIM) * slices, LANES), jnp.float32),
            pltpu.VMEM((windows, 3 * (inner + fields), LANES), jnp.float32),
            pltpu.VMEM((slices * inner, windows * LANES), jnp.bfloat16),
            pltpu.VMEM((fields, windows * LANES), jnp.bfloat16),
            pltpu.VMEM((2 * LANES, LANES), jnp.int16),
        ],
        compiler_params=params,
        cost_estimate=pl.CostEstimate(flops=100_000_000, bytes_accessed=2_000_000, transcendentals=0),
    )(rows, plans, own_rim, sent_rim, ids, analysis[0])

    held_coeffs = slices * (band_rows + EDGE)
    fourier = pl.pallas_call(
        functools.partial(rim_kernel, slices=slices, levs=levs),
        out_shape=jax.ShapeDtypeStruct((bands * levs, 4, held_coeffs), jnp.bfloat16),
        in_specs=[vmem] * 4,
        out_specs=vmem,
        scratch_shapes=[
            pltpu.VMEM((windows, fields, LANES), jnp.float32),
            pltpu.VMEM((windows, 3, fields, LANES), jnp.float32),
            pltpu.VMEM((fields, windows * LANES), jnp.bfloat16),
        ],
        compiler_params=params,
    )(arrived_rim, own_rim, basis, inner_fourier)
    fourier, late_ids = lax.optimization_barrier((fourier, pair_ids))
    own_id = lax.dynamic_slice_in_dim(late_ids, lax.axis_index("lat"), 1)

    columns = lax.axis_index("lev") * col_count + jnp.arange(col_count, dtype=jnp.int32)
    first_wave = jnp.where(columns < NMAX + 1 - own_id, 1.0, 0.0)
    first_wave = jnp.broadcast_to(first_wave[None, :], (8, col_count))

    coeffs = lax.all_to_all(
        fourier, ("lat", "lev"), split_axis=0, concat_axis=0, tiled=True
    )
    out = pl.pallas_call(
        functools.partial(legendre_kernel, levs=levs, slices=slices),
        out_shape=jax.ShapeDtypeStruct((levs * slices, 2, col_count), jnp.float32),
        in_specs=[vmem] * 3,
        out_specs=vmem,
        scratch_shapes=[pltpu.VMEM((4 * levs * slices, bands * LANES), jnp.bfloat16)],
        compiler_params=params,
    )(first_wave, coeffs, spread_analysis)
    return out[None]


def solution(mesh):
    return jax.shard_map(
        shards,
        mesh=mesh,
        in_specs=(
            P("lev", "lat", None),
            P("lat", None),
            P("lat", None),
            P("lat", None),
            P("lat", None),
            P(),
            P("lat", None, "lev"),
        ),
        out_specs=P("lat", None, None, "lev"),
        check_vma=False,
    )
```

```python
import functools
import math

import jax
import jax.numpy as jnp
from jax import lax
from jax.experimental import pallas as pl
from jax.experimental.pallas import tpu as pltpu
from jax.sharding import PartitionSpec as P

NMAX = 1279
LANES = 128
RIM = 2
EDGE = 2 * RIM
REACH = 8
SPAN = LANES - 2 * REACH - 1
ROW_BITS = 5
INNER_AT_ONCE = 2
RIM_AT_ONCE = 8


def lane_gather(values, indices):
    numbers = lax.GatherDimensionNumbers(
        offset_dims=(),
        collapsed_slice_dims=(1,),
        start_index_map=(1,),
        operand_batching_dims=(0,),
        start_indices_batching_dims=(0,),
    )
    return lax.gather(
        values,
        indices[..., None],
        numbers,
        (1, 1),
        mode=lax.GatherScatterMode.PROMISE_IN_BOUNDS,
    )


def tile_at(t):
    return slice(t * LANES, (t + 1) * LANES)


def cut(arrays, t, lon_count, steps):
    tiles = lon_count // LANES
    first, lane_at = divmod((t * SPAN - REACH) % lon_count, LANES)
    second = (first + 1) % tiles
    chosen = jnp.where(steps[...] == jnp.int16(lane_at), jnp.bfloat16(1), jnp.bfloat16(0))
    columns = jnp.concatenate(
        [
            jnp.concatenate([array[:, tile_at(tile)] for array in arrays], axis=0)
            for tile in (first, second)
        ],
        axis=1,
    )
    return jnp.dot(columns, chosen, preferred_element_type=jnp.float32)


def turned(array, t, lon_count):
    tiles = lon_count // LANES
    first, lane_at = divmod((t * SPAN - REACH) % lon_count, LANES)
    if lane_at == 0:
        return array[:, tile_at(first)]
    joined = array[:, tile_at(first)], array[:, tile_at((first + 1) % tiles)]
    lane = lax.broadcasted_iota(jnp.int32, joined[0].shape, 1).astype(jnp.int16)
    return pltpu.roll(jnp.where(lane >= jnp.int16(lane_at), *joined), LANES - lane_at, 1)


def fill_steps(steps):
    shape = steps.shape
    step = lax.broadcasted_iota(jnp.int32, shape, 0) - lax.broadcasted_iota(jnp.int32, shape, 1)
    steps[...] = step.astype(jnp.int16)


def lane_plan(code):
    code = code.astype(jnp.int32)
    lane = lax.broadcasted_iota(jnp.int32, code.shape, 1)
    west = lane - REACH + (code & (1 << ROW_BITS) - 1)
    west_lane = (west & (LANES - 1)).astype(jnp.int16)
    east_lane = ((west + 1) & (LANES - 1)).astype(jnp.int16)
    return west_lane, east_lane, code >> ROW_BITS


def corner_weights(lat_weight, lon_weight):
    south, north = 1.0 - lat_weight, lat_weight
    west, east = 1.0 - lon_weight, lon_weight
    return south * west, south * east, north * west, north * east


def interpolate(sources, plan, weights):
    west_lane, east_lane, row_step = plan
    row_step = row_step.astype(jnp.float32).astype(jnp.bfloat16)
    masks = [row_step == float(step) for step in range(2 * RIM - 1)]
    last = 2 * RIM - 1

    def pick(gathered):
        if len(gathered) > 2 * RIM:
            low, high = gathered[last], gathered[last + 1]
        else:
            zero = jnp.zeros_like(gathered[0])
            low = jnp.where(row_step == float(last), gathered[last], zero)
            high = jnp.where(row_step == -1.0, gathered[0], zero)
        for position in range(last - 1, -1, -1):
            low = jnp.where(masks[position], gathered[position], low)
            high = jnp.where(masks[position], gathered[position + 1], high)
        return low.astype(jnp.float32), high.astype(jnp.float32)

    west_low, west_high = pick([lane_gather(source, west_lane) for source in sources])
    east_low, east_high = pick([lane_gather(source, east_lane) for source in sources])
    departed = (
        weights[0] * west_low
        + weights[1] * east_low
        + weights[2] * west_high
        + weights[3] * east_high
    )
    return departed


def groups_of(count, at_once):
    return [range(at, min(at + at_once, count)) for at in range(0, count, at_once)]


def pack_kernel(
    band_start, rows, dep_row, dep_col, lat_frac, lon_frac, own_out, sent_out, plan_out, held
):
    band_rows, lon_count = dep_row.shape
    inner = band_rows - 2 * RIM
    slices = rows.shape[0] // band_rows
    rim = RIM * slices
    first_row = band_start[0]

    for t in range(lon_count // LANES):
        cols, slot = tile_at(t), t % 5
        row = lax.broadcasted_iota(jnp.int32, (band_rows, LANES), 0)
        lane = lax.broadcasted_iota(jnp.int32, (band_rows, LANES), 1)
        shift = dep_col[:, cols] - (lane + t * LANES)
        shift = jnp.where(shift > lon_count // 2, shift - lon_count, shift)
        shift = jnp.where(shift < -(lon_count // 2), shift + lon_count, shift)
        row_step = dep_row[:, cols] - (first_row + row) + RIM
        held[slot, 0, 0:band_rows, :] = row_step.astype(jnp.float32)
        held[slot, 1, 0:band_rows, :] = (shift + REACH).astype(jnp.float32)
        held[slot, 2, 0:band_rows, :] = lat_frac[:, cols].astype(jnp.float32)
        held[slot, 3, 0:band_rows, :] = lon_frac[:, cols].astype(jnp.float32)
        edges = rows[0 : 2 * rim, cols], rows[rows.shape[0] - 2 * rim :, cols]
        first_rows, last_rows = [edge.astype(jnp.float32) for edge in edges]
        for out, grid_rows, start in (
            (own_out, first_rows[:rim], 0),
            (sent_out, last_rows[rim:], band_rows - RIM),
        ):
            out[:, cols] = jnp.concatenate(
                [grid_rows] + [held[slot, at, start : start + RIM, :] for at in range(4)], axis=0
            ).astype(jnp.bfloat16)
        middle = [held[slot, at, RIM : RIM + inner, :] for at in range(4)]
        middle = [middle[0] * (1 << ROW_BITS) + middle[1], middle[2], middle[3]]
        for at in range(3):
            plan_out[at * inner : (at + 1) * inner, cols] = middle[at].astype(jnp.bfloat16)


def waves_of(ids, group):
    pair = jnp.concatenate(
        [jnp.broadcast_to(ids[pl.ds(4 * group + at, 1), :], (4, LANES)) for at in range(4)], axis=0
    )
    row = lax.broadcasted_iota(jnp.int32, (16, LANES), 0)
    return jnp.where((row & 2) == 0, pair, NMAX + 1 - pair)


def basis_tile(t, wave, lon_count):
    lane = lax.broadcasted_iota(jnp.int32, (16, LANES), 1)
    row = lax.broadcasted_iota(jnp.int32, (16, LANES), 0)
    longitude = lane + (t * SPAN - REACH)
    quarter = jnp.where((row & 1) == 0, 0.0, float(lon_count // 4))
    steps = longitude.astype(jnp.float32) * wave + quarter
    turns = jnp.floor(steps * (1.0 / lon_count) + 0.5)
    angle = lon_count // 4 - jnp.abs(steps - turns * lon_count)
    angle = angle * (2.0 * math.pi / lon_count)
    square = angle * angle
    series = jnp.float32(-1.0 / 39916800.0)
    for term in (1.0 / 362880.0, -1.0 / 5040.0, 1.0 / 120.0, -1.0 / 6.0, 1.0):
        series = series * square + term
    taken = (lane >= REACH) & (lane < REACH + SPAN) & (longitude < lon_count)
    return jnp.where(taken, angle * series, 0.0).astype(jnp.bfloat16)


def rim_spread(slices):
    fields = EDGE * slices
    shape = (3 * fields, 2 * RIM * (slices + 4))
    wanted = lax.broadcasted_iota(jnp.int32, shape, 0)
    held = lax.broadcasted_iota(jnp.int32, shape, 1)
    kind, rim_row = wanted // fields, wanted % fields // slices
    base = rim_row // RIM * RIM * (slices + 4) + RIM * slices + rim_row % RIM
    spread = jnp.where((kind == 0) & (held == base), float(1 << ROW_BITS), 0.0)
    spread += jnp.where(held == base + RIM * (kind + 1), 1.0, 0.0)
    return spread.astype(jnp.bfloat16)


def rim_plan(spread, packed):
    plan = jnp.dot(spread, packed.astype(jnp.bfloat16), preferred_element_type=jnp.float32)
    fields = spread.shape[0] // 3
    return [plan[fields * at : fields * (at + 1)] for at in range(3)]


def spread_rows(analysis, out, band_rows, slices):
    inner = band_rows - EDGE
    rim = RIM * slices
    place = lax.broadcasted_iota(jnp.int32, (LANES, 1), 0)
    edge = place - slices * inner
    edge_row = edge // slices
    row = jnp.where(edge < 0, RIM + place % inner, edge_row)
    row = jnp.where(edge >= rim, band_rows - EDGE + edge_row, row)
    row = jnp.where(edge >= 2 * rim, edge_row - 3 * RIM, row)
    row = jnp.where(edge >= 4 * rim, -band_rows, row)
    for band in range(out.shape[0] // LANES):
        start = max(0, band * band_rows - RIM) // 16 * 16
        end = min(analysis.shape[0], -(-(band + 1) * band_rows // 16) * 16)
        column = lax.broadcasted_iota(jnp.int32, (LANES, end - start), 1) + start
        chosen = jnp.where((column - band * band_rows == row) & (row >= -RIM), 1.0, 0.0)
        out[band * LANES : (band + 1) * LANES, :] = jnp.dot(
            chosen.astype(jnp.bfloat16),
            analysis[start:end, :],
            preferred_element_type=jnp.float32,
        ).astype(jnp.bfloat16)


def add_up(total, basis, values, windows):
    cols = slice(windows[0] * LANES, (windows[-1] + 1) * LANES)
    part = lax.dot_general(
        basis[:, cols], values[:, cols], (((1,), (1,)), ((), ())), preferred_element_type=jnp.float32
    )
    return part if total is None else total + part


def inner_kernel(
    grid, plans, own, sent, ids, analysis,
    fourier_out, basis, spread_analysis, windows, departed, rim_departed, steps, *, slices,
):
    lon_count = grid.shape[1]
    inner = plans.shape[0] // 3
    rim, fields, held = RIM * slices, EDGE * slices, grid.shape[0]
    plan_end = held + 3 * inner
    spread = rim_spread(slices)
    fill_steps(steps)
    rim_base = jnp.where(lax.broadcasted_iota(jnp.int32, (fields, LANES), 0) < rim, 1, 0)
    for slot in range(windows.shape[0]):
        windows[slot, 0:rim, :] = jnp.zeros((rim, LANES), jnp.float32)
        windows[slot, rim + held :, :] = jnp.zeros((rim, LANES), jnp.float32)
    quads = ids.shape[0] // 4
    few = quads <= 4
    waves = [waves_of(ids, at) for at in range(quads if few else 0)]

    def group_of(ts):
        blocks = [cut((grid, plans, own, sent), t, lon_count, steps) for t in ts]
        for t, block in zip(ts, blocks):
            windows[t, rim : rim + held, :] = block[:held]
        results, rim_results = [], []
        for slot, t in enumerate(ts):
            code, lat_weight, lon_weight = [
                blocks[slot][held + at * inner : held + (at + 1) * inner] for at in range(3)
            ]
            plan = lane_plan(code)
            weights = corner_weights(lat_weight, lon_weight)
            for f in range(slices):
                sources = [
                    windows[
                        t, pl.ds(rim + slices * position + f, inner, stride=slices), :
                    ].astype(jnp.bfloat16)
                    for position in range(2 * RIM + 1)
                ]
                results.append((t, f, interpolate(sources, plan, weights)))
            sources = [
                jnp.concatenate(
                    [
                        windows[t, start : start + rim, :]
                        for start in (slices * (position + 1), held - rim + slices * position)
                    ],
                    axis=0,
                ).astype(jnp.bfloat16)
                for position in range(2 * RIM)
            ]
            code, lat_weight, lon_weight = rim_plan(spread, blocks[slot][plan_end:])
            weights = corner_weights(lat_weight, lon_weight)
            west_lane, east_lane, row_step = lane_plan(code)
            plan = west_lane, east_lane, row_step - rim_base
            rim_results.append(interpolate(sources, plan, weights))
        for t, f, result in results:
            departed[f * inner : (f + 1) * inner, tile_at(t)] = result.astype(jnp.bfloat16)
        for t, result in zip(ts, rim_results):
            rim_departed[:, tile_at(t)] = result.astype(jnp.bfloat16)
        for t in ts if few else ():
            for at, wave in enumerate(waves):
                basis[16 * at : 16 * at + 16, tile_at(t)] = basis_tile(t, wave, lon_count)

    if not few:

        def rows_of(group, carry):
            rows = pl.ds(pl.multiple_of(group * 16, 16), 16)
            for t in range(basis.shape[1] // LANES):
                basis[rows, tile_at(t)] = basis_tile(t, waves_of(ids, group), lon_count)
            return carry

        lax.fori_loop(0, quads, rows_of, 0)
    count = departed.shape[1] // LANES
    for ts in groups_of(count, INNER_AT_ONCE):
        group_of(ts)
    spread_rows(analysis, spread_analysis, inner + EDGE, slices)
    fourier_out[...] = jnp.concatenate(
        [add_up(None, basis, values, range(count)) for values in (departed, rim_departed)], axis=1
    )


def rim_kernel(
    arrived, own, basis, inner_fourier, fourier_out, windows, plans, departed, *, slices, levs
):
    lon_count = arrived.shape[1]
    rim, fields = RIM * slices, EDGE * slices
    out_row = lax.broadcasted_iota(jnp.int32, (fields, LANES), 0) // slices
    far_step = jnp.where(out_row < RIM, 2.0 * RIM, 0.0)
    near_step = jnp.where(out_row == RIM - 1, 2.0 * RIM - 1.0, jnp.where(out_row == RIM, 1.0, -2.0))
    lane = lax.broadcasted_iota(jnp.int32, (fields, LANES), 1) - REACH
    sublane = lax.broadcasted_iota(jnp.int32, (rim, LANES), 0)

    def part(source, lanes, row_step, lat_weight, lon_weight, step):
        west, east = [lane_gather(source, lane).astype(jnp.float32) for lane in lanes]
        row_weight = jnp.where(
            row_step == step,
            1.0 - lat_weight,
            jnp.where(row_step == step - 1.0, lat_weight, 0.0),
        )
        return row_weight * (west + lon_weight * (east - west))

    def prepare(t):
        for at, side in enumerate((arrived, own)):
            block = turned(side, t, lon_count).astype(jnp.float32)
            windows[t, rim * at : rim * (at + 1), :] = block[:rim]
            plans[t, 4 * RIM * at : 4 * RIM * (at + 1), :] = block[rim:]

    def finish(t):
        row_step, shift, lat_weight, lon_weight = [
            jnp.concatenate(
                [
                    jnp.where(
                        sublane < slices,
                        *[
                            jnp.broadcast_to(plans[t, row : row + 1, :], (rim, LANES))
                            for row in (start, start + 1)
                        ],
                    )
                    for start in (RIM * at, RIM * (at + 4))
                ],
                axis=0,
            )
            for at in range(4)
        ]
        west = lane + shift.astype(jnp.int32)
        lanes = [(column & LANES - 1).astype(jnp.int16) for column in (west, west + 1)]
        plan = lanes, row_step, lat_weight, lon_weight
        far = jnp.concatenate([windows[t, rim:, :], windows[t, 0:rim, :]], axis=0)
        near = jnp.concatenate([windows[t, slices : slices + rim, :]] * 2, axis=0)
        result = part(far.astype(jnp.bfloat16), *plan, far_step)
        result += part(near.astype(jnp.bfloat16), *plan, near_step)
        departed[:, tile_at(t)] = result.astype(jnp.bfloat16)

    count = basis.shape[1] // LANES
    for t in range(count):
        prepare(t)
    total = None
    for ts in groups_of(count, RIM_AT_ONCE):
        for t in ts:
            finish(t)
        total = add_up(total, basis, departed, ts)
    fourier = jnp.concatenate([inner_fourier[...], total], axis=1)
    for at in range(fourier_out.shape[0]):
        pair = at // levs
        fourier_out[at] = fourier[4 * pair : 4 * pair + 4].astype(jnp.bfloat16)


def legendre_kernel(first_wave, coeffs, spread_analysis, out, spread_coeffs, *, levs, slices):
    members, _, rows = coeffs.shape
    bands = members // levs
    col_count = spread_analysis.shape[1]
    inner = rows // slices - 2 * EDGE
    column = lax.broadcasted_iota(jnp.int32, (1, LANES), 1)
    rim_at = column - inner * slices
    slice_of = jnp.where(rim_at < 0, column // inner, rim_at % slices)
    slice_of = jnp.where(column < rows, slice_of, -1)

    def spread(band):
        block = jnp.concatenate(
            [coeffs[band * levs + lev].astype(jnp.float32) for lev in range(levs)],
            axis=0,
        )
        block = jnp.concatenate(
            [block, jnp.zeros((block.shape[0], LANES - rows), jnp.float32)], axis=1
        )
        spread_coeffs[:, tile_at(band)] = jnp.concatenate(
            [jnp.where(slice_of == f, block, 0.0) for f in range(slices)], axis=0
        ).astype(jnp.bfloat16)

    for band in range(bands):
        spread(band)
    total = None
    for at in range(0, bands * LANES, 2 * LANES):
        part = slice(at, min(at + 2 * LANES, bands * LANES))
        product = jnp.dot(
            spread_coeffs[:, part], spread_analysis[part, :], preferred_element_type=jnp.float32
        )
        total = product if total is None else total + product
    first = first_wave[0:2, :] > 0.0
    for f in range(slices):
        for lev in range(levs):
            at = (f * levs + lev) * 4
            out[lev * slices + f] = jnp.where(first, total[at : at + 2], total[at + 2 : at + 4])


def shards(grid, dep_row, dep_col, lat_frac, lon_frac, pair_ids, analysis):
    slices, band_rows, lon_count = grid.shape
    pairs = pair_ids.shape[0]
    col_count = analysis.shape[2]
    bands, levs = lax.axis_size("lat"), lax.axis_size("lev")
    inner = band_rows - 2 * RIM
    windows = -(-lon_count // SPAN)
    held_rows = -(-band_rows // 8) * 8
    fields = slices * EDGE
    band_start = jnp.reshape(lax.axis_index("lat") * band_rows, (1,)).astype(jnp.int32)
    vmem = pl.BlockSpec(memory_space=pltpu.VMEM)
    smem = pl.BlockSpec(memory_space=pltpu.SMEM)
    params = pltpu.CompilerParams(vmem_limit_bytes=48 * 2**20)

    rows = grid.transpose(1, 0, 2).reshape(band_rows * slices, lon_count)
    rim_shape = jax.ShapeDtypeStruct((RIM * (slices + 4), lon_count), jnp.bfloat16)
    own_rim, sent_rim, plans = pl.pallas_call(
        pack_kernel,
        out_shape=(
            rim_shape,
            rim_shape,
            jax.ShapeDtypeStruct((3 * inner, lon_count), jnp.bfloat16),
        ),
        in_specs=[smem] + [vmem] * 5,
        out_specs=(vmem,) * 3,
        scratch_shapes=[pltpu.VMEM((5, 4, held_rows, LANES), jnp.float32)],
        compiler_params=params,
    )(band_start, rows, dep_row, dep_col, lat_frac, lon_frac)
    arrived_rim = lax.ppermute(sent_rim, "lat", [(i, (i + 1) % bands) for i in range(bands)])

    plans, ids = lax.optimization_barrier((plans, pair_ids))
    ids = jnp.broadcast_to(ids.astype(jnp.float32)[:, None], (pairs, LANES))
    inner_fourier, basis, spread_analysis = pl.pallas_call(
        functools.partial(inner_kernel, slices=slices),
        out_shape=(
            jax.ShapeDtypeStruct((4 * pairs, slices * band_rows), jnp.float32),
            jax.ShapeDtypeStruct((4 * pairs, windows * LANES), jnp.bfloat16),
            jax.ShapeDtypeStruct((bands * LANES, col_count), jnp.bfloat16),
        ),
        in_specs=[vmem] * 6,
        out_specs=(vmem,) * 3,
        scratch_shapes=[
            pltpu.VMEM((windows, (band_rows + 2 * RIM) * slices, LANES), jnp.float32),
            pltpu.VMEM((slices * inner, windows * LANES), jnp.bfloat16),
            pltpu.VMEM((fields, windows * LANES), jnp.bfloat16),
            pltpu.VMEM((2 * LANES, LANES), jnp.int16),
        ],
        compiler_params=params,
        cost_estimate=pl.CostEstimate(flops=100_000_000, bytes_accessed=2_000_000, transcendentals=0),
    )(rows, plans, own_rim, sent_rim, ids, analysis[0])

    held_coeffs = slices * (band_rows + EDGE)
    fourier = pl.pallas_call(
        functools.partial(rim_kernel, slices=slices, levs=levs),
        out_shape=jax.ShapeDtypeStruct((bands * levs, 4, held_coeffs), jnp.bfloat16),
        in_specs=[vmem] * 4,
        out_specs=vmem,
        scratch_shapes=[
            pltpu.VMEM((windows, fields, LANES), jnp.float32),
            pltpu.VMEM((windows, 8 * RIM, LANES), jnp.float32),
            pltpu.VMEM((fields, windows * LANES), jnp.bfloat16),
        ],
        compiler_params=params,
    )(arrived_rim, own_rim, basis, inner_fourier)
    fourier, late_ids = lax.optimization_barrier((fourier, pair_ids))
    own_id = lax.dynamic_slice_in_dim(late_ids, lax.axis_index("lat"), 1)

    columns = lax.axis_index("lev") * col_count + jnp.arange(col_count, dtype=jnp.int32)
    first_wave = jnp.where(columns < NMAX + 1 - own_id, 1.0, 0.0)
    first_wave = jnp.broadcast_to(first_wave[None, :], (8, col_count))

    coeffs = lax.all_to_all(
        fourier, ("lat", "lev"), split_axis=0, concat_axis=0, tiled=True
    )
    out = pl.pallas_call(
        functools.partial(legendre_kernel, levs=levs, slices=slices),
        out_shape=jax.ShapeDtypeStruct((levs * slices, 2, col_count), jnp.float32),
        in_specs=[vmem] * 3,
        out_specs=vmem,
        scratch_shapes=[pltpu.VMEM((4 * levs * slices, bands * LANES), jnp.bfloat16)],
        compiler_params=params,
    )(first_wave, coeffs, spread_analysis)
    return out[None]


def solution(mesh):
    return jax.shard_map(
        shards,
        mesh=mesh,
        in_specs=(
            P("lev", "lat", None),
            P("lat", None),
            P("lat", None),
            P("lat", None),
            P("lat", None),
            P(),
            P("lat", None, "lev"),
        ),
        out_specs=P("lat", None, None, "lev"),
        check_vma=False,
    )
```

```python
import functools
import math

import jax
import jax.numpy as jnp
from jax import lax
from jax.experimental import pallas as pl
from jax.experimental.pallas import tpu as pltpu
from jax.sharding import PartitionSpec as P

NMAX = 1279
LANES = 128
RIM = 2
EDGE = 2 * RIM
REACH = 8
SPAN = LANES - 2 * REACH - 1
ROW_BITS = 5
INNER_AT_ONCE = 2
RIM_AT_ONCE = 8


def lane_gather(values, indices):
    numbers = lax.GatherDimensionNumbers(
        offset_dims=(),
        collapsed_slice_dims=(1,),
        start_index_map=(1,),
        operand_batching_dims=(0,),
        start_indices_batching_dims=(0,),
    )
    return lax.gather(
        values,
        indices[..., None],
        numbers,
        (1, 1),
        mode=lax.GatherScatterMode.PROMISE_IN_BOUNDS,
    )


def tile_at(t):
    return slice(t * LANES, (t + 1) * LANES)


def cut(arrays, t, lon_count, steps):
    tiles = lon_count // LANES
    first, lane_at = divmod((t * SPAN - REACH) % lon_count, LANES)
    second = (first + 1) % tiles
    chosen = jnp.where(steps[...] == jnp.int16(lane_at), jnp.bfloat16(1), jnp.bfloat16(0))
    columns = jnp.concatenate(
        [
            jnp.concatenate([array[:, tile_at(tile)] for array in arrays], axis=0)
            for tile in (first, second)
        ],
        axis=1,
    )
    return jnp.dot(columns, chosen, preferred_element_type=jnp.float32)


def turned(array, t, lon_count):
    tiles = lon_count // LANES
    first, lane_at = divmod((t * SPAN - REACH) % lon_count, LANES)
    if lane_at == 0:
        return array[:, tile_at(first)]
    joined = array[:, tile_at(first)], array[:, tile_at((first + 1) % tiles)]
    lane = lax.broadcasted_iota(jnp.int32, joined[0].shape, 1).astype(jnp.int16)
    return pltpu.roll(jnp.where(lane >= jnp.int16(lane_at), *joined), LANES - lane_at, 1)


def fill_steps(steps):
    shape = steps.shape
    step = lax.broadcasted_iota(jnp.int32, shape, 0) - lax.broadcasted_iota(jnp.int32, shape, 1)
    steps[...] = step.astype(jnp.int16)


def lane_plan(code):
    code = code.astype(jnp.int32)
    lane = lax.broadcasted_iota(jnp.int32, code.shape, 1)
    west = lane - REACH + (code & (1 << ROW_BITS) - 1)
    west_lane = (west & (LANES - 1)).astype(jnp.int16)
    east_lane = ((west + 1) & (LANES - 1)).astype(jnp.int16)
    return west_lane, east_lane, code >> ROW_BITS


def corner_weights(lat_weight, lon_weight):
    south, north = 1.0 - lat_weight, lat_weight
    west, east = 1.0 - lon_weight, lon_weight
    return south * west, south * east, north * west, north * east


def interpolate(sources, plan, weights):
    west_lane, east_lane, row_step = plan
    row_step = row_step.astype(jnp.float32).astype(jnp.bfloat16)
    masks = [row_step == float(step) for step in range(2 * RIM - 1)]
    last = 2 * RIM - 1

    def pick(gathered):
        if len(gathered) > 2 * RIM:
            low, high = gathered[last], gathered[last + 1]
        else:
            zero = jnp.zeros_like(gathered[0])
            low = jnp.where(row_step == float(last), gathered[last], zero)
            high = jnp.where(row_step == -1.0, gathered[0], zero)
        for position in range(last - 1, -1, -1):
            low = jnp.where(masks[position], gathered[position], low)
            high = jnp.where(masks[position], gathered[position + 1], high)
        return low.astype(jnp.float32), high.astype(jnp.float32)

    west_low, west_high = pick([lane_gather(source, west_lane) for source in sources])
    east_low, east_high = pick([lane_gather(source, east_lane) for source in sources])
    departed = (
        weights[0] * west_low
        + weights[1] * east_low
        + weights[2] * west_high
        + weights[3] * east_high
    )
    return departed


def groups_of(count, at_once):
    return [range(at, min(at + at_once, count)) for at in range(0, count, at_once)]


def pack_kernel(
    place, pair_ids, grid, dep_row, dep_col, lat_frac, lon_frac, _,
    own_out, sent_out, plan_out, ids_out, first_wave_out, _blank, held, edges, *, levs,
):
    band_rows, lon_count = dep_row.shape
    inner = band_rows - 2 * RIM
    slices = grid.shape[1]
    rim = RIM * slices
    lat_at, lev_at = place[0] // levs, place[0] % levs
    first_row = lat_at * band_rows
    pairs, col_count = ids_out.shape[0], first_wave_out.shape[1]
    square = jnp.broadcast_to(pair_ids[...], (pairs, pairs)).astype(jnp.float32)
    row = lax.broadcasted_iota(jnp.int32, (pairs, pairs), 0)
    column = lax.broadcasted_iota(jnp.int32, (pairs, pairs), 1)
    ids = jnp.sum(jnp.where(row == column, square, 0.0), axis=1, keepdims=True)
    ids_out[...] = jnp.broadcast_to(ids, ids_out.shape)
    own_id = jnp.sum(jnp.where(column[:8] == lat_at, square[:8], 0.0), axis=1, keepdims=True)
    column = lax.broadcasted_iota(jnp.int32, (8, col_count), 1) + lev_at * col_count
    first_wave_out[...] = jnp.where(column.astype(jnp.float32) < NMAX + 1 - own_id, 1.0, 0.0)

    for t in range(lon_count // LANES):
        cols, slot = tile_at(t), t % 5
        row = lax.broadcasted_iota(jnp.int32, (band_rows, LANES), 0)
        lane = lax.broadcasted_iota(jnp.int32, (band_rows, LANES), 1)
        shift = dep_col[:, cols] - (lane + t * LANES)
        shift = jnp.where(shift > lon_count // 2, shift - lon_count, shift)
        shift = jnp.where(shift < -(lon_count // 2), shift + lon_count, shift)
        row_step = dep_row[:, cols] - (first_row + row) + RIM
        held[slot, 0, 0:band_rows, :] = row_step.astype(jnp.float32)
        held[slot, 1, 0:band_rows, :] = (shift + REACH).astype(jnp.float32)
        held[slot, 2, 0:band_rows, :] = lat_frac[:, cols].astype(jnp.float32)
        held[slot, 3, 0:band_rows, :] = lon_frac[:, cols].astype(jnp.float32)
        for at, row in enumerate((0, 1, band_rows - 2, band_rows - 1)):
            edges[slot, at * slices : (at + 1) * slices, :] = grid[row, :, cols].astype(jnp.float32)
        for out, grid_rows, start in (
            (own_out, edges[slot, 0:rim, :], 0),
            (sent_out, edges[slot, rim:, :], band_rows - RIM),
        ):
            out[:, cols] = jnp.concatenate(
                [grid_rows] + [held[slot, at, start : start + RIM, :] for at in range(4)], axis=0
            ).astype(jnp.bfloat16)
        middle = [held[slot, at, RIM : RIM + inner, :] for at in range(4)]
        middle = [middle[0] * (1 << ROW_BITS) + middle[1], middle[2], middle[3]]
        for at in range(3):
            plan_out[at * inner : (at + 1) * inner, cols] = middle[at].astype(jnp.bfloat16)


def waves_of(ids, group):
    pair = jnp.concatenate(
        [jnp.broadcast_to(ids[pl.ds(4 * group + at, 1), :], (4, LANES)) for at in range(4)], axis=0
    )
    row = lax.broadcasted_iota(jnp.int32, (16, LANES), 0)
    return jnp.where((row & 2) == 0, pair, NMAX + 1 - pair)


def basis_tile(t, wave, lon_count):
    lane = lax.broadcasted_iota(jnp.int32, (16, LANES), 1)
    row = lax.broadcasted_iota(jnp.int32, (16, LANES), 0)
    longitude = lane + (t * SPAN - REACH)
    quarter = jnp.where((row & 1) == 0, 0.0, float(lon_count // 4))
    steps = longitude.astype(jnp.float32) * wave + quarter
    turns = jnp.floor(steps * (1.0 / lon_count) + 0.5)
    angle = lon_count // 4 - jnp.abs(steps - turns * lon_count)
    angle = angle * (2.0 * math.pi / lon_count)
    square = angle * angle
    series = jnp.float32(-1.0 / 39916800.0)
    for term in (1.0 / 362880.0, -1.0 / 5040.0, 1.0 / 120.0, -1.0 / 6.0, 1.0):
        series = series * square + term
    taken = (lane >= REACH) & (lane < REACH + SPAN) & (longitude < lon_count)
    return jnp.where(taken, angle * series, 0.0).astype(jnp.bfloat16)


def rim_spread(slices):
    fields = EDGE * slices
    shape = (3 * fields, 2 * RIM * (slices + 4))
    wanted = lax.broadcasted_iota(jnp.int32, shape, 0)
    held = lax.broadcasted_iota(jnp.int32, shape, 1)
    kind, rim_row = wanted // fields, wanted % fields // slices
    base = rim_row // RIM * RIM * (slices + 4) + RIM * slices + rim_row % RIM
    spread = jnp.where((kind == 0) & (held == base), float(1 << ROW_BITS), 0.0)
    spread += jnp.where(held == base + RIM * (kind + 1), 1.0, 0.0)
    return spread.astype(jnp.bfloat16)


def rim_plan(spread, packed):
    plan = jnp.dot(spread, packed.astype(jnp.bfloat16), preferred_element_type=jnp.float32)
    fields = spread.shape[0] // 3
    return [plan[fields * at : fields * (at + 1)] for at in range(3)]


def spread_rows(analysis, out, band_rows, slices):
    inner = band_rows - EDGE
    rim = RIM * slices
    place = lax.broadcasted_iota(jnp.int32, (LANES, 1), 0)
    edge = place - slices * inner
    edge_row = edge // slices
    row = jnp.where(edge < 0, RIM + place % inner, edge_row)
    row = jnp.where(edge >= rim, band_rows - EDGE + edge_row, row)
    row = jnp.where(edge >= 2 * rim, edge_row - 3 * RIM, row)
    row = jnp.where(edge >= 4 * rim, -band_rows, row)
    for band in range(out.shape[0] // LANES):
        start = max(0, band * band_rows - RIM) // 16 * 16
        end = min(analysis.shape[0], -(-(band + 1) * band_rows // 16) * 16)
        column = lax.broadcasted_iota(jnp.int32, (LANES, end - start), 1) + start
        chosen = jnp.where((column - band * band_rows == row) & (row >= -RIM), 1.0, 0.0)
        out[band * LANES : (band + 1) * LANES, :] = jnp.dot(
            chosen.astype(jnp.bfloat16),
            analysis[start:end, :],
            preferred_element_type=jnp.float32,
        ).astype(jnp.bfloat16)


def add_up(total, basis, values, windows):
    cols = slice(windows[0] * LANES, (windows[-1] + 1) * LANES)
    part = lax.dot_general(
        basis[:, cols], values[:, cols], (((1,), (1,)), ((), ())), preferred_element_type=jnp.float32
    )
    return part if total is None else total + part


def inner_kernel(
    by_row, plans, own, sent, ids, analysis, _,
    fourier_out, basis, spread_analysis, windows, departed, rim_departed, steps, grid, rows, *, slices,
):
    lon_count = grid.shape[1]
    for t in range(lon_count // LANES):
        slot = t % rows.shape[0]
        for row in range(by_row.shape[0]):
            rows[slot, row * slices : (row + 1) * slices, :] = by_row[row, :, tile_at(t)].astype(
                jnp.float32
            )
        grid[:, tile_at(t)] = rows[slot].astype(jnp.bfloat16)
    inner = plans.shape[0] // 3
    rim, fields, held = RIM * slices, EDGE * slices, grid.shape[0]
    plan_end = held + 3 * inner
    spread = rim_spread(slices)
    fill_steps(steps)
    rim_base = jnp.where(lax.broadcasted_iota(jnp.int32, (fields, LANES), 0) < rim, 1, 0)
    quads = ids.shape[0] // 4
    few = quads <= 4
    waves = [waves_of(ids, at) for at in range(quads if few else 0)]

    def group_of(ts):
        blocks = [cut((grid, plans, own, sent), t, lon_count, steps) for t in ts]
        for t, block in zip(ts, blocks):
            windows[t, rim : rim + held, :] = block[:held]
        results, rim_results = [], []
        for slot, t in enumerate(ts):
            code, lat_weight, lon_weight = [
                blocks[slot][held + at * inner : held + (at + 1) * inner] for at in range(3)
            ]
            plan = lane_plan(code)
            weights = corner_weights(lat_weight, lon_weight)
            for f in range(slices):
                sources = [
                    windows[
                        t, pl.ds(rim + slices * position + f, inner, stride=slices), :
                    ].astype(jnp.bfloat16)
                    for position in range(2 * RIM + 1)
                ]
                results.append((t, f, interpolate(sources, plan, weights)))
            sources = [
                jnp.concatenate(
                    [
                        windows[t, start : start + rim, :]
                        for start in (slices * (position + 1), held - rim + slices * position)
                    ],
                    axis=0,
                ).astype(jnp.bfloat16)
                for position in range(2 * RIM)
            ]
            code, lat_weight, lon_weight = rim_plan(spread, blocks[slot][plan_end:])
            weights = corner_weights(lat_weight, lon_weight)
            west_lane, east_lane, row_step = lane_plan(code)
            plan = west_lane, east_lane, row_step - rim_base
            rim_results.append(interpolate(sources, plan, weights))
        for t, f, result in results:
            departed[f * inner : (f + 1) * inner, tile_at(t)] = result.astype(jnp.bfloat16)
        for t, result in zip(ts, rim_results):
            rim_departed[:, tile_at(t)] = result.astype(jnp.bfloat16)
        for t in ts if few else ():
            for at, wave in enumerate(waves):
                basis[16 * at : 16 * at + 16, tile_at(t)] = basis_tile(t, wave, lon_count)

    if not few:

        def rows_of(group, carry):
            rows = pl.ds(pl.multiple_of(group * 16, 16), 16)
            for t in range(basis.shape[1] // LANES):
                basis[rows, tile_at(t)] = basis_tile(t, waves_of(ids, group), lon_count)
            return carry

        lax.fori_loop(0, quads, rows_of, 0)
    count = departed.shape[1] // LANES
    for ts in groups_of(count, INNER_AT_ONCE):
        group_of(ts)
    spread_rows(analysis, spread_analysis, inner + EDGE, slices)
    fourier_out[...] = jnp.concatenate(
        [add_up(None, basis, values, range(count)) for values in (departed, rim_departed)], axis=1
    )


def rim_kernel(
    arrived, own, basis, inner_fourier, fourier_out, windows, plans, departed, *, slices, levs
):
    lon_count = arrived.shape[1]
    rim, fields = RIM * slices, EDGE * slices
    out_row = lax.broadcasted_iota(jnp.int32, (fields, LANES), 0) // slices
    far_step = jnp.where(out_row < RIM, 2.0 * RIM, 0.0)
    near_step = jnp.where(out_row == RIM - 1, 2.0 * RIM - 1.0, jnp.where(out_row == RIM, 1.0, -2.0))
    lane = lax.broadcasted_iota(jnp.int32, (fields, LANES), 1) - REACH
    sublane = lax.broadcasted_iota(jnp.int32, (rim, LANES), 0)

    def part(source, lanes, row_step, lat_weight, lon_weight, step):
        west, east = [lane_gather(source, lane).astype(jnp.float32) for lane in lanes]
        row_weight = jnp.where(
            row_step == step,
            1.0 - lat_weight,
            jnp.where(row_step == step - 1.0, lat_weight, 0.0),
        )
        return row_weight * (west + lon_weight * (east - west))

    def prepare(t):
        for at, side in enumerate((arrived, own)):
            block = turned(side, t, lon_count).astype(jnp.float32)
            windows[t, rim * at : rim * (at + 1), :] = block[:rim]
            plans[t, 4 * RIM * at : 4 * RIM * (at + 1), :] = block[rim:]

    def finish(t):
        row_step, shift, lat_weight, lon_weight = [
            jnp.concatenate(
                [
                    jnp.where(
                        sublane < slices,
                        *[
                            jnp.broadcast_to(plans[t, row : row + 1, :], (rim, LANES))
                            for row in (start, start + 1)
                        ],
                    )
                    for start in (RIM * at, RIM * (at + 4))
                ],
                axis=0,
            )
            for at in range(4)
        ]
        west = lane + shift.astype(jnp.int32)
        lanes = [(column & LANES - 1).astype(jnp.int16) for column in (west, west + 1)]
        plan = lanes, row_step, lat_weight, lon_weight
        far = jnp.concatenate([windows[t, rim:, :], windows[t, 0:rim, :]], axis=0)
        near = jnp.concatenate([windows[t, slices : slices + rim, :]] * 2, axis=0)
        result = part(far.astype(jnp.bfloat16), *plan, far_step)
        result += part(near.astype(jnp.bfloat16), *plan, near_step)
        departed[:, tile_at(t)] = result.astype(jnp.bfloat16)

    count = basis.shape[1] // LANES
    for t in range(count):
        prepare(t)
    total = None
    for ts in groups_of(count, RIM_AT_ONCE):
        for t in ts:
            finish(t)
        total = add_up(total, basis, departed, ts)
    fourier = jnp.concatenate([inner_fourier[...], total], axis=1)
    for at in range(fourier_out.shape[0]):
        pair = at // levs
        fourier_out[at] = fourier[4 * pair : 4 * pair + 4].astype(jnp.bfloat16)


def legendre_kernel(first_wave, coeffs, spread_analysis, out, spread_coeffs, *, levs, slices):
    members, _, rows = coeffs.shape
    bands = members // levs
    col_count = spread_analysis.shape[1]
    inner = rows // slices - 2 * EDGE
    column = lax.broadcasted_iota(jnp.int32, (1, LANES), 1)
    rim_at = column - inner * slices
    slice_of = jnp.where(rim_at < 0, column // inner, rim_at % slices)
    slice_of = jnp.where(column < rows, slice_of, -1)

    def spread(band):
        block = jnp.concatenate(
            [coeffs[band * levs + lev].astype(jnp.float32) for lev in range(levs)],
            axis=0,
        )
        block = jnp.concatenate(
            [block, jnp.zeros((block.shape[0], LANES - rows), jnp.float32)], axis=1
        )
        spread_coeffs[:, tile_at(band)] = jnp.concatenate(
            [jnp.where(slice_of == f, block, 0.0) for f in range(slices)], axis=0
        ).astype(jnp.bfloat16)

    for band in range(bands):
        spread(band)
    total = None
    for at in range(0, bands * LANES, 2 * LANES):
        part = slice(at, min(at + 2 * LANES, bands * LANES))
        product = jnp.dot(
            spread_coeffs[:, part], spread_analysis[part, :], preferred_element_type=jnp.float32
        )
        total = product if total is None else total + product
    first = first_wave[0:2, :] > 0.0
    for f in range(slices):
        for lev in range(levs):
            at = (f * levs + lev) * 4
            out[lev * slices + f] = jnp.where(first, total[at : at + 2], total[at + 2 : at + 4])


def shards(grid, dep_row, dep_col, lat_frac, lon_frac, pair_ids, analysis):
    slices, band_rows, lon_count = grid.shape
    pairs = pair_ids.shape[0]
    col_count = analysis.shape[2]
    bands, levs = lax.axis_size("lat"), lax.axis_size("lev")
    inner = band_rows - 2 * RIM
    windows = -(-lon_count // SPAN)
    held_rows = -(-band_rows // 8) * 8
    fields = slices * EDGE
    place = jnp.reshape(lax.axis_index(("lat", "lev")), (1,)).astype(jnp.int32)
    vmem = pl.BlockSpec(memory_space=pltpu.VMEM)
    smem = pl.BlockSpec(memory_space=pltpu.SMEM)
    params = pltpu.CompilerParams(vmem_limit_bytes=48 * 2**20)

    blank = jnp.zeros((windows, (band_rows + 2 * RIM) * slices, LANES), jnp.float32)
    by_row = grid.transpose(1, 0, 2)
    rim_shape = jax.ShapeDtypeStruct((RIM * (slices + 4), lon_count), jnp.bfloat16)
    own_rim, sent_rim, plans, ids, first_wave, blank = pl.pallas_call(
        functools.partial(pack_kernel, levs=levs),
        out_shape=(
            rim_shape,
            rim_shape,
            jax.ShapeDtypeStruct((3 * inner, lon_count), jnp.bfloat16),
            jax.ShapeDtypeStruct((pairs, LANES), jnp.float32),
            jax.ShapeDtypeStruct((8, col_count), jnp.float32),
            jax.ShapeDtypeStruct(blank.shape, jnp.float32),
        ),
        in_specs=[smem] + [vmem] * 7,
        out_specs=(vmem,) * 6,
        input_output_aliases={7: 5},
        scratch_shapes=[
            pltpu.VMEM((5, 4, held_rows, LANES), jnp.float32),
            pltpu.VMEM((5, 2 * RIM * slices, LANES), jnp.float32),
        ],
        compiler_params=params,
    )(place, pair_ids[None, :], by_row, dep_row, dep_col, lat_frac, lon_frac, blank)
    arrived_rim = lax.ppermute(sent_rim, "lat", [(i, (i + 1) % bands) for i in range(bands)])

    inner_fourier, basis, spread_analysis, _ = pl.pallas_call(
        functools.partial(inner_kernel, slices=slices),
        out_shape=(
            jax.ShapeDtypeStruct((4 * pairs, slices * band_rows), jnp.float32),
            jax.ShapeDtypeStruct((4 * pairs, windows * LANES), jnp.bfloat16),
            jax.ShapeDtypeStruct((bands * LANES, col_count), jnp.bfloat16),
            jax.ShapeDtypeStruct(blank.shape, jnp.float32),
        ),
        in_specs=[vmem] * 7,
        out_specs=(vmem,) * 4,
        input_output_aliases={6: 3},
        scratch_shapes=[
            pltpu.VMEM((slices * inner, windows * LANES), jnp.bfloat16),
            pltpu.VMEM((fields, windows * LANES), jnp.bfloat16),
            pltpu.VMEM((2 * LANES, LANES), jnp.int16),
            pltpu.VMEM((band_rows * slices, lon_count), jnp.bfloat16),
            pltpu.VMEM((5, band_rows * slices, LANES), jnp.float32),
        ],
        compiler_params=params,
        cost_estimate=pl.CostEstimate(flops=100_000_000, bytes_accessed=2_000_000, transcendentals=0),
    )(by_row, plans, own_rim, sent_rim, ids, analysis[0], blank)

    held_coeffs = slices * (band_rows + EDGE)
    fourier = pl.pallas_call(
        functools.partial(rim_kernel, slices=slices, levs=levs),
        out_shape=jax.ShapeDtypeStruct((bands * levs, 4, held_coeffs), jnp.bfloat16),
        in_specs=[vmem] * 4,
        out_specs=vmem,
        scratch_shapes=[
            pltpu.VMEM((windows, fields, LANES), jnp.float32),
            pltpu.VMEM((windows, 8 * RIM, LANES), jnp.float32),
            pltpu.VMEM((fields, windows * LANES), jnp.bfloat16),
        ],
        compiler_params=params,
    )(arrived_rim, own_rim, basis, inner_fourier)
    coeffs = lax.all_to_all(
        fourier, ("lat", "lev"), split_axis=0, concat_axis=0, tiled=True
    )
    out = pl.pallas_call(
        functools.partial(legendre_kernel, levs=levs, slices=slices),
        out_shape=jax.ShapeDtypeStruct((levs * slices, 2, col_count), jnp.float32),
        in_specs=[vmem] * 3,
        out_specs=vmem,
        scratch_shapes=[pltpu.VMEM((4 * levs * slices, bands * LANES), jnp.bfloat16)],
        compiler_params=params,
    )(first_wave, coeffs, spread_analysis)
    return out[None]


def solution(mesh):
    return jax.shard_map(
        shards,
        mesh=mesh,
        in_specs=(
            P("lev", "lat", None),
            P("lat", None),
            P("lat", None),
            P("lat", None),
            P("lat", None),
            P(),
            P("lat", None, "lev"),
        ),
        out_specs=P("lat", None, None, "lev"),
        check_vma=False,
    )
```

```python
import functools
import math

import jax
import jax.numpy as jnp
from jax import lax
from jax.experimental import pallas as pl
from jax.experimental.pallas import tpu as pltpu
from jax.sharding import PartitionSpec as P

NMAX = 1279
LANES = 128
RIM = 2
EDGE = 2 * RIM
REACH = 8
SPAN = LANES - 2 * REACH - 1
ROW_BITS = 5
INNER_AT_ONCE = 2
RIM_AT_ONCE = 8


def lane_gather(values, indices):
    numbers = lax.GatherDimensionNumbers(
        offset_dims=(),
        collapsed_slice_dims=(1,),
        start_index_map=(1,),
        operand_batching_dims=(0,),
        start_indices_batching_dims=(0,),
    )
    return lax.gather(
        values,
        indices[..., None],
        numbers,
        (1, 1),
        mode=lax.GatherScatterMode.PROMISE_IN_BOUNDS,
    )


def tile_at(t):
    return slice(t * LANES, (t + 1) * LANES)


def cut(arrays, t, lon_count, steps):
    tiles = lon_count // LANES
    first, lane_at = divmod((t * SPAN - REACH) % lon_count, LANES)
    second = (first + 1) % tiles
    chosen = jnp.where(steps[...] == jnp.int16(lane_at), jnp.bfloat16(1), jnp.bfloat16(0))
    columns = jnp.concatenate(
        [
            jnp.concatenate([array[:, tile_at(tile)] for array in arrays], axis=0)
            for tile in (first, second)
        ],
        axis=1,
    )
    return jnp.dot(columns, chosen, preferred_element_type=jnp.float32)


def turned(array, t, lon_count):
    tiles = lon_count // LANES
    first, lane_at = divmod((t * SPAN - REACH) % lon_count, LANES)
    if lane_at == 0:
        return array[:, tile_at(first)]
    joined = array[:, tile_at(first)], array[:, tile_at((first + 1) % tiles)]
    lane = lax.broadcasted_iota(jnp.int32, joined[0].shape, 1).astype(jnp.int16)
    return pltpu.roll(jnp.where(lane >= jnp.int16(lane_at), *joined), LANES - lane_at, 1)


def fill_steps(steps):
    shape = steps.shape
    step = lax.broadcasted_iota(jnp.int32, shape, 0) - lax.broadcasted_iota(jnp.int32, shape, 1)
    steps[...] = step.astype(jnp.int16)


def lane_plan(code):
    code = code.astype(jnp.int32)
    lane = lax.broadcasted_iota(jnp.int32, code.shape, 1)
    west = lane - REACH + (code & (1 << ROW_BITS) - 1)
    west_lane = (west & (LANES - 1)).astype(jnp.int16)
    east_lane = ((west + 1) & (LANES - 1)).astype(jnp.int16)
    return west_lane, east_lane, code >> ROW_BITS


def corner_weights(lat_weight, lon_weight):
    south, north = 1.0 - lat_weight, lat_weight
    west, east = 1.0 - lon_weight, lon_weight
    return south * west, south * east, north * west, north * east


def interpolate(sources, plan, weights):
    west_lane, east_lane, row_step = plan
    row_step = row_step.astype(jnp.float32).astype(jnp.bfloat16)
    masks = [row_step == float(step) for step in range(2 * RIM - 1)]
    last = 2 * RIM - 1

    def pick(gathered):
        if len(gathered) > 2 * RIM:
            low, high = gathered[last], gathered[last + 1]
        else:
            zero = jnp.zeros_like(gathered[0])
            low = jnp.where(row_step == float(last), gathered[last], zero)
            high = jnp.where(row_step == -1.0, gathered[0], zero)
        for position in range(last - 1, -1, -1):
            low = jnp.where(masks[position], gathered[position], low)
            high = jnp.where(masks[position], gathered[position + 1], high)
        return low.astype(jnp.float32), high.astype(jnp.float32)

    west_low, west_high = pick([lane_gather(source, west_lane) for source in sources])
    east_low, east_high = pick([lane_gather(source, east_lane) for source in sources])
    departed = (
        weights[0] * west_low
        + weights[1] * east_low
        + weights[2] * west_high
        + weights[3] * east_high
    )
    return departed


def groups_of(count, at_once):
    return [range(at, min(at + at_once, count)) for at in range(0, count, at_once)]


def departures(rows, t, first_row, dep_row, dep_col, lat_frac, lon_frac):
    lon_count = dep_row.shape[1]
    cols, shape = tile_at(t), (rows.stop - rows.start, LANES)
    row = lax.broadcasted_iota(jnp.int32, shape, 0) + rows.start
    lane = lax.broadcasted_iota(jnp.int32, shape, 1)
    shift = dep_col[rows, cols] - (lane + t * LANES)
    shift = jnp.where(shift > lon_count // 2, shift - lon_count, shift)
    shift = jnp.where(shift < -(lon_count // 2), shift + lon_count, shift)
    row_step = dep_row[rows, cols] - (first_row + row) + RIM
    fracs = [frac[:, cols].astype(jnp.float32)[rows] for frac in (lat_frac, lon_frac)]
    return [row_step.astype(jnp.float32), (shift + REACH).astype(jnp.float32)] + fracs


def pack_kernel(
    place, dep_row, dep_col, lat_frac, lon_frac, last_rows, _,
    sent_out, place_out, _blank, held, *, levs,
):
    band_rows, lon_count = dep_row.shape
    slices = last_rows.shape[1]
    rim = RIM * slices
    place_out[...] = jnp.full(place_out.shape, place[0], jnp.int32)
    first_row = place[0] // levs * band_rows
    start = band_rows // 8 * 8
    skip = band_rows - RIM - start
    for t in range(lon_count // LANES):
        cols = tile_at(t)
        for row in range(RIM):
            held[t, row * slices : (row + 1) * slices, :] = last_rows[row, :, cols].astype(
                jnp.float32
            )
        parts = departures(
            slice(start, band_rows), t, first_row, dep_row, dep_col, lat_frac, lon_frac
        )
        for at, part in enumerate(parts):
            held[t, rim + RIM * at : rim + RIM * (at + 1), :] = part[skip:]
        sent_out[:, cols] = held[t].astype(jnp.bfloat16)


def waves_of(ids, group):
    pair = jnp.concatenate(
        [jnp.broadcast_to(ids[4 * group + at : 4 * group + at + 1], (4, LANES)) for at in range(4)],
        axis=0,
    )
    row = lax.broadcasted_iota(jnp.int32, (16, LANES), 0)
    return jnp.where((row & 2) == 0, pair, NMAX + 1 - pair)


def basis_tile(t, wave, lon_count):
    lane = lax.broadcasted_iota(jnp.int32, (16, LANES), 1)
    row = lax.broadcasted_iota(jnp.int32, (16, LANES), 0)
    longitude = lane + (t * SPAN - REACH)
    quarter = jnp.where((row & 1) == 0, 0.0, float(lon_count // 4))
    steps = longitude.astype(jnp.float32) * wave + quarter
    turns = jnp.floor(steps * (1.0 / lon_count) + 0.5)
    angle = lon_count // 4 - jnp.abs(steps - turns * lon_count)
    angle = angle * (2.0 * math.pi / lon_count)
    square = angle * angle
    series = jnp.float32(-1.0 / 39916800.0)
    for term in (1.0 / 362880.0, -1.0 / 5040.0, 1.0 / 120.0, -1.0 / 6.0, 1.0):
        series = series * square + term
    taken = (lane >= REACH) & (lane < REACH + SPAN) & (longitude < lon_count)
    return jnp.where(taken, angle * series, 0.0).astype(jnp.bfloat16)


def rim_spread(slices):
    fields = EDGE * slices
    shape = (3 * fields, 2 * RIM * (slices + 4))
    wanted = lax.broadcasted_iota(jnp.int32, shape, 0)
    held = lax.broadcasted_iota(jnp.int32, shape, 1)
    kind, rim_row = wanted // fields, wanted % fields // slices
    base = rim_row // RIM * RIM * (slices + 4) + RIM * slices + rim_row % RIM
    spread = jnp.where((kind == 0) & (held == base), float(1 << ROW_BITS), 0.0)
    spread += jnp.where(held == base + RIM * (kind + 1), 1.0, 0.0)
    return spread.astype(jnp.bfloat16)


def rim_plan(spread, packed):
    plan = jnp.dot(spread, packed.astype(jnp.bfloat16), preferred_element_type=jnp.float32)
    fields = spread.shape[0] // 3
    return [plan[fields * at : fields * (at + 1)] for at in range(3)]


def spread_rows(analysis, out, band_rows, slices):
    inner = band_rows - EDGE
    rim = RIM * slices
    place = lax.broadcasted_iota(jnp.int32, (LANES, 1), 0)
    edge = place - slices * inner
    edge_row = edge // slices
    row = jnp.where(edge < 0, RIM + place % inner, edge_row)
    row = jnp.where(edge >= rim, band_rows - EDGE + edge_row, row)
    row = jnp.where(edge >= 2 * rim, edge_row - 3 * RIM, row)
    row = jnp.where(edge >= 4 * rim, -band_rows, row)
    for band in range(out.shape[0] // LANES):
        start = max(0, band * band_rows - RIM) // 16 * 16
        end = min(analysis.shape[0], -(-(band + 1) * band_rows // 16) * 16)
        column = lax.broadcasted_iota(jnp.int32, (LANES, end - start), 1) + start
        chosen = jnp.where((column - band * band_rows == row) & (row >= -RIM), 1.0, 0.0)
        out[band * LANES : (band + 1) * LANES, :] = jnp.dot(
            chosen.astype(jnp.bfloat16),
            analysis[start:end, :],
            preferred_element_type=jnp.float32,
        ).astype(jnp.bfloat16)


def add_up(total, basis, values, windows):
    cols = slice(windows[0] * LANES, (windows[-1] + 1) * LANES)
    part = lax.dot_general(
        basis[:, cols], values[:, cols], (((1,), (1,)), ((), ())), preferred_element_type=jnp.float32
    )
    return part if total is None else total + part


def inner_kernel(
    by_row, dep_row, dep_col, lat_frac, lon_frac, sent, place, pair_ids, analysis, _,
    fourier_out, basis, spread_analysis, own, first_wave_out, windows,
    departed, rim_departed, steps, grid, rows, parts, plans, *, slices, levs,
):
    band_rows, lon_count = dep_row.shape
    inner = band_rows - 2 * RIM
    rim, fields, held = RIM * slices, EDGE * slices, band_rows * slices

    place = place[0:1, :]
    lat_at, lev_at = place // levs, place % levs
    first_row = lat_at * band_rows
    for t in range(lon_count // LANES):
        cols, slot = tile_at(t), t % rows.shape[0]
        for row in range(band_rows):
            rows[slot, row * slices : (row + 1) * slices, :] = by_row[row, :, cols].astype(
                jnp.float32
            )
        grid[:, cols] = rows[slot].astype(jnp.bfloat16)
        data = departures(
            slice(0, band_rows), t, first_row, dep_row, dep_col, lat_frac, lon_frac
        )
        for at, part in enumerate([data[0] * (1 << ROW_BITS) + data[1]] + data[2:]):
            parts[slot, at, 0:band_rows, :] = part
            plans[at * inner : (at + 1) * inner, cols] = parts[
                slot, at, RIM : RIM + inner, :
            ].astype(jnp.bfloat16)
        own[:, cols] = jnp.concatenate(
            [rows[slot, 0:rim, :]] + [part[0:RIM] for part in data], axis=0
        ).astype(jnp.bfloat16)

    pairs, col_count = pair_ids.shape[1], first_wave_out.shape[1]
    square = jnp.broadcast_to(pair_ids[...], (pairs, pairs)).astype(jnp.float32)
    row = lax.broadcasted_iota(jnp.int32, (pairs, pairs), 0)
    column = lax.broadcasted_iota(jnp.int32, (pairs, pairs), 1)
    ids = jnp.sum(jnp.where(row == column, square, 0.0), axis=1, keepdims=True)
    ids = jnp.broadcast_to(ids, (pairs, LANES))
    own_id = jnp.sum(
        jnp.where(column[:8] == lat_at[0:1, 0:1], square[:8], 0.0), axis=1, keepdims=True
    )
    column = lax.broadcasted_iota(jnp.int32, (8, col_count), 1) + lev_at[0:1, 0:1] * col_count
    first_wave_out[...] = jnp.where(column.astype(jnp.float32) < NMAX + 1 - own_id, 1.0, 0.0)
    plan_end = held + 3 * inner
    spread = rim_spread(slices)
    fill_steps(steps)
    rim_base = jnp.where(lax.broadcasted_iota(jnp.int32, (fields, LANES), 0) < rim, 1, 0)
    quads = ids.shape[0] // 4
    few = quads <= 4
    waves = [waves_of(ids, at) for at in range(quads if few else 0)]

    def group_of(ts):
        blocks = [cut((grid, plans, own, sent), t, lon_count, steps) for t in ts]
        for t, block in zip(ts, blocks):
            windows[t, rim : rim + held, :] = block[:held]
        results, rim_results = [], []
        for slot, t in enumerate(ts):
            code, lat_weight, lon_weight = [
                blocks[slot][held + at * inner : held + (at + 1) * inner] for at in range(3)
            ]
            plan = lane_plan(code)
            weights = corner_weights(lat_weight, lon_weight)
            for f in range(slices):
                sources = [
                    windows[
                        t, pl.ds(rim + slices * position + f, inner, stride=slices), :
                    ].astype(jnp.bfloat16)
                    for position in range(2 * RIM + 1)
                ]
                results.append((t, f, interpolate(sources, plan, weights)))
            sources = [
                jnp.concatenate(
                    [
                        windows[t, start : start + rim, :]
                        for start in (slices * (position + 1), held - rim + slices * position)
                    ],
                    axis=0,
                ).astype(jnp.bfloat16)
                for position in range(2 * RIM)
            ]
            code, lat_weight, lon_weight = rim_plan(spread, blocks[slot][plan_end:])
            weights = corner_weights(lat_weight, lon_weight)
            west_lane, east_lane, row_step = lane_plan(code)
            plan = west_lane, east_lane, row_step - rim_base
            rim_results.append(interpolate(sources, plan, weights))
        for t, f, result in results:
            departed[f * inner : (f + 1) * inner, tile_at(t)] = result.astype(jnp.bfloat16)
        for t, result in zip(ts, rim_results):
            rim_departed[:, tile_at(t)] = result.astype(jnp.bfloat16)
        for t in ts if few else ():
            for at, wave in enumerate(waves):
                basis[16 * at : 16 * at + 16, tile_at(t)] = basis_tile(t, wave, lon_count)

    if not few:

        for group in range(quads):
            wave = waves_of(ids, group)
            for t in range(basis.shape[1] // LANES):
                basis[16 * group : 16 * group + 16, tile_at(t)] = basis_tile(t, wave, lon_count)
    count = departed.shape[1] // LANES
    for ts in groups_of(count, INNER_AT_ONCE):
        group_of(ts)
    spread_rows(analysis, spread_analysis, inner + EDGE, slices)
    fourier_out[...] = jnp.concatenate(
        [add_up(None, basis, values, range(count)) for values in (departed, rim_departed)], axis=1
    )


def rim_kernel(
    arrived, own, basis, inner_fourier, fourier_out, windows, plans, departed, *, slices, levs
):
    lon_count = arrived.shape[1]
    rim, fields = RIM * slices, EDGE * slices
    out_row = lax.broadcasted_iota(jnp.int32, (fields, LANES), 0) // slices
    far_step = jnp.where(out_row < RIM, 2.0 * RIM, 0.0)
    near_step = jnp.where(out_row == RIM - 1, 2.0 * RIM - 1.0, jnp.where(out_row == RIM, 1.0, -2.0))
    lane = lax.broadcasted_iota(jnp.int32, (fields, LANES), 1) - REACH
    sublane = lax.broadcasted_iota(jnp.int32, (rim, LANES), 0)

    def part(source, lanes, row_step, lat_weight, lon_weight, step):
        west, east = [lane_gather(source, lane).astype(jnp.float32) for lane in lanes]
        row_weight = jnp.where(
            row_step == step,
            1.0 - lat_weight,
            jnp.where(row_step == step - 1.0, lat_weight, 0.0),
        )
        return row_weight * (west + lon_weight * (east - west))

    def prepare(t):
        for at, side in enumerate((arrived, own)):
            block = turned(side, t, lon_count).astype(jnp.float32)
            windows[t, rim * at : rim * (at + 1), :] = block[:rim]
            plans[t, 4 * RIM * at : 4 * RIM * (at + 1), :] = block[rim:]

    def finish(t):
        row_step, shift, lat_weight, lon_weight = [
            jnp.concatenate(
                [
                    jnp.where(
                        sublane < slices,
                        *[
                            jnp.broadcast_to(plans[t, row : row + 1, :], (rim, LANES))
                            for row in (start, start + 1)
                        ],
                    )
                    for start in (RIM * at, RIM * (at + 4))
                ],
                axis=0,
            )
            for at in range(4)
        ]
        west = lane + shift.astype(jnp.int32)
        lanes = [(column & LANES - 1).astype(jnp.int16) for column in (west, west + 1)]
        plan = lanes, row_step, lat_weight, lon_weight
        far = jnp.concatenate([windows[t, rim:, :], windows[t, 0:rim, :]], axis=0)
        near = jnp.concatenate([windows[t, slices : slices + rim, :]] * 2, axis=0)
        result = part(far.astype(jnp.bfloat16), *plan, far_step)
        result += part(near.astype(jnp.bfloat16), *plan, near_step)
        departed[:, tile_at(t)] = result.astype(jnp.bfloat16)

    count = basis.shape[1] // LANES
    for t in range(count):
        prepare(t)
    total = None
    for ts in groups_of(count, RIM_AT_ONCE):
        for t in ts:
            finish(t)
        total = add_up(total, basis, departed, ts)
    fourier = jnp.concatenate([inner_fourier[...], total], axis=1)
    for at in range(fourier_out.shape[0]):
        pair = at // levs
        fourier_out[at] = fourier[4 * pair : 4 * pair + 4].astype(jnp.bfloat16)


def legendre_kernel(first_wave, coeffs, spread_analysis, out, spread_coeffs, *, levs, slices):
    members, _, rows = coeffs.shape
    bands = members // levs
    col_count = spread_analysis.shape[1]
    inner = rows // slices - 2 * EDGE
    column = lax.broadcasted_iota(jnp.int32, (1, LANES), 1)
    rim_at = column - inner * slices
    slice_of = jnp.where(rim_at < 0, column // inner, rim_at % slices)
    slice_of = jnp.where(column < rows, slice_of, -1)

    def spread(band):
        block = jnp.concatenate(
            [coeffs[band * levs + lev].astype(jnp.float32) for lev in range(levs)],
            axis=0,
        )
        block = jnp.concatenate(
            [block, jnp.zeros((block.shape[0], LANES - rows), jnp.float32)], axis=1
        )
        spread_coeffs[:, tile_at(band)] = jnp.concatenate(
            [jnp.where(slice_of == f, block, 0.0) for f in range(slices)], axis=0
        ).astype(jnp.bfloat16)

    for band in range(bands):
        spread(band)
    total = None
    for at in range(0, bands * LANES, 2 * LANES):
        part = slice(at, min(at + 2 * LANES, bands * LANES))
        product = jnp.dot(
            spread_coeffs[:, part], spread_analysis[part, :], preferred_element_type=jnp.float32
        )
        total = product if total is None else total + product
    first = first_wave[0:2, :] > 0.0
    for f in range(slices):
        for lev in range(levs):
            at = (f * levs + lev) * 4
            out[lev * slices + f] = jnp.where(first, total[at : at + 2], total[at + 2 : at + 4])


def shards(grid, dep_row, dep_col, lat_frac, lon_frac, pair_ids, analysis):
    slices, band_rows, lon_count = grid.shape
    pairs = pair_ids.shape[0]
    col_count = analysis.shape[2]
    bands, levs = lax.axis_size("lat"), lax.axis_size("lev")
    inner = band_rows - 2 * RIM
    windows = -(-lon_count // SPAN)
    held_rows = -(-band_rows // 8) * 8
    fields = slices * EDGE
    place = jnp.reshape(lax.axis_index(("lat", "lev")), (1,)).astype(jnp.int32)
    vmem = pl.BlockSpec(memory_space=pltpu.VMEM)
    smem = pl.BlockSpec(memory_space=pltpu.SMEM)
    params = pltpu.CompilerParams(vmem_limit_bytes=48 * 2**20)

    blank = jnp.zeros((windows, (band_rows + 2 * RIM) * slices, LANES), jnp.float32)
    by_row = grid.transpose(1, 0, 2)
    rim_shape = jax.ShapeDtypeStruct((RIM * (slices + 4), lon_count), jnp.bfloat16)
    sent_rim, wide_place, blank = pl.pallas_call(
        functools.partial(pack_kernel, levs=levs),
        out_shape=(
            rim_shape,
            jax.ShapeDtypeStruct((8, LANES), jnp.int32),
            jax.ShapeDtypeStruct(blank.shape, jnp.float32),
        ),
        in_specs=[smem] + [vmem] * 6,
        out_specs=(vmem,) * 3,
        input_output_aliases={6: 2},
        scratch_shapes=[
            pltpu.VMEM((lon_count // LANES, RIM * (slices + 4), LANES), jnp.float32)
        ],
        compiler_params=params,
    )(place, dep_row, dep_col, lat_frac, lon_frac, by_row[band_rows - RIM :], blank)
    arrived_rim = lax.ppermute(sent_rim, "lat", [(i, (i + 1) % bands) for i in range(bands)])

    inner_fourier, basis, spread_analysis, own_rim, first_wave, _ = pl.pallas_call(
        functools.partial(inner_kernel, slices=slices, levs=levs),
        out_shape=(
            jax.ShapeDtypeStruct((4 * pairs, slices * band_rows), jnp.float32),
            jax.ShapeDtypeStruct((4 * pairs, windows * LANES), jnp.bfloat16),
            jax.ShapeDtypeStruct((bands * LANES, col_count), jnp.bfloat16),
            rim_shape,
            jax.ShapeDtypeStruct((8, col_count), jnp.float32),
            jax.ShapeDtypeStruct(blank.shape, jnp.float32),
        ),
        in_specs=[vmem] * 10,
        out_specs=(vmem,) * 6,
        input_output_aliases={9: 5},
        scratch_shapes=[
            pltpu.VMEM((slices * inner, windows * LANES), jnp.bfloat16),
            pltpu.VMEM((fields, windows * LANES), jnp.bfloat16),
            pltpu.VMEM((2 * LANES, LANES), jnp.int16),
            pltpu.VMEM((band_rows * slices, lon_count), jnp.bfloat16),
            pltpu.VMEM((5, band_rows * slices, LANES), jnp.float32),
            pltpu.VMEM((5, 3, held_rows, LANES), jnp.float32),
            pltpu.VMEM((3 * inner, lon_count), jnp.bfloat16),
        ],
        compiler_params=params,
        cost_estimate=pl.CostEstimate(flops=100_000_000, bytes_accessed=2_000_000, transcendentals=0),
    )(
        by_row, dep_row, dep_col, lat_frac, lon_frac, sent_rim, wide_place, pair_ids[None, :],
        analysis[0], blank,
    )

    held_coeffs = slices * (band_rows + EDGE)
    fourier = pl.pallas_call(
        functools.partial(rim_kernel, slices=slices, levs=levs),
        out_shape=jax.ShapeDtypeStruct((bands * levs, 4, held_coeffs), jnp.bfloat16),
        in_specs=[vmem] * 4,
        out_specs=vmem,
        scratch_shapes=[
            pltpu.VMEM((windows, fields, LANES), jnp.float32),
            pltpu.VMEM((windows, 8 * RIM, LANES), jnp.float32),
            pltpu.VMEM((fields, windows * LANES), jnp.bfloat16),
        ],
        compiler_params=params,
    )(arrived_rim, own_rim, basis, inner_fourier)
    coeffs = lax.all_to_all(
        fourier, ("lat", "lev"), split_axis=0, concat_axis=0, tiled=True
    )
    out = pl.pallas_call(
        functools.partial(legendre_kernel, levs=levs, slices=slices),
        out_shape=jax.ShapeDtypeStruct((levs * slices, 2, col_count), jnp.float32),
        in_specs=[vmem] * 3,
        out_specs=vmem,
        scratch_shapes=[pltpu.VMEM((4 * levs * slices, bands * LANES), jnp.bfloat16)],
        compiler_params=params,
    )(first_wave, coeffs, spread_analysis)
    return out[None]


def solution(mesh):
    return jax.shard_map(
        shards,
        mesh=mesh,
        in_specs=(
            P("lev", "lat", None),
            P("lat", None),
            P("lat", None),
            P("lat", None),
            P("lat", None),
            P(),
            P("lat", None, "lev"),
        ),
        out_specs=P("lat", None, None, "lev"),
        check_vma=False,
    )
```

```python
import functools
import math

import jax
import jax.numpy as jnp
from jax import lax
from jax.experimental import pallas as pl
from jax.experimental.pallas import tpu as pltpu
from jax.sharding import PartitionSpec as P

NMAX = 1279
LANES = 128
RIM = 2
EDGE = 2 * RIM
REACH = 8
SPAN = LANES - 2 * REACH - 1
ROW_BITS = 5
INNER_AT_ONCE = 2
RIM_AT_ONCE = 8


def lane_gather(values, indices):
    numbers = lax.GatherDimensionNumbers(
        offset_dims=(),
        collapsed_slice_dims=(1,),
        start_index_map=(1,),
        operand_batching_dims=(0,),
        start_indices_batching_dims=(0,),
    )
    return lax.gather(
        values,
        indices[..., None],
        numbers,
        (1, 1),
        mode=lax.GatherScatterMode.PROMISE_IN_BOUNDS,
    )


def tile_at(t):
    return slice(t * LANES, (t + 1) * LANES)


def cut(arrays, t, lon_count, steps):
    tiles = lon_count // LANES
    first, lane_at = divmod((t * SPAN - REACH) % lon_count, LANES)
    second = (first + 1) % tiles
    chosen = jnp.where(steps[...] == jnp.int16(lane_at), jnp.bfloat16(1), jnp.bfloat16(0))
    columns = jnp.concatenate(
        [
            jnp.concatenate([array[:, tile_at(tile)] for array in arrays], axis=0)
            for tile in (first, second)
        ],
        axis=1,
    )
    return jnp.dot(columns, chosen, preferred_element_type=jnp.float32)


def turned(array, t, lon_count):
    tiles = lon_count // LANES
    first, lane_at = divmod((t * SPAN - REACH) % lon_count, LANES)
    if lane_at == 0:
        return array[:, tile_at(first)]
    joined = array[:, tile_at(first)], array[:, tile_at((first + 1) % tiles)]
    lane = lax.broadcasted_iota(jnp.int32, joined[0].shape, 1).astype(jnp.int16)
    return pltpu.roll(jnp.where(lane >= jnp.int16(lane_at), *joined), LANES - lane_at, 1)


def fill_steps(steps):
    shape = steps.shape
    step = lax.broadcasted_iota(jnp.int32, shape, 0) - lax.broadcasted_iota(jnp.int32, shape, 1)
    steps[...] = step.astype(jnp.int16)


def lane_plan(code):
    code = code.astype(jnp.int32)
    lane = lax.broadcasted_iota(jnp.int32, code.shape, 1)
    west = lane - REACH + (code & (1 << ROW_BITS) - 1)
    west_lane = (west & (LANES - 1)).astype(jnp.int16)
    east_lane = ((west + 1) & (LANES - 1)).astype(jnp.int16)
    return west_lane, east_lane, code >> ROW_BITS


def corner_weights(lat_weight, lon_weight):
    south, north = 1.0 - lat_weight, lat_weight
    west, east = 1.0 - lon_weight, lon_weight
    return south * west, south * east, north * west, north * east


def interpolate(sources, plan, weights):
    west_lane, east_lane, row_step = plan
    row_step = row_step.astype(jnp.float32).astype(jnp.bfloat16)
    masks = [row_step == float(step) for step in range(2 * RIM - 1)]
    last = 2 * RIM - 1

    def pick(gathered):
        if len(gathered) > 2 * RIM:
            low, high = gathered[last], gathered[last + 1]
        else:
            zero = jnp.zeros_like(gathered[0])
            low = jnp.where(row_step == float(last), gathered[last], zero)
            high = jnp.where(row_step == -1.0, gathered[0], zero)
        for position in range(last - 1, -1, -1):
            low = jnp.where(masks[position], gathered[position], low)
            high = jnp.where(masks[position], gathered[position + 1], high)
        return low.astype(jnp.float32), high.astype(jnp.float32)

    west_low, west_high = pick([lane_gather(source, west_lane) for source in sources])
    east_low, east_high = pick([lane_gather(source, east_lane) for source in sources])
    departed = (
        weights[0] * west_low
        + weights[1] * east_low
        + weights[2] * west_high
        + weights[3] * east_high
    )
    return departed


def groups_of(count, at_once):
    return [range(at, min(at + at_once, count)) for at in range(0, count, at_once)]


def departures(rows, t, first_row, dep_row, dep_col, lat_frac, lon_frac):
    lon_count = dep_row.shape[1]
    cols, shape = tile_at(t), (rows.stop - rows.start, LANES)
    row = lax.broadcasted_iota(jnp.int32, shape, 0) + rows.start
    lane = lax.broadcasted_iota(jnp.int32, shape, 1)
    shift = dep_col[rows, cols] - (lane + t * LANES)
    shift = jnp.where(shift > lon_count // 2, shift - lon_count, shift)
    shift = jnp.where(shift < -(lon_count // 2), shift + lon_count, shift)
    row_step = dep_row[rows, cols] - (first_row + row) + RIM
    fracs = [frac[:, cols].astype(jnp.float32)[rows] for frac in (lat_frac, lon_frac)]
    return [row_step.astype(jnp.float32), (shift + REACH).astype(jnp.float32)] + fracs


def pack_kernel(
    place, dep_row, dep_col, lat_frac, lon_frac, last_rows, _,
    sent_out, place_out, _blank, held, *, levs,
):
    band_rows, lon_count = dep_row.shape
    slices = last_rows.shape[1]
    rim = RIM * slices
    place_out[...] = jnp.full(place_out.shape, place[0], jnp.int32)
    first_row = place[0] // levs * band_rows
    start = band_rows // 8 * 8
    skip = band_rows - RIM - start
    for t in range(lon_count // LANES):
        cols = tile_at(t)
        for row in range(RIM):
            held[t, row * slices : (row + 1) * slices, :] = last_rows[row, :, cols].astype(
                jnp.float32
            )
        parts = departures(
            slice(start, band_rows), t, first_row, dep_row, dep_col, lat_frac, lon_frac
        )
        for at, part in enumerate(parts):
            held[t, rim + RIM * at : rim + RIM * (at + 1), :] = part[skip:]
        sent_out[:, cols] = held[t].astype(jnp.bfloat16)


def waves_of(ids, group):
    pair = jnp.concatenate(
        [jnp.broadcast_to(ids[4 * group + at : 4 * group + at + 1], (4, LANES)) for at in range(4)],
        axis=0,
    )
    row = lax.broadcasted_iota(jnp.int32, (16, LANES), 0)
    return jnp.where((row & 2) == 0, pair, NMAX + 1 - pair)


def basis_tile(t, wave, lon_count):
    lane = lax.broadcasted_iota(jnp.int32, (16, LANES), 1)
    row = lax.broadcasted_iota(jnp.int32, (16, LANES), 0)
    longitude = lane + (t * SPAN - REACH)
    quarter = jnp.where((row & 1) == 0, 0.0, float(lon_count // 4))
    steps = longitude.astype(jnp.float32) * wave + quarter
    turns = jnp.floor(steps * (1.0 / lon_count) + 0.5)
    angle = lon_count // 4 - jnp.abs(steps - turns * lon_count)
    angle = angle * (2.0 * math.pi / lon_count)
    square = angle * angle
    series = jnp.float32(-1.0 / 39916800.0)
    for term in (1.0 / 362880.0, -1.0 / 5040.0, 1.0 / 120.0, -1.0 / 6.0, 1.0):
        series = series * square + term
    taken = (lane >= REACH) & (lane < REACH + SPAN) & (longitude < lon_count)
    return jnp.where(taken, angle * series, 0.0).astype(jnp.bfloat16)


def rim_spread(slices):
    fields = EDGE * slices
    shape = (3 * fields, 2 * RIM * (slices + 4))
    wanted = lax.broadcasted_iota(jnp.int32, shape, 0)
    held = lax.broadcasted_iota(jnp.int32, shape, 1)
    kind, rim_row = wanted // fields, wanted % fields // slices
    base = rim_row // RIM * RIM * (slices + 4) + RIM * slices + rim_row % RIM
    spread = jnp.where((kind == 0) & (held == base), float(1 << ROW_BITS), 0.0)
    spread += jnp.where(held == base + RIM * (kind + 1), 1.0, 0.0)
    return spread.astype(jnp.bfloat16)


def rim_plan(spread, packed):
    plan = jnp.dot(spread, packed.astype(jnp.bfloat16), preferred_element_type=jnp.float32)
    fields = spread.shape[0] // 3
    return [plan[fields * at : fields * (at + 1)] for at in range(3)]


def spread_rows(analysis, out, band_rows, slices):
    inner = band_rows - EDGE
    rim = RIM * slices
    place = lax.broadcasted_iota(jnp.int32, (LANES, 1), 0)
    edge = place - slices * inner
    edge_row = edge // slices
    row = jnp.where(edge < 0, RIM + place % inner, edge_row)
    row = jnp.where(edge >= rim, band_rows - EDGE + edge_row, row)
    row = jnp.where(edge >= 2 * rim, edge_row - 3 * RIM, row)
    row = jnp.where(edge >= 4 * rim, -band_rows, row)
    for band in range(out.shape[0] // LANES):
        start = max(0, band * band_rows - RIM) // 16 * 16
        end = min(analysis.shape[0], -(-(band + 1) * band_rows // 16) * 16)
        column = lax.broadcasted_iota(jnp.int32, (LANES, end - start), 1) + start
        chosen = jnp.where((column - band * band_rows == row) & (row >= -RIM), 1.0, 0.0)
        out[band * LANES : (band + 1) * LANES, :] = jnp.dot(
            chosen.astype(jnp.bfloat16),
            analysis[start:end, :],
            preferred_element_type=jnp.float32,
        ).astype(jnp.bfloat16)


def add_up(total, basis, values, windows):
    cols = slice(windows[0] * LANES, (windows[-1] + 1) * LANES)
    part = lax.dot_general(
        basis[:, cols], values[:, cols], (((1,), (1,)), ((), ())), preferred_element_type=jnp.float32
    )
    return part if total is None else total + part


def inner_kernel(
    by_row, dep_row, dep_col, lat_frac, lon_frac, sent, place, pair_ids, analysis, _,
    fourier_out, basis, spread_analysis, own, first_wave_out, windows,
    departed, rim_departed, steps, grid, rows, parts, plans, *, slices, levs,
):
    band_rows, lon_count = dep_row.shape
    inner = band_rows - 2 * RIM
    rim, fields, held = RIM * slices, EDGE * slices, band_rows * slices

    place = place[0:1, :]
    lat_at, lev_at = place // levs, place % levs
    first_row = lat_at * band_rows
    for t in range(lon_count // LANES):
        cols, slot = tile_at(t), t % rows.shape[0]
        for row in range(band_rows):
            rows[slot, row * slices : (row + 1) * slices, :] = by_row[row, :, cols].astype(
                jnp.float32
            )
        grid[:, cols] = rows[slot].astype(jnp.bfloat16)
        data = departures(
            slice(0, band_rows), t, first_row, dep_row, dep_col, lat_frac, lon_frac
        )
        for at, part in enumerate([data[0] * (1 << ROW_BITS) + data[1]] + data[2:]):
            parts[slot, at, 0:band_rows, :] = part
            plans[at * inner : (at + 1) * inner, cols] = parts[
                slot, at, RIM : RIM + inner, :
            ].astype(jnp.bfloat16)
        own[:, cols] = jnp.concatenate(
            [rows[slot, 0:rim, :]] + [part[0:RIM] for part in data], axis=0
        ).astype(jnp.bfloat16)

    pairs, col_count = pair_ids.shape[1], first_wave_out.shape[1]
    square = jnp.broadcast_to(pair_ids[...], (pairs, pairs)).astype(jnp.float32)
    row = lax.broadcasted_iota(jnp.int32, (pairs, pairs), 0)
    column = lax.broadcasted_iota(jnp.int32, (pairs, pairs), 1)
    ids = jnp.sum(jnp.where(row == column, square, 0.0), axis=1, keepdims=True)
    ids = jnp.broadcast_to(ids, (pairs, LANES))
    own_id = jnp.sum(
        jnp.where(column[:8] == lat_at[0:1, 0:1], square[:8], 0.0), axis=1, keepdims=True
    )
    column = lax.broadcasted_iota(jnp.int32, (8, col_count), 1) + lev_at[0:1, 0:1] * col_count
    first_wave_out[...] = jnp.where(column.astype(jnp.float32) < NMAX + 1 - own_id, 1.0, 0.0)
    plan_end = held + 3 * inner
    spread = rim_spread(slices)
    fill_steps(steps)
    rim_base = jnp.where(lax.broadcasted_iota(jnp.int32, (fields, LANES), 0) < rim, 1, 0)
    quads = ids.shape[0] // 4
    few = quads <= 4
    waves = [waves_of(ids, at) for at in range(quads if few else 0)]

    def group_of(ts):
        blocks = [cut((grid, plans, own, sent), t, lon_count, steps) for t in ts]
        for t, block in zip(ts, blocks):
            windows[t, rim : rim + held, :] = block[:held]
        results, rim_results = [], []
        for slot, t in enumerate(ts):
            code, lat_weight, lon_weight = [
                blocks[slot][held + at * inner : held + (at + 1) * inner] for at in range(3)
            ]
            plan = lane_plan(code)
            weights = corner_weights(lat_weight, lon_weight)
            for f in range(slices):
                sources = [
                    windows[
                        t, pl.ds(rim + slices * position + f, inner, stride=slices), :
                    ].astype(jnp.bfloat16)
                    for position in range(2 * RIM + 1)
                ]
                results.append((t, f, interpolate(sources, plan, weights)))
            sources = [
                jnp.concatenate(
                    [
                        windows[t, start : start + rim, :]
                        for start in (slices * (position + 1), held - rim + slices * position)
                    ],
                    axis=0,
                ).astype(jnp.bfloat16)
                for position in range(2 * RIM)
            ]
            code, lat_weight, lon_weight = rim_plan(spread, blocks[slot][plan_end:])
            weights = corner_weights(lat_weight, lon_weight)
            west_lane, east_lane, row_step = lane_plan(code)
            plan = west_lane, east_lane, row_step - rim_base
            rim_results.append(interpolate(sources, plan, weights))
        for t, f, result in results:
            departed[f * inner : (f + 1) * inner, tile_at(t)] = result.astype(jnp.bfloat16)
        for t, result in zip(ts, rim_results):
            rim_departed[:, tile_at(t)] = result.astype(jnp.bfloat16)
        for t in ts if few else ():
            for at, wave in enumerate(waves):
                basis[16 * at : 16 * at + 16, tile_at(t)] = basis_tile(t, wave, lon_count)

    if not few:

        for group in range(quads):
            wave = waves_of(ids, group)
            for t in range(basis.shape[1] // LANES):
                basis[16 * group : 16 * group + 16, tile_at(t)] = basis_tile(t, wave, lon_count)
    count = departed.shape[1] // LANES
    for ts in groups_of(count, INNER_AT_ONCE):
        group_of(ts)
    spread_rows(analysis, spread_analysis, inner + EDGE, slices)
    fourier_out[...] = jnp.concatenate(
        [add_up(None, basis, values, range(count)) for values in (departed, rim_departed)], axis=1
    )


def rim_kernel(
    arrived, own, basis, inner_fourier, fourier_out, windows, plans, departed, *, slices, levs
):
    lon_count = arrived.shape[1]
    rim, fields = RIM * slices, EDGE * slices
    out_row = lax.broadcasted_iota(jnp.int32, (fields, LANES), 0) // slices
    far_step = jnp.where(out_row < RIM, 2.0 * RIM, 0.0)
    near_step = jnp.where(out_row == RIM - 1, 2.0 * RIM - 1.0, jnp.where(out_row == RIM, 1.0, -2.0))
    lane = lax.broadcasted_iota(jnp.int32, (fields, LANES), 1) - REACH
    sublane = lax.broadcasted_iota(jnp.int32, (rim, LANES), 0)

    def part(source, lanes, row_step, lat_weight, lon_weight, step):
        west, east = [lane_gather(source, lane).astype(jnp.float32) for lane in lanes]
        row_weight = jnp.where(
            row_step == step,
            1.0 - lat_weight,
            jnp.where(row_step == step - 1.0, lat_weight, 0.0),
        )
        return row_weight * (west + lon_weight * (east - west))

    def prepare(t):
        for at, side in enumerate((arrived, own)):
            block = turned(side, t, lon_count).astype(jnp.float32)
            windows[t, rim * at : rim * (at + 1), :] = block[:rim]
            plans[t, 4 * RIM * at : 4 * RIM * (at + 1), :] = block[rim:]

    def finish(t):
        row_step, shift, lat_weight, lon_weight = [
            jnp.concatenate(
                [
                    jnp.where(
                        sublane < slices,
                        *[
                            jnp.broadcast_to(plans[t, row : row + 1, :], (rim, LANES))
                            for row in (start, start + 1)
                        ],
                    )
                    for start in (RIM * at, RIM * (at + 4))
                ],
                axis=0,
            )
            for at in range(4)
        ]
        west = lane + shift.astype(jnp.int32)
        lanes = [(column & LANES - 1).astype(jnp.int16) for column in (west, west + 1)]
        plan = lanes, row_step, lat_weight, lon_weight
        far = jnp.concatenate([windows[t, rim:, :], windows[t, 0:rim, :]], axis=0)
        near = jnp.concatenate([windows[t, slices : slices + rim, :]] * 2, axis=0)
        result = part(far.astype(jnp.bfloat16), *plan, far_step)
        result += part(near.astype(jnp.bfloat16), *plan, near_step)
        departed[:, tile_at(t)] = result.astype(jnp.bfloat16)

    count = basis.shape[1] // LANES
    for t in range(count):
        prepare(t)
    total = None
    for ts in groups_of(count, RIM_AT_ONCE):
        for t in ts:
            finish(t)
        total = add_up(total, basis, departed, ts)
    fourier = jnp.concatenate([inner_fourier[...], total], axis=1)
    for at in range(fourier_out.shape[0]):
        pair = at // levs
        fourier_out[at] = fourier[4 * pair : 4 * pair + 4].astype(jnp.bfloat16)


def legendre_kernel(
    first_wave, coeffs, spread_analysis, out, spread_coeffs, totals, blocks, *, levs, slices
):
    members, _, rows = coeffs.shape
    bands = members // levs
    col_count = spread_analysis.shape[1]
    inner = rows // slices - 2 * EDGE
    column = lax.broadcasted_iota(jnp.int32, (1, LANES), 1)
    rim_at = column - inner * slices
    slice_of = jnp.where(rim_at < 0, column // inner, rim_at % slices)
    slice_of = jnp.where(column < rows, slice_of, -1)

    def spread(band):
        for lev in range(levs):
            blocks[band, 4 * lev : 4 * lev + 4, 0:rows] = coeffs[band * levs + lev].astype(
                jnp.float32
            )
        block = blocks[band]
        spread_coeffs[:, tile_at(band)] = jnp.concatenate(
            [jnp.where(slice_of == f, block, 0.0) for f in range(slices)], axis=0
        ).astype(jnp.bfloat16)

    for band in range(bands):
        spread(band)
    total = None
    for at in range(0, bands * LANES, 2 * LANES):
        part = slice(at, min(at + 2 * LANES, bands * LANES))
        product = jnp.dot(
            spread_coeffs[:, part], spread_analysis[part, :], preferred_element_type=jnp.float32
        )
        total = product if total is None else total + product
    for t in range(totals.shape[0]):
        cols = slice(t * LANES, min((t + 1) * LANES, col_count))
        width = cols.stop - cols.start
        totals[t, 0 : total.shape[0], 0:width] = total[:, cols]
        first = first_wave[0:2, cols] > 0.0
        for f in range(slices):
            for lev in range(levs):
                at = (f * levs + lev) * 4
                out[lev * slices + f, :, cols] = jnp.where(
                    first, totals[t, at : at + 2, 0:width], totals[t, at + 2 : at + 4, 0:width]
                )


def shards(grid, dep_row, dep_col, lat_frac, lon_frac, pair_ids, analysis):
    slices, band_rows, lon_count = grid.shape
    pairs = pair_ids.shape[0]
    col_count = analysis.shape[2]
    bands, levs = lax.axis_size("lat"), lax.axis_size("lev")
    inner = band_rows - 2 * RIM
    windows = -(-lon_count // SPAN)
    held_rows = -(-band_rows // 8) * 8
    fields = slices * EDGE
    place = jnp.reshape(lax.axis_index(("lat", "lev")), (1,)).astype(jnp.int32)
    vmem = pl.BlockSpec(memory_space=pltpu.VMEM)
    smem = pl.BlockSpec(memory_space=pltpu.SMEM)
    params = pltpu.CompilerParams(vmem_limit_bytes=48 * 2**20)

    blank = jnp.zeros((windows, (band_rows + 2 * RIM) * slices, LANES), jnp.float32)
    by_row = grid.transpose(1, 0, 2)
    rim_shape = jax.ShapeDtypeStruct((RIM * (slices + 4), lon_count), jnp.bfloat16)
    sent_rim, wide_place, blank = pl.pallas_call(
        functools.partial(pack_kernel, levs=levs),
        out_shape=(
            rim_shape,
            jax.ShapeDtypeStruct((8, LANES), jnp.int32),
            jax.ShapeDtypeStruct(blank.shape, jnp.float32),
        ),
        in_specs=[smem] + [vmem] * 6,
        out_specs=(vmem,) * 3,
        input_output_aliases={6: 2},
        scratch_shapes=[
            pltpu.VMEM((lon_count // LANES, RIM * (slices + 4), LANES), jnp.float32)
        ],
        compiler_params=params,
    )(place, dep_row, dep_col, lat_frac, lon_frac, by_row[band_rows - RIM :], blank)
    arrived_rim = lax.ppermute(sent_rim, "lat", [(i, (i + 1) % bands) for i in range(bands)])

    inner_fourier, basis, spread_analysis, own_rim, first_wave, _ = pl.pallas_call(
        functools.partial(inner_kernel, slices=slices, levs=levs),
        out_shape=(
            jax.ShapeDtypeStruct((4 * pairs, slices * band_rows), jnp.float32),
            jax.ShapeDtypeStruct((4 * pairs, windows * LANES), jnp.bfloat16),
            jax.ShapeDtypeStruct((bands * LANES, col_count), jnp.bfloat16),
            rim_shape,
            jax.ShapeDtypeStruct((8, col_count), jnp.float32),
            jax.ShapeDtypeStruct(blank.shape, jnp.float32),
        ),
        in_specs=[vmem] * 10,
        out_specs=(vmem,) * 6,
        input_output_aliases={9: 5},
        scratch_shapes=[
            pltpu.VMEM((slices * inner, windows * LANES), jnp.bfloat16),
            pltpu.VMEM((fields, windows * LANES), jnp.bfloat16),
            pltpu.VMEM((2 * LANES, LANES), jnp.int16),
            pltpu.VMEM((band_rows * slices, lon_count), jnp.bfloat16),
            pltpu.VMEM((5, band_rows * slices, LANES), jnp.float32),
            pltpu.VMEM((5, 3, held_rows, LANES), jnp.float32),
            pltpu.VMEM((3 * inner, lon_count), jnp.bfloat16),
        ],
        compiler_params=params,
        cost_estimate=pl.CostEstimate(flops=100_000_000, bytes_accessed=2_000_000, transcendentals=0),
    )(
        by_row, dep_row, dep_col, lat_frac, lon_frac, sent_rim, wide_place, pair_ids[None, :],
        analysis[0], blank,
    )

    held_coeffs = slices * (band_rows + EDGE)
    fourier = pl.pallas_call(
        functools.partial(rim_kernel, slices=slices, levs=levs),
        out_shape=jax.ShapeDtypeStruct((bands * levs, 4, held_coeffs), jnp.bfloat16),
        in_specs=[vmem] * 4,
        out_specs=vmem,
        scratch_shapes=[
            pltpu.VMEM((windows, fields, LANES), jnp.float32),
            pltpu.VMEM((windows, 8 * RIM, LANES), jnp.float32),
            pltpu.VMEM((fields, windows * LANES), jnp.bfloat16),
        ],
        compiler_params=params,
    )(arrived_rim, own_rim, basis, inner_fourier)
    coeffs = lax.all_to_all(
        fourier, ("lat", "lev"), split_axis=0, concat_axis=0, tiled=True
    )
    out = pl.pallas_call(
        functools.partial(legendre_kernel, levs=levs, slices=slices),
        out_shape=jax.ShapeDtypeStruct((levs * slices, 2, col_count), jnp.float32),
        in_specs=[vmem] * 3,
        out_specs=vmem,
        scratch_shapes=[
            pltpu.VMEM((4 * levs * slices, bands * LANES), jnp.bfloat16),
            pltpu.VMEM((-(-col_count // LANES), 4 * levs * slices, LANES), jnp.float32),
            pltpu.VMEM((bands, 4 * levs, LANES), jnp.float32),
        ],
        compiler_params=params,
    )(first_wave, coeffs, spread_analysis)
    return out[None]


def solution(mesh):
    return jax.shard_map(
        shards,
        mesh=mesh,
        in_specs=(
            P("lev", "lat", None),
            P("lat", None),
            P("lat", None),
            P("lat", None),
            P("lat", None),
            P(),
            P("lat", None, "lev"),
        ),
        out_specs=P("lat", None, None, "lev"),
        check_vma=False,
    )
```

```python
import functools
import math

import jax
import jax.numpy as jnp
from jax import lax
from jax.experimental import pallas as pl
from jax.experimental.pallas import tpu as pltpu
from jax.sharding import PartitionSpec as P

NMAX = 1279
LANES = 128
RIM = 2
EDGE = 2 * RIM
REACH = 8
SPAN = LANES - 2 * REACH - 1
ROW_BITS = 5
INNER_AT_ONCE = 2
RIM_AT_ONCE = 8


def lane_gather(values, indices):
    numbers = lax.GatherDimensionNumbers(
        offset_dims=(),
        collapsed_slice_dims=(1,),
        start_index_map=(1,),
        operand_batching_dims=(0,),
        start_indices_batching_dims=(0,),
    )
    return lax.gather(
        values,
        indices[..., None],
        numbers,
        (1, 1),
        mode=lax.GatherScatterMode.PROMISE_IN_BOUNDS,
    )


def tile_at(t):
    return slice(t * LANES, (t + 1) * LANES)


def cut(arrays, t, lon_count, steps):
    tiles = lon_count // LANES
    first, lane_at = divmod((t * SPAN - REACH) % lon_count, LANES)
    second = (first + 1) % tiles
    chosen = jnp.where(steps[...] == jnp.int16(lane_at), jnp.bfloat16(1), jnp.bfloat16(0))
    columns = jnp.concatenate(
        [
            jnp.concatenate([array[:, tile_at(tile)] for array in arrays], axis=0)
            for tile in (first, second)
        ],
        axis=1,
    )
    return jnp.dot(columns, chosen, preferred_element_type=jnp.float32)


def turned(array, t, lon_count):
    tiles = lon_count // LANES
    first, lane_at = divmod((t * SPAN - REACH) % lon_count, LANES)
    if lane_at == 0:
        return array[:, tile_at(first)]
    joined = array[:, tile_at(first)], array[:, tile_at((first + 1) % tiles)]
    lane = lax.broadcasted_iota(jnp.int32, joined[0].shape, 1).astype(jnp.int16)
    return pltpu.roll(jnp.where(lane >= jnp.int16(lane_at), *joined), LANES - lane_at, 1)


def fill_steps(steps):
    shape = steps.shape
    step = lax.broadcasted_iota(jnp.int32, shape, 0) - lax.broadcasted_iota(jnp.int32, shape, 1)
    steps[...] = step.astype(jnp.int16)


def lane_plan(code):
    code = code.astype(jnp.int32)
    lane = lax.broadcasted_iota(jnp.int32, code.shape, 1)
    west = lane - REACH + (code & (1 << ROW_BITS) - 1)
    west_lane = (west & (LANES - 1)).astype(jnp.int16)
    east_lane = ((west + 1) & (LANES - 1)).astype(jnp.int16)
    return west_lane, east_lane, code >> ROW_BITS


def corner_weights(lat_weight, lon_weight):
    south, north = 1.0 - lat_weight, lat_weight
    west, east = 1.0 - lon_weight, lon_weight
    return south * west, south * east, north * west, north * east


def interpolate(sources, plan, weights):
    west_lane, east_lane, row_step = plan
    row_step = row_step.astype(jnp.float32).astype(jnp.bfloat16)
    masks = [row_step == float(step) for step in range(2 * RIM - 1)]
    last = 2 * RIM - 1

    def pick(gathered):
        if len(gathered) > 2 * RIM:
            low, high = gathered[last], gathered[last + 1]
        else:
            zero = jnp.zeros_like(gathered[0])
            low = jnp.where(row_step == float(last), gathered[last], zero)
            high = jnp.where(row_step == -1.0, gathered[0], zero)
        for position in range(last - 1, -1, -1):
            low = jnp.where(masks[position], gathered[position], low)
            high = jnp.where(masks[position], gathered[position + 1], high)
        return low.astype(jnp.float32), high.astype(jnp.float32)

    west_low, west_high = pick([lane_gather(source, west_lane) for source in sources])
    east_low, east_high = pick([lane_gather(source, east_lane) for source in sources])
    departed = (
        weights[0] * west_low
        + weights[1] * east_low
        + weights[2] * west_high
        + weights[3] * east_high
    )
    return departed


def groups_of(count, at_once):
    return [range(at, min(at + at_once, count)) for at in range(0, count, at_once)]


def departures(rows, t, first_row, dep_row, dep_col, lat_frac, lon_frac):
    lon_count = dep_row.shape[1]
    cols, shape = tile_at(t), (rows.stop - rows.start, LANES)
    row = lax.broadcasted_iota(jnp.int32, shape, 0) + rows.start
    lane = lax.broadcasted_iota(jnp.int32, shape, 1)
    shift = dep_col[rows, cols] - (lane + t * LANES)
    shift = jnp.where(shift > lon_count // 2, shift - lon_count, shift)
    shift = jnp.where(shift < -(lon_count // 2), shift + lon_count, shift)
    row_step = dep_row[rows, cols] - (first_row + row) + RIM
    fracs = [frac[:, cols].astype(jnp.float32)[rows] for frac in (lat_frac, lon_frac)]
    return [row_step.astype(jnp.float32), (shift + REACH).astype(jnp.float32)] + fracs


def pack_kernel(
    place, dep_row, dep_col, lat_frac, lon_frac, last_rows, _,
    sent_out, place_out, _blank, held, *, levs,
):
    band_rows, lon_count = dep_row.shape
    slices = last_rows.shape[1]
    rim = RIM * slices
    place_out[...] = jnp.full(place_out.shape, place[0], jnp.int32)
    first_row = place[0] // levs * band_rows
    start = band_rows // 8 * 8
    skip = band_rows - RIM - start
    for t in range(lon_count // LANES):
        cols = tile_at(t)
        for row in range(RIM):
            held[t, row * slices : (row + 1) * slices, :] = last_rows[row, :, cols].astype(
                jnp.float32
            )
        parts = departures(
            slice(start, band_rows), t, first_row, dep_row, dep_col, lat_frac, lon_frac
        )
        for at, part in enumerate(parts):
            held[t, rim + RIM * at : rim + RIM * (at + 1), :] = part[skip:]
        sent_out[:, cols] = held[t].astype(jnp.bfloat16)


def waves_of(ids, group):
    pair = jnp.concatenate(
        [jnp.broadcast_to(ids[4 * group + at : 4 * group + at + 1], (4, LANES)) for at in range(4)],
        axis=0,
    )
    row = lax.broadcasted_iota(jnp.int32, (16, LANES), 0)
    return jnp.where((row & 2) == 0, pair, NMAX + 1 - pair)


def basis_tile(t, wave, lon_count):
    lane = lax.broadcasted_iota(jnp.int32, (16, LANES), 1)
    row = lax.broadcasted_iota(jnp.int32, (16, LANES), 0)
    longitude = lane + (t * SPAN - REACH)
    quarter = jnp.where((row & 1) == 0, 0.0, float(lon_count // 4))
    steps = longitude.astype(jnp.float32) * wave + quarter
    turns = jnp.floor(steps * (1.0 / lon_count) + 0.5)
    angle = lon_count // 4 - jnp.abs(steps - turns * lon_count)
    angle = angle * (2.0 * math.pi / lon_count)
    square = angle * angle
    series = jnp.float32(-1.0 / 39916800.0)
    for term in (1.0 / 362880.0, -1.0 / 5040.0, 1.0 / 120.0, -1.0 / 6.0, 1.0):
        series = series * square + term
    taken = (lane >= REACH) & (lane < REACH + SPAN) & (longitude < lon_count)
    return jnp.where(taken, angle * series, 0.0).astype(jnp.bfloat16)


def rim_spread(slices):
    fields = EDGE * slices
    shape = (3 * fields, 2 * RIM * (slices + 4))
    wanted = lax.broadcasted_iota(jnp.int32, shape, 0)
    held = lax.broadcasted_iota(jnp.int32, shape, 1)
    kind, rim_row = wanted // fields, wanted % fields // slices
    base = rim_row // RIM * RIM * (slices + 4) + RIM * slices + rim_row % RIM
    spread = jnp.where((kind == 0) & (held == base), float(1 << ROW_BITS), 0.0)
    spread += jnp.where(held == base + RIM * (kind + 1), 1.0, 0.0)
    return spread.astype(jnp.bfloat16)


def rim_plan(spread, packed):
    plan = jnp.dot(spread, packed.astype(jnp.bfloat16), preferred_element_type=jnp.float32)
    fields = spread.shape[0] // 3
    return [plan[fields * at : fields * (at + 1)] for at in range(3)]


def slots_of(band_rows):
    width = band_rows + EDGE
    return width, LANES // width


def spread_rows(analysis, out, band_rows):
    width, shared = slots_of(band_rows)
    inner = band_rows - EDGE
    place = lax.broadcasted_iota(jnp.int32, (LANES, 1), 0)
    slot, rank = place // width, place % width
    row = jnp.where(rank < inner, RIM + rank, rank - inner)
    row = jnp.where(rank >= inner + RIM, band_rows - EDGE + rank - inner, row)
    row = jnp.where(rank >= inner + EDGE, rank - inner - 3 * RIM, row)
    row = row + slot * band_rows
    row = jnp.where(slot < shared, row, -band_rows)
    for group in range(out.shape[0] // LANES):
        first = group * shared * band_rows
        start = max(0, first - RIM) // 16 * 16
        end = min(analysis.shape[0], -(-(first + shared * band_rows) // 16) * 16)
        column = lax.broadcasted_iota(jnp.int32, (LANES, end - start), 1) + start
        chosen = jnp.where((column - first == row) & (row >= -RIM), 1.0, 0.0)
        out[group * LANES : (group + 1) * LANES, :] = jnp.dot(
            chosen.astype(jnp.bfloat16),
            analysis[start:end, :],
            preferred_element_type=jnp.float32,
        ).astype(jnp.bfloat16)


def add_up(total, basis, values, windows):
    cols = slice(windows[0] * LANES, (windows[-1] + 1) * LANES)
    part = lax.dot_general(
        basis[:, cols], values[:, cols], (((1,), (1,)), ((), ())), preferred_element_type=jnp.float32
    )
    return part if total is None else total + part


def inner_kernel(
    by_row, dep_row, dep_col, lat_frac, lon_frac, sent, place, pair_ids, analysis, _,
    fourier_out, basis, spread_analysis, own, first_wave_out, windows,
    departed, rim_departed, steps, grid, rows, parts, plans, *, slices, levs,
):
    band_rows, lon_count = dep_row.shape
    inner = band_rows - 2 * RIM
    rim, fields, held = RIM * slices, EDGE * slices, band_rows * slices

    place = place[0:1, :]
    lat_at, lev_at = place // levs, place % levs
    first_row = lat_at * band_rows
    for t in range(lon_count // LANES):
        cols, slot = tile_at(t), t % rows.shape[0]
        for row in range(band_rows):
            rows[slot, row * slices : (row + 1) * slices, :] = by_row[row, :, cols].astype(
                jnp.float32
            )
        grid[:, cols] = rows[slot].astype(jnp.bfloat16)
        data = departures(
            slice(0, band_rows), t, first_row, dep_row, dep_col, lat_frac, lon_frac
        )
        for at, part in enumerate([data[0] * (1 << ROW_BITS) + data[1]] + data[2:]):
            parts[slot, at, 0:band_rows, :] = part
            plans[at * inner : (at + 1) * inner, cols] = parts[
                slot, at, RIM : RIM + inner, :
            ].astype(jnp.bfloat16)
        own[:, cols] = jnp.concatenate(
            [rows[slot, 0:rim, :]] + [part[0:RIM] for part in data], axis=0
        ).astype(jnp.bfloat16)

    pairs, col_count = pair_ids.shape[1], first_wave_out.shape[1]
    square = jnp.broadcast_to(pair_ids[...], (pairs, pairs)).astype(jnp.float32)
    row = lax.broadcasted_iota(jnp.int32, (pairs, pairs), 0)
    column = lax.broadcasted_iota(jnp.int32, (pairs, pairs), 1)
    ids = jnp.sum(jnp.where(row == column, square, 0.0), axis=1, keepdims=True)
    ids = jnp.broadcast_to(ids, (pairs, LANES))
    own_id = jnp.sum(
        jnp.where(column[:8] == lat_at[0:1, 0:1], square[:8], 0.0), axis=1, keepdims=True
    )
    column = lax.broadcasted_iota(jnp.int32, (8, col_count), 1) + lev_at[0:1, 0:1] * col_count
    first_wave_out[...] = jnp.where(column.astype(jnp.float32) < NMAX + 1 - own_id, 1.0, 0.0)
    plan_end = held + 3 * inner
    spread = rim_spread(slices)
    fill_steps(steps)
    rim_base = jnp.where(lax.broadcasted_iota(jnp.int32, (fields, LANES), 0) < rim, 1, 0)
    quads = ids.shape[0] // 4
    few = quads <= 4
    waves = [waves_of(ids, at) for at in range(quads if few else 0)]

    def group_of(ts):
        blocks = [cut((grid, plans, own, sent), t, lon_count, steps) for t in ts]
        for t, block in zip(ts, blocks):
            windows[t, rim : rim + held, :] = block[:held]
        results, rim_results = [], []
        for slot, t in enumerate(ts):
            code, lat_weight, lon_weight = [
                blocks[slot][held + at * inner : held + (at + 1) * inner] for at in range(3)
            ]
            plan = lane_plan(code)
            weights = corner_weights(lat_weight, lon_weight)
            for f in range(slices):
                sources = [
                    windows[
                        t, pl.ds(rim + slices * position + f, inner, stride=slices), :
                    ].astype(jnp.bfloat16)
                    for position in range(2 * RIM + 1)
                ]
                results.append((t, f, interpolate(sources, plan, weights)))
            sources = [
                jnp.concatenate(
                    [
                        windows[t, start : start + rim, :]
                        for start in (slices * (position + 1), held - rim + slices * position)
                    ],
                    axis=0,
                ).astype(jnp.bfloat16)
                for position in range(2 * RIM)
            ]
            code, lat_weight, lon_weight = rim_plan(spread, blocks[slot][plan_end:])
            weights = corner_weights(lat_weight, lon_weight)
            west_lane, east_lane, row_step = lane_plan(code)
            plan = west_lane, east_lane, row_step - rim_base
            rim_results.append(interpolate(sources, plan, weights))
        for t, f, result in results:
            departed[f * inner : (f + 1) * inner, tile_at(t)] = result.astype(jnp.bfloat16)
        for t, result in zip(ts, rim_results):
            rim_departed[:, tile_at(t)] = result.astype(jnp.bfloat16)
        for t in ts if few else ():
            for at, wave in enumerate(waves):
                basis[16 * at : 16 * at + 16, tile_at(t)] = basis_tile(t, wave, lon_count)

    if not few:

        for group in range(quads):
            wave = waves_of(ids, group)
            for t in range(basis.shape[1] // LANES):
                basis[16 * group : 16 * group + 16, tile_at(t)] = basis_tile(t, wave, lon_count)
    count = departed.shape[1] // LANES
    for ts in groups_of(count, INNER_AT_ONCE):
        group_of(ts)
    spread_rows(analysis, spread_analysis, band_rows)
    fourier_out[...] = jnp.concatenate(
        [add_up(None, basis, values, range(count)) for values in (departed, rim_departed)], axis=1
    )


def rim_kernel(
    arrived, own, basis, inner_fourier, fourier_out, windows, plans, departed, *, slices, levs
):
    lon_count = arrived.shape[1]
    rim, fields = RIM * slices, EDGE * slices
    out_row = lax.broadcasted_iota(jnp.int32, (fields, LANES), 0) // slices
    far_step = jnp.where(out_row < RIM, 2.0 * RIM, 0.0)
    near_step = jnp.where(out_row == RIM - 1, 2.0 * RIM - 1.0, jnp.where(out_row == RIM, 1.0, -2.0))
    lane = lax.broadcasted_iota(jnp.int32, (fields, LANES), 1) - REACH
    sublane = lax.broadcasted_iota(jnp.int32, (rim, LANES), 0)

    def part(source, lanes, row_step, lat_weight, lon_weight, step):
        west, east = [lane_gather(source, lane).astype(jnp.float32) for lane in lanes]
        row_weight = jnp.where(
            row_step == step,
            1.0 - lat_weight,
            jnp.where(row_step == step - 1.0, lat_weight, 0.0),
        )
        return row_weight * (west + lon_weight * (east - west))

    def prepare(t):
        for at, side in enumerate((arrived, own)):
            block = turned(side, t, lon_count).astype(jnp.float32)
            windows[t, rim * at : rim * (at + 1), :] = block[:rim]
            plans[t, 4 * RIM * at : 4 * RIM * (at + 1), :] = block[rim:]

    def finish(t):
        row_step, shift, lat_weight, lon_weight = [
            jnp.concatenate(
                [
                    jnp.where(
                        sublane < slices,
                        *[
                            jnp.broadcast_to(plans[t, row : row + 1, :], (rim, LANES))
                            for row in (start, start + 1)
                        ],
                    )
                    for start in (RIM * at, RIM * (at + 4))
                ],
                axis=0,
            )
            for at in range(4)
        ]
        west = lane + shift.astype(jnp.int32)
        lanes = [(column & LANES - 1).astype(jnp.int16) for column in (west, west + 1)]
        plan = lanes, row_step, lat_weight, lon_weight
        far = jnp.concatenate([windows[t, rim:, :], windows[t, 0:rim, :]], axis=0)
        near = jnp.concatenate([windows[t, slices : slices + rim, :]] * 2, axis=0)
        result = part(far.astype(jnp.bfloat16), *plan, far_step)
        result += part(near.astype(jnp.bfloat16), *plan, near_step)
        departed[:, tile_at(t)] = result.astype(jnp.bfloat16)

    count = basis.shape[1] // LANES
    for t in range(count):
        prepare(t)
    total = None
    for ts in groups_of(count, RIM_AT_ONCE):
        for t in ts:
            finish(t)
        total = add_up(total, basis, departed, ts)
    fourier = jnp.concatenate([inner_fourier[...], total], axis=1)
    for at in range(fourier_out.shape[0]):
        pair = at // levs
        fourier_out[at] = fourier[4 * pair : 4 * pair + 4].astype(jnp.bfloat16)


def legendre_kernel(
    first_wave, coeffs, spread_analysis, out, spread_coeffs, totals, blocks, *, levs, slices
):
    members, _, rows = coeffs.shape
    bands = members // levs
    col_count = spread_analysis.shape[1]
    width, shared = slots_of(rows // slices - EDGE)
    inner = width - 2 * EDGE
    lane = lax.broadcasted_iota(jnp.int32, (4 * levs, LANES), 1)
    slot, rank = lane // width, lane % width
    rim_rank = inner * slices + (rank - inner) * slices
    held_at = [
        jnp.where(rank < inner, f * inner + rank, rim_rank + f).astype(jnp.int16)
        for f in range(slices)
    ]
    slot = slot.astype(jnp.int16)
    for band in range(bands):
        for lev in range(levs):
            blocks[band, 4 * lev : 4 * lev + 4, 0:rows] = coeffs[band * levs + lev].astype(
                jnp.float32
            )
    for group in range(-(-bands // shared)):
        here = range(group * shared, min((group + 1) * shared, bands))
        taken = [blocks[band].astype(jnp.bfloat16) for band in here]
        for f in range(slices):
            joined = jnp.zeros(slot.shape, jnp.bfloat16)
            for at, block in enumerate(taken):
                joined = jnp.where(slot == jnp.int16(at), lane_gather(block, held_at[f]), joined)
            spread_coeffs[4 * levs * f : 4 * levs * (f + 1), tile_at(group)] = joined
    total = jnp.dot(
        spread_coeffs[...], spread_analysis[...], preferred_element_type=jnp.float32
    )
    for t in range(totals.shape[0]):
        cols = slice(t * LANES, min((t + 1) * LANES, col_count))
        width = cols.stop - cols.start
        totals[t, 0 : total.shape[0], 0:width] = total[:, cols]
        first = first_wave[0:2, cols] > 0.0
        for f in range(slices):
            for lev in range(levs):
                at = (f * levs + lev) * 4
                out[lev * slices + f, :, cols] = jnp.where(
                    first, totals[t, at : at + 2, 0:width], totals[t, at + 2 : at + 4, 0:width]
                )


def shards(grid, dep_row, dep_col, lat_frac, lon_frac, pair_ids, analysis):
    slices, band_rows, lon_count = grid.shape
    pairs = pair_ids.shape[0]
    col_count = analysis.shape[2]
    bands, levs = lax.axis_size("lat"), lax.axis_size("lev")
    inner = band_rows - 2 * RIM
    windows = -(-lon_count // SPAN)
    held_rows = -(-band_rows // 8) * 8
    fields = slices * EDGE
    spread_count = -(-bands // slots_of(band_rows)[1]) * LANES
    place = jnp.reshape(lax.axis_index(("lat", "lev")), (1,)).astype(jnp.int32)
    vmem = pl.BlockSpec(memory_space=pltpu.VMEM)
    smem = pl.BlockSpec(memory_space=pltpu.SMEM)
    params = pltpu.CompilerParams(vmem_limit_bytes=48 * 2**20)

    blank = jnp.zeros((windows, (band_rows + 2 * RIM) * slices, LANES), jnp.float32)
    by_row = grid.transpose(1, 0, 2)
    rim_shape = jax.ShapeDtypeStruct((RIM * (slices + 4), lon_count), jnp.bfloat16)
    sent_rim, wide_place, blank = pl.pallas_call(
        functools.partial(pack_kernel, levs=levs),
        out_shape=(
            rim_shape,
            jax.ShapeDtypeStruct((8, LANES), jnp.int32),
            jax.ShapeDtypeStruct(blank.shape, jnp.float32),
        ),
        in_specs=[smem] + [vmem] * 6,
        out_specs=(vmem,) * 3,
        input_output_aliases={6: 2},
        scratch_shapes=[
            pltpu.VMEM((lon_count // LANES, RIM * (slices + 4), LANES), jnp.float32)
        ],
        compiler_params=params,
    )(place, dep_row, dep_col, lat_frac, lon_frac, by_row[band_rows - RIM :], blank)
    arrived_rim = lax.ppermute(sent_rim, "lat", [(i, (i + 1) % bands) for i in range(bands)])

    inner_fourier, basis, spread_analysis, own_rim, first_wave, _ = pl.pallas_call(
        functools.partial(inner_kernel, slices=slices, levs=levs),
        out_shape=(
            jax.ShapeDtypeStruct((4 * pairs, slices * band_rows), jnp.float32),
            jax.ShapeDtypeStruct((4 * pairs, windows * LANES), jnp.bfloat16),
            jax.ShapeDtypeStruct((spread_count, col_count), jnp.bfloat16),
            rim_shape,
            jax.ShapeDtypeStruct((8, col_count), jnp.float32),
            jax.ShapeDtypeStruct(blank.shape, jnp.float32),
        ),
        in_specs=[vmem] * 10,
        out_specs=(vmem,) * 6,
        input_output_aliases={9: 5},
        scratch_shapes=[
            pltpu.VMEM((slices * inner, windows * LANES), jnp.bfloat16),
            pltpu.VMEM((fields, windows * LANES), jnp.bfloat16),
            pltpu.VMEM((2 * LANES, LANES), jnp.int16),
            pltpu.VMEM((band_rows * slices, lon_count), jnp.bfloat16),
            pltpu.VMEM((5, band_rows * slices, LANES), jnp.float32),
            pltpu.VMEM((5, 3, held_rows, LANES), jnp.float32),
            pltpu.VMEM((3 * inner, lon_count), jnp.bfloat16),
        ],
        compiler_params=params,
        cost_estimate=pl.CostEstimate(flops=100_000_000, bytes_accessed=2_000_000, transcendentals=0),
    )(
        by_row, dep_row, dep_col, lat_frac, lon_frac, sent_rim, wide_place, pair_ids[None, :],
        analysis[0], blank,
    )

    held_coeffs = slices * (band_rows + EDGE)
    fourier = pl.pallas_call(
        functools.partial(rim_kernel, slices=slices, levs=levs),
        out_shape=jax.ShapeDtypeStruct((bands * levs, 4, held_coeffs), jnp.bfloat16),
        in_specs=[vmem] * 4,
        out_specs=vmem,
        scratch_shapes=[
            pltpu.VMEM((windows, fields, LANES), jnp.float32),
            pltpu.VMEM((windows, 8 * RIM, LANES), jnp.float32),
            pltpu.VMEM((fields, windows * LANES), jnp.bfloat16),
        ],
        compiler_params=params,
    )(arrived_rim, own_rim, basis, inner_fourier)
    coeffs = lax.all_to_all(
        fourier, ("lat", "lev"), split_axis=0, concat_axis=0, tiled=True
    )
    out = pl.pallas_call(
        functools.partial(legendre_kernel, levs=levs, slices=slices),
        out_shape=jax.ShapeDtypeStruct((levs * slices, 2, col_count), jnp.float32),
        in_specs=[vmem] * 3,
        out_specs=vmem,
        scratch_shapes=[
            pltpu.VMEM((4 * levs * slices, spread_count), jnp.bfloat16),
            pltpu.VMEM((-(-col_count // LANES), 4 * levs * slices, LANES), jnp.float32),
            pltpu.VMEM((bands, 4 * levs, LANES), jnp.float32),
        ],
        compiler_params=params,
    )(first_wave, coeffs, spread_analysis)
    return out[None]


def solution(mesh):
    return jax.shard_map(
        shards,
        mesh=mesh,
        in_specs=(
            P("lev", "lat", None),
            P("lat", None),
            P("lat", None),
            P("lat", None),
            P("lat", None),
            P(),
            P("lat", None, "lev"),
        ),
        out_specs=P("lat", None, None, "lev"),
        check_vma=False,
    )
```

```python
import functools
import math

import jax
import jax.numpy as jnp
from jax import lax
from jax.experimental import pallas as pl
from jax.experimental.pallas import tpu as pltpu
from jax.sharding import PartitionSpec as P

NMAX = 1279
LANES = 128
RIM = 2
EDGE = 2 * RIM
REACH = 8
SPAN = LANES - 2 * REACH - 1
ROW_BITS = 5
INNER_AT_ONCE = 2
RIM_AT_ONCE = 8


def lane_gather(values, indices):
    numbers = lax.GatherDimensionNumbers(
        offset_dims=(),
        collapsed_slice_dims=(1,),
        start_index_map=(1,),
        operand_batching_dims=(0,),
        start_indices_batching_dims=(0,),
    )
    return lax.gather(
        values,
        indices[..., None],
        numbers,
        (1, 1),
        mode=lax.GatherScatterMode.PROMISE_IN_BOUNDS,
    )


def tile_at(t):
    return slice(t * LANES, (t + 1) * LANES)


def cut(arrays, t, lon_count, steps):
    tiles = lon_count // LANES
    first, lane_at = divmod((t * SPAN - REACH) % lon_count, LANES)
    second = (first + 1) % tiles
    chosen = jnp.where(steps[...] == jnp.int16(lane_at), jnp.bfloat16(1), jnp.bfloat16(0))
    columns = jnp.concatenate(
        [
            jnp.concatenate([array[:, tile_at(tile)] for array in arrays], axis=0)
            for tile in (first, second)
        ],
        axis=1,
    )
    return jnp.dot(columns, chosen, preferred_element_type=jnp.float32)


def turned(array, t, lon_count):
    tiles = lon_count // LANES
    first, lane_at = divmod((t * SPAN - REACH) % lon_count, LANES)
    if lane_at == 0:
        return array[:, tile_at(first)]
    joined = array[:, tile_at(first)], array[:, tile_at((first + 1) % tiles)]
    lane = lax.broadcasted_iota(jnp.int32, joined[0].shape, 1).astype(jnp.int16)
    return pltpu.roll(jnp.where(lane >= jnp.int16(lane_at), *joined), LANES - lane_at, 1)


def fill_steps(steps):
    shape = steps.shape
    step = lax.broadcasted_iota(jnp.int32, shape, 0) - lax.broadcasted_iota(jnp.int32, shape, 1)
    steps[...] = step.astype(jnp.int16)


def lane_plan(code):
    code = code.astype(jnp.int32)
    lane = lax.broadcasted_iota(jnp.int32, code.shape, 1)
    west = lane - REACH + (code & (1 << ROW_BITS) - 1)
    west_lane = (west & (LANES - 1)).astype(jnp.int16)
    east_lane = ((west + 1) & (LANES - 1)).astype(jnp.int16)
    return west_lane, east_lane, code >> ROW_BITS


def corner_weights(lat_weight, lon_weight):
    south, north = 1.0 - lat_weight, lat_weight
    west, east = 1.0 - lon_weight, lon_weight
    return south * west, south * east, north * west, north * east


def interpolate(sources, plan, weights):
    west_lane, east_lane, row_step = plan
    row_step = row_step.astype(jnp.float32).astype(jnp.bfloat16)
    masks = [row_step == float(step) for step in range(2 * RIM - 1)]
    last = 2 * RIM - 1

    def pick(gathered):
        if len(gathered) > 2 * RIM:
            low, high = gathered[last], gathered[last + 1]
        else:
            zero = jnp.zeros_like(gathered[0])
            low = jnp.where(row_step == float(last), gathered[last], zero)
            high = jnp.where(row_step == -1.0, gathered[0], zero)
        for position in range(last - 1, -1, -1):
            low = jnp.where(masks[position], gathered[position], low)
            high = jnp.where(masks[position], gathered[position + 1], high)
        return low.astype(jnp.float32), high.astype(jnp.float32)

    west_low, west_high = pick([lane_gather(source, west_lane) for source in sources])
    east_low, east_high = pick([lane_gather(source, east_lane) for source in sources])
    departed = (
        weights[0] * west_low
        + weights[1] * east_low
        + weights[2] * west_high
        + weights[3] * east_high
    )
    return departed


def groups_of(count, at_once):
    return [range(at, min(at + at_once, count)) for at in range(0, count, at_once)]


def departures(rows, t, first_row, dep_row, dep_col, lat_frac, lon_frac):
    lon_count = dep_row.shape[1]
    cols, shape = tile_at(t), (rows.stop - rows.start, LANES)
    row = lax.broadcasted_iota(jnp.int32, shape, 0) + rows.start
    lane = lax.broadcasted_iota(jnp.int32, shape, 1)
    shift = dep_col[rows, cols] - (lane + t * LANES)
    shift = jnp.where(shift > lon_count // 2, shift - lon_count, shift)
    shift = jnp.where(shift < -(lon_count // 2), shift + lon_count, shift)
    row_step = dep_row[rows, cols] - (first_row + row) + RIM
    fracs = [frac[:, cols].astype(jnp.float32)[rows] for frac in (lat_frac, lon_frac)]
    return [row_step.astype(jnp.float32), (shift + REACH).astype(jnp.float32)] + fracs


def rows_kernel(by_row, _, sent_out, _blank, held):
    band_rows, slices, lon_count = by_row.shape
    for t in range(lon_count // LANES):
        for row in range(RIM):
            held[t, row * slices : (row + 1) * slices, :] = by_row[
                band_rows - RIM + row, :, tile_at(t)
            ].astype(jnp.float32)
        sent_out[:, tile_at(t)] = held[t].astype(jnp.bfloat16)


def data_kernel(
    place, dep_row, dep_col, lat_frac, lon_frac, _rows, sent_out, place_out, held, *, levs
):
    band_rows, lon_count = dep_row.shape
    place_out[...] = jnp.full(place_out.shape, place[0], jnp.int32)
    first_row = place[0] // levs * band_rows
    start = band_rows // 8 * 8
    skip = band_rows - RIM - start
    for t in range(lon_count // LANES):
        parts = departures(
            slice(start, band_rows), t, first_row, dep_row, dep_col, lat_frac, lon_frac
        )
        for at, part in enumerate(parts):
            held[t, RIM * at : RIM * (at + 1), :] = part[skip:]
        sent_out[:, tile_at(t)] = held[t].astype(jnp.bfloat16)


def waves_of(ids, group):
    pair = jnp.concatenate(
        [jnp.broadcast_to(ids[4 * group + at : 4 * group + at + 1], (4, LANES)) for at in range(4)],
        axis=0,
    )
    row = lax.broadcasted_iota(jnp.int32, (16, LANES), 0)
    return jnp.where((row & 2) == 0, pair, NMAX + 1 - pair)


def basis_tile(t, wave, lon_count):
    lane = lax.broadcasted_iota(jnp.int32, (16, LANES), 1)
    row = lax.broadcasted_iota(jnp.int32, (16, LANES), 0)
    longitude = lane + (t * SPAN - REACH)
    quarter = jnp.where((row & 1) == 0, 0.0, float(lon_count // 4))
    steps = longitude.astype(jnp.float32) * wave + quarter
    turns = jnp.floor(steps * (1.0 / lon_count) + 0.5)
    angle = lon_count // 4 - jnp.abs(steps - turns * lon_count)
    angle = angle * (2.0 * math.pi / lon_count)
    square = angle * angle
    series = jnp.float32(-1.0 / 39916800.0)
    for term in (1.0 / 362880.0, -1.0 / 5040.0, 1.0 / 120.0, -1.0 / 6.0, 1.0):
        series = series * square + term
    taken = (lane >= REACH) & (lane < REACH + SPAN) & (longitude < lon_count)
    return jnp.where(taken, angle * series, 0.0).astype(jnp.bfloat16)


def rim_spread(slices):
    fields = EDGE * slices
    shape = (3 * fields, 8 * RIM)
    wanted = lax.broadcasted_iota(jnp.int32, shape, 0)
    held = lax.broadcasted_iota(jnp.int32, shape, 1)
    kind, rim_row = wanted // fields, wanted % fields // slices
    base = rim_row // RIM * 4 * RIM + rim_row % RIM
    spread = jnp.where((kind == 0) & (held == base), float(1 << ROW_BITS), 0.0)
    spread += jnp.where(held == base + RIM * (kind + 1), 1.0, 0.0)
    return spread.astype(jnp.bfloat16)


def rim_plan(spread, packed):
    plan = jnp.dot(spread, packed.astype(jnp.bfloat16), preferred_element_type=jnp.float32)
    fields = spread.shape[0] // 3
    return [plan[fields * at : fields * (at + 1)] for at in range(3)]


def slots_of(band_rows):
    width = band_rows + EDGE
    return width, LANES // width


def spread_rows(analysis, out, band_rows):
    width, shared = slots_of(band_rows)
    inner = band_rows - EDGE
    place = lax.broadcasted_iota(jnp.int32, (LANES, 1), 0)
    slot, rank = place // width, place % width
    row = jnp.where(rank < inner, RIM + rank, rank - inner)
    row = jnp.where(rank >= inner + RIM, band_rows - EDGE + rank - inner, row)
    row = jnp.where(rank >= inner + EDGE, rank - inner - 3 * RIM, row)
    row = row + slot * band_rows
    row = jnp.where(slot < shared, row, -band_rows)
    for group in range(out.shape[0] // LANES):
        first = group * shared * band_rows
        start = max(0, first - RIM) // 16 * 16
        end = min(analysis.shape[0], -(-(first + shared * band_rows) // 16) * 16)
        column = lax.broadcasted_iota(jnp.int32, (LANES, end - start), 1) + start
        chosen = jnp.where((column - first == row) & (row >= -RIM), 1.0, 0.0)
        out[group * LANES : (group + 1) * LANES, :] = jnp.dot(
            chosen.astype(jnp.bfloat16),
            analysis[start:end, :],
            preferred_element_type=jnp.float32,
        ).astype(jnp.bfloat16)


def add_up(total, basis, values, windows):
    cols = slice(windows[0] * LANES, (windows[-1] + 1) * LANES)
    part = lax.dot_general(
        basis[:, cols], values[:, cols], (((1,), (1,)), ((), ())), preferred_element_type=jnp.float32
    )
    return part if total is None else total + part


def inner_kernel(
    by_row, dep_row, dep_col, lat_frac, lon_frac, place, pair_ids, analysis, _,
    fourier_out, basis, spread_analysis, own, first_wave_out, windows,
    departed, rim_departed, steps, grid, rows, parts, plans, edges, *, slices, levs,
):
    band_rows, lon_count = dep_row.shape
    inner = band_rows - 2 * RIM
    rim, fields, held = RIM * slices, EDGE * slices, band_rows * slices

    place = place[0:1, :]
    lat_at, lev_at = place // levs, place % levs
    first_row = lat_at * band_rows
    for t in range(lon_count // LANES):
        cols, slot = tile_at(t), t % rows.shape[0]
        for row in range(band_rows):
            rows[slot, row * slices : (row + 1) * slices, :] = by_row[row, :, cols].astype(
                jnp.float32
            )
        grid[:, cols] = rows[slot].astype(jnp.bfloat16)
        data = departures(
            slice(0, band_rows), t, first_row, dep_row, dep_col, lat_frac, lon_frac
        )
        for at, part in enumerate([data[0] * (1 << ROW_BITS) + data[1]] + data[2:]):
            parts[slot, at, 0:band_rows, :] = part
            plans[at * inner : (at + 1) * inner, cols] = parts[
                slot, at, RIM : RIM + inner, :
            ].astype(jnp.bfloat16)
        own_data = [part[0:RIM] for part in data]
        own[:, cols] = jnp.concatenate([rows[slot, 0:rim, :]] + own_data, axis=0).astype(
            jnp.bfloat16
        )
        edges[:, cols] = jnp.concatenate(
            own_data + [part[band_rows - RIM :] for part in data], axis=0
        ).astype(jnp.bfloat16)

    pairs, col_count = pair_ids.shape[1], first_wave_out.shape[1]
    square = jnp.broadcast_to(pair_ids[...], (pairs, pairs)).astype(jnp.float32)
    row = lax.broadcasted_iota(jnp.int32, (pairs, pairs), 0)
    column = lax.broadcasted_iota(jnp.int32, (pairs, pairs), 1)
    ids = jnp.sum(jnp.where(row == column, square, 0.0), axis=1, keepdims=True)
    ids = jnp.broadcast_to(ids, (pairs, LANES))
    own_id = jnp.sum(
        jnp.where(column[:8] == lat_at[0:1, 0:1], square[:8], 0.0), axis=1, keepdims=True
    )
    column = lax.broadcasted_iota(jnp.int32, (8, col_count), 1) + lev_at[0:1, 0:1] * col_count
    first_wave_out[...] = jnp.where(column.astype(jnp.float32) < NMAX + 1 - own_id, 1.0, 0.0)
    plan_end = held + 3 * inner
    spread = rim_spread(slices)
    fill_steps(steps)
    rim_base = jnp.where(lax.broadcasted_iota(jnp.int32, (fields, LANES), 0) < rim, 1, 0)
    quads = ids.shape[0] // 4
    few = quads <= 4
    waves = [waves_of(ids, at) for at in range(quads if few else 0)]

    def group_of(ts):
        blocks = [cut((grid, plans, edges), t, lon_count, steps) for t in ts]
        for t, block in zip(ts, blocks):
            windows[t, rim : rim + held, :] = block[:held]
        results, rim_results = [], []
        for slot, t in enumerate(ts):
            code, lat_weight, lon_weight = [
                blocks[slot][held + at * inner : held + (at + 1) * inner] for at in range(3)
            ]
            plan = lane_plan(code)
            weights = corner_weights(lat_weight, lon_weight)
            for f in range(slices):
                sources = [
                    windows[
                        t, pl.ds(rim + slices * position + f, inner, stride=slices), :
                    ].astype(jnp.bfloat16)
                    for position in range(2 * RIM + 1)
                ]
                results.append((t, f, interpolate(sources, plan, weights)))
            sources = [
                jnp.concatenate(
                    [
                        windows[t, start : start + rim, :]
                        for start in (slices * (position + 1), held - rim + slices * position)
                    ],
                    axis=0,
                ).astype(jnp.bfloat16)
                for position in range(2 * RIM)
            ]
            code, lat_weight, lon_weight = rim_plan(spread, blocks[slot][plan_end:])
            weights = corner_weights(lat_weight, lon_weight)
            west_lane, east_lane, row_step = lane_plan(code)
            plan = west_lane, east_lane, row_step - rim_base
            rim_results.append(interpolate(sources, plan, weights))
        for t, f, result in results:
            departed[f * inner : (f + 1) * inner, tile_at(t)] = result.astype(jnp.bfloat16)
        for t, result in zip(ts, rim_results):
            rim_departed[:, tile_at(t)] = result.astype(jnp.bfloat16)
        for t in ts if few else ():
            for at, wave in enumerate(waves):
                basis[16 * at : 16 * at + 16, tile_at(t)] = basis_tile(t, wave, lon_count)

    if not few:

        for group in range(quads):
            wave = waves_of(ids, group)
            for t in range(basis.shape[1] // LANES):
                basis[16 * group : 16 * group + 16, tile_at(t)] = basis_tile(t, wave, lon_count)
    count = departed.shape[1] // LANES
    for ts in groups_of(count, INNER_AT_ONCE):
        group_of(ts)
    spread_rows(analysis, spread_analysis, band_rows)
    fourier_out[...] = jnp.concatenate(
        [add_up(None, basis, values, range(count)) for values in (departed, rim_departed)], axis=1
    )


def rim_kernel(
    arrived, arrived_data, own, basis, inner_fourier, fourier_out, windows, plans, departed,
    *, slices, levs,
):
    lon_count = arrived.shape[1]
    rim, fields = RIM * slices, EDGE * slices
    out_row = lax.broadcasted_iota(jnp.int32, (fields, LANES), 0) // slices
    far_step = jnp.where(out_row < RIM, 2.0 * RIM, 0.0)
    near_step = jnp.where(out_row == RIM - 1, 2.0 * RIM - 1.0, jnp.where(out_row == RIM, 1.0, -2.0))
    lane = lax.broadcasted_iota(jnp.int32, (fields, LANES), 1) - REACH
    sublane = lax.broadcasted_iota(jnp.int32, (rim, LANES), 0)

    def part(source, lanes, row_step, lat_weight, lon_weight, step):
        west, east = [lane_gather(source, lane).astype(jnp.float32) for lane in lanes]
        row_weight = jnp.where(
            row_step == step,
            1.0 - lat_weight,
            jnp.where(row_step == step - 1.0, lat_weight, 0.0),
        )
        return row_weight * (west + lon_weight * (east - west))

    def prepare(t):
        block = turned(own, t, lon_count).astype(jnp.float32)
        windows[t, 0:rim, :] = turned(arrived, t, lon_count).astype(jnp.float32)
        windows[t, rim:, :] = block[:rim]
        plans[t, 0 : 4 * RIM, :] = turned(arrived_data, t, lon_count).astype(jnp.float32)
        plans[t, 4 * RIM :, :] = block[rim:]

    def finish(t):
        row_step, shift, lat_weight, lon_weight = [
            jnp.concatenate(
                [
                    jnp.where(
                        sublane < slices,
                        *[
                            jnp.broadcast_to(plans[t, row : row + 1, :], (rim, LANES))
                            for row in (start, start + 1)
                        ],
                    )
                    for start in (RIM * at, RIM * (at + 4))
                ],
                axis=0,
            )
            for at in range(4)
        ]
        west = lane + shift.astype(jnp.int32)
        lanes = [(column & LANES - 1).astype(jnp.int16) for column in (west, west + 1)]
        plan = lanes, row_step, lat_weight, lon_weight
        far = jnp.concatenate([windows[t, rim:, :], windows[t, 0:rim, :]], axis=0)
        near = jnp.concatenate([windows[t, slices : slices + rim, :]] * 2, axis=0)
        result = part(far.astype(jnp.bfloat16), *plan, far_step)
        result += part(near.astype(jnp.bfloat16), *plan, near_step)
        departed[:, tile_at(t)] = result.astype(jnp.bfloat16)

    count = basis.shape[1] // LANES
    for t in range(count):
        prepare(t)
    total = None
    for ts in groups_of(count, RIM_AT_ONCE):
        for t in ts:
            finish(t)
        total = add_up(total, basis, departed, ts)
    fourier = jnp.concatenate([inner_fourier[...], total], axis=1)
    for at in range(fourier_out.shape[0]):
        pair = at // levs
        fourier_out[at] = fourier[4 * pair : 4 * pair + 4].astype(jnp.bfloat16)


def legendre_kernel(
    first_wave, coeffs, spread_analysis, out, spread_coeffs, totals, blocks, *, levs, slices
):
    members, _, rows = coeffs.shape
    bands = members // levs
    col_count = spread_analysis.shape[1]
    width, shared = slots_of(rows // slices - EDGE)
    inner = width - 2 * EDGE
    lane = lax.broadcasted_iota(jnp.int32, (4 * levs, LANES), 1)
    slot, rank = lane // width, lane % width
    rim_rank = inner * slices + (rank - inner) * slices
    held_at = [
        jnp.where(rank < inner, f * inner + rank, rim_rank + f).astype(jnp.int16)
        for f in range(slices)
    ]
    slot = slot.astype(jnp.int16)
    for band in range(bands):
        for lev in range(levs):
            blocks[band, 4 * lev : 4 * lev + 4, 0:rows] = coeffs[band * levs + lev].astype(
                jnp.float32
            )
    for group in range(-(-bands // shared)):
        here = range(group * shared, min((group + 1) * shared, bands))
        taken = [blocks[band].astype(jnp.bfloat16) for band in here]
        for f in range(slices):
            joined = jnp.zeros(slot.shape, jnp.bfloat16)
            for at, block in enumerate(taken):
                joined = jnp.where(slot == jnp.int16(at), lane_gather(block, held_at[f]), joined)
            spread_coeffs[4 * levs * f : 4 * levs * (f + 1), tile_at(group)] = joined
    total = jnp.dot(
        spread_coeffs[...], spread_analysis[...], preferred_element_type=jnp.float32
    )
    for t in range(totals.shape[0]):
        cols = slice(t * LANES, min((t + 1) * LANES, col_count))
        width = cols.stop - cols.start
        totals[t, 0 : total.shape[0], 0:width] = total[:, cols]
        first = first_wave[0:2, cols] > 0.0
        for f in range(slices):
            for lev in range(levs):
                at = (f * levs + lev) * 4
                out[lev * slices + f, :, cols] = jnp.where(
                    first, totals[t, at : at + 2, 0:width], totals[t, at + 2 : at + 4, 0:width]
                )


def shards(grid, dep_row, dep_col, lat_frac, lon_frac, pair_ids, analysis):
    slices, band_rows, lon_count = grid.shape
    pairs = pair_ids.shape[0]
    col_count = analysis.shape[2]
    bands, levs = lax.axis_size("lat"), lax.axis_size("lev")
    inner = band_rows - 2 * RIM
    windows = -(-lon_count // SPAN)
    held_rows = -(-band_rows // 8) * 8
    fields = slices * EDGE
    spread_count = -(-bands // slots_of(band_rows)[1]) * LANES
    place = jnp.reshape(lax.axis_index(("lat", "lev")), (1,)).astype(jnp.int32)
    vmem = pl.BlockSpec(memory_space=pltpu.VMEM)
    smem = pl.BlockSpec(memory_space=pltpu.SMEM)
    params = pltpu.CompilerParams(vmem_limit_bytes=48 * 2**20)

    blank = jnp.zeros((windows, (band_rows + 2 * RIM) * slices, LANES), jnp.float32)
    by_row = grid.transpose(1, 0, 2)
    upwards = [(i, (i + 1) % bands) for i in range(bands)]
    rows_shape = jax.ShapeDtypeStruct((RIM * slices, lon_count), jnp.bfloat16)
    data_shape = jax.ShapeDtypeStruct((4 * RIM, lon_count), jnp.bfloat16)
    sent_rows, blank = pl.pallas_call(
        rows_kernel,
        out_shape=(rows_shape, jax.ShapeDtypeStruct(blank.shape, jnp.float32)),
        in_specs=[vmem] * 2,
        out_specs=(vmem,) * 2,
        input_output_aliases={1: 1},
        scratch_shapes=[pltpu.VMEM((lon_count // LANES, RIM * slices, LANES), jnp.float32)],
        compiler_params=params,
    )(by_row, blank)
    arrived_rows = lax.ppermute(sent_rows, "lat", upwards)
    sent_data, wide_place = pl.pallas_call(
        functools.partial(data_kernel, levs=levs),
        out_shape=(
            data_shape,
            jax.ShapeDtypeStruct((8, LANES), jnp.int32),
        ),
        in_specs=[smem] + [vmem] * 5,
        out_specs=(vmem,) * 2,
        scratch_shapes=[pltpu.VMEM((lon_count // LANES, 4 * RIM, LANES), jnp.float32)],
        compiler_params=params,
    )(place, dep_row, dep_col, lat_frac, lon_frac, sent_rows)
    arrived_data = lax.ppermute(sent_data, "lat", upwards)

    inner_fourier, basis, spread_analysis, own_rim, first_wave, _ = pl.pallas_call(
        functools.partial(inner_kernel, slices=slices, levs=levs),
        out_shape=(
            jax.ShapeDtypeStruct((4 * pairs, slices * band_rows), jnp.float32),
            jax.ShapeDtypeStruct((4 * pairs, windows * LANES), jnp.bfloat16),
            jax.ShapeDtypeStruct((spread_count, col_count), jnp.bfloat16),
            jax.ShapeDtypeStruct((RIM * (slices + 4), lon_count), jnp.bfloat16),
            jax.ShapeDtypeStruct((8, col_count), jnp.float32),
            jax.ShapeDtypeStruct(blank.shape, jnp.float32),
        ),
        in_specs=[vmem] * 9,
        out_specs=(vmem,) * 6,
        input_output_aliases={8: 5},
        scratch_shapes=[
            pltpu.VMEM((slices * inner, windows * LANES), jnp.bfloat16),
            pltpu.VMEM((fields, windows * LANES), jnp.bfloat16),
            pltpu.VMEM((2 * LANES, LANES), jnp.int16),
            pltpu.VMEM((band_rows * slices, lon_count), jnp.bfloat16),
            pltpu.VMEM((5, band_rows * slices, LANES), jnp.float32),
            pltpu.VMEM((5, 3, held_rows, LANES), jnp.float32),
            pltpu.VMEM((3 * inner, lon_count), jnp.bfloat16),
            pltpu.VMEM((8 * RIM, lon_count), jnp.bfloat16),
        ],
        compiler_params=params,
        cost_estimate=pl.CostEstimate(flops=100_000_000, bytes_accessed=2_000_000, transcendentals=0),
    )(
        by_row, dep_row, dep_col, lat_frac, lon_frac, wide_place, pair_ids[None, :],
        analysis[0], blank,
    )

    held_coeffs = slices * (band_rows + EDGE)
    fourier = pl.pallas_call(
        functools.partial(rim_kernel, slices=slices, levs=levs),
        out_shape=jax.ShapeDtypeStruct((bands * levs, 4, held_coeffs), jnp.bfloat16),
        in_specs=[vmem] * 5,
        out_specs=vmem,
        scratch_shapes=[
            pltpu.VMEM((windows, fields, LANES), jnp.float32),
            pltpu.VMEM((windows, 8 * RIM, LANES), jnp.float32),
            pltpu.VMEM((fields, windows * LANES), jnp.bfloat16),
        ],
        compiler_params=params,
    )(arrived_rows, arrived_data, own_rim, basis, inner_fourier)
    coeffs = lax.all_to_all(
        fourier, ("lat", "lev"), split_axis=0, concat_axis=0, tiled=True
    )
    out = pl.pallas_call(
        functools.partial(legendre_kernel, levs=levs, slices=slices),
        out_shape=jax.ShapeDtypeStruct((levs * slices, 2, col_count), jnp.float32),
        in_specs=[vmem] * 3,
        out_specs=vmem,
        scratch_shapes=[
            pltpu.VMEM((4 * levs * slices, spread_count), jnp.bfloat16),
            pltpu.VMEM((-(-col_count // LANES), 4 * levs * slices, LANES), jnp.float32),
            pltpu.VMEM((bands, 4 * levs, LANES), jnp.float32),
        ],
        compiler_params=params,
    )(first_wave, coeffs, spread_analysis)
    return out[None]


def solution(mesh):
    return jax.shard_map(
        shards,
        mesh=mesh,
        in_specs=(
            P("lev", "lat", None),
            P("lat", None),
            P("lat", None),
            P("lat", None),
            P("lat", None),
            P(),
            P("lat", None, "lev"),
        ),
        out_specs=P("lat", None, None, "lev"),
        check_vma=False,
    )
```

```python
import functools
import math

import jax
import jax.numpy as jnp
from jax import lax
from jax.experimental import pallas as pl
from jax.experimental.pallas import tpu as pltpu
from jax.sharding import PartitionSpec as P

NMAX = 1279
LANES = 128
RIM = 2
EDGE = 2 * RIM
REACH = 8
SPAN = LANES - 2 * REACH - 1
ROW_BITS = 5
INNER_AT_ONCE = 4
RIM_AT_ONCE = 15


def lane_gather(values, indices):
    numbers = lax.GatherDimensionNumbers(
        offset_dims=(),
        collapsed_slice_dims=(1,),
        start_index_map=(1,),
        operand_batching_dims=(0,),
        start_indices_batching_dims=(0,),
    )
    return lax.gather(
        values,
        indices[..., None],
        numbers,
        (1, 1),
        mode=lax.GatherScatterMode.PROMISE_IN_BOUNDS,
    )


def tile_at(t):
    return slice(t * LANES, (t + 1) * LANES)


def cut(arrays, t, lon_count, steps):
    tiles = lon_count // LANES
    first, lane_at = divmod((t * SPAN - REACH) % lon_count, LANES)
    second = (first + 1) % tiles
    chosen = jnp.where(steps[...] == jnp.int16(lane_at), jnp.bfloat16(1), jnp.bfloat16(0))
    columns = jnp.concatenate(
        [
            jnp.concatenate([array[:, tile_at(tile)] for array in arrays], axis=0)
            for tile in (first, second)
        ],
        axis=1,
    )
    return jnp.dot(columns, chosen, preferred_element_type=jnp.float32)


def turned(array, t, lon_count):
    tiles = lon_count // LANES
    first, lane_at = divmod((t * SPAN - REACH) % lon_count, LANES)
    if lane_at == 0:
        return array[:, tile_at(first)]
    joined = array[:, tile_at(first)], array[:, tile_at((first + 1) % tiles)]
    lane = lax.broadcasted_iota(jnp.int32, joined[0].shape, 1).astype(jnp.int16)
    return pltpu.roll(jnp.where(lane >= jnp.int16(lane_at), *joined), LANES - lane_at, 1)


def fill_steps(steps):
    shape = steps.shape
    step = lax.broadcasted_iota(jnp.int32, shape, 0) - lax.broadcasted_iota(jnp.int32, shape, 1)
    steps[...] = step.astype(jnp.int16)


def lane_plan(code):
    code = code.astype(jnp.int32)
    lane = lax.broadcasted_iota(jnp.int32, code.shape, 1)
    west = lane - REACH + (code & (1 << ROW_BITS) - 1)
    west_lane = (west & (LANES - 1)).astype(jnp.int16)
    east_lane = ((west + 1) & (LANES - 1)).astype(jnp.int16)
    return west_lane, east_lane, code >> ROW_BITS


def corner_weights(lat_weight, lon_weight):
    south, north = 1.0 - lat_weight, lat_weight
    west, east = 1.0 - lon_weight, lon_weight
    return south * west, south * east, north * west, north * east


def interpolate(sources, plan, weights):
    west_lane, east_lane, row_step = plan
    row_step = row_step.astype(jnp.float32).astype(jnp.bfloat16)
    masks = [row_step == float(step) for step in range(2 * RIM - 1)]
    last = 2 * RIM - 1

    def pick(gathered):
        if len(gathered) > 2 * RIM:
            low, high = gathered[last], gathered[last + 1]
        else:
            zero = jnp.zeros_like(gathered[0])
            low = jnp.where(row_step == float(last), gathered[last], zero)
            high = jnp.where(row_step == -1.0, gathered[0], zero)
        for position in range(last - 1, -1, -1):
            low = jnp.where(masks[position], gathered[position], low)
            high = jnp.where(masks[position], gathered[position + 1], high)
        return low.astype(jnp.float32), high.astype(jnp.float32)

    west_low, west_high = pick([lane_gather(source, west_lane) for source in sources])
    east_low, east_high = pick([lane_gather(source, east_lane) for source in sources])
    departed = (
        weights[0] * west_low
        + weights[1] * east_low
        + weights[2] * west_high
        + weights[3] * east_high
    )
    return departed


def groups_of(count, at_once):
    return [range(at, min(at + at_once, count)) for at in range(0, count, at_once)]


def departures(rows, t, first_row, dep_row, dep_col, lat_frac, lon_frac):
    lon_count = dep_row.shape[1]
    cols, shape = tile_at(t), (rows.stop - rows.start, LANES)
    row = lax.broadcasted_iota(jnp.int32, shape, 0) + rows.start
    lane = lax.broadcasted_iota(jnp.int32, shape, 1)
    shift = dep_col[rows, cols] - (lane + t * LANES)
    shift = jnp.where(shift > lon_count // 2, shift - lon_count, shift)
    shift = jnp.where(shift < -(lon_count // 2), shift + lon_count, shift)
    row_step = dep_row[rows, cols] - (first_row + row) + RIM
    fracs = [frac[:, cols].astype(jnp.float32)[rows] for frac in (lat_frac, lon_frac)]
    return [row_step.astype(jnp.float32), (shift + REACH).astype(jnp.float32)] + fracs


def pack_kernel(
    place, dep_row, dep_col, lat_frac, lon_frac, last_rows, _,
    sent_out, place_out, _blank, held, *, levs,
):
    band_rows, lon_count = dep_row.shape
    slices = last_rows.shape[1]
    rim = RIM * slices
    place_out[...] = jnp.full(place_out.shape, place[0], jnp.int32)
    first_row = place[0] // levs * band_rows
    start = band_rows // 8 * 8
    skip = band_rows - RIM - start
    for t in range(lon_count // LANES):
        cols = tile_at(t)
        for row in range(RIM):
            held[t, row * slices : (row + 1) * slices, :] = last_rows[row, :, cols].astype(
                jnp.float32
            )
        parts = departures(
            slice(start, band_rows), t, first_row, dep_row, dep_col, lat_frac, lon_frac
        )
        for at, part in enumerate(parts):
            held[t, rim + RIM * at : rim + RIM * (at + 1), :] = part[skip:]
        sent_out[:, cols] = held[t].astype(jnp.bfloat16)


def waves_of(ids, group):
    pair = jnp.concatenate(
        [jnp.broadcast_to(ids[4 * group + at : 4 * group + at + 1], (4, LANES)) for at in range(4)],
        axis=0,
    )
    row = lax.broadcasted_iota(jnp.int32, (16, LANES), 0)
    return jnp.where((row & 2) == 0, pair, NMAX + 1 - pair)


def basis_tile(t, wave, lon_count):
    lane = lax.broadcasted_iota(jnp.int32, (16, LANES), 1)
    row = lax.broadcasted_iota(jnp.int32, (16, LANES), 0)
    longitude = lane + (t * SPAN - REACH)
    quarter = jnp.where((row & 1) == 0, 0.0, float(lon_count // 4))
    steps = longitude.astype(jnp.float32) * wave + quarter
    turns = jnp.floor(steps * (1.0 / lon_count) + 0.5)
    angle = lon_count // 4 - jnp.abs(steps - turns * lon_count)
    angle = angle * (2.0 * math.pi / lon_count)
    square = angle * angle
    series = jnp.float32(-1.0 / 39916800.0)
    for term in (1.0 / 362880.0, -1.0 / 5040.0, 1.0 / 120.0, -1.0 / 6.0, 1.0):
        series = series * square + term
    taken = (lane >= REACH) & (lane < REACH + SPAN) & (longitude < lon_count)
    return jnp.where(taken, angle * series, 0.0).astype(jnp.bfloat16)


def rim_spread(slices):
    fields = EDGE * slices
    shape = (3 * fields, 2 * RIM * (slices + 4))
    wanted = lax.broadcasted_iota(jnp.int32, shape, 0)
    held = lax.broadcasted_iota(jnp.int32, shape, 1)
    kind, rim_row = wanted // fields, wanted % fields // slices
    base = rim_row // RIM * RIM * (slices + 4) + RIM * slices + rim_row % RIM
    spread = jnp.where((kind == 0) & (held == base), float(1 << ROW_BITS), 0.0)
    spread += jnp.where(held == base + RIM * (kind + 1), 1.0, 0.0)
    return spread.astype(jnp.bfloat16)


def rim_plan(spread, packed):
    plan = jnp.dot(spread, packed.astype(jnp.bfloat16), preferred_element_type=jnp.float32)
    fields = spread.shape[0] // 3
    return [plan[fields * at : fields * (at + 1)] for at in range(3)]


def spread_rows(analysis, out, band_rows, slices):
    inner = band_rows - EDGE
    rim = RIM * slices
    place = lax.broadcasted_iota(jnp.int32, (LANES, 1), 0)
    edge = place - slices * inner
    edge_row = edge // slices
    row = jnp.where(edge < 0, RIM + place % inner, edge_row)
    row = jnp.where(edge >= rim, band_rows - EDGE + edge_row, row)
    row = jnp.where(edge >= 2 * rim, edge_row - 3 * RIM, row)
    row = jnp.where(edge >= 4 * rim, -band_rows, row)
    for band in range(out.shape[0] // LANES):
        start = max(0, band * band_rows - RIM) // 16 * 16
        end = min(analysis.shape[0], -(-(band + 1) * band_rows // 16) * 16)
        column = lax.broadcasted_iota(jnp.int32, (LANES, end - start), 1) + start
        chosen = jnp.where((column - band * band_rows == row) & (row >= -RIM), 1.0, 0.0)
        out[band * LANES : (band + 1) * LANES, :] = jnp.dot(
            chosen.astype(jnp.bfloat16),
            analysis[start:end, :],
            preferred_element_type=jnp.float32,
        ).astype(jnp.bfloat16)


def add_up(total, basis, values, windows):
    cols = slice(windows[0] * LANES, (windows[-1] + 1) * LANES)
    part = lax.dot_general(
        basis[:, cols], values[:, cols], (((1,), (1,)), ((), ())), preferred_element_type=jnp.float32
    )
    return part if total is None else total + part


def inner_kernel(
    by_row, dep_row, dep_col, lat_frac, lon_frac, sent, place, pair_ids, analysis, _,
    fourier_out, basis, spread_analysis, own, first_wave_out, windows,
    departed, rim_departed, steps, grid, rows, parts, plans, *, slices, levs,
):
    band_rows, lon_count = dep_row.shape
    inner = band_rows - 2 * RIM
    rim, fields, held = RIM * slices, EDGE * slices, band_rows * slices

    place = place[0:1, :]
    lat_at, lev_at = place // levs, place % levs
    first_row = lat_at * band_rows
    for t in range(lon_count // LANES):
        cols, slot = tile_at(t), t % rows.shape[0]
        for row in range(band_rows):
            rows[slot, row * slices : (row + 1) * slices, :] = by_row[row, :, cols].astype(
                jnp.float32
            )
        grid[:, cols] = rows[slot].astype(jnp.bfloat16)
        data = departures(
            slice(0, band_rows), t, first_row, dep_row, dep_col, lat_frac, lon_frac
        )
        for at, part in enumerate([data[0] * (1 << ROW_BITS) + data[1]] + data[2:]):
            parts[slot, at, 0:band_rows, :] = part
            plans[at * inner : (at + 1) * inner, cols] = parts[
                slot, at, RIM : RIM + inner, :
            ].astype(jnp.bfloat16)
        own[:, cols] = jnp.concatenate(
            [rows[slot, 0:rim, :]] + [part[0:RIM] for part in data], axis=0
        ).astype(jnp.bfloat16)

    pairs, col_count = pair_ids.shape[1], first_wave_out.shape[1]
    square = jnp.broadcast_to(pair_ids[...], (pairs, pairs)).astype(jnp.float32)
    row = lax.broadcasted_iota(jnp.int32, (pairs, pairs), 0)
    column = lax.broadcasted_iota(jnp.int32, (pairs, pairs), 1)
    ids = jnp.sum(jnp.where(row == column, square, 0.0), axis=1, keepdims=True)
    ids = jnp.broadcast_to(ids, (pairs, LANES))
    own_id = jnp.sum(
        jnp.where(column[:8] == lat_at[0:1, 0:1], square[:8], 0.0), axis=1, keepdims=True
    )
    column = lax.broadcasted_iota(jnp.int32, (8, col_count), 1) + lev_at[0:1, 0:1] * col_count
    first_wave_out[...] = jnp.where(column.astype(jnp.float32) < NMAX + 1 - own_id, 1.0, 0.0)
    plan_end = held + 3 * inner
    spread = rim_spread(slices)
    fill_steps(steps)
    rim_base = jnp.where(lax.broadcasted_iota(jnp.int32, (fields, LANES), 0) < rim, 1, 0)
    quads = ids.shape[0] // 4
    few = quads <= 4
    waves = [waves_of(ids, at) for at in range(quads if few else 0)]

    def group_of(ts):
        blocks = [cut((grid, plans, own, sent), t, lon_count, steps) for t in ts]
        for t, block in zip(ts, blocks):
            windows[t, rim : rim + held, :] = block[:held]
        results, rim_results = [], []
        for slot, t in enumerate(ts):
            code, lat_weight, lon_weight = [
                blocks[slot][held + at * inner : held + (at + 1) * inner] for at in range(3)
            ]
            plan = lane_plan(code)
            weights = corner_weights(lat_weight, lon_weight)
            for f in range(slices):
                sources = [
                    windows[
                        t, pl.ds(rim + slices * position + f, inner, stride=slices), :
                    ].astype(jnp.bfloat16)
                    for position in range(2 * RIM + 1)
                ]
                results.append((t, f, interpolate(sources, plan, weights)))
            sources = [
                jnp.concatenate(
                    [
                        windows[t, start : start + rim, :]
                        for start in (slices * (position + 1), held - rim + slices * position)
                    ],
                    axis=0,
                ).astype(jnp.bfloat16)
                for position in range(2 * RIM)
            ]
            code, lat_weight, lon_weight = rim_plan(spread, blocks[slot][plan_end:])
            weights = corner_weights(lat_weight, lon_weight)
            west_lane, east_lane, row_step = lane_plan(code)
            plan = west_lane, east_lane, row_step - rim_base
            rim_results.append(interpolate(sources, plan, weights))
        for t, f, result in results:
            departed[f * inner : (f + 1) * inner, tile_at(t)] = result.astype(jnp.bfloat16)
        for t, result in zip(ts, rim_results):
            rim_departed[:, tile_at(t)] = result.astype(jnp.bfloat16)
        for t in ts if few else ():
            for at, wave in enumerate(waves):
                basis[16 * at : 16 * at + 16, tile_at(t)] = basis_tile(t, wave, lon_count)

    if not few:

        for group in range(quads):
            wave = waves_of(ids, group)
            for t in range(basis.shape[1] // LANES):
                basis[16 * group : 16 * group + 16, tile_at(t)] = basis_tile(t, wave, lon_count)
    count = departed.shape[1] // LANES
    for ts in groups_of(count, INNER_AT_ONCE):
        group_of(ts)
    spread_rows(analysis, spread_analysis, inner + EDGE, slices)
    fourier_out[...] = jnp.concatenate(
        [add_up(None, basis, values, range(count)) for values in (departed, rim_departed)], axis=1
    )


def rim_kernel(
    arrived, own, basis, inner_fourier, fourier_out, windows, plans, departed, *, slices, levs
):
    lon_count = arrived.shape[1]
    rim, fields = RIM * slices, EDGE * slices
    out_row = lax.broadcasted_iota(jnp.int32, (fields, LANES), 0) // slices
    far_step = jnp.where(out_row < RIM, 2.0 * RIM, 0.0)
    near_step = jnp.where(out_row == RIM - 1, 2.0 * RIM - 1.0, jnp.where(out_row == RIM, 1.0, -2.0))
    lane = lax.broadcasted_iota(jnp.int32, (fields, LANES), 1) - REACH
    sublane = lax.broadcasted_iota(jnp.int32, (rim, LANES), 0)

    def part(source, lanes, row_step, lat_weight, lon_weight, step):
        west, east = [lane_gather(source, lane).astype(jnp.float32) for lane in lanes]
        row_weight = jnp.where(
            row_step == step,
            1.0 - lat_weight,
            jnp.where(row_step == step - 1.0, lat_weight, 0.0),
        )
        return row_weight * (west + lon_weight * (east - west))

    def prepare(t):
        for at, side in enumerate((arrived, own)):
            block = turned(side, t, lon_count).astype(jnp.float32)
            windows[t, rim * at : rim * (at + 1), :] = block[:rim]
            plans[t, 4 * RIM * at : 4 * RIM * (at + 1), :] = block[rim:]

    def finish(t):
        row_step, shift, lat_weight, lon_weight = [
            jnp.concatenate(
                [
                    jnp.where(
                        sublane < slices,
                        *[
                            jnp.broadcast_to(plans[t, row : row + 1, :], (rim, LANES))
                            for row in (start, start + 1)
                        ],
                    )
                    for start in (RIM * at, RIM * (at + 4))
                ],
                axis=0,
            )
            for at in range(4)
        ]
        west = lane + shift.astype(jnp.int32)
        lanes = [(column & LANES - 1).astype(jnp.int16) for column in (west, west + 1)]
        plan = lanes, row_step, lat_weight, lon_weight
        far = jnp.concatenate([windows[t, rim:, :], windows[t, 0:rim, :]], axis=0)
        near = jnp.concatenate([windows[t, slices : slices + rim, :]] * 2, axis=0)
        result = part(far.astype(jnp.bfloat16), *plan, far_step)
        result += part(near.astype(jnp.bfloat16), *plan, near_step)
        departed[:, tile_at(t)] = result.astype(jnp.bfloat16)

    count = basis.shape[1] // LANES
    for t in range(count):
        prepare(t)
    total = None
    for ts in groups_of(count, RIM_AT_ONCE):
        for t in ts:
            finish(t)
        total = add_up(total, basis, departed, ts)
    fourier = jnp.concatenate([inner_fourier[...], total], axis=1)
    for at in range(fourier_out.shape[0]):
        pair = at // levs
        fourier_out[at] = fourier[4 * pair : 4 * pair + 4].astype(jnp.bfloat16)


def legendre_kernel(
    first_wave, coeffs, spread_analysis, out, spread_coeffs, totals, blocks, *, levs, slices
):
    members, _, rows = coeffs.shape
    bands = members // levs
    col_count = spread_analysis.shape[1]
    inner = rows // slices - 2 * EDGE
    column = lax.broadcasted_iota(jnp.int32, (1, LANES), 1)
    rim_at = column - inner * slices
    slice_of = jnp.where(rim_at < 0, column // inner, rim_at % slices)
    slice_of = jnp.where(column < rows, slice_of, -1)

    def spread(band):
        for lev in range(levs):
            blocks[band, 4 * lev : 4 * lev + 4, 0:rows] = coeffs[band * levs + lev].astype(
                jnp.float32
            )
        block = blocks[band]
        spread_coeffs[:, tile_at(band)] = jnp.concatenate(
            [jnp.where(slice_of == f, block, 0.0) for f in range(slices)], axis=0
        ).astype(jnp.bfloat16)

    for band in range(bands):
        spread(band)
    total = None
    for at in range(0, bands * LANES, 2 * LANES):
        part = slice(at, min(at + 2 * LANES, bands * LANES))
        product = jnp.dot(
            spread_coeffs[:, part], spread_analysis[part, :], preferred_element_type=jnp.float32
        )
        total = product if total is None else total + product
    for t in range(totals.shape[0]):
        cols = slice(t * LANES, min((t + 1) * LANES, col_count))
        width = cols.stop - cols.start
        totals[t, 0 : total.shape[0], 0:width] = total[:, cols]
        first = first_wave[0:2, cols] > 0.0
        for f in range(slices):
            for lev in range(levs):
                at = (f * levs + lev) * 4
                out[lev * slices + f, :, cols] = jnp.where(
                    first, totals[t, at : at + 2, 0:width], totals[t, at + 2 : at + 4, 0:width]
                )


def shards(grid, dep_row, dep_col, lat_frac, lon_frac, pair_ids, analysis):
    slices, band_rows, lon_count = grid.shape
    pairs = pair_ids.shape[0]
    col_count = analysis.shape[2]
    bands, levs = lax.axis_size("lat"), lax.axis_size("lev")
    inner = band_rows - 2 * RIM
    windows = -(-lon_count // SPAN)
    held_rows = -(-band_rows // 8) * 8
    fields = slices * EDGE
    place = jnp.reshape(lax.axis_index(("lat", "lev")), (1,)).astype(jnp.int32)
    vmem = pl.BlockSpec(memory_space=pltpu.VMEM)
    smem = pl.BlockSpec(memory_space=pltpu.SMEM)
    params = pltpu.CompilerParams(vmem_limit_bytes=48 * 2**20)

    blank = jnp.zeros((windows, (band_rows + 2 * RIM) * slices, LANES), jnp.float32)
    by_row = grid.transpose(1, 0, 2)
    rim_shape = jax.ShapeDtypeStruct((RIM * (slices + 4), lon_count), jnp.bfloat16)
    sent_rim, wide_place, blank = pl.pallas_call(
        functools.partial(pack_kernel, levs=levs),
        out_shape=(
            rim_shape,
            jax.ShapeDtypeStruct((8, LANES), jnp.int32),
            jax.ShapeDtypeStruct(blank.shape, jnp.float32),
        ),
        in_specs=[smem] + [vmem] * 6,
        out_specs=(vmem,) * 3,
        input_output_aliases={6: 2},
        scratch_shapes=[
            pltpu.VMEM((lon_count // LANES, RIM * (slices + 4), LANES), jnp.float32)
        ],
        compiler_params=params,
    )(place, dep_row, dep_col, lat_frac, lon_frac, by_row[band_rows - RIM :], blank)
    arrived_rim = lax.ppermute(sent_rim, "lat", [(i, (i + 1) % bands) for i in range(bands)])

    inner_fourier, basis, spread_analysis, own_rim, first_wave, _ = pl.pallas_call(
        functools.partial(inner_kernel, slices=slices, levs=levs),
        out_shape=(
            jax.ShapeDtypeStruct((4 * pairs, slices * band_rows), jnp.float32),
            jax.ShapeDtypeStruct((4 * pairs, windows * LANES), jnp.bfloat16),
            jax.ShapeDtypeStruct((bands * LANES, col_count), jnp.bfloat16),
            rim_shape,
            jax.ShapeDtypeStruct((8, col_count), jnp.float32),
            jax.ShapeDtypeStruct(blank.shape, jnp.float32),
        ),
        in_specs=[vmem] * 10,
        out_specs=(vmem,) * 6,
        input_output_aliases={9: 5},
        scratch_shapes=[
            pltpu.VMEM((slices * inner, windows * LANES), jnp.bfloat16),
            pltpu.VMEM((fields, windows * LANES), jnp.bfloat16),
            pltpu.VMEM((2 * LANES, LANES), jnp.int16),
            pltpu.VMEM((band_rows * slices, lon_count), jnp.bfloat16),
            pltpu.VMEM((5, band_rows * slices, LANES), jnp.float32),
            pltpu.VMEM((5, 3, held_rows, LANES), jnp.float32),
            pltpu.VMEM((3 * inner, lon_count), jnp.bfloat16),
        ],
        compiler_params=params,
        cost_estimate=pl.CostEstimate(flops=100_000_000, bytes_accessed=2_000_000, transcendentals=0),
    )(
        by_row, dep_row, dep_col, lat_frac, lon_frac, sent_rim, wide_place, pair_ids[None, :],
        analysis[0], blank,
    )

    held_coeffs = slices * (band_rows + EDGE)
    fourier = pl.pallas_call(
        functools.partial(rim_kernel, slices=slices, levs=levs),
        out_shape=jax.ShapeDtypeStruct((bands * levs, 4, held_coeffs), jnp.bfloat16),
        in_specs=[vmem] * 4,
        out_specs=vmem,
        scratch_shapes=[
            pltpu.VMEM((windows, fields, LANES), jnp.float32),
            pltpu.VMEM((windows, 8 * RIM, LANES), jnp.float32),
            pltpu.VMEM((fields, windows * LANES), jnp.bfloat16),
        ],
        compiler_params=params,
    )(arrived_rim, own_rim, basis, inner_fourier)
    coeffs = lax.all_to_all(
        fourier, ("lat", "lev"), split_axis=0, concat_axis=0, tiled=True
    )
    out = pl.pallas_call(
        functools.partial(legendre_kernel, levs=levs, slices=slices),
        out_shape=jax.ShapeDtypeStruct((levs * slices, 2, col_count), jnp.float32),
        in_specs=[vmem] * 3,
        out_specs=vmem,
        scratch_shapes=[
            pltpu.VMEM((4 * levs * slices, bands * LANES), jnp.bfloat16),
            pltpu.VMEM((-(-col_count // LANES), 4 * levs * slices, LANES), jnp.float32),
            pltpu.VMEM((bands, 4 * levs, LANES), jnp.float32),
        ],
        compiler_params=params,
    )(first_wave, coeffs, spread_analysis)
    return out[None]


def solution(mesh):
    return jax.shard_map(
        shards,
        mesh=mesh,
        in_specs=(
            P("lev", "lat", None),
            P("lat", None),
            P("lat", None),
            P("lat", None),
            P("lat", None),
            P(),
            P("lat", None, "lev"),
        ),
        out_specs=P("lat", None, None, "lev"),
        check_vma=False,
    )
```

```python
import functools
import math

import jax
import jax.numpy as jnp
from jax import lax
from jax.experimental import pallas as pl
from jax.experimental.pallas import tpu as pltpu
from jax.sharding import PartitionSpec as P

NMAX = 1279
LANES = 128
RIM = 2
EDGE = 2 * RIM
REACH = 8
SPAN = LANES - 2 * REACH - 1
ROW_BITS = 5
INNER_AT_ONCE = 2
RIM_AT_ONCE = 15


def lane_gather(values, indices):
    numbers = lax.GatherDimensionNumbers(
        offset_dims=(),
        collapsed_slice_dims=(1,),
        start_index_map=(1,),
        operand_batching_dims=(0,),
        start_indices_batching_dims=(0,),
    )
    return lax.gather(
        values,
        indices[..., None],
        numbers,
        (1, 1),
        mode=lax.GatherScatterMode.PROMISE_IN_BOUNDS,
    )


def tile_at(t):
    return slice(t * LANES, (t + 1) * LANES)


def cut(arrays, t, lon_count, steps):
    tiles = lon_count // LANES
    first, lane_at = divmod((t * SPAN - REACH) % lon_count, LANES)
    second = (first + 1) % tiles
    chosen = jnp.where(steps[...] == jnp.int16(lane_at), jnp.bfloat16(1), jnp.bfloat16(0))
    columns = jnp.concatenate(
        [
            jnp.concatenate([array[:, tile_at(tile)] for array in arrays], axis=0)
            for tile in (first, second)
        ],
        axis=1,
    )
    return jnp.dot(columns, chosen, preferred_element_type=jnp.float32)


def turned(array, t, lon_count):
    tiles = lon_count // LANES
    first, lane_at = divmod((t * SPAN - REACH) % lon_count, LANES)
    if lane_at == 0:
        return array[:, tile_at(first)]
    joined = array[:, tile_at(first)], array[:, tile_at((first + 1) % tiles)]
    lane = lax.broadcasted_iota(jnp.int32, joined[0].shape, 1).astype(jnp.int16)
    return pltpu.roll(jnp.where(lane >= jnp.int16(lane_at), *joined), LANES - lane_at, 1)


def fill_steps(steps):
    shape = steps.shape
    step = lax.broadcasted_iota(jnp.int32, shape, 0) - lax.broadcasted_iota(jnp.int32, shape, 1)
    steps[...] = step.astype(jnp.int16)


def lane_plan(code):
    code = code.astype(jnp.int32)
    lane = lax.broadcasted_iota(jnp.int32, code.shape, 1)
    west = lane - REACH + (code & (1 << ROW_BITS) - 1)
    west_lane = (west & (LANES - 1)).astype(jnp.int16)
    east_lane = ((west + 1) & (LANES - 1)).astype(jnp.int16)
    return west_lane, east_lane, code >> ROW_BITS


def corner_weights(lat_weight, lon_weight):
    south, north = 1.0 - lat_weight, lat_weight
    west, east = 1.0 - lon_weight, lon_weight
    return south * west, south * east, north * west, north * east


def interpolate(sources, plan, weights):
    west_lane, east_lane, row_step = plan
    row_step = row_step.astype(jnp.float32).astype(jnp.bfloat16)
    masks = [row_step == float(step) for step in range(2 * RIM - 1)]
    last = 2 * RIM - 1

    def pick(gathered):
        if len(gathered) > 2 * RIM:
            low, high = gathered[last], gathered[last + 1]
        else:
            zero = jnp.zeros_like(gathered[0])
            low = jnp.where(row_step == float(last), gathered[last], zero)
            high = jnp.where(row_step == -1.0, gathered[0], zero)
        for position in range(last - 1, -1, -1):
            low = jnp.where(masks[position], gathered[position], low)
            high = jnp.where(masks[position], gathered[position + 1], high)
        return low.astype(jnp.float32), high.astype(jnp.float32)

    west_low, west_high = pick([lane_gather(source, west_lane) for source in sources])
    east_low, east_high = pick([lane_gather(source, east_lane) for source in sources])
    departed = (
        weights[0] * west_low
        + weights[1] * east_low
        + weights[2] * west_high
        + weights[3] * east_high
    )
    return departed


def groups_of(count, at_once):
    return [range(at, min(at + at_once, count)) for at in range(0, count, at_once)]


def departures(rows, t, first_row, dep_row, dep_col, lat_frac, lon_frac):
    lon_count = dep_row.shape[1]
    cols, shape = tile_at(t), (rows.stop - rows.start, LANES)
    row = lax.broadcasted_iota(jnp.int32, shape, 0) + rows.start
    lane = lax.broadcasted_iota(jnp.int32, shape, 1)
    shift = dep_col[rows, cols] - (lane + t * LANES)
    shift = jnp.where(shift > lon_count // 2, shift - lon_count, shift)
    shift = jnp.where(shift < -(lon_count // 2), shift + lon_count, shift)
    row_step = dep_row[rows, cols] - (first_row + row) + RIM
    fracs = [frac[:, cols].astype(jnp.float32)[rows] for frac in (lat_frac, lon_frac)]
    return [row_step.astype(jnp.float32), (shift + REACH).astype(jnp.float32)] + fracs


def pack_kernel(
    place, dep_row, dep_col, lat_frac, lon_frac, last_rows, _,
    sent_out, place_out, _blank, held, *, levs,
):
    band_rows, lon_count = dep_row.shape
    slices = last_rows.shape[1]
    rim = RIM * slices
    place_out[...] = jnp.full(place_out.shape, place[0], jnp.int32)
    first_row = place[0] // levs * band_rows
    start = band_rows // 8 * 8
    skip = band_rows - RIM - start
    for t in range(lon_count // LANES):
        cols = tile_at(t)
        for row in range(RIM):
            held[t, row * slices : (row + 1) * slices, :] = last_rows[row, :, cols].astype(
                jnp.float32
            )
        parts = departures(
            slice(start, band_rows), t, first_row, dep_row, dep_col, lat_frac, lon_frac
        )
        for at, part in enumerate(parts):
            held[t, rim + RIM * at : rim + RIM * (at + 1), :] = part[skip:]
        sent_out[:, cols] = held[t].astype(jnp.bfloat16)


def waves_of(ids, group):
    pair = jnp.concatenate(
        [jnp.broadcast_to(ids[4 * group + at : 4 * group + at + 1], (4, LANES)) for at in range(4)],
        axis=0,
    )
    row = lax.broadcasted_iota(jnp.int32, (16, LANES), 0)
    return jnp.where((row & 2) == 0, pair, NMAX + 1 - pair)


def basis_tile(t, wave, lon_count):
    lane = lax.broadcasted_iota(jnp.int32, (16, LANES), 1)
    row = lax.broadcasted_iota(jnp.int32, (16, LANES), 0)
    longitude = lane + (t * SPAN - REACH)
    quarter = jnp.where((row & 1) == 0, 0.0, float(lon_count // 4))
    steps = longitude.astype(jnp.float32) * wave + quarter
    turns = jnp.floor(steps * (1.0 / lon_count) + 0.5)
    angle = lon_count // 4 - jnp.abs(steps - turns * lon_count)
    angle = angle * (2.0 * math.pi / lon_count)
    square = angle * angle
    series = jnp.float32(-1.0 / 39916800.0)
    for term in (1.0 / 362880.0, -1.0 / 5040.0, 1.0 / 120.0, -1.0 / 6.0, 1.0):
        series = series * square + term
    taken = (lane >= REACH) & (lane < REACH + SPAN) & (longitude < lon_count)
    return jnp.where(taken, angle * series, 0.0).astype(jnp.bfloat16)


def rim_spread(slices):
    fields = EDGE * slices
    shape = (3 * fields, 2 * RIM * (slices + 4))
    wanted = lax.broadcasted_iota(jnp.int32, shape, 0)
    held = lax.broadcasted_iota(jnp.int32, shape, 1)
    kind, rim_row = wanted // fields, wanted % fields // slices
    base = rim_row // RIM * RIM * (slices + 4) + RIM * slices + rim_row % RIM
    spread = jnp.where((kind == 0) & (held == base), float(1 << ROW_BITS), 0.0)
    spread += jnp.where(held == base + RIM * (kind + 1), 1.0, 0.0)
    return spread.astype(jnp.bfloat16)


def rim_plan(spread, packed):
    plan = jnp.dot(spread, packed.astype(jnp.bfloat16), preferred_element_type=jnp.float32)
    fields = spread.shape[0] // 3
    return [plan[fields * at : fields * (at + 1)] for at in range(3)]


def slots_of(band_rows):
    width = band_rows + EDGE
    return width, LANES // width


def spread_rows(analysis, out, band_rows):
    width, shared = slots_of(band_rows)
    inner = band_rows - EDGE
    place = lax.broadcasted_iota(jnp.int32, (LANES, 1), 0)
    slot, rank = place // width, place % width
    row = jnp.where(rank < inner, RIM + rank, rank - inner)
    row = jnp.where(rank >= inner + RIM, band_rows - EDGE + rank - inner, row)
    row = jnp.where(rank >= inner + EDGE, rank - inner - 3 * RIM, row)
    row = row + slot * band_rows
    row = jnp.where(slot < shared, row, -band_rows)
    for group in range(out.shape[0] // LANES):
        first = group * shared * band_rows
        start = max(0, first - RIM) // 16 * 16
        end = min(analysis.shape[0], -(-(first + shared * band_rows) // 16) * 16)
        column = lax.broadcasted_iota(jnp.int32, (LANES, end - start), 1) + start
        chosen = jnp.where((column - first == row) & (row >= -RIM), 1.0, 0.0)
        out[group * LANES : (group + 1) * LANES, :] = jnp.dot(
            chosen.astype(jnp.bfloat16),
            analysis[start:end, :],
            preferred_element_type=jnp.float32,
        ).astype(jnp.bfloat16)


def add_up(total, basis, values, windows):
    cols = slice(windows[0] * LANES, (windows[-1] + 1) * LANES)
    part = lax.dot_general(
        basis[:, cols], values[:, cols], (((1,), (1,)), ((), ())), preferred_element_type=jnp.float32
    )
    return part if total is None else total + part


def inner_kernel(
    by_row, dep_row, dep_col, lat_frac, lon_frac, sent, place, pair_ids, analysis, _,
    fourier_out, basis, spread_analysis, own, first_wave_out, windows,
    departed, rim_departed, steps, grid, rows, parts, plans, *, slices, levs,
):
    band_rows, lon_count = dep_row.shape
    inner = band_rows - 2 * RIM
    rim, fields, held = RIM * slices, EDGE * slices, band_rows * slices

    place = place[0:1, :]
    lat_at, lev_at = place // levs, place % levs
    first_row = lat_at * band_rows
    for t in range(lon_count // LANES):
        cols, slot = tile_at(t), t % rows.shape[0]
        for row in range(band_rows):
            rows[slot, row * slices : (row + 1) * slices, :] = by_row[row, :, cols].astype(
                jnp.float32
            )
        grid[:, cols] = rows[slot].astype(jnp.bfloat16)
        data = departures(
            slice(0, band_rows), t, first_row, dep_row, dep_col, lat_frac, lon_frac
        )
        for at, part in enumerate([data[0] * (1 << ROW_BITS) + data[1]] + data[2:]):
            parts[slot, at, 0:band_rows, :] = part
            plans[at * inner : (at + 1) * inner, cols] = parts[
                slot, at, RIM : RIM + inner, :
            ].astype(jnp.bfloat16)
        own[:, cols] = jnp.concatenate(
            [rows[slot, 0:rim, :]] + [part[0:RIM] for part in data], axis=0
        ).astype(jnp.bfloat16)

    pairs, col_count = pair_ids.shape[1], first_wave_out.shape[1]
    square = jnp.broadcast_to(pair_ids[...], (pairs, pairs)).astype(jnp.float32)
    row = lax.broadcasted_iota(jnp.int32, (pairs, pairs), 0)
    column = lax.broadcasted_iota(jnp.int32, (pairs, pairs), 1)
    ids = jnp.sum(jnp.where(row == column, square, 0.0), axis=1, keepdims=True)
    ids = jnp.broadcast_to(ids, (pairs, LANES))
    own_id = jnp.sum(
        jnp.where(column[:8] == lat_at[0:1, 0:1], square[:8], 0.0), axis=1, keepdims=True
    )
    column = lax.broadcasted_iota(jnp.int32, (8, col_count), 1) + lev_at[0:1, 0:1] * col_count
    first_wave_out[...] = jnp.where(column.astype(jnp.float32) < NMAX + 1 - own_id, 1.0, 0.0)
    plan_end = held + 3 * inner
    spread = rim_spread(slices)
    fill_steps(steps)
    rim_base = jnp.where(lax.broadcasted_iota(jnp.int32, (fields, LANES), 0) < rim, 1, 0)
    quads = ids.shape[0] // 4
    few = quads <= 4
    waves = [waves_of(ids, at) for at in range(quads if few else 0)]

    def group_of(ts):
        blocks = [cut((grid, plans, own, sent), t, lon_count, steps) for t in ts]
        for t, block in zip(ts, blocks):
            windows[t, rim : rim + held, :] = block[:held]
        results, rim_results = [], []
        for slot, t in enumerate(ts):
            code, lat_weight, lon_weight = [
                blocks[slot][held + at * inner : held + (at + 1) * inner] for at in range(3)
            ]
            plan = lane_plan(code)
            weights = corner_weights(lat_weight, lon_weight)
            for f in range(slices):
                sources = [
                    windows[
                        t, pl.ds(rim + slices * position + f, inner, stride=slices), :
                    ].astype(jnp.bfloat16)
                    for position in range(2 * RIM + 1)
                ]
                results.append((t, f, interpolate(sources, plan, weights)))
            sources = [
                jnp.concatenate(
                    [
                        windows[t, start : start + rim, :]
                        for start in (slices * (position + 1), held - rim + slices * position)
                    ],
                    axis=0,
                ).astype(jnp.bfloat16)
                for position in range(2 * RIM)
            ]
            code, lat_weight, lon_weight = rim_plan(spread, blocks[slot][plan_end:])
            weights = corner_weights(lat_weight, lon_weight)
            west_lane, east_lane, row_step = lane_plan(code)
            plan = west_lane, east_lane, row_step - rim_base
            rim_results.append(interpolate(sources, plan, weights))
        for t, f, result in results:
            departed[f * inner : (f + 1) * inner, tile_at(t)] = result.astype(jnp.bfloat16)
        for t, result in zip(ts, rim_results):
            rim_departed[:, tile_at(t)] = result.astype(jnp.bfloat16)
        for t in ts if few else ():
            for at, wave in enumerate(waves):
                basis[16 * at : 16 * at + 16, tile_at(t)] = basis_tile(t, wave, lon_count)

    if not few:

        for group in range(quads):
            wave = waves_of(ids, group)
            for t in range(basis.shape[1] // LANES):
                basis[16 * group : 16 * group + 16, tile_at(t)] = basis_tile(t, wave, lon_count)
    count = departed.shape[1] // LANES
    for ts in groups_of(count, INNER_AT_ONCE):
        group_of(ts)
    spread_rows(analysis, spread_analysis, band_rows)
    fourier_out[...] = jnp.concatenate(
        [add_up(None, basis, values, range(count)) for values in (departed, rim_departed)], axis=1
    )


def rim_kernel(
    arrived, own, basis, inner_fourier, fourier_out, windows, plans, departed, *, slices, levs
):
    lon_count = arrived.shape[1]
    rim, fields = RIM * slices, EDGE * slices
    out_row = lax.broadcasted_iota(jnp.int32, (fields, LANES), 0) // slices
    far_step = jnp.where(out_row < RIM, 2.0 * RIM, 0.0)
    near_step = jnp.where(out_row == RIM - 1, 2.0 * RIM - 1.0, jnp.where(out_row == RIM, 1.0, -2.0))
    lane = lax.broadcasted_iota(jnp.int32, (fields, LANES), 1) - REACH
    sublane = lax.broadcasted_iota(jnp.int32, (rim, LANES), 0)

    def part(source, lanes, row_step, lat_weight, lon_weight, step):
        west, east = [lane_gather(source, lane).astype(jnp.float32) for lane in lanes]
        row_weight = jnp.where(
            row_step == step,
            1.0 - lat_weight,
            jnp.where(row_step == step - 1.0, lat_weight, 0.0),
        )
        return row_weight * (west + lon_weight * (east - west))

    def prepare(t):
        for at, side in enumerate((arrived, own)):
            block = turned(side, t, lon_count).astype(jnp.float32)
            windows[t, rim * at : rim * (at + 1), :] = block[:rim]
            plans[t, 4 * RIM * at : 4 * RIM * (at + 1), :] = block[rim:]

    def finish(t):
        row_step, shift, lat_weight, lon_weight = [
            jnp.concatenate(
                [
                    jnp.where(
                        sublane < slices,
                        *[
                            jnp.broadcast_to(plans[t, row : row + 1, :], (rim, LANES))
                            for row in (start, start + 1)
                        ],
                    )
                    for start in (RIM * at, RIM * (at + 4))
                ],
                axis=0,
            )
            for at in range(4)
        ]
        west = lane + shift.astype(jnp.int32)
        lanes = [(column & LANES - 1).astype(jnp.int16) for column in (west, west + 1)]
        plan = lanes, row_step, lat_weight, lon_weight
        far = jnp.concatenate([windows[t, rim:, :], windows[t, 0:rim, :]], axis=0)
        near = jnp.concatenate([windows[t, slices : slices + rim, :]] * 2, axis=0)
        result = part(far.astype(jnp.bfloat16), *plan, far_step)
        result += part(near.astype(jnp.bfloat16), *plan, near_step)
        departed[:, tile_at(t)] = result.astype(jnp.bfloat16)

    count = basis.shape[1] // LANES
    for t in range(count):
        prepare(t)
    total = None
    for ts in groups_of(count, RIM_AT_ONCE):
        for t in ts:
            finish(t)
        total = add_up(total, basis, departed, ts)
    fourier = jnp.concatenate([inner_fourier[...], total], axis=1)
    for at in range(fourier_out.shape[0]):
        pair = at // levs
        fourier_out[at] = fourier[4 * pair : 4 * pair + 4].astype(jnp.bfloat16)


def legendre_kernel(
    first_wave, coeffs, spread_analysis, out, spread_coeffs, totals, blocks, *, levs, slices
):
    members, _, rows = coeffs.shape
    bands = members // levs
    col_count = spread_analysis.shape[1]
    width, shared = slots_of(rows // slices - EDGE)
    inner = width - 2 * EDGE
    lane = lax.broadcasted_iota(jnp.int32, (4 * levs, LANES), 1)
    slot, rank = lane // width, lane % width
    rim_rank = inner * slices + (rank - inner) * slices
    held_at = [
        jnp.where(rank < inner, f * inner + rank, rim_rank + f).astype(jnp.int16)
        for f in range(slices)
    ]
    slot = slot.astype(jnp.int16)
    for band in range(bands):
        for lev in range(levs):
            blocks[band, 4 * lev : 4 * lev + 4, 0:rows] = coeffs[band * levs + lev].astype(
                jnp.float32
            )
    for group in range(-(-bands // shared)):
        here = range(group * shared, min((group + 1) * shared, bands))
        taken = [blocks[band].astype(jnp.bfloat16) for band in here]
        for f in range(slices):
            joined = jnp.zeros(slot.shape, jnp.bfloat16)
            for at, block in enumerate(taken):
                joined = jnp.where(slot == jnp.int16(at), lane_gather(block, held_at[f]), joined)
            spread_coeffs[4 * levs * f : 4 * levs * (f + 1), tile_at(group)] = joined
    total = jnp.dot(
        spread_coeffs[...], spread_analysis[...], preferred_element_type=jnp.float32
    )
    for t in range(totals.shape[0]):
        cols = slice(t * LANES, min((t + 1) * LANES, col_count))
        width = cols.stop - cols.start
        totals[t, 0 : total.shape[0], 0:width] = total[:, cols]
        first = first_wave[0:2, cols] > 0.0
        for f in range(slices):
            for lev in range(levs):
                at = (f * levs + lev) * 4
                out[lev * slices + f, :, cols] = jnp.where(
                    first, totals[t, at : at + 2, 0:width], totals[t, at + 2 : at + 4, 0:width]
                )


def shards(grid, dep_row, dep_col, lat_frac, lon_frac, pair_ids, analysis):
    slices, band_rows, lon_count = grid.shape
    pairs = pair_ids.shape[0]
    col_count = analysis.shape[2]
    bands, levs = lax.axis_size("lat"), lax.axis_size("lev")
    inner = band_rows - 2 * RIM
    windows = -(-lon_count // SPAN)
    held_rows = -(-band_rows // 8) * 8
    fields = slices * EDGE
    spread_count = -(-bands // slots_of(band_rows)[1]) * LANES
    place = jnp.reshape(lax.axis_index(("lat", "lev")), (1,)).astype(jnp.int32)
    vmem = pl.BlockSpec(memory_space=pltpu.VMEM)
    smem = pl.BlockSpec(memory_space=pltpu.SMEM)
    params = pltpu.CompilerParams(vmem_limit_bytes=48 * 2**20)

    blank = jnp.zeros((windows, (band_rows + 2 * RIM) * slices, LANES), jnp.float32)
    by_row = grid.transpose(1, 0, 2)
    rim_shape = jax.ShapeDtypeStruct((RIM * (slices + 4), lon_count), jnp.bfloat16)
    sent_rim, wide_place, blank = pl.pallas_call(
        functools.partial(pack_kernel, levs=levs),
        out_shape=(
            rim_shape,
            jax.ShapeDtypeStruct((8, LANES), jnp.int32),
            jax.ShapeDtypeStruct(blank.shape, jnp.float32),
        ),
        in_specs=[smem] + [vmem] * 6,
        out_specs=(vmem,) * 3,
        input_output_aliases={6: 2},
        scratch_shapes=[
            pltpu.VMEM((lon_count // LANES, RIM * (slices + 4), LANES), jnp.float32)
        ],
        compiler_params=params,
    )(place, dep_row, dep_col, lat_frac, lon_frac, by_row[band_rows - RIM :], blank)
    arrived_rim = lax.ppermute(sent_rim, "lat", [(i, (i + 1) % bands) for i in range(bands)])

    inner_fourier, basis, spread_analysis, own_rim, first_wave, _ = pl.pallas_call(
        functools.partial(inner_kernel, slices=slices, levs=levs),
        out_shape=(
            jax.ShapeDtypeStruct((4 * pairs, slices * band_rows), jnp.float32),
            jax.ShapeDtypeStruct((4 * pairs, windows * LANES), jnp.bfloat16),
            jax.ShapeDtypeStruct((spread_count, col_count), jnp.bfloat16),
            rim_shape,
            jax.ShapeDtypeStruct((8, col_count), jnp.float32),
            jax.ShapeDtypeStruct(blank.shape, jnp.float32),
        ),
        in_specs=[vmem] * 10,
        out_specs=(vmem,) * 6,
        input_output_aliases={9: 5},
        scratch_shapes=[
            pltpu.VMEM((slices * inner, windows * LANES), jnp.bfloat16),
            pltpu.VMEM((fields, windows * LANES), jnp.bfloat16),
            pltpu.VMEM((2 * LANES, LANES), jnp.int16),
            pltpu.VMEM((band_rows * slices, lon_count), jnp.bfloat16),
            pltpu.VMEM((5, band_rows * slices, LANES), jnp.float32),
            pltpu.VMEM((5, 3, held_rows, LANES), jnp.float32),
            pltpu.VMEM((3 * inner, lon_count), jnp.bfloat16),
        ],
        compiler_params=params,
        cost_estimate=pl.CostEstimate(flops=100_000_000, bytes_accessed=2_000_000, transcendentals=0),
    )(
        by_row, dep_row, dep_col, lat_frac, lon_frac, sent_rim, wide_place, pair_ids[None, :],
        analysis[0], blank,
    )

    held_coeffs = slices * (band_rows + EDGE)
    fourier = pl.pallas_call(
        functools.partial(rim_kernel, slices=slices, levs=levs),
        out_shape=jax.ShapeDtypeStruct((bands * levs, 4, held_coeffs), jnp.bfloat16),
        in_specs=[vmem] * 4,
        out_specs=vmem,
        scratch_shapes=[
            pltpu.VMEM((windows, fields, LANES), jnp.float32),
            pltpu.VMEM((windows, 8 * RIM, LANES), jnp.float32),
            pltpu.VMEM((fields, windows * LANES), jnp.bfloat16),
        ],
        compiler_params=params,
    )(arrived_rim, own_rim, basis, inner_fourier)
    coeffs = lax.all_to_all(
        fourier, ("lat", "lev"), split_axis=0, concat_axis=0, tiled=True
    )
    out = pl.pallas_call(
        functools.partial(legendre_kernel, levs=levs, slices=slices),
        out_shape=jax.ShapeDtypeStruct((levs * slices, 2, col_count), jnp.float32),
        in_specs=[vmem] * 3,
        out_specs=vmem,
        scratch_shapes=[
            pltpu.VMEM((4 * levs * slices, spread_count), jnp.bfloat16),
            pltpu.VMEM((-(-col_count // LANES), 4 * levs * slices, LANES), jnp.float32),
            pltpu.VMEM((bands, 4 * levs, LANES), jnp.float32),
        ],
        compiler_params=params,
    )(first_wave, coeffs, spread_analysis)
    return out[None]


def solution(mesh):
    return jax.shard_map(
        shards,
        mesh=mesh,
        in_specs=(
            P("lev", "lat", None),
            P("lat", None),
            P("lat", None),
            P("lat", None),
            P("lat", None),
            P(),
            P("lat", None, "lev"),
        ),
        out_specs=P("lat", None, None, "lev"),
        check_vma=False,
    )
```
